32 devices in a mesh: dp: 8 (over y, x, core), tensor: 4 (over z).
Axes of the slice: x: 2, y: 2, z: 4, core: 2. Of those that a mesh axis runs over, the one named last changes fastest.
Arguments:
- inputs: bfloat16 [8192, 2048], P(('dp', 'tensor')), may hold values from -6 to 6
- gain_first: bfloat16 [2048], P('dp'), may hold values from 0.5 to 1.5
- shift_first: bfloat16 [2048], P('dp'), may hold values from -3 to 3
- projections: bfloat16 [3, 2048, 2048], P(None, 'dp', 'tensor'), may hold values from -0.125 to 0.125
- biases: bfloat16 [3, 2048], P(None, 'tensor'), may hold values from -3 to 3
- output_weight: bfloat16 [2048, 2048], P('tensor', 'dp'), may hold values from -0.5 to 0.5
- gain_second: bfloat16 [2048], P('dp'), may hold values from 0.5 to 1.5
- shift_second: bfloat16 [2048], P('dp'), may hold values from -3 to 3
- gate_up: bfloat16 [2, 2048, 5632], P(None, 'dp', 'tensor'), may hold values from -0.125 to 0.125
- down_weight: bfloat16 [5632, 2048], P('tensor', 'dp'), may hold values from -0.15625 to 0.15625
- cotangent: bfloat16 [8192, 2048], P(('dp', 'tensor')), may hold values from -6 to 6
Outputs:
- outputs: bfloat16 [8192, 2048], P(('dp', 'tensor'))
- input_grads: float32 [8192, 2048], P(('dp', 'tensor'))
- gain_first_grad: float32 [2048], P('dp')
- shift_first_grad: float32 [2048], P('dp')
- projections_grad: float32 [3, 2048, 2048], P(None, 'dp', 'tensor')
- biases_grad: float32 [3, 2048], P(None, 'tensor')
- output_weight_grad: float32 [2048, 2048], P('tensor', 'dp')
- gain_second_grad: float32 [2048], P('dp')
- shift_second_grad: float32 [2048], P('dp')
- gate_up_grad: float32 [2, 2048, 5632], P(None, 'dp', 'tensor')
- down_weight_grad: float32 [5632, 2048], P('tensor', 'dp')
The draws below stay inside these ranges and needn't reach their ends.
All inputs are finite; a program needn't handle non-finite values.
Results may differ from the reference program's by a relative error of at most 0.014.
Values may be sent and summed in bfloat16 or wider, within the bound.
A program may use at most 192 MiB of HBM per device.

```python
import math
import jax
import jax.numpy as jnp
from jax import lax

D = 2048
H = 32
HD = 64
ROTARY = 16
FF = 5632
SEQ_LEN = 512
TOKENS = 8192


def with_spikes(entries, stream_key, source, target, blocks, factor):
    def block_of(position):
        return (jnp.arange(entries.shape[position]) // (entries.shape[position] // blocks)).reshape((-1,) + (1,) * (entries.ndim - 1 - position))

    near = jax.random.permutation(stream_key, blocks)[block_of(target)]
    far = (block_of(target) + blocks // 2) % blocks
    return jnp.where((block_of(source) == near) | (block_of(source) == far), factor * entries, entries)


def shard_levels(stream_key, extent, cuts, low, top_value):
    def one(position, parts):
        heights = jax.random.uniform(jax.random.fold_in(jax.random.fold_in(stream_key, 6), position), (parts,), jnp.float32, low / len(cuts), top_value / len(cuts))
        return jnp.repeat(jnp.exp(heights), extent[position] // parts).reshape((-1,) + (1,) * (len(extent) - position - 1))

    loudness = one(*cuts[0])
    for cut in cuts[1:]:
        loudness = loudness * one(*cut)
    return loudness


def scatter_about(key, dims, spread, bound, cuts=(), held_as=jnp.bfloat16):
    level = shard_levels(key, dims, cuts, -0.22, 0.18) if cuts else 1.0
    values = jax.random.normal(key, dims, jnp.float32) * spread * level
    return jnp.minimum(jnp.maximum(values, -bound), bound).astype(held_as)


def noise_with(stream_key, extent, spread, limit, split, heavy, kind=jnp.bfloat16):
    values = spread * jax.random.normal(stream_key, extent, jnp.float32)
    if split:
        values = values * shard_levels(stream_key, extent, split, -0.22, 0.18)
    return jnp.clip(with_spikes(values, jax.random.fold_in(stream_key, 3), *heavy), -limit, limit).astype(kind)


def setup_inputs(seed: int = 0) -> dict:
    seeds = jax.random.split(jax.random.key(seed), 12)
    return {
        "inputs": scatter_about(seeds[0], (TOKENS, D), 1.0, 6.0, ((0, 32),)),
        "gain_first": jnp.clip(1.0 + 0.1 * jax.random.normal(seeds[1], (D,), jnp.float32), 0.5, 1.5).astype(jnp.bfloat16),
        "shift_first": scatter_about(seeds[2], (D,), 0.5, 3.0, ((0, 8),)),
        "projections": scatter_about(seeds[3], (3, D, H * HD), D ** -0.5, 0.125, ((1, 8), (2, 4))),
        "biases": scatter_about(seeds[4], (3, H * HD), 0.5, 3.0, ((1, 4),)),
        "output_weight": scatter_about(seeds[5], (H * HD, D), (H * HD // 16) ** -0.5, 0.5, ((0, 4), (1, 8))),
        "gain_second": jnp.clip(1.0 + 0.1 * jax.random.normal(seeds[6], (D,), jnp.float32), 0.5, 1.5).astype(jnp.bfloat16),
        "shift_second": scatter_about(seeds[7], (D,), 0.5, 3.0, ((0, 8),)),
        "gate_up": scatter_about(seeds[8], (2, D, FF), D ** -0.5, 0.125, ((1, 8), (2, 4))),
        "down_weight": scatter_about(seeds[9], (FF, D), (FF // 4) ** -0.5, 0.15625, ((0, 4), (1, 8))),
        "cotangent": noise_with(seeds[10], (TOKENS, D), 1.0, 6.0, ((0, 32),), (0, 1, 32, 2.75)),
    }


EPSILON = 1e-05
ANGLE_BASE = 10000.0
NEGATIVE = -1e+30
HIGHEST = lax.Precision.HIGHEST

@jax.custom_vjp
def low(v):
    return lax.optimization_barrier(v.astype(jnp.bfloat16)).astype(jnp.float32)

@jax.custom_vjp
def low_back(v):
    return v

def low_keep(v):
    return (low(v), None)

def low_pass(kept, grad):
    return (grad,)

def back_keep(v):
    return (v, None)

def back_low(kept, grad):
    return (low(grad),)
low.defvjp(low_keep, low_pass)
low_back.defvjp(back_keep, back_low)

def product(left, right):
    return jnp.dot(left, right, precision=HIGHEST, preferred_element_type=jnp.float32)

def norm_rows(rows, gain, shift):
    average = lax.optimization_barrier(jnp.mean(rows, axis=-1, keepdims=True))
    centred = rows - average
    inverse = lax.rsqrt(lax.optimization_barrier(jnp.mean(centred * centred, axis=-1, keepdims=True)) + EPSILON)
    return centred * inverse * gain + shift

def angle_tables():
    freqs = 1.0 / ANGLE_BASE ** (jnp.arange(0, ROTARY, 2).astype(jnp.float32) / ROTARY)
    angles = jnp.arange(SEQ_LEN).astype(jnp.float32)[:, None] * freqs[None, :]
    return (jnp.cos(angles), jnp.sin(angles))

def rotate(heads, cosine, sine, sign):
    half_rot = ROTARY // 2
    first = heads[..., :half_rot]
    latter = heads[..., half_rot:ROTARY]
    cos_part = cosine[:, None, :]
    sin_part = sine[:, None, :] * sign
    return jnp.concatenate([first * cos_part - latter * sin_part, latter * cos_part + first * sin_part, heads[..., ROTARY:]], axis=-1)

def attend_one(pieces):
    queries, key_rows, value_rows = pieces
    scaling = 1.0 / math.sqrt(HD)
    scores = low_back(scaling * jnp.einsum('qhd,khd->hqk', queries, key_rows, precision=HIGHEST))
    causal = jnp.arange(SEQ_LEN)[:, None] >= jnp.arange(SEQ_LEN)[None, :]
    scores = jnp.where(causal[None], scores, NEGATIVE)
    exponent = jnp.exp(scores - lax.optimization_barrier(jnp.max(scores, axis=-1, keepdims=True)))
    weights = low(exponent / lax.optimization_barrier(jnp.sum(exponent, axis=-1, keepdims=True)))
    return jnp.einsum('hqk,khd->qhd', weights, value_rows, precision=HIGHEST)

def layer(inputs, gain_first, shift_first, projections, biases, output_weight, gain_second, shift_second, gate_up, down_weight):
    token_count = inputs.shape[0]
    sequences = token_count // SEQ_LEN
    head_shape = (sequences, SEQ_LEN, H, HD)
    normed = low(norm_rows(inputs, gain_first, shift_first))
    cosine, sine = angle_tables()
    pre_query = low_back(product(normed, projections[0]) + biases[0])
    pre_key = low_back(product(normed, projections[1]) + biases[1])
    pre_value = low_back(product(normed, projections[2]) + biases[2])
    queries = low(rotate(pre_query.reshape(head_shape), cosine, sine, 1.0))
    key_rows = low(rotate(pre_key.reshape(head_shape), cosine, sine, 1.0))
    value_rows = low(pre_value.reshape(head_shape))
    mixed = lax.map(jax.checkpoint(attend_one), (queries, key_rows, value_rows))
    mixed = low(low_back(mixed.reshape(token_count, H * HD)))
    middle = inputs + low_back(product(mixed, output_weight))
    second = low(norm_rows(middle, gain_second, shift_second))
    gate_act = low_back(product(second, gate_up[0]))
    up_act = low_back(product(second, gate_up[1]))
    hidden = low(gate_act * jax.nn.sigmoid(gate_act) * up_act)
    return middle + low_back(product(hidden, down_weight))

def reference(inputs, gain_first, shift_first, projections, biases, output_weight, gain_second, shift_second, gate_up, down_weight, cotangent):
    params = tuple((array.astype(jnp.float32) for array in (gain_first, shift_first, projections, biases, output_weight, gain_second, shift_second, gate_up, down_weight)))
    block_rows = math.gcd(TOKENS // SEQ_LEN, 8) * SEQ_LEN
    block_count = TOKENS // block_rows
    input_blocks = inputs.astype(jnp.float32).reshape(block_count, block_rows, D)
    cot_blocks = cotangent.astype(jnp.float32).reshape(block_count, block_rows, D)

    def one_block(totals, pieces):
        rows_in, rows_cot = pieces

        def whole_layer(rows, gfirst, sfirst, projs, bvec, wout, gsecond, ssecond, wgu, wdown):
            return layer(rows, gfirst, sfirst, projs, bvec, wout, gsecond, ssecond, wgu, wdown)
        result, pullback = jax.vjp(whole_layer, rows_in, params[0], params[1], params[2], params[3], params[4], params[5], params[6], params[7], params[8])
        grads = pullback(rows_cot)
        totals = tuple((total + grad for total, grad in zip(totals, grads[1:])))
        return (totals, (result.astype(jnp.bfloat16), grads[0]))
    zeros = tuple((jnp.zeros_like(array) for array in params))
    totals, (results, input_grads) = lax.scan(one_block, zeros, (input_blocks, cot_blocks))
    return (results.reshape(TOKENS, D), input_grads.reshape(TOKENS, D), totals[0], totals[1], totals[2], totals[3], totals[4], totals[5], totals[6], totals[7], totals[8])
```

```python
import math

import jax
import jax.numpy as jnp
from jax import lax
from jax.sharding import PartitionSpec as P

HD = 64
ROTARY = 16
SEQ_LEN = 512


EPSILON = 1e-05
ANGLE_BASE = 10000.0
NEGATIVE = -1e30


def norm_rows(rows, gain, shift):
    average = jnp.mean(rows, axis=-1, keepdims=True)
    centred = rows - average
    inverse = lax.rsqrt(jnp.mean(centred * centred, axis=-1, keepdims=True) + EPSILON)
    unit_rows = centred * inverse
    return (unit_rows * gain + shift, unit_rows, inverse)


def norm_back(incoming, unit_rows, inverse, gain):
    scaled = incoming * gain
    inner = (
        scaled
        - jnp.mean(scaled, axis=-1, keepdims=True)
        - unit_rows * jnp.mean(scaled * unit_rows, axis=-1, keepdims=True)
    )
    return (inner * inverse, jnp.sum(incoming * unit_rows, axis=0), jnp.sum(incoming, axis=0))


def angle_tables():
    freqs = 1.0 / ANGLE_BASE ** (jnp.arange(0, ROTARY, 2).astype(jnp.float32) / ROTARY)
    angles = jnp.arange(SEQ_LEN).astype(jnp.float32)[:, None] * freqs[None, :]
    return (jnp.cos(angles), jnp.sin(angles))


def rotate(heads, cosine, sine, sign):
    half_rot = ROTARY // 2
    first = heads[..., :half_rot]
    latter = heads[..., half_rot:ROTARY]
    cos_part = cosine[:, None, :]
    sin_part = sine[:, None, :] * sign
    return jnp.concatenate(
        [
            first * cos_part - latter * sin_part,
            latter * cos_part + first * sin_part,
            heads[..., ROTARY:],
        ],
        axis=-1,
    )


def causal_scores(queries, key_rows):
    scaling = 1.0 / math.sqrt(HD)
    scores = scaling * jnp.einsum(
        "qhd,khd->hqk", queries, key_rows, preferred_element_type=jnp.float32
    )
    causal = jnp.arange(SEQ_LEN)[:, None] >= jnp.arange(SEQ_LEN)[None, :]
    return jnp.where(causal[None], scores, NEGATIVE)


def attend_forward(pieces):
    queries, key_rows, value_rows = pieces
    scores = causal_scores(queries, key_rows)
    row_top = jnp.max(scores, axis=-1, keepdims=True)
    exponent = jnp.exp(scores - row_top)
    totals = jnp.sum(exponent, axis=-1, keepdims=True)
    weights = (exponent / totals).astype(jnp.bfloat16)
    mixed = jnp.einsum("hqk,khd->qhd", weights, value_rows, preferred_element_type=jnp.float32)
    return (mixed.astype(jnp.bfloat16), (row_top + jnp.log(totals))[..., 0])


def attend_back(pieces):
    queries, key_rows, value_rows, grad_mixed, log_totals = pieces
    scaling = 1.0 / math.sqrt(HD)
    scores = causal_scores(queries, key_rows)
    weights = jnp.exp(scores - log_totals[..., None])
    grad_values = jnp.einsum(
        "hqk,qhd->khd", weights.astype(jnp.bfloat16), grad_mixed, preferred_element_type=jnp.float32
    )
    grad_weights = jnp.einsum(
        "qhd,khd->hqk", grad_mixed, value_rows, preferred_element_type=jnp.float32
    )
    grad_scores = weights * (grad_weights - jnp.sum(weights * grad_weights, axis=-1, keepdims=True))
    grad_scores = grad_scores.astype(jnp.bfloat16)
    grad_queries = scaling * jnp.einsum(
        "hqk,khd->qhd", grad_scores, key_rows, preferred_element_type=jnp.float32
    )
    grad_keys = scaling * jnp.einsum(
        "hqk,qhd->khd", grad_scores, queries, preferred_element_type=jnp.float32
    )
    return (grad_queries, grad_keys, grad_values)


def scatter_sum(terms, axis, dimension):
    owned = lax.psum_scatter(
        terms.astype(jnp.bfloat16), axis, scatter_dimension=dimension, tiled=True
    )
    return owned.astype(jnp.float32)


def local(
    inputs,
    gain_first,
    shift_first,
    projections,
    biases,
    output_weight,
    gain_second,
    shift_second,
    gate_up,
    down_weight,
    cotangent,
):
    tensor_ways = lax.axis_size("tensor")
    row_count = inputs.shape[0]
    group_rows = row_count * tensor_ways
    sequences = group_rows // SEQ_LEN
    head_width = output_weight.shape[0]
    local_heads = head_width // HD
    head_shape = (sequences, SEQ_LEN, local_heads, HD)
    cosine, sine = angle_tables()
    proj_full, out_full, gain_one, shift_one = (
        lax.all_gather(projections, "dp", axis=1, tiled=True),
        lax.all_gather(output_weight, "dp", axis=1, tiled=True),
        lax.all_gather(gain_first, "dp", axis=0, tiled=True),
        lax.all_gather(shift_first, "dp", axis=0, tiled=True),
    )
    gain_one = gain_one.astype(jnp.float32)
    residual = inputs.astype(jnp.float32)
    normed_one, unit_one, inverse_one = norm_rows(residual, gain_one, shift_one.astype(jnp.float32))
    gathered_one = lax.all_gather(normed_one.astype(jnp.bfloat16), "tensor", axis=0, tiled=True)
    pre_all = jnp.einsum("gd,jde->jge", gathered_one, proj_full, preferred_element_type=jnp.float32)
    pre_all = pre_all + biases.astype(jnp.float32)[:, None, :]
    queries = rotate(pre_all[0].reshape(head_shape), cosine, sine, 1.0).astype(jnp.bfloat16)
    key_rows = rotate(pre_all[1].reshape(head_shape), cosine, sine, 1.0).astype(jnp.bfloat16)
    value_rows = pre_all[2].reshape(head_shape).astype(jnp.bfloat16)
    mixed, log_totals = lax.map(attend_forward, (queries, key_rows, value_rows))
    mixed_rows = mixed.reshape(group_rows, head_width)
    part = mixed_rows
    middle = residual + scatter_sum(
        jnp.dot(part, out_full, preferred_element_type=jnp.float32), "tensor", 0
    )
    gu_full, down_full, gain_two, shift_two = (
        lax.all_gather(gate_up, "dp", axis=1, tiled=True),
        lax.all_gather(down_weight, "dp", axis=1, tiled=True),
        lax.all_gather(gain_second, "dp", axis=0, tiled=True),
        lax.all_gather(shift_second, "dp", axis=0, tiled=True),
    )
    gain_two = gain_two.astype(jnp.float32)
    normed_two, unit_two, inverse_two = norm_rows(middle, gain_two, shift_two.astype(jnp.float32))
    gathered_two = lax.all_gather(normed_two.astype(jnp.bfloat16), "tensor", axis=0, tiled=True)
    gate_act = jnp.dot(gathered_two, gu_full[0], preferred_element_type=jnp.float32)
    up_act = jnp.dot(gathered_two, gu_full[1], preferred_element_type=jnp.float32)
    sigmoid_gate = jax.nn.sigmoid(gate_act)
    hidden = (gate_act * sigmoid_gate * up_act).astype(jnp.bfloat16)
    part = hidden
    outputs = (
        middle
        + scatter_sum(jnp.dot(part, down_full, preferred_element_type=jnp.float32), "tensor", 0)
    ).astype(jnp.bfloat16)
    gu_back, down_back, gain_two_back = (
        lax.all_gather(gate_up, "dp", axis=1, tiled=True),
        lax.all_gather(down_weight, "dp", axis=1, tiled=True),
        lax.all_gather(gain_second, "dp", axis=0, tiled=True),
    )
    gain_two_back = gain_two_back.astype(jnp.float32)
    gathered_cot = lax.all_gather(cotangent, "tensor", axis=0, tiled=True)
    grad_hidden = jnp.einsum(
        "gd,fd->gf", gathered_cot, down_back, preferred_element_type=jnp.float32
    )
    down_grad = jnp.einsum("gf,gd->fd", hidden, gathered_cot, preferred_element_type=jnp.float32)
    grad_up = (grad_hidden * gate_act * sigmoid_gate).astype(jnp.bfloat16)
    grad_gate = (
        grad_hidden * up_act * sigmoid_gate * (1.0 + gate_act * (1.0 - sigmoid_gate))
    ).astype(jnp.bfloat16)
    gu_grad = jnp.stack(
        [
            jnp.einsum("gd,gf->df", gathered_two, grad_gate, preferred_element_type=jnp.float32),
            jnp.einsum("gd,gf->df", gathered_two, grad_up, preferred_element_type=jnp.float32),
        ]
    )
    first_term = jnp.einsum("gf,df->gd", grad_gate, gu_back[0], preferred_element_type=jnp.float32)
    grad_second = scatter_sum(
        first_term
        + jnp.einsum("gf,df->gd", grad_up, gu_back[1], preferred_element_type=jnp.float32),
        "tensor",
        0,
    )
    gu_owned, down_owned = (
        scatter_sum(gu_grad, "dp", 1),
        scatter_sum(down_grad, "dp", 1),
    )
    grad_mid_norm, gain_two_part, shift_two_part = norm_back(
        grad_second, unit_two, inverse_two, gain_two_back
    )
    grad_middle = cotangent.astype(jnp.float32) + grad_mid_norm
    proj_back, out_back, gain_one_back = (
        lax.all_gather(projections, "dp", axis=1, tiled=True),
        lax.all_gather(output_weight, "dp", axis=1, tiled=True),
        lax.all_gather(gain_first, "dp", axis=0, tiled=True),
    )
    gain_one_back = gain_one_back.astype(jnp.float32)
    gathered_branch = lax.all_gather(grad_middle.astype(jnp.bfloat16), "tensor", axis=0, tiled=True)
    out_grad = jnp.einsum(
        "ge,gd->ed", mixed_rows, gathered_branch, preferred_element_type=jnp.float32
    )
    grad_mixed = jnp.einsum(
        "gd,ed->ge", gathered_branch, out_back, preferred_element_type=jnp.float32
    ).astype(jnp.bfloat16)
    grad_queries, grad_keys, grad_values = lax.map(
        attend_back, (queries, key_rows, value_rows, grad_mixed.reshape(head_shape), log_totals)
    )
    grad_queries = rotate(grad_queries, cosine, sine, -1.0)
    grad_keys = rotate(grad_keys, cosine, sine, -1.0)
    grad_pre = (
        jnp.stack([grad_queries, grad_keys, grad_values])
        .reshape(3, group_rows, head_width)
        .astype(jnp.bfloat16)
    )
    bias_part = jnp.sum(grad_pre, axis=1, dtype=jnp.float32)
    proj_grad = jnp.einsum(
        "gd,jge->jde", gathered_one, grad_pre, preferred_element_type=jnp.float32
    )
    part = grad_pre
    grad_normed = scatter_sum(
        jnp.einsum("jge,jde->gd", part, proj_back, preferred_element_type=jnp.float32),
        "tensor",
        0,
    )
    proj_owned, out_owned = (
        scatter_sum(proj_grad, "dp", 1),
        scatter_sum(out_grad, "dp", 1),
    )
    grad_in_norm, gain_one_part, shift_one_part = norm_back(
        grad_normed, unit_one, inverse_one, gain_one_back
    )
    input_grads = grad_middle + grad_in_norm
    one_hot = (jnp.arange(tensor_ways) == lax.axis_index("tensor")).astype(jnp.float32)
    spread_bias = (bias_part[:, None, :] * one_hot[None, :, None]).reshape(
        3, tensor_ways * head_width
    )
    summed = lax.psum(
        (gain_one_part, shift_one_part, gain_two_part, shift_two_part, spread_bias),
        ("dp", "tensor"),
    )
    own_width = gain_first.shape[0]
    own_offset = lax.axis_index("dp") * own_width

    def own_part(vector):
        return lax.dynamic_slice_in_dim(vector, own_offset, own_width, 0)

    bias_grad = jnp.sum(
        summed[4].reshape(3, tensor_ways, head_width) * one_hot[None, :, None], axis=1
    )
    return (
        outputs,
        input_grads,
        own_part(summed[0]),
        own_part(summed[1]),
        proj_owned,
        bias_grad,
        out_owned,
        own_part(summed[2]),
        own_part(summed[3]),
        gu_owned,
        down_owned,
    )


def solution(mesh):
    return jax.shard_map(
        local,
        mesh=mesh,
        in_specs=(
            P(("dp", "tensor"), None),
            P("dp"),
            P("dp"),
            P(None, "dp", "tensor"),
            P(None, "tensor"),
            P("tensor", "dp"),
            P("dp"),
            P("dp"),
            P(None, "dp", "tensor"),
            P("tensor", "dp"),
            P(("dp", "tensor"), None),
        ),
        out_specs=(
            P(("dp", "tensor"), None),
            P(("dp", "tensor"), None),
            P("dp"),
            P("dp"),
            P(None, "dp", "tensor"),
            P(None, "tensor"),
            P("tensor", "dp"),
            P("dp"),
            P("dp"),
            P(None, "dp", "tensor"),
            P("tensor", "dp"),
        ),
        check_vma=False,
    )
```

```python
import math

import jax
import jax.numpy as jnp
from jax import lax
from jax.sharding import PartitionSpec as P

HD = 64
ROTARY = 16
SEQ_LEN = 512


EPSILON = 1e-05
ANGLE_BASE = 10000.0
NEGATIVE = -1e30


def norm_rows(rows, gain, shift):
    average = jnp.mean(rows, axis=-1, keepdims=True)
    centred = rows - average
    inverse = lax.rsqrt(jnp.mean(centred * centred, axis=-1, keepdims=True) + EPSILON)
    unit_rows = centred * inverse
    return (unit_rows * gain + shift, unit_rows, inverse)


def norm_back(incoming, unit_rows, inverse, gain):
    scaled = incoming * gain
    inner = (
        scaled
        - jnp.mean(scaled, axis=-1, keepdims=True)
        - unit_rows * jnp.mean(scaled * unit_rows, axis=-1, keepdims=True)
    )
    return (inner * inverse, jnp.sum(incoming * unit_rows, axis=0), jnp.sum(incoming, axis=0))


def angle_tables():
    freqs = 1.0 / ANGLE_BASE ** (jnp.arange(0, ROTARY, 2).astype(jnp.float32) / ROTARY)
    angles = jnp.arange(SEQ_LEN).astype(jnp.float32)[:, None] * freqs[None, :]
    return (jnp.cos(angles), jnp.sin(angles))


def rotate(heads, cosine, sine, sign):
    half_rot = ROTARY // 2
    first = heads[..., :half_rot]
    latter = heads[..., half_rot:ROTARY]
    cos_part = cosine[:, None, :]
    sin_part = sine[:, None, :] * sign
    return jnp.concatenate(
        [
            first * cos_part - latter * sin_part,
            latter * cos_part + first * sin_part,
            heads[..., ROTARY:],
        ],
        axis=-1,
    )


def causal_scores(queries, key_rows, positions):
    scaling = 1.0 / math.sqrt(HD)
    scores = scaling * jnp.einsum(
        "qhd,khd->hqk", queries, key_rows, preferred_element_type=jnp.float32
    )
    causal = positions[:, None] >= positions[None, :]
    return jnp.where(causal[None], scores, NEGATIVE)


def attend_forward(pieces, positions):
    queries, key_rows, value_rows = pieces
    scores = causal_scores(queries, key_rows, positions)
    row_top = jnp.max(scores, axis=-1, keepdims=True)
    exponent = jnp.exp(scores - row_top)
    totals = jnp.sum(exponent, axis=-1, keepdims=True)
    weights = (exponent / totals).astype(jnp.bfloat16)
    mixed = jnp.einsum("hqk,khd->qhd", weights, value_rows, preferred_element_type=jnp.float32)
    return (mixed.astype(jnp.bfloat16), (row_top + jnp.log(totals))[..., 0])


def attend_back(pieces, positions):
    queries, key_rows, value_rows, grad_mixed, log_totals = pieces
    scaling = 1.0 / math.sqrt(HD)
    scores = causal_scores(queries, key_rows, positions)
    weights = jnp.exp(scores - log_totals[..., None])
    grad_values = jnp.einsum(
        "hqk,qhd->khd", weights.astype(jnp.bfloat16), grad_mixed, preferred_element_type=jnp.float32
    )
    grad_weights = jnp.einsum(
        "qhd,khd->hqk", grad_mixed, value_rows, preferred_element_type=jnp.float32
    )
    grad_scores = weights * (grad_weights - jnp.sum(weights * grad_weights, axis=-1, keepdims=True))
    grad_scores = grad_scores.astype(jnp.bfloat16)
    grad_queries = scaling * jnp.einsum(
        "hqk,khd->qhd", grad_scores, key_rows, preferred_element_type=jnp.float32
    )
    grad_keys = scaling * jnp.einsum(
        "hqk,qhd->khd", grad_scores, queries, preferred_element_type=jnp.float32
    )
    return (grad_queries, grad_keys, grad_values)


def scatter_sum(terms, axis, dimension):
    owned = lax.psum_scatter(
        terms.astype(jnp.bfloat16), axis, scatter_dimension=dimension, tiled=True
    )
    return owned.astype(jnp.float32)


def local(
    inputs,
    gain_first,
    shift_first,
    projections,
    biases,
    output_weight,
    gain_second,
    shift_second,
    gate_up,
    down_weight,
    cotangent,
):
    tensor_ways = lax.axis_size("tensor")
    row_count = inputs.shape[0]
    group_rows = row_count * tensor_ways
    sequences = group_rows // SEQ_LEN
    head_width = output_weight.shape[0]
    local_heads = head_width // HD
    head_shape = (sequences, SEQ_LEN, local_heads, HD)
    cosine, sine = angle_tables()
    positions = jnp.arange(SEQ_LEN)
    proj_full, out_full, gain_one, shift_one = (
        lax.all_gather(projections, "dp", axis=1, tiled=True),
        lax.all_gather(output_weight, "dp", axis=1, tiled=True),
        lax.all_gather(gain_first, "dp", axis=0, tiled=True),
        lax.all_gather(shift_first, "dp", axis=0, tiled=True),
    )
    gain_one = gain_one.astype(jnp.float32)
    residual = inputs.astype(jnp.float32)
    normed_one, unit_one, inverse_one = norm_rows(residual, gain_one, shift_one.astype(jnp.float32))
    gathered_one = lax.all_gather(normed_one.astype(jnp.bfloat16), "tensor", axis=0, tiled=True)
    pre_all = jnp.einsum("gd,jde->jge", gathered_one, proj_full, preferred_element_type=jnp.float32)
    pre_all = pre_all + biases.astype(jnp.float32)[:, None, :]
    queries = rotate(pre_all[0].reshape(head_shape), cosine, sine, 1.0).astype(jnp.bfloat16)
    key_rows = rotate(pre_all[1].reshape(head_shape), cosine, sine, 1.0).astype(jnp.bfloat16)
    value_rows = pre_all[2].reshape(head_shape).astype(jnp.bfloat16)
    mixed, log_totals = lax.map(
        lambda pieces: attend_forward(pieces, positions), (queries, key_rows, value_rows)
    )
    mixed_rows = mixed.reshape(group_rows, head_width)
    part = mixed_rows
    middle = residual + scatter_sum(
        jnp.dot(part, out_full, preferred_element_type=jnp.float32), "tensor", 0
    )
    gu_full, down_full, gain_two, shift_two = (
        lax.all_gather(gate_up, "dp", axis=1, tiled=True),
        lax.all_gather(down_weight, "dp", axis=1, tiled=True),
        lax.all_gather(gain_second, "dp", axis=0, tiled=True),
        lax.all_gather(shift_second, "dp", axis=0, tiled=True),
    )
    gain_two = gain_two.astype(jnp.float32)
    normed_two, unit_two, inverse_two = norm_rows(middle, gain_two, shift_two.astype(jnp.float32))
    gathered_two = lax.all_gather(normed_two.astype(jnp.bfloat16), "tensor", axis=0, tiled=True)
    gate_act = jnp.dot(gathered_two, gu_full[0], preferred_element_type=jnp.float32)
    up_act = jnp.dot(gathered_two, gu_full[1], preferred_element_type=jnp.float32)
    sigmoid_gate = jax.nn.sigmoid(gate_act)
    hidden = (gate_act * sigmoid_gate * up_act).astype(jnp.bfloat16)
    part = hidden
    outputs = (
        middle
        + scatter_sum(jnp.dot(part, down_full, preferred_element_type=jnp.float32), "tensor", 0)
    ).astype(jnp.bfloat16)
    gu_back, down_back, gain_two_back = (
        lax.all_gather(gate_up, "dp", axis=1, tiled=True),
        lax.all_gather(down_weight, "dp", axis=1, tiled=True),
        lax.all_gather(gain_second, "dp", axis=0, tiled=True),
    )
    gain_two_back = gain_two_back.astype(jnp.float32)
    gathered_cot = lax.all_gather(cotangent, "tensor", axis=0, tiled=True)
    grad_hidden = jnp.einsum(
        "gd,fd->gf", gathered_cot, down_back, preferred_element_type=jnp.float32
    )
    down_grad = jnp.einsum("gf,gd->fd", hidden, gathered_cot, preferred_element_type=jnp.float32)
    grad_up = (grad_hidden * gate_act * sigmoid_gate).astype(jnp.bfloat16)
    grad_gate = (
        grad_hidden * up_act * sigmoid_gate * (1.0 + gate_act * (1.0 - sigmoid_gate))
    ).astype(jnp.bfloat16)
    gu_grad = jnp.stack(
        [
            jnp.einsum("gd,gf->df", gathered_two, grad_gate, preferred_element_type=jnp.float32),
            jnp.einsum("gd,gf->df", gathered_two, grad_up, preferred_element_type=jnp.float32),
        ]
    )
    first_term = jnp.einsum("gf,df->gd", grad_gate, gu_back[0], preferred_element_type=jnp.float32)
    grad_second = scatter_sum(
        first_term
        + jnp.einsum("gf,df->gd", grad_up, gu_back[1], preferred_element_type=jnp.float32),
        "tensor",
        0,
    )
    gu_owned, down_owned = (
        scatter_sum(gu_grad, "dp", 1),
        scatter_sum(down_grad, "dp", 1),
    )
    grad_mid_norm, gain_two_part, shift_two_part = norm_back(
        grad_second, unit_two, inverse_two, gain_two_back
    )
    grad_middle = cotangent.astype(jnp.float32) + grad_mid_norm
    proj_back, out_back, gain_one_back = (
        lax.all_gather(projections, "dp", axis=1, tiled=True),
        lax.all_gather(output_weight, "dp", axis=1, tiled=True),
        lax.all_gather(gain_first, "dp", axis=0, tiled=True),
    )
    gain_one_back = gain_one_back.astype(jnp.float32)
    gathered_branch = lax.all_gather(grad_middle.astype(jnp.bfloat16), "tensor", axis=0, tiled=True)
    out_grad = jnp.einsum(
        "ge,gd->ed", mixed_rows, gathered_branch, preferred_element_type=jnp.float32
    )
    grad_mixed = jnp.einsum(
        "gd,ed->ge", gathered_branch, out_back, preferred_element_type=jnp.float32
    ).astype(jnp.bfloat16)
    grad_queries, grad_keys, grad_values = lax.map(
        lambda pieces: attend_back(pieces, positions),
        (queries, key_rows, value_rows, grad_mixed.reshape(head_shape), log_totals),
    )
    grad_queries = rotate(grad_queries, cosine, sine, -1.0)
    grad_keys = rotate(grad_keys, cosine, sine, -1.0)
    grad_pre = (
        jnp.stack([grad_queries, grad_keys, grad_values])
        .reshape(3, group_rows, head_width)
        .astype(jnp.bfloat16)
    )
    bias_part = jnp.sum(grad_pre, axis=1, dtype=jnp.float32)
    proj_grad = jnp.einsum(
        "gd,jge->jde", gathered_one, grad_pre, preferred_element_type=jnp.float32
    )
    part = grad_pre
    grad_normed = scatter_sum(
        jnp.einsum("jge,jde->gd", part, proj_back, preferred_element_type=jnp.float32),
        "tensor",
        0,
    )
    proj_owned, out_owned = (
        scatter_sum(proj_grad, "dp", 1),
        scatter_sum(out_grad, "dp", 1),
    )
    grad_in_norm, gain_one_part, shift_one_part = norm_back(
        grad_normed, unit_one, inverse_one, gain_one_back
    )
    input_grads = grad_middle + grad_in_norm
    one_hot = (jnp.arange(tensor_ways) == lax.axis_index("tensor")).astype(jnp.float32)
    spread_bias = (bias_part[:, None, :] * one_hot[None, :, None]).reshape(
        3, tensor_ways * head_width
    )
    summed = lax.psum(
        (gain_one_part, shift_one_part, gain_two_part, shift_two_part, spread_bias),
        ("dp", "tensor"),
    )
    own_width = gain_first.shape[0]
    own_offset = lax.axis_index("dp") * own_width

    def own_part(vector):
        return lax.dynamic_slice_in_dim(vector, own_offset, own_width, 0)

    bias_grad = jnp.sum(
        summed[4].reshape(3, tensor_ways, head_width) * one_hot[None, :, None], axis=1
    )
    return (
        outputs,
        input_grads,
        own_part(summed[0]),
        own_part(summed[1]),
        proj_owned,
        bias_grad,
        out_owned,
        own_part(summed[2]),
        own_part(summed[3]),
        gu_owned,
        down_owned,
    )


def swap(array, dp_bit, tensor_bit):
    dp_ways, tensor_ways = lax.axis_size("dp"), lax.axis_size("tensor")
    pairs = [
        (d * tensor_ways + t, (d ^ dp_bit) * tensor_ways + (t ^ tensor_bit))
        for d in range(dp_ways)
        for t in range(tensor_ways)
    ]
    return lax.ppermute(array, ("dp", "tensor"), pairs)


def send_between(array, routes):
    tensor_ways = lax.axis_size("tensor")
    pairs = [(d * tensor_ways + t, e * tensor_ways + s) for (d, t), (e, s) in routes]
    return lax.ppermute(array, ("dp", "tensor"), pairs)


CORE, X_BIT, Y_BIT = 1, 2, 4


def places():
    return [(d, t) for d in range(lax.axis_size("dp")) for t in range(lax.axis_size("tensor"))]


def own_quarter(array):
    return send_between(
        array,
        [((d, t), (d ^ 1, t) if d & 1 else (d ^ 1, t ^ 2)) for d, t in places()],
    )


def far_quarter(array):
    return send_between(array, [((d, t), (d, t ^ 2)) for d, t in places() if d & 1])


def quarter_home(array):
    return send_between(
        array,
        [((d ^ 1, t) if d & 1 else (d ^ 1, t ^ 2), (d, t)) for d, t in places()],
    )


def gather_weight(shard, axis, first_core):
    near = own_quarter(shard)
    far = far_quarter(shard)
    even = jnp.where(first_core, shard, near)
    odd = jnp.where(first_core, near, far)
    even_x, odd_y = swap(even, X_BIT, 0), swap(odd, Y_BIT, 0)
    even_y, odd_x = swap(even, Y_BIT, 0), swap(odd, X_BIT, 0)
    even_xy, odd_xy = swap(even_x, Y_BIT, 0), swap(odd_y, X_BIT, 0)
    return jnp.concatenate([even_y, even_xy, odd_x, odd_xy, even, even_x, odd, odd_y], axis=axis)


def scatter_weight(part, axis, first_core):
    send_even = part(0).astype(jnp.bfloat16)
    got_even = swap(send_even, Y_BIT, 0)
    send_odd = part(1).astype(jnp.bfloat16)
    got_odd = swap(send_odd, X_BIT, 0)
    keep_even = part(2).astype(jnp.bfloat16)
    keep_odd = part(3).astype(jnp.bfloat16)

    def halves(array):
        return [h.astype(jnp.float32) for h in jnp.split(array, 2, axis=axis)]

    even_here, even_there = [a + b for a, b in zip(halves(keep_even), halves(got_even))]
    odd_here, odd_there = [a + b for a, b in zip(halves(keep_odd), halves(got_odd))]
    even_last = swap(even_there.astype(jnp.bfloat16), X_BIT, 0)
    odd_last = swap(odd_there.astype(jnp.bfloat16), Y_BIT, 0)
    even_sum = even_here + even_last.astype(jnp.float32)
    odd_sum = odd_here + odd_last.astype(jnp.float32)
    return home_sum(even_sum, odd_sum, first_core)


def home_sum(even_sum, odd_sum, first_core):
    odd_out = odd_sum.astype(jnp.bfloat16)
    crossing = quarter_home(jnp.where(first_core, odd_out, even_sum.astype(jnp.bfloat16)))
    far = far_quarter(odd_out)
    return jnp.where(first_core, even_sum, far.astype(jnp.float32)) + crossing.astype(jnp.float32)


def gather_rows(own):
    beside = swap(own, 0, 1)
    sibling = swap(own, CORE, 0)
    return jnp.concatenate([own, beside, sibling, swap(beside, CORE, 0)], axis=0)


def scatter_rows(product, rows):
    count = rows // 4
    far = product(slice(2 * count, rows)).astype(jnp.bfloat16)
    got = swap(far, CORE, 0).astype(jnp.float32)
    near = product(slice(0, 2 * count))
    beside = (near[count:] + got[count:]).astype(jnp.bfloat16)
    return near[:count] + got[:count] + swap(beside, 0, 1).astype(jnp.float32)


ORDER = ((1, 0, 0), (1, 1, 0), (0, 1, 1), (1, 1, 1), (0, 0, 0), (0, 1, 0), (0, 0, 1), (1, 0, 1))


def flip(array, y_here, x_here, axis):
    array = jnp.where(x_here, jnp.flip(array, axis + 1), array)
    return jnp.where(y_here, jnp.flip(array, axis), array)


def to_local(array, y_here, x_here):
    lead, width = array.shape[:-1], array.shape[-1]
    k = len(lead)
    blocks = flip(array.reshape(*lead, 2, 2, 2, width // 8), y_here, x_here, k)
    return jnp.concatenate([blocks[..., a, b, c, :] for a, b, c in ORDER], axis=-1)


def from_local(array, y_here, x_here):
    lead, width = array.shape[:-1], array.shape[-1]
    pieces = dict(zip(ORDER, jnp.split(array, 8, axis=-1)))
    natural = jnp.concatenate([pieces[key] for key in sorted(pieces)], axis=-1)
    blocks = flip(natural.reshape(*lead, 2, 2, 2, width // 8), y_here, x_here, len(lead))
    return blocks.reshape(*lead, width)


def local_pairs(
    inputs,
    gain_first,
    shift_first,
    projections,
    biases,
    output_weight,
    gain_second,
    shift_second,
    gate_up,
    down_weight,
    cotangent,
):
    dp_index, tensor_index = lax.axis_index("dp"), lax.axis_index("tensor")
    first_core = dp_index % 2 == 0
    x_here = (dp_index // 2) % 2 == 1
    y_here = dp_index // 4 == 1
    late_half = tensor_index % 2 == 1
    row_count, model_width = inputs.shape
    group_rows = 4 * row_count
    head_width = output_weight.shape[0]
    local_heads = head_width // HD
    head_shape = (2, SEQ_LEN, local_heads, HD)
    quarter_width = model_width // 4

    def width_part(array, k):
        return array[:, k * quarter_width : (k + 1) * quarter_width]

    positions = jnp.arange(SEQ_LEN)
    positions = jnp.where(late_half, (positions + SEQ_LEN // 2) % SEQ_LEN, positions)
    cosine, sine = (
        jnp.where(late_half, jnp.roll(table, SEQ_LEN // 2, axis=0), table)
        for table in angle_tables()
    )
    vectors = lax.all_gather(
        jnp.stack([gain_first, shift_first, gain_second, shift_second]), "dp", axis=1, tiled=True
    )
    gain_one, shift_one, gain_two, shift_two = to_local(
        vectors.astype(jnp.float32), y_here, x_here
    )
    far_biases = own_quarter(biases)
    quarter_biases = jnp.where(first_core, biases, far_biases).astype(jnp.float32)

    proj_full = gather_weight(projections, 1, first_core)
    residual = to_local(inputs, y_here, x_here).astype(jnp.float32)
    normed_one, unit_one, inverse_one = norm_rows(residual, gain_one, shift_one)
    gathered_one = gather_rows(normed_one.astype(jnp.bfloat16))
    own_cot = to_local(cotangent, y_here, x_here)
    gathered_cot = gather_rows(own_cot)
    out_full = gather_weight(output_weight, 1, first_core)
    gu_full = gather_weight(gate_up, 1, first_core)
    down_full = gather_weight(down_weight, 1, first_core)

    pre_all = jnp.einsum("gd,jde->jge", gathered_one, proj_full, preferred_element_type=jnp.float32)
    pre_all = pre_all + quarter_biases[:, None, :]
    queries = rotate(pre_all[0].reshape(head_shape), cosine, sine, 1.0).astype(jnp.bfloat16)
    key_rows = rotate(pre_all[1].reshape(head_shape), cosine, sine, 1.0).astype(jnp.bfloat16)
    value_rows = pre_all[2].reshape(head_shape).astype(jnp.bfloat16)
    mixed, log_totals = lax.map(
        lambda pieces: attend_forward(pieces, positions), (queries, key_rows, value_rows)
    )
    mixed_rows = mixed.reshape(group_rows, head_width)
    middle = residual + scatter_rows(
        lambda rows: jnp.dot(mixed_rows[rows], out_full, preferred_element_type=jnp.float32),
        group_rows,
    )
    normed_two, unit_two, inverse_two = norm_rows(middle, gain_two, shift_two)
    gathered_two = gather_rows(normed_two.astype(jnp.bfloat16))
    gate_act = jnp.dot(gathered_two, gu_full[0], preferred_element_type=jnp.float32)
    up_act = jnp.dot(gathered_two, gu_full[1], preferred_element_type=jnp.float32)
    sigmoid_gate = jax.nn.sigmoid(gate_act)
    hidden = (gate_act * sigmoid_gate * up_act).astype(jnp.bfloat16)

    down_owned = scatter_weight(
        lambda k: jnp.einsum(
            "gf,gd->fd", hidden, width_part(gathered_cot, k), preferred_element_type=jnp.float32
        ),
        1,
        first_core,
    )
    grad_hidden = jnp.einsum(
        "gd,fd->gf", gathered_cot, down_full, preferred_element_type=jnp.float32
    )
    grad_up = (grad_hidden * gate_act * sigmoid_gate).astype(jnp.bfloat16)
    grad_gate = (
        grad_hidden * up_act * sigmoid_gate * (1.0 + gate_act * (1.0 - sigmoid_gate))
    ).astype(jnp.bfloat16)
    grad_second = scatter_rows(
        lambda rows: jnp.einsum(
            "gf,df->gd", grad_gate[rows], gu_full[0], preferred_element_type=jnp.float32
        )
        + jnp.einsum("gf,df->gd", grad_up[rows], gu_full[1], preferred_element_type=jnp.float32),
        group_rows,
    )
    gate_owned, up_owned = (
        scatter_weight(
            lambda k: jnp.einsum(
                "gd,gf->df",
                width_part(gathered_two, k),
                incoming,
                preferred_element_type=jnp.float32,
            ),
            0,
            first_core,
        )
        for incoming in (grad_gate, grad_up)
    )
    outputs = middle + scatter_rows(
        lambda rows: jnp.dot(hidden[rows], down_full, preferred_element_type=jnp.float32),
        group_rows,
    )
    outputs = from_local(outputs.astype(jnp.bfloat16), y_here, x_here)

    grad_mid_norm, gain_two_part, shift_two_part = norm_back(
        grad_second, unit_two, inverse_two, gain_two
    )
    grad_middle = own_cot.astype(jnp.float32) + grad_mid_norm
    gathered_branch = gather_rows(grad_middle.astype(jnp.bfloat16))
    grad_mixed = jnp.einsum(
        "gd,ed->ge", gathered_branch, out_full, preferred_element_type=jnp.float32
    ).astype(jnp.bfloat16)
    out_owned = scatter_weight(
        lambda k: jnp.einsum(
            "ge,gd->ed",
            mixed_rows,
            width_part(gathered_branch, k),
            preferred_element_type=jnp.float32,
        ),
        1,
        first_core,
    )
    grad_queries, grad_keys, grad_values = lax.map(
        lambda pieces: attend_back(pieces, positions),
        (queries, key_rows, value_rows, grad_mixed.reshape(head_shape), log_totals),
    )
    grad_queries = rotate(grad_queries, cosine, sine, -1.0)
    grad_keys = rotate(grad_keys, cosine, sine, -1.0)
    grad_pre = (
        jnp.stack([grad_queries, grad_keys, grad_values])
        .reshape(3, group_rows, head_width)
        .astype(jnp.bfloat16)
    )
    proj_owned = scatter_weight(
        lambda k: jnp.einsum(
            "gd,jge->jde",
            width_part(gathered_one, k),
            grad_pre,
            preferred_element_type=jnp.float32,
        ),
        1,
        first_core,
    )
    grad_normed = scatter_rows(
        lambda rows: jnp.einsum(
            "jge,jde->gd", grad_pre[:, rows], proj_full, preferred_element_type=jnp.float32
        ),
        group_rows,
    )
    bias_part = jnp.sum(grad_pre, axis=1, dtype=jnp.float32)
    bias_part = bias_part + swap(bias_part, X_BIT, 0)
    bias_part = bias_part + swap(bias_part, Y_BIT, 0)
    bias_grad = quarter_home(bias_part) + jnp.where(
        first_core, bias_part, far_quarter(bias_part)
    )

    grad_in_norm, gain_one_part, shift_one_part = norm_back(
        grad_normed, unit_one, inverse_one, gain_one
    )
    input_grads = from_local(grad_middle + grad_in_norm, y_here, x_here)

    sums = from_local(
        jnp.stack([gain_one_part, shift_one_part, gain_two_part, shift_two_part]), y_here, x_here
    )
    sums = flip(sums.reshape(4, 2, 2, 2, model_width // 8), y_here, x_here, 1)
    sums = sums[:, 0] + swap(sums[:, 1], Y_BIT, 0)
    sums = sums[:, 0] + swap(sums[:, 1], X_BIT, 0)
    sums = sums + swap(sums, 0, 1)
    sums = sums + swap(sums, 0, 2)
    sums = sums + swap(sums, CORE, 0)
    sums = jnp.where(first_core, sums[:, 0], sums[:, 1])
    return (
        outputs,
        input_grads,
        sums[0],
        sums[1],
        proj_owned,
        bias_grad,
        out_owned,
        sums[2],
        sums[3],
        jnp.stack([gate_owned, up_owned]),
        down_owned,
    )


def solution(mesh):
    whole_pairs = dict(mesh.shape) == {"dp": 8, "tensor": 4}
    return jax.shard_map(
        local_pairs if whole_pairs else local,
        mesh=mesh,
        in_specs=(
            P(("dp", "tensor"), None),
            P("dp"),
            P("dp"),
            P(None, "dp", "tensor"),
            P(None, "tensor"),
            P("tensor", "dp"),
            P("dp"),
            P("dp"),
            P(None, "dp", "tensor"),
            P("tensor", "dp"),
            P(("dp", "tensor"), None),
        ),
        out_specs=(
            P(("dp", "tensor"), None),
            P(("dp", "tensor"), None),
            P("dp"),
            P("dp"),
            P(None, "dp", "tensor"),
            P(None, "tensor"),
            P("tensor", "dp"),
            P("dp"),
            P("dp"),
            P(None, "dp", "tensor"),
            P("tensor", "dp"),
        ),
        check_vma=False,
    )
```

```python
import math

import jax
import jax.numpy as jnp
from jax import lax
from jax.experimental import pallas as pl
from jax.experimental.pallas import tpu as pltpu
from jax.sharding import PartitionSpec as P

HD = 64
ROTARY = 16
SEQ_LEN = 512


EPSILON = 1e-05
ANGLE_BASE = 10000.0
NEGATIVE = -1e30


def norm_rows(rows, gain, shift):
    average = jnp.mean(rows, axis=-1, keepdims=True)
    centred = rows - average
    inverse = lax.rsqrt(jnp.mean(centred * centred, axis=-1, keepdims=True) + EPSILON)
    unit_rows = centred * inverse
    return (unit_rows * gain + shift, unit_rows, inverse)


def norm_back(incoming, unit_rows, inverse, gain):
    scaled = incoming * gain
    inner = (
        scaled
        - jnp.mean(scaled, axis=-1, keepdims=True)
        - unit_rows * jnp.mean(scaled * unit_rows, axis=-1, keepdims=True)
    )
    return (inner * inverse, jnp.sum(incoming * unit_rows, axis=0), jnp.sum(incoming, axis=0))


def angle_tables():
    freqs = 1.0 / ANGLE_BASE ** (jnp.arange(0, ROTARY, 2).astype(jnp.float32) / ROTARY)
    angles = jnp.arange(SEQ_LEN).astype(jnp.float32)[:, None] * freqs[None, :]
    return (jnp.cos(angles), jnp.sin(angles))


def rotate(heads, cosine, sine, sign):
    half_rot = ROTARY // 2
    first = heads[..., :half_rot]
    latter = heads[..., half_rot:ROTARY]
    cos_part = cosine[:, None, :]
    sin_part = sine[:, None, :] * sign
    return jnp.concatenate(
        [
            first * cos_part - latter * sin_part,
            latter * cos_part + first * sin_part,
            heads[..., ROTARY:],
        ],
        axis=-1,
    )


def causal_scores(queries, key_rows, positions):
    scaling = 1.0 / math.sqrt(HD)
    scores = scaling * jnp.einsum(
        "qhd,khd->hqk", queries, key_rows, preferred_element_type=jnp.float32
    )
    causal = positions[:, None] >= positions[None, :]
    return jnp.where(causal[None], scores, NEGATIVE)


def attend_forward(pieces, positions):
    queries, key_rows, value_rows = pieces
    scores = causal_scores(queries, key_rows, positions)
    row_top = jnp.max(scores, axis=-1, keepdims=True)
    exponent = jnp.exp(scores - row_top)
    totals = jnp.sum(exponent, axis=-1, keepdims=True)
    weights = (exponent / totals).astype(jnp.bfloat16)
    mixed = jnp.einsum("hqk,khd->qhd", weights, value_rows, preferred_element_type=jnp.float32)
    return (mixed.astype(jnp.bfloat16), (row_top + jnp.log(totals))[..., 0])


def attend_back(pieces, positions):
    queries, key_rows, value_rows, grad_mixed, log_totals = pieces
    scaling = 1.0 / math.sqrt(HD)
    scores = causal_scores(queries, key_rows, positions)
    weights = jnp.exp(scores - log_totals[..., None])
    grad_values = jnp.einsum(
        "hqk,qhd->khd", weights.astype(jnp.bfloat16), grad_mixed, preferred_element_type=jnp.float32
    )
    grad_weights = jnp.einsum(
        "qhd,khd->hqk", grad_mixed, value_rows, preferred_element_type=jnp.float32
    )
    grad_scores = weights * (grad_weights - jnp.sum(weights * grad_weights, axis=-1, keepdims=True))
    grad_scores = grad_scores.astype(jnp.bfloat16)
    grad_queries = scaling * jnp.einsum(
        "hqk,khd->qhd", grad_scores, key_rows, preferred_element_type=jnp.float32
    )
    grad_keys = scaling * jnp.einsum(
        "hqk,qhd->khd", grad_scores, queries, preferred_element_type=jnp.float32
    )
    return (grad_queries, grad_keys, grad_values)


def scatter_sum(terms, axis, dimension):
    owned = lax.psum_scatter(
        terms.astype(jnp.bfloat16), axis, scatter_dimension=dimension, tiled=True
    )
    return owned.astype(jnp.float32)


def local(
    inputs,
    gain_first,
    shift_first,
    projections,
    biases,
    output_weight,
    gain_second,
    shift_second,
    gate_up,
    down_weight,
    cotangent,
):
    tensor_ways = lax.axis_size("tensor")
    row_count = inputs.shape[0]
    group_rows = row_count * tensor_ways
    sequences = group_rows // SEQ_LEN
    head_width = output_weight.shape[0]
    local_heads = head_width // HD
    head_shape = (sequences, SEQ_LEN, local_heads, HD)
    cosine, sine = angle_tables()
    positions = jnp.arange(SEQ_LEN)
    proj_full, out_full, gain_one, shift_one = (
        lax.all_gather(projections, "dp", axis=1, tiled=True),
        lax.all_gather(output_weight, "dp", axis=1, tiled=True),
        lax.all_gather(gain_first, "dp", axis=0, tiled=True),
        lax.all_gather(shift_first, "dp", axis=0, tiled=True),
    )
    gain_one = gain_one.astype(jnp.float32)
    residual = inputs.astype(jnp.float32)
    normed_one, unit_one, inverse_one = norm_rows(residual, gain_one, shift_one.astype(jnp.float32))
    gathered_one = lax.all_gather(normed_one.astype(jnp.bfloat16), "tensor", axis=0, tiled=True)
    pre_all = jnp.einsum("gd,jde->jge", gathered_one, proj_full, preferred_element_type=jnp.float32)
    pre_all = pre_all + biases.astype(jnp.float32)[:, None, :]
    queries = rotate(pre_all[0].reshape(head_shape), cosine, sine, 1.0).astype(jnp.bfloat16)
    key_rows = rotate(pre_all[1].reshape(head_shape), cosine, sine, 1.0).astype(jnp.bfloat16)
    value_rows = pre_all[2].reshape(head_shape).astype(jnp.bfloat16)
    mixed, log_totals = lax.map(
        lambda pieces: attend_forward(pieces, positions), (queries, key_rows, value_rows)
    )
    mixed_rows = mixed.reshape(group_rows, head_width)
    part = mixed_rows
    middle = residual + scatter_sum(
        jnp.dot(part, out_full, preferred_element_type=jnp.float32), "tensor", 0
    )
    gu_full, down_full, gain_two, shift_two = (
        lax.all_gather(gate_up, "dp", axis=1, tiled=True),
        lax.all_gather(down_weight, "dp", axis=1, tiled=True),
        lax.all_gather(gain_second, "dp", axis=0, tiled=True),
        lax.all_gather(shift_second, "dp", axis=0, tiled=True),
    )
    gain_two = gain_two.astype(jnp.float32)
    normed_two, unit_two, inverse_two = norm_rows(middle, gain_two, shift_two.astype(jnp.float32))
    gathered_two = lax.all_gather(normed_two.astype(jnp.bfloat16), "tensor", axis=0, tiled=True)
    gate_act = jnp.dot(gathered_two, gu_full[0], preferred_element_type=jnp.float32)
    up_act = jnp.dot(gathered_two, gu_full[1], preferred_element_type=jnp.float32)
    sigmoid_gate = jax.nn.sigmoid(gate_act)
    hidden = (gate_act * sigmoid_gate * up_act).astype(jnp.bfloat16)
    part = hidden
    outputs = (
        middle
        + scatter_sum(jnp.dot(part, down_full, preferred_element_type=jnp.float32), "tensor", 0)
    ).astype(jnp.bfloat16)
    gu_back, down_back, gain_two_back = (
        lax.all_gather(gate_up, "dp", axis=1, tiled=True),
        lax.all_gather(down_weight, "dp", axis=1, tiled=True),
        lax.all_gather(gain_second, "dp", axis=0, tiled=True),
    )
    gain_two_back = gain_two_back.astype(jnp.float32)
    gathered_cot = lax.all_gather(cotangent, "tensor", axis=0, tiled=True)
    grad_hidden = jnp.einsum(
        "gd,fd->gf", gathered_cot, down_back, preferred_element_type=jnp.float32
    )
    down_grad = jnp.einsum("gf,gd->fd", hidden, gathered_cot, preferred_element_type=jnp.float32)
    grad_up = (grad_hidden * gate_act * sigmoid_gate).astype(jnp.bfloat16)
    grad_gate = (
        grad_hidden * up_act * sigmoid_gate * (1.0 + gate_act * (1.0 - sigmoid_gate))
    ).astype(jnp.bfloat16)
    gu_grad = jnp.stack(
        [
            jnp.einsum("gd,gf->df", gathered_two, grad_gate, preferred_element_type=jnp.float32),
            jnp.einsum("gd,gf->df", gathered_two, grad_up, preferred_element_type=jnp.float32),
        ]
    )
    first_term = jnp.einsum("gf,df->gd", grad_gate, gu_back[0], preferred_element_type=jnp.float32)
    grad_second = scatter_sum(
        first_term
        + jnp.einsum("gf,df->gd", grad_up, gu_back[1], preferred_element_type=jnp.float32),
        "tensor",
        0,
    )
    gu_owned, down_owned = (
        scatter_sum(gu_grad, "dp", 1),
        scatter_sum(down_grad, "dp", 1),
    )
    grad_mid_norm, gain_two_part, shift_two_part = norm_back(
        grad_second, unit_two, inverse_two, gain_two_back
    )
    grad_middle = cotangent.astype(jnp.float32) + grad_mid_norm
    proj_back, out_back, gain_one_back = (
        lax.all_gather(projections, "dp", axis=1, tiled=True),
        lax.all_gather(output_weight, "dp", axis=1, tiled=True),
        lax.all_gather(gain_first, "dp", axis=0, tiled=True),
    )
    gain_one_back = gain_one_back.astype(jnp.float32)
    gathered_branch = lax.all_gather(grad_middle.astype(jnp.bfloat16), "tensor", axis=0, tiled=True)
    out_grad = jnp.einsum(
        "ge,gd->ed", mixed_rows, gathered_branch, preferred_element_type=jnp.float32
    )
    grad_mixed = jnp.einsum(
        "gd,ed->ge", gathered_branch, out_back, preferred_element_type=jnp.float32
    ).astype(jnp.bfloat16)
    grad_queries, grad_keys, grad_values = lax.map(
        lambda pieces: attend_back(pieces, positions),
        (queries, key_rows, value_rows, grad_mixed.reshape(head_shape), log_totals),
    )
    grad_queries = rotate(grad_queries, cosine, sine, -1.0)
    grad_keys = rotate(grad_keys, cosine, sine, -1.0)
    grad_pre = (
        jnp.stack([grad_queries, grad_keys, grad_values])
        .reshape(3, group_rows, head_width)
        .astype(jnp.bfloat16)
    )
    bias_part = jnp.sum(grad_pre, axis=1, dtype=jnp.float32)
    proj_grad = jnp.einsum(
        "gd,jge->jde", gathered_one, grad_pre, preferred_element_type=jnp.float32
    )
    part = grad_pre
    grad_normed = scatter_sum(
        jnp.einsum("jge,jde->gd", part, proj_back, preferred_element_type=jnp.float32),
        "tensor",
        0,
    )
    proj_owned, out_owned = (
        scatter_sum(proj_grad, "dp", 1),
        scatter_sum(out_grad, "dp", 1),
    )
    grad_in_norm, gain_one_part, shift_one_part = norm_back(
        grad_normed, unit_one, inverse_one, gain_one_back
    )
    input_grads = grad_middle + grad_in_norm
    one_hot = (jnp.arange(tensor_ways) == lax.axis_index("tensor")).astype(jnp.float32)
    spread_bias = (bias_part[:, None, :] * one_hot[None, :, None]).reshape(
        3, tensor_ways * head_width
    )
    summed = lax.psum(
        (gain_one_part, shift_one_part, gain_two_part, shift_two_part, spread_bias),
        ("dp", "tensor"),
    )
    own_width = gain_first.shape[0]
    own_offset = lax.axis_index("dp") * own_width

    def own_part(vector):
        return lax.dynamic_slice_in_dim(vector, own_offset, own_width, 0)

    bias_grad = jnp.sum(
        summed[4].reshape(3, tensor_ways, head_width) * one_hot[None, :, None], axis=1
    )
    return (
        outputs,
        input_grads,
        own_part(summed[0]),
        own_part(summed[1]),
        proj_owned,
        bias_grad,
        out_owned,
        own_part(summed[2]),
        own_part(summed[3]),
        gu_owned,
        down_owned,
    )


def send_between(array, routes):
    tensor_ways = lax.axis_size("tensor")
    pairs = [(d * tensor_ways + t, e * tensor_ways + s) for (d, t), (e, s) in routes]
    return lax.ppermute(array, ("dp", "tensor"), pairs)


def places():
    return [(d, t) for d in range(lax.axis_size("dp")) for t in range(lax.axis_size("tensor"))]


def own_quarter(array):
    return send_between(
        array,
        [((d, t), (d ^ 1, t) if d & 1 else (d ^ 1, t ^ 2)) for d, t in places()],
    )


ORDER = ((1, 0, 0), (1, 1, 0), (0, 1, 1), (1, 1, 1), (0, 0, 0), (0, 1, 0), (0, 0, 1), (1, 0, 1))
EVEN_Y, EVEN_XY, ODD_X, ODD_XY, EVEN, EVEN_X, ODD, ODD_Y = range(8)
ANY = pl.BlockSpec(memory_space=pl.ANY)
VMEM_BYTES = 60 * 1024 * 1024


class Place:
    def __init__(self, send_sems, recv_sems, local_sems):
        self.dp, self.tensor = lax.axis_index("dp"), lax.axis_index("tensor")
        self.core = lax.rem(self.dp, 2)
        self.x = lax.rem(self.dp // 2, 2)
        self.y = self.dp // 4
        self.pools = {"send": send_sems, "recv": recv_sems, "local": local_sems}
        self.used = {"send": 0, "recv": 0, "local": 0}

    def take(self, kind):
        self.used[kind] += 1
        return self.pools[kind].at[self.used[kind] - 1]

    def at(self, x=0, y=0, core=0, near=0, far=0):
        dp = self.dp
        dp = dp + x * (2 - 4 * self.x) + y * (4 - 8 * self.y) + core * (1 - 2 * self.core)
        tensor = self.tensor
        tensor = tensor + near * (1 - 2 * lax.rem(tensor, 2)) + far * (2 - 4 * (tensor // 2))
        return (dp, tensor)

    def column(self, key):
        dy, dx, core = key
        y = self.y + dy * (1 - 2 * self.y)
        x = self.x + dx * (1 - 2 * self.x)
        return pl.multiple_of((y * 4 + x * 2 + core) * EIGHTH, EIGHTH)

    def greet(self):
        barrier = pltpu.get_barrier_semaphore()
        partners = [
            self.at(x=x, y=y, core=core)
            for x in (0, 1)
            for y in (0, 1)
            for core in (0, 1)
            if x or y or core
        ] + [self.at(near=1), self.at(far=1), self.at(far=1, core=1)]
        for partner in partners:
            pl.semaphore_signal(
                barrier, inc=1, device_id=partner, device_id_type=pl.DeviceIdType.MESH
            )
        pl.semaphore_wait(barrier, len(partners))

    def send(self, source, target, device, recv_sem=None, when=None):
        return Sent(
            pltpu.make_async_remote_copy(
                src_ref=source,
                dst_ref=target,
                send_sem=self.take("send"),
                recv_sem=self.take("recv") if recv_sem is None else recv_sem,
                device_id=device,
                device_id_type=pl.DeviceIdType.MESH,
            ),
            when,
        )

    def copy(self, source, target, when=None):
        return Copied(pltpu.make_async_copy(source, target, self.take("local")), when)


def guarded(when, action):
    if when is None:
        action()
    else:
        pl.when(when)(action)


class Sent:
    def __init__(self, copy, when):
        self.copy, self.when = copy, when

    def start(self):
        guarded(self.when, self.copy.start)
        return self

    def arrived(self, when=None):
        guarded(when, self.copy.wait_recv)

    def left(self):
        guarded(self.when, self.copy.wait_send)


class Copied:
    def __init__(self, copy, when):
        self.copy, self.when = copy, when

    def start(self):
        guarded(self.when, self.copy.start)
        return self

    def wait(self):
        guarded(self.when, self.copy.wait)


class GatherWeight:
    def __init__(self, place, shard, block, pair=None):
        self.place, self.shard, self.block = place, shard, block
        self.sent = []
        self.pair = pair

    def fetch(self, even=None, odd=None):
        p = self.place
        even = self.block(EVEN) if even is None else even
        odd = self.block(ODD) if odd is None else odd
        first, second = p.core == 0, p.core == 1
        self.own = p.copy(self.shard, even, first).start()
        even_sem, odd_sem = p.take("recv"), p.take("recv")
        self.to_far_even = p.send(self.shard, even, p.at(core=1, far=1), even_sem, first).start()
        self.to_sibling = p.send(self.shard, odd, p.at(core=1), odd_sem, second).start()
        self.to_far_odd = p.send(self.shard, odd, p.at(far=1), odd_sem, second).start()
        return self

    def fetched(self):
        p = self.place
        self.own.wait()
        self.to_far_even.arrived(p.core == 1)
        self.to_sibling.arrived()
        return self

    def fetch_left(self):
        self.to_far_even.left()
        self.to_sibling.left()
        self.to_far_odd.left()

    def spread(self, even=None, odd=None):
        p, block = self.place, self.block
        even = block(EVEN) if even is None else even
        odd = block(ODD) if odd is None else odd
        self.even_x = p.send(even, block(EVEN_X), p.at(x=1)).start()
        self.odd_y = p.send(odd, block(ODD_Y), p.at(y=1)).start()
        self.odd_x = p.send(odd, block(ODD_X), p.at(x=1)).start()
        self.even_y = p.send(even, block(EVEN_Y), p.at(y=1)).start()
        return self

    def relay(self):
        p, block = self.place, self.block
        self.even_x.arrived()
        self.even_xy = p.send(block(EVEN_X), block(EVEN_XY), p.at(y=1)).start()
        self.odd_y.arrived()
        self.odd_xy = p.send(block(ODD_Y), block(ODD_XY), p.at(x=1)).start()
        return self

    def finish(self):
        for copy in (self.odd_x, self.even_y, self.even_xy, self.odd_xy):
            copy.arrived()
        for copy in (
            self.even_x, self.odd_y, self.odd_x, self.even_y, self.even_xy, self.odd_xy,
        ):
            copy.left()


class GatherRows:
    def __init__(self, place, own, rows):
        self.place, self.own, self.rows = place, own, rows
        self.count = own.shape[0]

    def slot(self, k):
        return self.rows.at[pl.ds(k * self.count, self.count)]

    def start(self):
        p = self.place
        self.beside = p.send(self.own, self.slot(1), p.at(near=1)).start()
        self.sibling = p.send(self.own, self.slot(2), p.at(core=1)).start()
        self.here = p.copy(self.own, self.slot(0)).start()
        return self

    def relay(self):
        p = self.place
        self.beside.arrived()
        self.across = p.send(self.slot(1), self.slot(3), p.at(core=1)).start()
        return self

    def finish(self):
        self.sibling.arrived()
        self.across.arrived()
        self.here.wait()
        for copy in (self.beside, self.sibling, self.across):
            copy.left()


def combine(target, terms, chunk):
    @pl.loop(0, target.shape[0] // chunk)
    def _(i):
        rows = pl.ds(pl.multiple_of(i * chunk, chunk), chunk)
        total = terms[0][rows].astype(jnp.float32)
        for term in terms[1:]:
            total = total + term[rows].astype(jnp.float32)
        target[rows] = total.astype(target.dtype)


class ScatterRows:
    def __init__(self, place, term, near, got, got_beside):
        self.place, self.term, self.near = place, term, near
        self.got, self.got_beside = got, got_beside
        self.count = term.shape[0] // 4

    def start(self):
        p, n = self.place, self.count
        self.sibling = p.send(self.term.at[pl.ds(2 * n, 2 * n)], self.got, p.at(core=1)).start()
        self.load = p.copy(self.term.at[pl.ds(0, 2 * n)], self.near).start()
        return self

    def relay(self):
        p, n = self.place, self.count
        self.load.wait()
        self.sibling.arrived()
        late = pl.ds(n, n)
        combine(self.near.at[late], [self.near.at[late], self.got.at[late]], 32)
        self.beside = p.send(self.near.at[late], self.got_beside, p.at(near=1)).start()
        return self

    def total(self, rows):
        return (
            self.near[rows].astype(jnp.float32)
            + self.got[rows].astype(jnp.float32)
            + self.got_beside[rows].astype(jnp.float32)
        )

    def arrived(self):
        self.beside.arrived()

    def finish(self):
        self.sibling.left()
        self.beside.left()


class ScatterWeight:
    def __init__(self, place, parts, rows, keep, got, last, home, result):
        self.place, self.parts, self.rows = place, parts, rows
        self.keep, self.got, self.last, self.home, self.result = keep, got, last, home, result

    def half(self, ref, k):
        if self.rows:
            size = ref.shape[0] // 2
            return ref.at[pl.ds(k * size, size)]
        size = ref.shape[1] // 2
        return ref.at[:, pl.ds(k * size, size)]

    def start(self):
        p = self.place
        self.even = p.send(self.parts[0], self.got.at[0], p.at(y=1)).start()
        self.odd = p.send(self.parts[1], self.got.at[1], p.at(x=1)).start()
        self.loads = [p.copy(self.parts[2 + k], self.keep.at[k]).start() for k in (0, 1)]
        return self

    def relay(self):
        p = self.place
        for k, arrival in enumerate((self.even, self.odd)):
            self.loads[k].wait()
            arrival.arrived()
            there = self.half(self.keep.at[k], 1)
            combine(there, [there, self.half(self.got.at[k], 1)], 64)
            sent = p.send(there, self.last.at[k], p.at(x=1) if k == 0 else p.at(y=1)).start()
            if k == 0:
                self.even_last = sent
            else:
                self.odd_last = sent
        return self

    def settle(self):
        p = self.place
        self.even_last.arrived()
        self.odd_last.arrived()

        def terms(k):
            return [self.half(self.keep.at[k], 0), self.half(self.got.at[k], 0), self.last.at[k]]

        even_out, odd_out = self.half(self.keep.at[0], 0), self.half(self.keep.at[1], 0)
        combine(odd_out, terms(1), 64)
        first, second = p.core == 0, p.core == 1
        pl.when(first)(lambda: combine(self.result, terms(0), 64))
        pl.when(second)(lambda: combine(even_out, terms(0), 64))
        near_sem, far_sem = p.take("recv"), p.take("recv")
        self.to_sibling = p.send(odd_out, self.home.at[0], p.at(core=1), near_sem, first).start()
        self.to_first = p.send(
            even_out, self.home.at[0], p.at(core=1, far=1), near_sem, second
        ).start()
        self.to_far = p.send(odd_out, self.home.at[1], p.at(far=1), far_sem, second).start()
        return self

    def finish(self, output):
        p = self.place
        first, second = p.core == 0, p.core == 1
        self.to_sibling.arrived()
        self.to_far.arrived(second)
        pl.when(first)(lambda: combine(self.result, [self.result, self.home.at[0]], 64))
        pl.when(second)(lambda: combine(self.result, [self.home.at[0], self.home.at[1]], 64))
        self.store = p.copy(self.result, output).start()
        for copy in (
            self.even, self.odd, self.even_last, self.odd_last,
            self.to_sibling, self.to_first, self.to_far,
        ):
            copy.left()

    def stored(self):
        self.store.wait()


def load_local(place, source, target):
    return [
        place.copy(
            source.at[:, pl.ds(place.column(key), EIGHTH)], target.at[:, pl.ds(j * EIGHTH, EIGHTH)]
        ).start()
        for j, key in enumerate(ORDER)
    ]


def store_natural(place, source, target):
    return [
        place.copy(
            source.at[:, pl.ds(j * EIGHTH, EIGHTH)], target.at[:, pl.ds(place.column(key), EIGHTH)]
        ).start()
        for j, key in enumerate(ORDER)
    ]


def wait_all(copies):
    for copy in copies:
        copy.wait()


CHUNK = 32


def norm_into(count, rows_of, gain, shift, target):
    @pl.loop(0, count // CHUNK)
    def _(i):
        rows = pl.ds(pl.multiple_of(i * CHUNK, CHUNK), CHUNK)
        target[rows] = norm_rows(rows_of(rows), gain, shift)[0].astype(target.dtype)


def front_kernel(
    inputs, cotangent, vectors, projections, output_weight, gate_up,
    proj_full, out_full, gate_pair, vectors_full, rows_one, rows_cot,
    own, normed, own_cot, vectors_here, send_sems, recv_sems, local_sems,
):
    p = Place(send_sems, recv_sems, local_sems)
    loads = load_local(p, inputs, own)
    cot_loads = load_local(p, cotangent, own_cot)
    p.greet()
    slots = {key: j for j, key in enumerate(ORDER)}
    vector_sem = [p.take("recv") for _ in ORDER]
    del vector_sem
    vector_base = p.used["recv"] - len(ORDER)

    def vector_copy(dy, dx, core):
        here, there = slots[(dy, dx, 0)], slots[(dy, dx, 1)]
        slot = here + p.core * (there - here)
        columns = pl.ds(pl.multiple_of(slot * EIGHTH, EIGHTH), EIGHTH)
        return p.send(
            vectors, vectors_here.at[:, columns], p.at(x=dx, y=dy, core=core),
            recv_sems.at[vector_base + slot],
        )

    vector_sends = [
        vector_copy(dy, dx, core).start()
        for dy in (0, 1) for dx in (0, 1) for core in (0, 1) if dy or dx or core
    ]
    own_slot = slots[(0, 0, 0)] + p.core * (slots[(0, 0, 1)] - slots[(0, 0, 0)])
    own_vectors = p.copy(
        vectors, vectors_here.at[:, pl.ds(pl.multiple_of(own_slot * EIGHTH, EIGHTH), EIGHTH)]
    ).start()

    def quarter(j):
        return GatherWeight(
            p, projections.at[j], lambda k: proj_full.at[j, pl.ds(k * EIGHTH, EIGHTH)]
        )

    weights = [quarter(0), quarter(1), quarter(2)]
    weights.append(
        GatherWeight(p, output_weight, lambda k: out_full.at[:, pl.ds(k * EIGHTH, EIGHTH)])
    )
    gate = GatherWeight(p, gate_up.at[0], lambda k: gate_pair.at[k])
    weights[0].fetch()
    weights[1].fetch()
    wait_all(cot_loads)
    wait_all(loads)
    own_vectors.wait()
    sibling_slot = slots[(0, 0, 1)] + p.core * (slots[(0, 0, 0)] - slots[(0, 0, 1)])
    for dy in (0, 1):
        for dx in (0, 1):
            for core in (0, 1):
                if dy or dx:
                    slot = slots[(dy, dx, core)]
                elif core:
                    slot = sibling_slot
                else:
                    continue
                pltpu.make_async_copy(
                    vectors, vectors_here.at[:, pl.ds(0, EIGHTH)], recv_sems.at[vector_base + slot]
                ).wait()
    gain, shift = vectors_here[0:1], vectors_here[1:2]
    norm_into(own.shape[0], lambda rows: own[rows].astype(jnp.float32), gain, shift, normed)
    gather_one = GatherRows(p, normed, rows_one).start()
    gather_cot = GatherRows(p, own_cot, rows_cot)
    vector_store = p.copy(vectors_here, vectors_full).start()

    weights[0].fetched().spread()
    weights[2].fetch()
    weights[1].fetched().spread()
    weights[3].fetch()
    weights[0].relay()
    weights[2].fetched().spread()
    gather_one.relay()
    gather_cot.start()
    weights[1].relay()
    gate.fetch(gate_pair.at[0], gate_pair.at[1])
    weights[3].fetched().spread()
    weights[2].relay()
    weights[3].relay()
    gather_cot.relay()
    for weight in weights:
        weight.finish()
        weight.fetch_left()
    gather_one.finish()
    gather_cot.finish()
    gate.fetched()
    gate.fetch_left()
    for sent in vector_sends:
        sent.left()
    vector_store.wait()


def middle_kernel(
    term, inputs, vectors, gate_pair, gate_up, down_weight,
    gu_full, down_full, middle, rows_two,
    own, near, got, got_beside, total, normed, send_sems, recv_sems, local_sems,
):
    p = Place(send_sems, recv_sems, local_sems)
    loads = load_local(p, inputs, own)
    p.greet()
    scatter = ScatterRows(p, term, near, got, got_beside).start()

    def gu_block(j):
        return lambda k: gu_full.at[j, pl.ds(k * EIGHTH, EIGHTH)]

    gate = GatherWeight(p, None, gu_block(0))
    up = GatherWeight(p, gate_up.at[1], gu_block(1))
    down = GatherWeight(p, down_weight, lambda k: down_full.at[:, pl.ds(k * EIGHTH, EIGHTH)])
    gate.spread(gate_pair.at[0], gate_pair.at[1])
    places = [
        p.copy(gate_pair.at[0], gate.block(EVEN)).start(),
        p.copy(gate_pair.at[1], gate.block(ODD)).start(),
    ]
    up.fetch()
    scatter.relay()
    wait_all(loads)
    scatter.arrived()
    count = own.shape[0]
    gain, shift = vectors[2:3], vectors[3:4]

    @pl.loop(0, count // CHUNK)
    def _(i):
        rows = pl.ds(pl.multiple_of(i * CHUNK, CHUNK), CHUNK)
        value = own[rows].astype(jnp.float32) + scatter.total(rows)
        total[rows] = value
        normed[rows] = norm_rows(value, gain, shift)[0].astype(normed.dtype)

    gather = GatherRows(p, normed, rows_two).start()
    store = p.copy(total, middle).start()
    up.fetched()
    down.fetch()
    up.spread()
    gate.relay()
    gather.relay()
    down.fetched()
    up.relay()
    down.spread()
    down.relay()
    for weight in (gate, up, down):
        weight.finish()
    up.fetch_left()
    down.fetch_left()
    scatter.finish()
    gather.finish()
    wait_all(places)
    store.wait()


def norm_back_rows(value, incoming, gain):
    average = jnp.mean(value, axis=-1, keepdims=True)
    centred = value - average
    inverse = lax.rsqrt(jnp.mean(centred * centred, axis=-1, keepdims=True) + EPSILON)
    unit = centred * inverse
    scaled = incoming * gain
    inner = (
        scaled
        - jnp.mean(scaled, axis=-1, keepdims=True)
        - unit * jnp.mean(scaled * unit, axis=-1, keepdims=True)
    )
    return inner * inverse, incoming * unit


def fold(array):
    return jnp.sum(array.reshape(array.shape[0] // 8, 8, array.shape[1]), axis=0)


def back_kernel(
    term, out_term, middle, cotangent, vectors, *rest,
):
    down_parts, gate_parts, up_parts = rest[0:4], rest[4:8], rest[8:12]
    (
        outputs, grad_middle, rows_branch, sums, gu_owned, down_owned,
        value, own_cot, near, got, got_beside, near_out, got_out, got_out_beside, branch, result,
        gain_sum, shift_sum,
        d_keep, d_got, d_last, d_home, d_result,
        g_keep, g_got, g_last, g_home, g_result,
        u_keep, u_got, u_last, u_home, u_result,
        send_sems, recv_sems, local_sems,
    ) = rest[12:]
    p = Place(send_sems, recv_sems, local_sems)
    cot_loads = load_local(p, cotangent, own_cot)
    value_load = p.copy(middle, value).start()
    p.greet()
    scatter = ScatterRows(p, term, near, got, got_beside).start()
    out_scatter = ScatterRows(p, out_term, near_out, got_out, got_out_beside)
    down = ScatterWeight(p, down_parts, False, d_keep, d_got, d_last, d_home, d_result).start()
    gate = ScatterWeight(p, gate_parts, True, g_keep, g_got, g_last, g_home, g_result)
    up = ScatterWeight(p, up_parts, True, u_keep, u_got, u_last, u_home, u_result)
    scatter.relay()
    out_scatter.start()
    wait_all(cot_loads)
    value_load.wait()
    scatter.arrived()
    out_scatter.relay()
    count = value.shape[0]
    gain = vectors[2:3]
    gain_sum[...] = jnp.zeros_like(gain_sum)
    shift_sum[...] = jnp.zeros_like(shift_sum)

    @pl.loop(0, count // CHUNK)
    def _(i):
        rows = pl.ds(pl.multiple_of(i * CHUNK, CHUNK), CHUNK)
        incoming = scatter.total(rows)
        back, product = norm_back_rows(value[rows], incoming, gain)
        gain_sum[...] += fold(product)
        shift_sum[...] += fold(incoming)
        grad = own_cot[rows].astype(jnp.float32) + back
        result[rows] = grad
        branch[rows] = grad.astype(branch.dtype)

    gather = GatherRows(p, branch, rows_branch).start()
    grad_store = p.copy(result, grad_middle).start()
    gain_sum[0:1] = jnp.sum(gain_sum[...], axis=0, keepdims=True)
    gain_sum[1:2] = jnp.sum(shift_sum[...], axis=0, keepdims=True)
    sum_store = p.copy(gain_sum, sums).start()
    gate.start()
    down.relay()
    out_scatter.arrived()

    @pl.loop(0, count // CHUNK)
    def _(i):
        rows = pl.ds(pl.multiple_of(i * CHUNK, CHUNK), CHUNK)
        own_cot[rows] = (value[rows] + out_scatter.total(rows)).astype(own_cot.dtype)

    out_stores = store_natural(p, own_cot, outputs)
    gather.relay()
    up.start()
    gate.relay()
    down.settle()
    up.relay()
    gate.settle()
    down.finish(down_owned)
    up.settle()
    gate.finish(gu_owned.at[0])
    up.finish(gu_owned.at[1])
    for weight in (down, gate, up):
        weight.stored()
    scatter.finish()
    out_scatter.finish()
    gather.finish()
    wait_all(out_stores)
    grad_store.wait()
    sum_store.wait()


def last_kernel(
    term, inputs, vectors, grad_middle, sums, bias_part, *rest,
):
    out_parts, proj_parts = rest[0:4], rest[4:8]
    (
        input_grads, proj_owned, out_owned, vector_grads, bias_grad,
        own, near, got, got_beside, result, all_sums, shift_sum, vector_got, vector_total, z_got,
        bias_here, bias_got,
        o_keep, o_got, o_last, o_home, o_result,
        q_keep, q_got, q_last, q_home, q_result,
        k_keep, k_got, k_last, k_home, k_result,
        v_keep, v_got, v_last, v_home, v_result,
        send_sems, recv_sems, local_sems,
    ) = rest[8:]
    p = Place(send_sems, recv_sems, local_sems)
    loads = load_local(p, inputs, own)
    loads.append(p.copy(grad_middle, result).start())
    p.greet()
    first, second = p.core == 0, p.core == 1
    scatter = ScatterRows(p, term, near, got, got_beside).start()
    out = ScatterWeight(p, out_parts, False, o_keep, o_got, o_last, o_home, o_result).start()
    thirds = [
        ScatterWeight(p, [part.at[j] for part in proj_parts], True, *refs)
        for j, refs in enumerate(
            (
                (q_keep, q_got, q_last, q_home, q_result),
                (k_keep, k_got, k_last, k_home, k_result),
                (v_keep, v_got, v_last, v_home, v_result),
            )
        )
    ]
    thirds[0].start()
    bias_load = p.copy(bias_part, bias_here).start()
    scatter.relay()
    bias_load.wait()
    bias_x = p.send(bias_here, bias_got.at[0], p.at(x=1)).start()
    bias_x.arrived()
    bias_x.left()
    bias_here[...] += bias_got[0]
    bias_y = p.send(bias_here, bias_got.at[1], p.at(y=1)).start()
    out.relay()
    thirds[1].start()
    bias_y.arrived()
    bias_y.left()
    bias_here[...] += bias_got[1]
    near_sem, far_sem = p.take("recv"), p.take("recv")
    bias_home = [
        p.send(bias_here, bias_got.at[2], p.at(core=1), near_sem, first).start(),
        p.send(bias_here, bias_got.at[2], p.at(core=1, far=1), near_sem, second).start(),
        p.send(bias_here, bias_got.at[3], p.at(far=1), far_sem, second).start(),
    ]
    wait_all(loads)
    scatter.arrived()
    count = own.shape[0]
    gain = vectors[0:1]
    all_sums[...] = jnp.zeros_like(all_sums)
    shift_sum[...] = jnp.zeros_like(shift_sum)

    @pl.loop(0, count // CHUNK)
    def _(i):
        rows = pl.ds(pl.multiple_of(i * CHUNK, CHUNK), CHUNK)
        incoming = scatter.total(rows)
        back, product = norm_back_rows(own[rows].astype(jnp.float32), incoming, gain)
        all_sums[...] += fold(product)
        shift_sum[...] += fold(incoming)
        result[rows] = result[rows] + back

    stores = store_natural(p, result, input_grads)
    all_sums[0:1] = jnp.sum(all_sums[...], axis=0, keepdims=True)
    all_sums[1:2] = jnp.sum(shift_sum[...], axis=0, keepdims=True)
    all_sums[2:4] = sums[0:2]
    slots = {key: j for j, key in enumerate(ORDER)}
    vector_sends = []
    n = 0
    for dy in (0, 1):
        for dx in (0, 1):
            for core in (0, 1):
                if not (dy or dx or core):
                    continue
                straight, crossed = slots[(dy, dx, core)], slots[(dy, dx, 1 - core)]
                slot = straight + p.core * (crossed - straight)
                columns = pl.ds(pl.multiple_of(slot * EIGHTH, EIGHTH), EIGHTH)
                vector_sends.append(
                    p.send(
                        all_sums.at[:, columns], vector_got.at[n], p.at(x=dx, y=dy, core=core)
                    ).start()
                )
                n += 1
    thirds[0].relay()
    thirds[2].start()
    own_slot = slots[(0, 0, 0)] + p.core * (slots[(0, 0, 1)] - slots[(0, 0, 0)])
    total = all_sums[:, pl.ds(pl.multiple_of(own_slot * EIGHTH, EIGHTH), EIGHTH)]
    for k, sent in enumerate(vector_sends):
        sent.arrived()
        total = total + vector_got[k]
    vector_total[0] = total
    z_near = p.send(vector_total.at[0], z_got.at[0], p.at(near=1)).start()
    out.settle()
    z_near.arrived()
    vector_total[1] = total + z_got[0]
    z_far = p.send(vector_total.at[1], z_got.at[1], p.at(far=1)).start()
    thirds[1].relay()
    thirds[0].settle()
    z_far.arrived()
    z_near.left()
    z_far.left()
    vector_total[0] = vector_total[1] + z_got[1]
    vector_store = p.copy(vector_total.at[0], vector_grads).start()
    bias_home[0].arrived()
    bias_home[2].arrived(second)
    for sent in bias_home:
        sent.left()
    pl.when(second)(lambda: combine(bias_got.at[2], [bias_got.at[2], bias_got.at[3]], 8))
    pl.when(first)(lambda: combine(bias_got.at[2], [bias_got.at[2], bias_here], 8))
    bias_store = p.copy(bias_got.at[2], bias_grad).start()
    thirds[2].relay()
    thirds[1].settle()
    out.finish(out_owned)
    thirds[0].finish(proj_owned.at[0])
    thirds[2].settle()
    thirds[1].finish(proj_owned.at[1])
    thirds[2].finish(proj_owned.at[2])
    for weight in [out, *thirds]:
        weight.stored()
    scatter.finish()
    for sent in vector_sends:
        sent.left()
    wait_all(stores)
    vector_store.wait()
    bias_store.wait()


def call(body, name, collective, inputs, in_specs, outs, scratch, counts):
    bf16_bytes = sum(math.prod(o.shape) * o.dtype.itemsize for o in outs)
    return pl.pallas_call(
        body,
        out_shape=outs,
        in_specs=in_specs,
        out_specs=[ANY] * len(outs),
        scratch_shapes=[
            *scratch,
            pltpu.SemaphoreType.DMA((counts[0],)),
            pltpu.SemaphoreType.DMA((counts[1],)),
            pltpu.SemaphoreType.DMA((counts[2],)),
        ],
        compiler_params=pltpu.CompilerParams(
            collective_id=collective, has_side_effects=True, vmem_limit_bytes=VMEM_BYTES
        ),
        cost_estimate=pl.CostEstimate(
            flops=0, bytes_accessed=2 * bf16_bytes, transcendentals=0
        ),
        name=name,
    )(*inputs)


def bf16(*shape):
    return jax.ShapeDtypeStruct(shape, jnp.bfloat16)


def f32(*shape):
    return jax.ShapeDtypeStruct(shape, jnp.float32)


def held(shape_struct):
    return pltpu.VMEM(shape_struct.shape, shape_struct.dtype)


def weight_scratch(quarter, eighth):
    return [
        held(bf16(2, *quarter)), held(bf16(2, *quarter)), held(bf16(2, *eighth)),
        held(bf16(2, *eighth)), held(f32(*eighth)),
    ]


WHOLE = pl.BlockSpec(memory_space=pltpu.VMEM)
EIGHTH = 256


def local_pairs(
    inputs,
    gain_first,
    shift_first,
    projections,
    biases,
    output_weight,
    gain_second,
    shift_second,
    gate_up,
    down_weight,
    cotangent,
):
    dp_index, tensor_index = lax.axis_index("dp"), lax.axis_index("tensor")
    first_core = dp_index % 2 == 0
    late_half = tensor_index % 2 == 1
    count, width = inputs.shape
    rows = 4 * count
    heads_width = output_weight.shape[0]
    hidden_width = down_weight.shape[0]
    local_heads = heads_width // HD
    head_shape = (2, SEQ_LEN, local_heads, HD)
    quarter_width = width // 4

    def width_part(array, k):
        return array[:, k * quarter_width : (k + 1) * quarter_width]

    positions = jnp.arange(SEQ_LEN)
    positions = jnp.where(late_half, (positions + SEQ_LEN // 2) % SEQ_LEN, positions)
    cosine, sine = (
        jnp.where(late_half, jnp.roll(table, SEQ_LEN // 2, axis=0), table)
        for table in angle_tables()
    )
    vectors = jnp.pad(
        jnp.stack([gain_first, shift_first, gain_second, shift_second]).astype(jnp.float32),
        ((0, 4), (0, 0)),
    )
    quarter_biases = jnp.where(first_core, biases, own_quarter(biases)).astype(jnp.float32)

    proj_full, out_full, gate_pair, vectors, gathered_one, gathered_cot = call(
        front_kernel, "gather_first", 1,
        (inputs, cotangent, vectors, projections, output_weight, gate_up),
        [ANY] * 6,
        [
            bf16(3, width, heads_width), bf16(heads_width, width), bf16(2, EIGHTH, hidden_width),
            f32(8, width), bf16(rows, width), bf16(rows, width),
        ],
        [held(bf16(count, width)), held(bf16(count, width)), held(bf16(count, width)), held(f32(8, width))],
        (64, 64, 40),
    )

    pre_all = jnp.einsum("gd,jde->jge", gathered_one, proj_full, preferred_element_type=jnp.float32)
    pre_all = pre_all + quarter_biases[:, None, :]
    queries = rotate(pre_all[0].reshape(head_shape), cosine, sine, 1.0).astype(jnp.bfloat16)
    key_rows = rotate(pre_all[1].reshape(head_shape), cosine, sine, 1.0).astype(jnp.bfloat16)
    value_rows = pre_all[2].reshape(head_shape).astype(jnp.bfloat16)
    mixed, log_totals = lax.map(
        lambda pieces: attend_forward(pieces, positions), (queries, key_rows, value_rows)
    )
    mixed_rows = mixed.reshape(rows, heads_width)
    term = jnp.dot(mixed_rows, out_full, preferred_element_type=jnp.float32).astype(jnp.bfloat16)

    gu_full, down_full, middle, gathered_two = call(
        middle_kernel, "gather_second", 2,
        (term, inputs, vectors, gate_pair, gate_up, down_weight),
        [ANY, ANY, WHOLE, ANY, ANY, ANY],
        [
            bf16(2, width, hidden_width), bf16(hidden_width, width), f32(count, width),
            bf16(rows, width),
        ],
        [
            held(bf16(count, width)), held(bf16(2 * count, width)), held(bf16(2 * count, width)),
            held(bf16(count, width)), held(f32(count, width)), held(bf16(count, width)),
        ],
        (48, 48, 24),
    )
    gate_act = jnp.dot(gathered_two, gu_full[0], preferred_element_type=jnp.float32)
    up_act = jnp.dot(gathered_two, gu_full[1], preferred_element_type=jnp.float32)
    sigmoid_gate = jax.nn.sigmoid(gate_act)
    hidden = (gate_act * sigmoid_gate * up_act).astype(jnp.bfloat16)
    out_term = jnp.dot(hidden, down_full, preferred_element_type=jnp.float32).astype(jnp.bfloat16)

    def quarters(product):
        return [product(k).astype(jnp.bfloat16) for k in range(4)]

    down_parts = quarters(
        lambda k: jnp.einsum(
            "gf,gd->fd", hidden, width_part(gathered_cot, k), preferred_element_type=jnp.float32
        )
    )
    grad_hidden = jnp.einsum(
        "gd,fd->gf", gathered_cot, down_full, preferred_element_type=jnp.float32
    )
    grad_up = (grad_hidden * gate_act * sigmoid_gate).astype(jnp.bfloat16)
    grad_gate = (
        grad_hidden * up_act * sigmoid_gate * (1.0 + gate_act * (1.0 - sigmoid_gate))
    ).astype(jnp.bfloat16)
    second_term = (
        jnp.einsum("gf,df->gd", grad_gate, gu_full[0], preferred_element_type=jnp.float32)
        + jnp.einsum("gf,df->gd", grad_up, gu_full[1], preferred_element_type=jnp.float32)
    ).astype(jnp.bfloat16)
    gate_parts, up_parts = (
        quarters(
            lambda k: jnp.einsum(
                "gd,gf->df",
                width_part(gathered_two, k),
                incoming,
                preferred_element_type=jnp.float32,
            )
        )
        for incoming in (grad_gate, grad_up)
    )

    by_rows = ((2 * EIGHTH, hidden_width), (EIGHTH, hidden_width))
    by_columns = ((hidden_width, 2 * EIGHTH), (hidden_width, EIGHTH))
    outputs, grad_middle, gathered_branch, sums, gu_owned, down_owned = call(
        back_kernel, "scatter_first", 3,
        (second_term, out_term, middle, cotangent, vectors, *down_parts, *gate_parts, *up_parts),
        [ANY] * 4 + [WHOLE] + [ANY] * 12,
        [
            bf16(count, width), f32(count, width), bf16(rows, width), f32(8, width),
            f32(2, EIGHTH, hidden_width), f32(hidden_width, EIGHTH),
        ],
        [
            held(f32(count, width)), held(bf16(count, width)),
            held(bf16(2 * count, width)), held(bf16(2 * count, width)), held(bf16(count, width)),
            held(bf16(2 * count, width)), held(bf16(2 * count, width)), held(bf16(count, width)),
            held(bf16(count, width)), held(f32(count, width)), held(f32(8, width)), held(f32(8, width)),
            *weight_scratch(*by_columns), *weight_scratch(*by_rows), *weight_scratch(*by_rows),
        ],
        (64, 64, 48),
    )

    grad_mixed = jnp.einsum(
        "gd,ed->ge", gathered_branch, out_full, preferred_element_type=jnp.float32
    ).astype(jnp.bfloat16)
    out_parts = quarters(
        lambda k: jnp.einsum(
            "ge,gd->ed",
            mixed_rows,
            width_part(gathered_branch, k),
            preferred_element_type=jnp.float32,
        )
    )
    grad_queries, grad_keys, grad_values = lax.map(
        lambda pieces: attend_back(pieces, positions),
        (queries, key_rows, value_rows, grad_mixed.reshape(head_shape), log_totals),
    )
    grad_queries = rotate(grad_queries, cosine, sine, -1.0)
    grad_keys = rotate(grad_keys, cosine, sine, -1.0)
    grad_pre = (
        jnp.stack([grad_queries, grad_keys, grad_values])
        .reshape(3, rows, heads_width)
        .astype(jnp.bfloat16)
    )
    proj_parts = quarters(
        lambda k: jnp.einsum(
            "gd,jge->jde",
            width_part(gathered_one, k),
            grad_pre,
            preferred_element_type=jnp.float32,
        )
    )
    first_term = jnp.einsum(
        "jge,jde->gd", grad_pre, proj_full, preferred_element_type=jnp.float32
    ).astype(jnp.bfloat16)
    bias_part = jnp.pad(jnp.sum(grad_pre, axis=1, dtype=jnp.float32), ((0, 5), (0, 0)))

    by_rows = ((2 * EIGHTH, heads_width), (EIGHTH, heads_width))
    by_columns = ((heads_width, 2 * EIGHTH), (heads_width, EIGHTH))
    input_grads, proj_owned, out_owned, vector_grads, bias_grad = call(
        last_kernel, "scatter_second", 4,
        (first_term, inputs, vectors, grad_middle, sums, bias_part, *out_parts, *proj_parts),
        [ANY, ANY, WHOLE, ANY, WHOLE, ANY] + [ANY] * 8,
        [
            f32(count, width), f32(3, EIGHTH, heads_width), f32(heads_width, EIGHTH),
            f32(8, EIGHTH), f32(8, heads_width),
        ],
        [
            held(bf16(count, width)), held(bf16(2 * count, width)), held(bf16(2 * count, width)),
            held(bf16(count, width)), held(f32(count, width)), held(f32(8, width)), held(f32(8, width)),
            held(f32(7, 8, EIGHTH)), held(f32(2, 8, EIGHTH)), held(f32(2, 8, EIGHTH)),
            held(f32(8, heads_width)), held(f32(4, 8, heads_width)),
            *weight_scratch(*by_columns),
            *weight_scratch(*by_rows), *weight_scratch(*by_rows), *weight_scratch(*by_rows),
        ],
        (64, 64, 48),
    )
    return (
        outputs,
        input_grads,
        vector_grads[0],
        vector_grads[1],
        proj_owned,
        bias_grad[:3],
        out_owned,
        vector_grads[2],
        vector_grads[3],
        gu_owned,
        down_owned,
    )


def solution(mesh):
    whole_pairs = dict(mesh.shape) == {"dp": 8, "tensor": 4}
    return jax.shard_map(
        local_pairs if whole_pairs else local,
        mesh=mesh,
        in_specs=(
            P(("dp", "tensor"), None),
            P("dp"),
            P("dp"),
            P(None, "dp", "tensor"),
            P(None, "tensor"),
            P("tensor", "dp"),
            P("dp"),
            P("dp"),
            P(None, "dp", "tensor"),
            P("tensor", "dp"),
            P(("dp", "tensor"), None),
        ),
        out_specs=(
            P(("dp", "tensor"), None),
            P(("dp", "tensor"), None),
            P("dp"),
            P("dp"),
            P(None, "dp", "tensor"),
            P(None, "tensor"),
            P("tensor", "dp"),
            P("dp"),
            P("dp"),
            P(None, "dp", "tensor"),
            P("tensor", "dp"),
        ),
        check_vma=False,
    )
```

```python
import math

import jax
import jax.numpy as jnp
from jax import lax
from jax.experimental import pallas as pl
from jax.experimental.pallas import tpu as pltpu
from jax.sharding import PartitionSpec as P

HD = 64
ROTARY = 16
SEQ_LEN = 512


EPSILON = 1e-05
ANGLE_BASE = 10000.0
NEGATIVE = -1e30


def norm_rows(rows, gain, shift):
    average = jnp.mean(rows, axis=-1, keepdims=True)
    centred = rows - average
    inverse = lax.rsqrt(jnp.mean(centred * centred, axis=-1, keepdims=True) + EPSILON)
    unit_rows = centred * inverse
    return (unit_rows * gain + shift, unit_rows, inverse)


def norm_back(incoming, unit_rows, inverse, gain):
    scaled = incoming * gain
    inner = (
        scaled
        - jnp.mean(scaled, axis=-1, keepdims=True)
        - unit_rows * jnp.mean(scaled * unit_rows, axis=-1, keepdims=True)
    )
    return (inner * inverse, jnp.sum(incoming * unit_rows, axis=0), jnp.sum(incoming, axis=0))


def angle_tables():
    freqs = 1.0 / ANGLE_BASE ** (jnp.arange(0, ROTARY, 2).astype(jnp.float32) / ROTARY)
    angles = jnp.arange(SEQ_LEN).astype(jnp.float32)[:, None] * freqs[None, :]
    return (jnp.cos(angles), jnp.sin(angles))


def rotate(heads, cosine, sine, sign):
    half_rot = ROTARY // 2
    first = heads[..., :half_rot]
    latter = heads[..., half_rot:ROTARY]
    cos_part = cosine[:, None, :]
    sin_part = sine[:, None, :] * sign
    return jnp.concatenate(
        [
            first * cos_part - latter * sin_part,
            latter * cos_part + first * sin_part,
            heads[..., ROTARY:],
        ],
        axis=-1,
    )


def causal_scores(queries, key_rows, positions):
    scaling = 1.0 / math.sqrt(HD)
    scores = scaling * jnp.einsum(
        "qhd,khd->hqk", queries, key_rows, preferred_element_type=jnp.float32
    )
    causal = positions[:, None] >= positions[None, :]
    return jnp.where(causal[None], scores, NEGATIVE)


def attend_forward(pieces, positions):
    queries, key_rows, value_rows = pieces
    scores = causal_scores(queries, key_rows, positions)
    row_top = jnp.max(scores, axis=-1, keepdims=True)
    exponent = jnp.exp(scores - row_top)
    totals = jnp.sum(exponent, axis=-1, keepdims=True)
    weights = (exponent / totals).astype(jnp.bfloat16)
    mixed = jnp.einsum("hqk,khd->qhd", weights, value_rows, preferred_element_type=jnp.float32)
    return (mixed.astype(jnp.bfloat16), (row_top + jnp.log(totals))[..., 0])


def attend_back(pieces, positions):
    queries, key_rows, value_rows, grad_mixed, log_totals = pieces
    scaling = 1.0 / math.sqrt(HD)
    scores = causal_scores(queries, key_rows, positions)
    weights = jnp.exp(scores - log_totals[..., None])
    grad_values = jnp.einsum(
        "hqk,qhd->khd", weights.astype(jnp.bfloat16), grad_mixed, preferred_element_type=jnp.float32
    )
    grad_weights = jnp.einsum(
        "qhd,khd->hqk", grad_mixed, value_rows, preferred_element_type=jnp.float32
    )
    grad_scores = weights * (grad_weights - jnp.sum(weights * grad_weights, axis=-1, keepdims=True))
    grad_scores = grad_scores.astype(jnp.bfloat16)
    grad_queries = scaling * jnp.einsum(
        "hqk,khd->qhd", grad_scores, key_rows, preferred_element_type=jnp.float32
    )
    grad_keys = scaling * jnp.einsum(
        "hqk,qhd->khd", grad_scores, queries, preferred_element_type=jnp.float32
    )
    return (grad_queries, grad_keys, grad_values)


def scatter_sum(terms, axis, dimension):
    owned = lax.psum_scatter(
        terms.astype(jnp.bfloat16), axis, scatter_dimension=dimension, tiled=True
    )
    return owned.astype(jnp.float32)


def local(
    inputs,
    gain_first,
    shift_first,
    projections,
    biases,
    output_weight,
    gain_second,
    shift_second,
    gate_up,
    down_weight,
    cotangent,
):
    tensor_ways = lax.axis_size("tensor")
    row_count = inputs.shape[0]
    group_rows = row_count * tensor_ways
    sequences = group_rows // SEQ_LEN
    head_width = output_weight.shape[0]
    local_heads = head_width // HD
    head_shape = (sequences, SEQ_LEN, local_heads, HD)
    cosine, sine = angle_tables()
    positions = jnp.arange(SEQ_LEN)
    proj_full, out_full, gain_one, shift_one = (
        lax.all_gather(projections, "dp", axis=1, tiled=True),
        lax.all_gather(output_weight, "dp", axis=1, tiled=True),
        lax.all_gather(gain_first, "dp", axis=0, tiled=True),
        lax.all_gather(shift_first, "dp", axis=0, tiled=True),
    )
    gain_one = gain_one.astype(jnp.float32)
    residual = inputs.astype(jnp.float32)
    normed_one, unit_one, inverse_one = norm_rows(residual, gain_one, shift_one.astype(jnp.float32))
    gathered_one = lax.all_gather(normed_one.astype(jnp.bfloat16), "tensor", axis=0, tiled=True)
    pre_all = jnp.einsum("gd,jde->jge", gathered_one, proj_full, preferred_element_type=jnp.float32)
    pre_all = pre_all + biases.astype(jnp.float32)[:, None, :]
    queries = rotate(pre_all[0].reshape(head_shape), cosine, sine, 1.0).astype(jnp.bfloat16)
    key_rows = rotate(pre_all[1].reshape(head_shape), cosine, sine, 1.0).astype(jnp.bfloat16)
    value_rows = pre_all[2].reshape(head_shape).astype(jnp.bfloat16)
    mixed, log_totals = lax.map(
        lambda pieces: attend_forward(pieces, positions), (queries, key_rows, value_rows)
    )
    mixed_rows = mixed.reshape(group_rows, head_width)
    part = mixed_rows
    middle = residual + scatter_sum(
        jnp.dot(part, out_full, preferred_element_type=jnp.float32), "tensor", 0
    )
    gu_full, down_full, gain_two, shift_two = (
        lax.all_gather(gate_up, "dp", axis=1, tiled=True),
        lax.all_gather(down_weight, "dp", axis=1, tiled=True),
        lax.all_gather(gain_second, "dp", axis=0, tiled=True),
        lax.all_gather(shift_second, "dp", axis=0, tiled=True),
    )
    gain_two = gain_two.astype(jnp.float32)
    normed_two, unit_two, inverse_two = norm_rows(middle, gain_two, shift_two.astype(jnp.float32))
    gathered_two = lax.all_gather(normed_two.astype(jnp.bfloat16), "tensor", axis=0, tiled=True)
    gate_act = jnp.dot(gathered_two, gu_full[0], preferred_element_type=jnp.float32)
    up_act = jnp.dot(gathered_two, gu_full[1], preferred_element_type=jnp.float32)
    sigmoid_gate = jax.nn.sigmoid(gate_act)
    hidden = (gate_act * sigmoid_gate * up_act).astype(jnp.bfloat16)
    part = hidden
    outputs = (
        middle
        + scatter_sum(jnp.dot(part, down_full, preferred_element_type=jnp.float32), "tensor", 0)
    ).astype(jnp.bfloat16)
    gu_back, down_back, gain_two_back = (
        lax.all_gather(gate_up, "dp", axis=1, tiled=True),
        lax.all_gather(down_weight, "dp", axis=1, tiled=True),
        lax.all_gather(gain_second, "dp", axis=0, tiled=True),
    )
    gain_two_back = gain_two_back.astype(jnp.float32)
    gathered_cot = lax.all_gather(cotangent, "tensor", axis=0, tiled=True)
    grad_hidden = jnp.einsum(
        "gd,fd->gf", gathered_cot, down_back, preferred_element_type=jnp.float32
    )
    down_grad = jnp.einsum("gf,gd->fd", hidden, gathered_cot, preferred_element_type=jnp.float32)
    grad_up = (grad_hidden * gate_act * sigmoid_gate).astype(jnp.bfloat16)
    grad_gate = (
        grad_hidden * up_act * sigmoid_gate * (1.0 + gate_act * (1.0 - sigmoid_gate))
    ).astype(jnp.bfloat16)
    gu_grad = jnp.stack(
        [
            jnp.einsum("gd,gf->df", gathered_two, grad_gate, preferred_element_type=jnp.float32),
            jnp.einsum("gd,gf->df", gathered_two, grad_up, preferred_element_type=jnp.float32),
        ]
    )
    first_term = jnp.einsum("gf,df->gd", grad_gate, gu_back[0], preferred_element_type=jnp.float32)
    grad_second = scatter_sum(
        first_term
        + jnp.einsum("gf,df->gd", grad_up, gu_back[1], preferred_element_type=jnp.float32),
        "tensor",
        0,
    )
    gu_owned, down_owned = (
        scatter_sum(gu_grad, "dp", 1),
        scatter_sum(down_grad, "dp", 1),
    )
    grad_mid_norm, gain_two_part, shift_two_part = norm_back(
        grad_second, unit_two, inverse_two, gain_two_back
    )
    grad_middle = cotangent.astype(jnp.float32) + grad_mid_norm
    proj_back, out_back, gain_one_back = (
        lax.all_gather(projections, "dp", axis=1, tiled=True),
        lax.all_gather(output_weight, "dp", axis=1, tiled=True),
        lax.all_gather(gain_first, "dp", axis=0, tiled=True),
    )
    gain_one_back = gain_one_back.astype(jnp.float32)
    gathered_branch = lax.all_gather(grad_middle.astype(jnp.bfloat16), "tensor", axis=0, tiled=True)
    out_grad = jnp.einsum(
        "ge,gd->ed", mixed_rows, gathered_branch, preferred_element_type=jnp.float32
    )
    grad_mixed = jnp.einsum(
        "gd,ed->ge", gathered_branch, out_back, preferred_element_type=jnp.float32
    ).astype(jnp.bfloat16)
    grad_queries, grad_keys, grad_values = lax.map(
        lambda pieces: attend_back(pieces, positions),
        (queries, key_rows, value_rows, grad_mixed.reshape(head_shape), log_totals),
    )
    grad_queries = rotate(grad_queries, cosine, sine, -1.0)
    grad_keys = rotate(grad_keys, cosine, sine, -1.0)
    grad_pre = (
        jnp.stack([grad_queries, grad_keys, grad_values])
        .reshape(3, group_rows, head_width)
        .astype(jnp.bfloat16)
    )
    bias_part = jnp.sum(grad_pre, axis=1, dtype=jnp.float32)
    proj_grad = jnp.einsum(
        "gd,jge->jde", gathered_one, grad_pre, preferred_element_type=jnp.float32
    )
    part = grad_pre
    grad_normed = scatter_sum(
        jnp.einsum("jge,jde->gd", part, proj_back, preferred_element_type=jnp.float32),
        "tensor",
        0,
    )
    proj_owned, out_owned = (
        scatter_sum(proj_grad, "dp", 1),
        scatter_sum(out_grad, "dp", 1),
    )
    grad_in_norm, gain_one_part, shift_one_part = norm_back(
        grad_normed, unit_one, inverse_one, gain_one_back
    )
    input_grads = grad_middle + grad_in_norm
    one_hot = (jnp.arange(tensor_ways) == lax.axis_index("tensor")).astype(jnp.float32)
    spread_bias = (bias_part[:, None, :] * one_hot[None, :, None]).reshape(
        3, tensor_ways * head_width
    )
    summed = lax.psum(
        (gain_one_part, shift_one_part, gain_two_part, shift_two_part, spread_bias),
        ("dp", "tensor"),
    )
    own_width = gain_first.shape[0]
    own_offset = lax.axis_index("dp") * own_width

    def own_part(vector):
        return lax.dynamic_slice_in_dim(vector, own_offset, own_width, 0)

    bias_grad = jnp.sum(
        summed[4].reshape(3, tensor_ways, head_width) * one_hot[None, :, None], axis=1
    )
    return (
        outputs,
        input_grads,
        own_part(summed[0]),
        own_part(summed[1]),
        proj_owned,
        bias_grad,
        out_owned,
        own_part(summed[2]),
        own_part(summed[3]),
        gu_owned,
        down_owned,
    )


def send_between(array, routes):
    tensor_ways = lax.axis_size("tensor")
    pairs = [(d * tensor_ways + t, e * tensor_ways + s) for (d, t), (e, s) in routes]
    return lax.ppermute(array, ("dp", "tensor"), pairs)


def places():
    return [(d, t) for d in range(lax.axis_size("dp")) for t in range(lax.axis_size("tensor"))]


def own_quarter(array):
    return send_between(
        array,
        [((d, t), (d ^ 1, t) if d & 1 else (d ^ 1, t ^ 2)) for d, t in places()],
    )


ORDER = ((1, 0, 0), (1, 1, 0), (0, 1, 1), (1, 1, 1), (0, 0, 0), (0, 1, 0), (0, 0, 1), (1, 0, 1))
EVEN_Y, EVEN_XY, ODD_X, ODD_XY, EVEN, EVEN_X, ODD, ODD_Y = range(8)
ANY = pl.BlockSpec(memory_space=pl.ANY)
VMEM_BYTES = 63 * 1024 * 1024


class Place:
    def __init__(self, send_sems, recv_sems, local_sems):
        self.dp, self.tensor = lax.axis_index("dp"), lax.axis_index("tensor")
        self.core = lax.rem(self.dp, 2)
        self.x = lax.rem(self.dp // 2, 2)
        self.y = self.dp // 4
        self.pools = {"send": send_sems, "recv": recv_sems, "local": local_sems}
        self.used = {"send": 0, "recv": 0, "local": 0}

    def take(self, kind):
        self.used[kind] += 1
        return self.pools[kind].at[self.used[kind] - 1]

    def at(self, x=0, y=0, core=0, near=0, far=0):
        dp = self.dp
        dp = dp + x * (2 - 4 * self.x) + y * (4 - 8 * self.y) + core * (1 - 2 * self.core)
        tensor = self.tensor
        tensor = tensor + near * (1 - 2 * lax.rem(tensor, 2)) + far * (2 - 4 * (tensor // 2))
        return (dp, tensor)

    def column(self, key):
        dy, dx, core = key
        y = self.y + dy * (1 - 2 * self.y)
        x = self.x + dx * (1 - 2 * self.x)
        return pl.multiple_of((y * 4 + x * 2 + core) * EIGHTH, EIGHTH)

    def greet(self):
        barrier = pltpu.get_barrier_semaphore()
        partners = [
            self.at(x=x, y=y, core=core)
            for x in (0, 1)
            for y in (0, 1)
            for core in (0, 1)
            if x or y or core
        ] + [self.at(near=1), self.at(far=1), self.at(far=1, core=1)]
        for partner in partners:
            pl.semaphore_signal(
                barrier, inc=1, device_id=partner, device_id_type=pl.DeviceIdType.MESH
            )
        pl.semaphore_wait(barrier, len(partners))

    def send(self, source, target, device, recv_sem=None, when=None):
        return Sent(
            pltpu.make_async_remote_copy(
                src_ref=source,
                dst_ref=target,
                send_sem=self.take("send"),
                recv_sem=self.take("recv") if recv_sem is None else recv_sem,
                device_id=device,
                device_id_type=pl.DeviceIdType.MESH,
            ),
            when,
        )

    def copy(self, source, target, when=None):
        return Copied(pltpu.make_async_copy(source, target, self.take("local")), when)


def guarded(when, action):
    if when is None:
        action()
    else:
        pl.when(when)(action)


class Sent:
    def __init__(self, copy, when):
        self.copy, self.when = copy, when

    def start(self):
        guarded(self.when, self.copy.start)
        return self

    def arrived(self, when=None):
        guarded(when, self.copy.wait_recv)

    def left(self):
        guarded(self.when, self.copy.wait_send)


class Copied:
    def __init__(self, copy, when):
        self.copy, self.when = copy, when

    def start(self):
        guarded(self.when, self.copy.start)
        return self

    def wait(self):
        guarded(self.when, self.copy.wait)


class GatherWeight:
    def __init__(self, place, shard, block, pair=None):
        self.place, self.shard, self.block = place, shard, block
        self.sent = []
        self.pair = pair

    def fetch(self, even=None, odd=None):
        p = self.place
        even = self.block(EVEN) if even is None else even
        odd = self.block(ODD) if odd is None else odd
        first, second = p.core == 0, p.core == 1
        self.own = p.copy(self.shard, even, first).start()
        even_sem, odd_sem = p.take("recv"), p.take("recv")
        self.to_far_even = p.send(self.shard, even, p.at(core=1, far=1), even_sem, first).start()
        self.to_sibling = p.send(self.shard, odd, p.at(core=1), odd_sem, second).start()
        self.to_far_odd = p.send(self.shard, odd, p.at(far=1), odd_sem, second).start()
        return self

    def fetched(self):
        p = self.place
        self.own.wait()
        self.to_far_even.arrived(p.core == 1)
        self.to_sibling.arrived()
        return self

    def fetch_left(self):
        self.to_far_even.left()
        self.to_sibling.left()
        self.to_far_odd.left()

    def spread(self, even=None, odd=None):
        p, block = self.place, self.block
        even = block(EVEN) if even is None else even
        odd = block(ODD) if odd is None else odd
        self.even_x = p.send(even, block(EVEN_X), p.at(x=1)).start()
        self.odd_y = p.send(odd, block(ODD_Y), p.at(y=1)).start()
        self.odd_x = p.send(odd, block(ODD_X), p.at(x=1)).start()
        self.even_y = p.send(even, block(EVEN_Y), p.at(y=1)).start()
        return self

    def relay(self):
        p, block = self.place, self.block
        self.even_x.arrived()
        self.even_xy = p.send(block(EVEN_X), block(EVEN_XY), p.at(y=1)).start()
        self.odd_y.arrived()
        self.odd_xy = p.send(block(ODD_Y), block(ODD_XY), p.at(x=1)).start()
        return self

    def finish(self):
        for copy in (self.odd_x, self.even_y, self.even_xy, self.odd_xy):
            copy.arrived()
        for copy in (
            self.even_x, self.odd_y, self.odd_x, self.even_y, self.even_xy, self.odd_xy,
        ):
            copy.left()


class GatherRows:
    def __init__(self, place, own, rows):
        self.place, self.own, self.rows = place, own, rows
        self.count = own.shape[0]

    def slot(self, k):
        return self.rows.at[pl.ds(k * self.count, self.count)]

    def start(self):
        p = self.place
        self.beside = p.send(self.own, self.slot(1), p.at(near=1)).start()
        self.sibling = p.send(self.own, self.slot(2), p.at(core=1)).start()
        self.here = p.copy(self.own, self.slot(0)).start()
        return self

    def relay(self):
        p = self.place
        self.beside.arrived()
        self.across = p.send(self.slot(1), self.slot(3), p.at(core=1)).start()
        return self

    def finish(self):
        self.sibling.arrived()
        self.across.arrived()
        self.here.wait()
        for copy in (self.beside, self.sibling, self.across):
            copy.left()


def combine(target, terms, chunk):
    @pl.loop(0, target.shape[0] // chunk)
    def _(i):
        rows = pl.ds(pl.multiple_of(i * chunk, chunk), chunk)
        total = terms[0][rows].astype(jnp.float32)
        for term in terms[1:]:
            total = total + term[rows].astype(jnp.float32)
        target[rows] = total.astype(target.dtype)


class ScatterRows:
    def __init__(self, place, far, near, got, got_beside):
        self.place, self.far, self.near = place, far, near
        self.got, self.got_beside = got, got_beside
        self.count = near.shape[0] // 2

    def start(self):
        self.sibling = self.place.send(self.far, self.got, self.place.at(core=1)).start()
        return self

    def relay(self):
        p, n = self.place, self.count
        self.sibling.arrived()
        late = pl.ds(n, n)
        combine(self.near.at[late], [self.near.at[late], self.got.at[late]], 32)
        self.beside = p.send(self.near.at[late], self.got_beside, p.at(near=1)).start()
        return self

    def total(self, rows):
        return (
            self.near[rows].astype(jnp.float32)
            + self.got[rows].astype(jnp.float32)
            + self.got_beside[rows].astype(jnp.float32)
        )

    def arrived(self):
        self.beside.arrived()

    def finish(self):
        self.sibling.left()
        self.beside.left()


class ScatterWeight:
    def __init__(self, place, send, keep, rows, got, last, home, result):
        self.place, self.parts, self.keep, self.rows = place, send, keep, rows
        self.got, self.last, self.home, self.result = got, last, home, result
        self.loads = []

    def half(self, ref, k):
        if self.rows:
            size = ref.shape[0] // 2
            return ref.at[pl.ds(k * size, size)]
        size = ref.shape[1] // 2
        return ref.at[:, pl.ds(k * size, size)]

    def load(self, sources):
        self.loads = [self.place.copy(a, b).start() for a, b in zip(sources, self.keep)]
        return self

    def start_even(self):
        p = self.place
        self.even = p.send(self.parts[0], self.got.at[0], p.at(y=1)).start()
        return self

    def start_odd(self):
        p = self.place
        self.odd = p.send(self.parts[1], self.got.at[1], p.at(x=1)).start()
        return self

    def start(self):
        return self.start_even().start_odd()

    def relay(self):
        p = self.place
        wait_all(self.loads)
        self.second = []
        for k, arrival in enumerate((self.even, self.odd)):
            arrival.arrived()
            there = self.half(self.keep[k], 1)
            combine(there, [there, self.half(self.got.at[k], 1)], 64)
            device = p.at(x=1) if k == 0 else p.at(y=1)
            self.second.append(p.send(there, self.last.at[k], device).start())
        return self

    def settle(self):
        p = self.place

        def terms(k):
            return [self.half(self.keep[k], 0), self.half(self.got.at[k], 0), self.last.at[k]]

        even_out, odd_out = self.half(self.keep[0], 0), self.half(self.keep[1], 0)
        first, second = p.core == 0, p.core == 1
        near_sem, far_sem = p.take("recv"), p.take("recv")
        self.second[1].arrived()
        combine(odd_out, terms(1), 64)
        self.to_sibling = p.send(odd_out, self.home.at[0], p.at(core=1), near_sem, first).start()
        self.to_far = p.send(odd_out, self.home.at[1], p.at(far=1), far_sem, second).start()
        self.second[0].arrived()
        pl.when(first)(lambda: combine(self.result, terms(0), 64))
        pl.when(second)(lambda: combine(even_out, terms(0), 64))
        self.to_first = p.send(
            even_out, self.home.at[0], p.at(core=1, far=1), near_sem, second
        ).start()
        return self

    def finish(self, output):
        p = self.place
        first, second = p.core == 0, p.core == 1
        self.to_sibling.arrived()
        self.to_far.arrived(second)
        pl.when(first)(lambda: combine(self.result, [self.result, self.home.at[0]], 64))
        pl.when(second)(lambda: combine(self.result, [self.home.at[0], self.home.at[1]], 64))
        self.store = p.copy(self.result, output).start()
        for copy in (self.even, self.odd, *self.second, self.to_sibling, self.to_first, self.to_far):
            copy.left()

    def stored(self):
        self.store.wait()


def load_local(place, source, target):
    return [
        place.copy(
            source.at[:, pl.ds(place.column(key), EIGHTH)], target.at[:, pl.ds(j * EIGHTH, EIGHTH)]
        ).start()
        for j, key in enumerate(ORDER)
    ]


def store_natural(place, source, target):
    return [
        place.copy(
            source.at[:, pl.ds(j * EIGHTH, EIGHTH)], target.at[:, pl.ds(place.column(key), EIGHTH)]
        ).start()
        for j, key in enumerate(ORDER)
    ]


def wait_all(copies):
    for copy in copies:
        copy.wait()


CHUNK = 32


def norm_into(count, rows_of, gain, shift, target):
    @pl.loop(0, count // CHUNK)
    def _(i):
        rows = pl.ds(pl.multiple_of(i * CHUNK, CHUNK), CHUNK)
        target[rows] = norm_rows(rows_of(rows), gain, shift)[0].astype(target.dtype)


def front_kernel(
    inputs, cotangent, vectors, projections, output_weight, gate_up,
    proj_full, out_full, gate_pair, vectors_full, rows_one, rows_cot,
    own, normed, own_cot, vectors_here, send_sems, recv_sems, local_sems,
):
    p = Place(send_sems, recv_sems, local_sems)
    loads = load_local(p, inputs, own)
    cot_loads = load_local(p, cotangent, own_cot)
    p.greet()
    slots = {key: j for j, key in enumerate(ORDER)}
    vector_sem = [p.take("recv") for _ in ORDER]
    del vector_sem
    vector_base = p.used["recv"] - len(ORDER)

    def vector_copy(dy, dx, core):
        here, there = slots[(dy, dx, 0)], slots[(dy, dx, 1)]
        slot = here + p.core * (there - here)
        columns = pl.ds(pl.multiple_of(slot * EIGHTH, EIGHTH), EIGHTH)
        return p.send(
            vectors, vectors_here.at[:, columns], p.at(x=dx, y=dy, core=core),
            recv_sems.at[vector_base + slot],
        )

    vector_sends = [
        vector_copy(dy, dx, core).start()
        for dy in (0, 1) for dx in (0, 1) for core in (0, 1) if dy or dx or core
    ]
    own_slot = slots[(0, 0, 0)] + p.core * (slots[(0, 0, 1)] - slots[(0, 0, 0)])
    own_vectors = p.copy(
        vectors, vectors_here.at[:, pl.ds(pl.multiple_of(own_slot * EIGHTH, EIGHTH), EIGHTH)]
    ).start()

    def quarter(j):
        return GatherWeight(
            p, projections.at[j], lambda k: proj_full.at[j, pl.ds(k * EIGHTH, EIGHTH)]
        )

    weights = [quarter(0), quarter(1), quarter(2)]
    weights.append(
        GatherWeight(p, output_weight, lambda k: out_full.at[:, pl.ds(k * EIGHTH, EIGHTH)])
    )
    gate = GatherWeight(p, gate_up.at[0], lambda k: gate_pair.at[k])
    weights[0].fetch()
    weights[1].fetch()
    wait_all(cot_loads)
    wait_all(loads)
    own_vectors.wait()
    sibling_slot = slots[(0, 0, 1)] + p.core * (slots[(0, 0, 0)] - slots[(0, 0, 1)])
    for dy in (0, 1):
        for dx in (0, 1):
            for core in (0, 1):
                if dy or dx:
                    slot = slots[(dy, dx, core)]
                elif core:
                    slot = sibling_slot
                else:
                    continue
                pltpu.make_async_copy(
                    vectors, vectors_here.at[:, pl.ds(0, EIGHTH)], recv_sems.at[vector_base + slot]
                ).wait()
    gain, shift = vectors_here[0:1], vectors_here[1:2]
    norm_into(own.shape[0], lambda rows: own[rows].astype(jnp.float32), gain, shift, normed)
    gather_one = GatherRows(p, normed, rows_one).start()
    gather_cot = GatherRows(p, own_cot, rows_cot)
    vector_store = p.copy(vectors_here, vectors_full).start()

    weights[0].fetched().spread()
    weights[2].fetch()
    weights[1].fetched().spread()
    weights[3].fetch()
    weights[0].relay()
    weights[2].fetched().spread()
    gather_one.relay()
    gather_cot.start()
    weights[1].relay()
    gate.fetch(gate_pair.at[0], gate_pair.at[1])
    weights[3].fetched().spread()
    weights[2].relay()
    weights[3].relay()
    gather_cot.relay()
    for weight in weights:
        weight.finish()
        weight.fetch_left()
    gather_one.finish()
    gather_cot.finish()
    gate.fetched()
    gate.fetch_left()
    for sent in vector_sends:
        sent.left()
    vector_store.wait()


def tiles(count, tile, body):
    @pl.loop(0, count // tile)
    def _(i):
        body(pl.ds(pl.multiple_of(i * tile, tile), tile))


def shifted(rows, offset):
    return pl.ds(pl.multiple_of(rows.start + offset, 256), rows.size)


def dot(left, right, contract):
    return lax.dot_general(
        left, right, (((contract[0],), (contract[1],)), ((), ())), preferred_element_type=jnp.float32
    )


def middle_kernel(
    term, inputs, vectors, gate_pair, gate_up, down_weight,
    gu_full, down_full, middle, rows_two, hidden_out, gate_out, up_out,
    own, near, got, got_beside, total, normed, gu_here, rows_here, gate_wide, hidden, gate_act, up_act,
    send_sems, recv_sems, local_sems,
):
    p = Place(send_sems, recv_sems, local_sems)
    count = own.shape[0]
    loads = load_local(p, inputs, own)
    near_load = p.copy(term.at[pl.ds(0, 2 * count)], near).start()

    def gu_block(j):
        return lambda k: gu_here.at[j, pl.ds(k * EIGHTH, EIGHTH)]

    gate = GatherWeight(p, None, gu_block(0))
    up = GatherWeight(p, gate_up.at[1], gu_block(1))
    down = GatherWeight(p, down_weight, lambda k: down_full.at[:, pl.ds(k * EIGHTH, EIGHTH)])
    p.greet()
    scatter = ScatterRows(p, term.at[pl.ds(2 * count, 2 * count)], near, got, got_beside).start()
    gate.spread(gate_pair.at[0], gate_pair.at[1])
    places = [
        p.copy(gate_pair.at[0], gate.block(EVEN)).start(),
        p.copy(gate_pair.at[1], gate.block(ODD)).start(),
    ]
    up.fetch()
    near_load.wait()
    scatter.relay()
    gate.relay()
    up.fetched()
    up.spread()
    wait_all(loads)
    scatter.arrived()
    gain, shift = vectors[2:3], vectors[3:4]

    def norm(rows):
        value = own[rows].astype(jnp.float32) + scatter.total(rows)
        total[rows] = value
        normed[rows] = norm_rows(value, gain, shift)[0].astype(normed.dtype)

    tiles(count, CHUNK, norm)
    gather = GatherRows(p, normed, rows_here).start()
    stores = [p.copy(total, middle).start()]
    down.fetch()
    gather.relay()
    up.relay()
    down.fetched()
    down.spread()
    gate.finish()
    wait_all(places)
    gather.finish()
    stores.append(p.copy(rows_here, rows_two).start())
    stores.append(p.copy(gu_here.at[0], gu_full.at[0]).start())

    def gate_rows(rows):
        gate_wide[rows] = dot(rows_here[rows], gu_here[0], (1, 0))

    tiles(4 * count, 256, gate_rows)
    up.finish()
    stores.append(p.copy(gu_here.at[1], gu_full.at[1]).start())

    def up_rows(rows):
        wide_up = dot(rows_here[rows], gu_here[1], (1, 0))
        wide_gate = gate_wide[rows]
        hidden[rows] = (wide_gate * jax.nn.sigmoid(wide_gate) * wide_up).astype(hidden.dtype)
        gate_act[rows] = wide_gate.astype(gate_act.dtype)
        up_act[rows] = wide_up.astype(up_act.dtype)

    tiles(2 * count, 256, up_rows)
    down.relay()
    tiles(2 * count, 256, lambda rows: up_rows(shifted(rows, 2 * count)))
    stores.append(p.copy(hidden, hidden_out).start())
    stores.append(p.copy(gate_act, gate_out).start())
    stores.append(p.copy(up_act, up_out).start())
    down.finish()
    up.fetch_left()
    down.fetch_left()
    scatter.finish()
    wait_all(stores)


def norm_back_rows(value, incoming, gain):
    average = jnp.mean(value, axis=-1, keepdims=True)
    centred = value - average
    inverse = lax.rsqrt(jnp.mean(centred * centred, axis=-1, keepdims=True) + EPSILON)
    unit = centred * inverse
    scaled = incoming * gain
    inner = (
        scaled
        - jnp.mean(scaled, axis=-1, keepdims=True)
        - unit * jnp.mean(scaled * unit, axis=-1, keepdims=True)
    )
    return inner * inverse, incoming * unit


def fold(array):
    return jnp.sum(array.reshape(array.shape[0] // 8, 8, array.shape[1]), axis=0)


def back_kernel(
    hidden_in, gate_in, up_in, cot_rows, rows_two, gu_full, down_full, middle, vectors,
    outputs, grad_middle, rows_branch, sums, down_owned, gate_owned, up_parts, down_parts, gate_parts,
    hidden, gate_act, up_act, cot, rows_here, gate, up, down, value, near, got, got_beside,
    got_out, got_out_beside, gain_sum, shift_sum, staging,
    down_got, down_last, down_home, down_result, gate_got, gate_last, gate_home,
    send_sems, recv_sems, local_sems,
):
    p = Place(send_sems, recv_sems, local_sems)
    count, width = value.shape
    hidden_width = hidden.shape[1]
    quarter = width // 4
    first_loads = [p.copy(hidden_in, hidden).start(), p.copy(cot_rows, cot).start()]
    second_loads = [
        p.copy(down_full, down).start(), p.copy(gate_in, gate_act).start(), p.copy(up_in, up_act).start(),
    ]
    third_loads = [p.copy(gu_full.at[0], gate).start(), p.copy(gu_full.at[1], up).start()]
    last_loads = [p.copy(rows_two, rows_here).start(), p.copy(middle, value).start()]
    p.greet()
    down_sum = ScatterWeight(
        p, [down_parts.at[0], down_parts.at[1]], [staging.at[0], staging.at[1]], False,
        down_got, down_last, down_home, down_result,
    )
    gate_sum = ScatterWeight(
        p, [gate_parts.at[0], gate_parts.at[1]],
        [gate.at[pl.ds(k * quarter, quarter)] for k in (2, 3)], True,
        gate_got, gate_last, gate_home, value.at[:, pl.ds(0, hidden_width)],
    )
    far = cot.at[pl.ds(2 * count, 2 * count)]
    scatter = ScatterRows(p, far, near, got, got_beside)
    out_scatter = ScatterRows(p, far, near, got_out, got_out_beside)

    def down_part(k):
        columns = pl.ds(k * quarter, quarter)
        staging[k % 2] = dot(hidden[...], cot[:, columns], (0, 0)).astype(staging.dtype)

    wait_all(first_loads)
    down_part(0)
    store_even = p.copy(staging.at[0], down_parts.at[0]).start()
    down_part(1)
    store_odd = p.copy(staging.at[1], down_parts.at[1]).start()
    store_even.wait()
    down_sum.start_even()
    down_part(2)
    store_odd.wait()
    down_sum.start_odd()
    down_part(3)
    wait_all(second_loads)

    def hidden_back(rows):
        grad = dot(cot[rows], down[...], (1, 1))
        gate_value = gate_act[rows].astype(jnp.float32)
        up_value = up_act[rows].astype(jnp.float32)
        sigmoid = jax.nn.sigmoid(gate_value)
        scaled = grad * sigmoid
        up_act[rows] = (scaled * gate_value).astype(up_act.dtype)
        gate_act[rows] = (
            scaled * up_value * (1.0 + gate_value * (1.0 - sigmoid))
        ).astype(gate_act.dtype)

    tiles(4 * count, 256, hidden_back)
    wait_all(third_loads)

    def second_rows(target, offset):
        def part(rows):
            here = shifted(rows, offset)
            target[rows] = (
                dot(gate_act[here], gate[...], (1, 1)) + dot(up_act[here], up[...], (1, 1))
            ).astype(target.dtype)

        return part

    tiles(2 * count, 256, second_rows(far, 2 * count))
    scatter.start()
    tiles(2 * count, 256, second_rows(near, 0))
    scatter.relay()
    wait_all(last_loads)

    def weight_part(target, grads, k):
        here = pl.ds(k * quarter, quarter)
        target[here] = dot(rows_here[:, here], grads[...], (0, 0)).astype(target.dtype)

    weight_part(gate, gate_act, 0)
    even_store = p.copy(gate.at[pl.ds(0, quarter)], gate_parts.at[0]).start()
    down_sum.relay()
    weight_part(gate, gate_act, 1)
    odd_store = p.copy(gate.at[pl.ds(quarter, quarter)], gate_parts.at[1]).start()
    even_store.wait()
    gate_sum.start_even()
    scatter.arrived()
    odd_store.wait()
    gate_sum.start_odd()
    gain = vectors[2:3]
    gain_sum[...] = jnp.zeros_like(gain_sum)
    shift_sum[...] = jnp.zeros_like(shift_sum)

    def middle_back(rows):
        incoming = scatter.total(rows)
        back, product = norm_back_rows(value[rows], incoming, gain)
        gain_sum[...] += fold(product)
        shift_sum[...] += fold(incoming)
        grad = cot[rows].astype(jnp.float32) + back
        value[rows] = grad
        cot[rows] = grad.astype(cot.dtype)

    tiles(count, CHUNK, middle_back)
    gather = GatherRows(p, cot.at[pl.ds(0, count)], rows_branch).start()
    grad_store = p.copy(value, grad_middle).start()
    gain_sum[0:1] = jnp.sum(gain_sum[...], axis=0, keepdims=True)
    gain_sum[1:2] = jnp.sum(shift_sum[...], axis=0, keepdims=True)
    stores = [p.copy(gain_sum, sums).start()]
    scatter.finish()

    def out_rows(target, offset):
        def part(rows):
            target[rows] = dot(hidden[shifted(rows, offset)], down[...], (1, 0)).astype(target.dtype)

        return part

    tiles(2 * count, 256, out_rows(far, 2 * count))
    out_scatter.start()
    tiles(2 * count, 256, out_rows(near, 0))
    down_sum.settle()
    grad_store.wait()
    middle_load = p.copy(middle, value).start()
    weight_part(gate, gate_act, 2)
    out_scatter.relay()
    weight_part(gate, gate_act, 3)
    gather.relay()
    weight_part(up, up_act, 0)
    weight_part(up, up_act, 1)
    gate_sum.relay()
    weight_part(up, up_act, 2)
    weight_part(up, up_act, 3)
    stores.append(p.copy(up, up_parts).start())
    out_scatter.arrived()
    middle_load.wait()
    own_out = cot.at[pl.ds(count, count)]

    def out_total(rows):
        own_out[rows] = (value[rows] + out_scatter.total(rows)).astype(own_out.dtype)

    tiles(count, CHUNK, out_total)
    stores += store_natural(p, own_out, outputs)
    down_sum.finish(down_owned)
    gate_sum.settle()
    gate_sum.finish(gate_owned)
    down_sum.stored()
    gate_sum.stored()
    out_scatter.finish()
    gather.finish()
    wait_all(stores)


def last_kernel(
    term, inputs, vectors, grad_middle, sums, bias_part, *rest,
):
    up_parts, out_parts, proj_parts = rest[0], rest[1:5], rest[5:9]
    input_grads, proj_owned, out_owned, vector_grads, bias_grad, up_owned = rest[9:15]
    (
        own, near, got, got_beside, result, all_sums, shift_sum, vector_got, vector_total, z_got,
        bias_here, bias_got,
    ) = rest[15:27]
    weight_refs = [rest[27 + 5 * k : 32 + 5 * k] for k in range(5)]
    send_sems, recv_sems, local_sems = rest[52:]
    p = Place(send_sems, recv_sems, local_sems)
    loads = load_local(p, inputs, own)
    loads.append(p.copy(grad_middle, result).start())
    p.greet()
    first, second = p.core == 0, p.core == 1
    count = own.shape[0]
    near_load = p.copy(term.at[pl.ds(0, 2 * count)], near).start()
    scatter = ScatterRows(p, term.at[pl.ds(2 * count, 2 * count)], near, got, got_beside).start()
    quarter = up_parts.shape[0] // 4

    def weight_sum(parts, rows, refs):
        keep, got_quarters, last, home, total = refs
        return ScatterWeight(
            p, parts[:2], [keep.at[0], keep.at[1]], rows, got_quarters, last, home, total
        ).load(parts[2:])

    up = weight_sum(
        [up_parts.at[pl.ds(k * quarter, quarter)] for k in range(4)], True, weight_refs[0]
    ).start()
    out = weight_sum(out_parts, False, weight_refs[1])
    thirds = [
        weight_sum([part.at[j] for part in proj_parts], True, weight_refs[2 + j]) for j in range(3)
    ]
    bias_load = p.copy(bias_part, bias_here).start()
    near_load.wait()
    scatter.relay()
    bias_load.wait()
    bias_x = p.send(bias_here, bias_got.at[0], p.at(x=1)).start()
    bias_x.arrived()
    bias_x.left()
    bias_here[...] += bias_got[0]
    bias_y = p.send(bias_here, bias_got.at[1], p.at(y=1)).start()
    up.relay()
    out.start()
    thirds[0].start()
    bias_y.arrived()
    bias_y.left()
    bias_here[...] += bias_got[1]
    near_sem, far_sem = p.take("recv"), p.take("recv")
    bias_home = [
        p.send(bias_here, bias_got.at[2], p.at(core=1), near_sem, first).start(),
        p.send(bias_here, bias_got.at[2], p.at(core=1, far=1), near_sem, second).start(),
        p.send(bias_here, bias_got.at[3], p.at(far=1), far_sem, second).start(),
    ]
    wait_all(loads)
    scatter.arrived()
    gain = vectors[0:1]
    all_sums[...] = jnp.zeros_like(all_sums)
    shift_sum[...] = jnp.zeros_like(shift_sum)

    @pl.loop(0, count // CHUNK)
    def _(i):
        rows = pl.ds(pl.multiple_of(i * CHUNK, CHUNK), CHUNK)
        incoming = scatter.total(rows)
        back, product = norm_back_rows(own[rows].astype(jnp.float32), incoming, gain)
        all_sums[...] += fold(product)
        shift_sum[...] += fold(incoming)
        result[rows] = result[rows] + back

    stores = store_natural(p, result, input_grads)
    all_sums[0:1] = jnp.sum(all_sums[...], axis=0, keepdims=True)
    all_sums[1:2] = jnp.sum(shift_sum[...], axis=0, keepdims=True)
    all_sums[2:4] = sums[0:2]
    slots = {key: j for j, key in enumerate(ORDER)}
    vector_sends = []
    n = 0
    for dy in (0, 1):
        for dx in (0, 1):
            for core in (0, 1):
                if not (dy or dx or core):
                    continue
                straight, crossed = slots[(dy, dx, core)], slots[(dy, dx, 1 - core)]
                slot = straight + p.core * (crossed - straight)
                columns = pl.ds(pl.multiple_of(slot * EIGHTH, EIGHTH), EIGHTH)
                vector_sends.append(
                    p.send(
                        all_sums.at[:, columns], vector_got.at[n], p.at(x=dx, y=dy, core=core)
                    ).start()
                )
                n += 1
    out.relay()
    thirds[1].start()
    up.settle()
    own_slot = slots[(0, 0, 0)] + p.core * (slots[(0, 0, 1)] - slots[(0, 0, 0)])
    total = all_sums[:, pl.ds(pl.multiple_of(own_slot * EIGHTH, EIGHTH), EIGHTH)]
    for k, sent in enumerate(vector_sends):
        sent.arrived()
        total = total + vector_got[k]
    vector_total[0] = total
    z_near = p.send(vector_total.at[0], z_got.at[0], p.at(near=1)).start()
    thirds[0].relay()
    thirds[2].start()
    out.settle()
    z_near.arrived()
    vector_total[1] = total + z_got[0]
    z_far = p.send(vector_total.at[1], z_got.at[1], p.at(far=1)).start()
    thirds[1].relay()
    thirds[0].settle()
    z_far.arrived()
    z_near.left()
    z_far.left()
    vector_total[0] = vector_total[1] + z_got[1]
    vector_store = p.copy(vector_total.at[0], vector_grads).start()
    bias_home[0].arrived()
    bias_home[2].arrived(second)
    for sent in bias_home:
        sent.left()
    pl.when(second)(lambda: combine(bias_got.at[2], [bias_got.at[2], bias_got.at[3]], 8))
    pl.when(first)(lambda: combine(bias_got.at[2], [bias_got.at[2], bias_here], 8))
    bias_store = p.copy(bias_got.at[2], bias_grad).start()
    up.finish(up_owned)
    thirds[2].relay()
    thirds[1].settle()
    out.finish(out_owned)
    thirds[0].finish(proj_owned.at[0])
    thirds[2].settle()
    thirds[1].finish(proj_owned.at[1])
    thirds[2].finish(proj_owned.at[2])
    for weight in (up, out, *thirds):
        weight.stored()
    scatter.finish()
    for sent in vector_sends:
        sent.left()
    wait_all(stores)
    vector_store.wait()
    bias_store.wait()


def call(body, name, collective, inputs, in_specs, outs, scratch, counts):
    bf16_bytes = sum(math.prod(o.shape) * o.dtype.itemsize for o in outs)
    return pl.pallas_call(
        body,
        out_shape=outs,
        in_specs=in_specs,
        out_specs=[ANY] * len(outs),
        scratch_shapes=[
            *scratch,
            pltpu.SemaphoreType.DMA((counts[0],)),
            pltpu.SemaphoreType.DMA((counts[1],)),
            pltpu.SemaphoreType.DMA((counts[2],)),
        ],
        compiler_params=pltpu.CompilerParams(
            collective_id=collective, has_side_effects=True, vmem_limit_bytes=VMEM_BYTES
        ),
        cost_estimate=pl.CostEstimate(
            flops=0, bytes_accessed=2 * bf16_bytes, transcendentals=0
        ),
        name=name,
    )(*inputs)


def bf16(*shape):
    return jax.ShapeDtypeStruct(shape, jnp.bfloat16)


def f32(*shape):
    return jax.ShapeDtypeStruct(shape, jnp.float32)


def held(shape_struct):
    return pltpu.VMEM(shape_struct.shape, shape_struct.dtype)


def weight_scratch(quarter, eighth):
    return [
        held(bf16(2, *quarter)), held(bf16(2, *quarter)), held(bf16(2, *eighth)),
        held(bf16(2, *eighth)), held(f32(*eighth)),
    ]


WHOLE = pl.BlockSpec(memory_space=pltpu.VMEM)
EIGHTH = 256


def local_pairs(
    inputs,
    gain_first,
    shift_first,
    projections,
    biases,
    output_weight,
    gain_second,
    shift_second,
    gate_up,
    down_weight,
    cotangent,
):
    dp_index, tensor_index = lax.axis_index("dp"), lax.axis_index("tensor")
    first_core = dp_index % 2 == 0
    late_half = tensor_index % 2 == 1
    count, width = inputs.shape
    rows = 4 * count
    heads_width = output_weight.shape[0]
    hidden_width = down_weight.shape[0]
    local_heads = heads_width // HD
    head_shape = (2, SEQ_LEN, local_heads, HD)
    quarter_width = width // 4

    def width_part(array, k):
        return array[:, k * quarter_width : (k + 1) * quarter_width]

    positions = jnp.arange(SEQ_LEN)
    positions = jnp.where(late_half, (positions + SEQ_LEN // 2) % SEQ_LEN, positions)
    cosine, sine = (
        jnp.where(late_half, jnp.roll(table, SEQ_LEN // 2, axis=0), table)
        for table in angle_tables()
    )
    vectors = jnp.pad(
        jnp.stack([gain_first, shift_first, gain_second, shift_second]).astype(jnp.float32),
        ((0, 4), (0, 0)),
    )
    quarter_biases = jnp.where(first_core, biases, own_quarter(biases)).astype(jnp.float32)

    proj_full, out_full, gate_pair, vectors, gathered_one, gathered_cot = call(
        front_kernel, "gather_first", 1,
        (inputs, cotangent, vectors, projections, output_weight, gate_up),
        [ANY] * 6,
        [
            bf16(3, width, heads_width), bf16(heads_width, width), bf16(2, EIGHTH, hidden_width),
            f32(8, width), bf16(rows, width), bf16(rows, width),
        ],
        [held(bf16(count, width)), held(bf16(count, width)), held(bf16(count, width)), held(f32(8, width))],
        (64, 64, 40),
    )

    pre_all = jnp.einsum("gd,jde->jge", gathered_one, proj_full, preferred_element_type=jnp.float32)
    pre_all = pre_all + quarter_biases[:, None, :]
    queries = rotate(pre_all[0].reshape(head_shape), cosine, sine, 1.0).astype(jnp.bfloat16)
    key_rows = rotate(pre_all[1].reshape(head_shape), cosine, sine, 1.0).astype(jnp.bfloat16)
    value_rows = pre_all[2].reshape(head_shape).astype(jnp.bfloat16)
    mixed, log_totals = lax.map(
        lambda pieces: attend_forward(pieces, positions), (queries, key_rows, value_rows)
    )
    mixed_rows = mixed.reshape(rows, heads_width)
    term = jnp.dot(mixed_rows, out_full, preferred_element_type=jnp.float32).astype(jnp.bfloat16)

    (
        gu_full, down_full, middle, gathered_two, hidden, gate_act, up_act,
    ) = call(
        middle_kernel, "gather_second", 2,
        (term, inputs, vectors, gate_pair, gate_up, down_weight),
        [ANY, ANY, WHOLE, ANY, ANY, ANY],
        [
            bf16(2, width, hidden_width), bf16(hidden_width, width), f32(count, width),
            bf16(rows, width), *[bf16(rows, hidden_width)] * 3,
        ],
        [
            held(bf16(count, width)), held(bf16(2 * count, width)), held(bf16(2 * count, width)),
            held(bf16(count, width)), held(f32(count, width)), held(bf16(count, width)),
            held(bf16(2, width, hidden_width)), held(bf16(rows, width)), held(f32(rows, hidden_width)),
            *[held(bf16(rows, hidden_width))] * 3,
        ],
        (48, 48, 32),
    )

    def quarters(product):
        return [product(k).astype(jnp.bfloat16) for k in range(4)]

    by_rows = ((2 * EIGHTH, hidden_width), (EIGHTH, hidden_width))
    by_columns = ((hidden_width, 2 * EIGHTH), (hidden_width, EIGHTH))
    (
        outputs, grad_middle, gathered_branch, sums, down_owned, gate_owned, up_parts, *_,
    ) = call(
        back_kernel, "scatter_first", 3,
        (
            hidden, gate_act, up_act, gathered_cot, gathered_two, gu_full, down_full, middle, vectors,
        ),
        [ANY] * 8 + [WHOLE],
        [
            bf16(count, width), f32(count, width), bf16(rows, width), f32(8, width),
            f32(hidden_width, EIGHTH), f32(EIGHTH, hidden_width), bf16(width, hidden_width),
            bf16(2, hidden_width, 2 * EIGHTH), bf16(2, 2 * EIGHTH, hidden_width),
        ],
        [
            *[held(bf16(rows, hidden_width))] * 3, held(bf16(rows, width)), held(bf16(rows, width)),
            held(bf16(width, hidden_width)), held(bf16(width, hidden_width)),
            held(bf16(hidden_width, width)), held(f32(count, width)),
            held(bf16(2 * count, width)), held(bf16(2 * count, width)),
            held(bf16(count, width)), held(bf16(2 * count, width)), held(bf16(count, width)),
            held(f32(8, width)), held(f32(8, width)), held(bf16(2, hidden_width, 2 * EIGHTH)),
            *weight_scratch(*by_columns)[1:], *weight_scratch(*by_rows)[1:4],
        ],
        (64, 64, 48),
    )

    grad_mixed = jnp.einsum(
        "gd,ed->ge", gathered_branch, out_full, preferred_element_type=jnp.float32
    ).astype(jnp.bfloat16)
    out_parts = quarters(
        lambda k: jnp.einsum(
            "ge,gd->ed",
            mixed_rows,
            width_part(gathered_branch, k),
            preferred_element_type=jnp.float32,
        )
    )
    grad_queries, grad_keys, grad_values = lax.map(
        lambda pieces: attend_back(pieces, positions),
        (queries, key_rows, value_rows, grad_mixed.reshape(head_shape), log_totals),
    )
    grad_queries = rotate(grad_queries, cosine, sine, -1.0)
    grad_keys = rotate(grad_keys, cosine, sine, -1.0)
    grad_pre = (
        jnp.stack([grad_queries, grad_keys, grad_values])
        .reshape(3, rows, heads_width)
        .astype(jnp.bfloat16)
    )
    proj_parts = quarters(
        lambda k: jnp.einsum(
            "gd,jge->jde",
            width_part(gathered_one, k),
            grad_pre,
            preferred_element_type=jnp.float32,
        )
    )
    first_term = jnp.einsum(
        "jge,jde->gd", grad_pre, proj_full, preferred_element_type=jnp.float32
    ).astype(jnp.bfloat16)
    bias_part = jnp.pad(jnp.sum(grad_pre, axis=1, dtype=jnp.float32), ((0, 5), (0, 0)))

    third = ((2 * EIGHTH, heads_width), (EIGHTH, heads_width))
    input_grads, proj_owned, out_owned, vector_grads, bias_grad, up_owned = call(
        last_kernel, "scatter_second", 4,
        (
            first_term, inputs, vectors, grad_middle, sums, bias_part, up_parts, *out_parts,
            *proj_parts,
        ),
        [ANY, ANY, WHOLE, ANY, WHOLE, ANY] + [ANY] * 9,
        [
            f32(count, width), f32(3, EIGHTH, heads_width), f32(heads_width, EIGHTH),
            f32(8, EIGHTH), f32(8, heads_width), f32(EIGHTH, hidden_width),
        ],
        [
            held(bf16(count, width)), held(bf16(2 * count, width)), held(bf16(2 * count, width)),
            held(bf16(count, width)), held(f32(count, width)), held(f32(8, width)), held(f32(8, width)),
            held(f32(7, 8, EIGHTH)), held(f32(2, 8, EIGHTH)), held(f32(2, 8, EIGHTH)),
            held(f32(8, heads_width)), held(f32(4, 8, heads_width)),
            *weight_scratch(*by_rows),
            *weight_scratch((heads_width, 2 * EIGHTH), (heads_width, EIGHTH)),
            *weight_scratch(*third), *weight_scratch(*third), *weight_scratch(*third),
        ],
        (64, 64, 48),
    )
    return (
        outputs,
        input_grads,
        vector_grads[0],
        vector_grads[1],
        proj_owned,
        bias_grad[:3],
        out_owned,
        vector_grads[2],
        vector_grads[3],
        jnp.stack([gate_owned, up_owned]),
        down_owned,
    )


def solution(mesh):
    whole_pairs = dict(mesh.shape) == {"dp": 8, "tensor": 4}
    return jax.shard_map(
        local_pairs if whole_pairs else local,
        mesh=mesh,
        in_specs=(
            P(("dp", "tensor"), None),
            P("dp"),
            P("dp"),
            P(None, "dp", "tensor"),
            P(None, "tensor"),
            P("tensor", "dp"),
            P("dp"),
            P("dp"),
            P(None, "dp", "tensor"),
            P("tensor", "dp"),
            P(("dp", "tensor"), None),
        ),
        out_specs=(
            P(("dp", "tensor"), None),
            P(("dp", "tensor"), None),
            P("dp"),
            P("dp"),
            P(None, "dp", "tensor"),
            P(None, "tensor"),
            P("tensor", "dp"),
            P("dp"),
            P("dp"),
            P(None, "dp", "tensor"),
            P("tensor", "dp"),
        ),
        check_vma=False,
    )
```

```python
import math

import jax
import jax.numpy as jnp
from jax import lax
from jax.experimental import pallas as pl
from jax.experimental.pallas import tpu as pltpu
from jax.sharding import PartitionSpec as P

HD = 64
ROTARY = 16
SEQ_LEN = 512


EPSILON = 1e-05
ANGLE_BASE = 10000.0
NEGATIVE = -1e30


def norm_rows(rows, gain, shift):
    average = jnp.mean(rows, axis=-1, keepdims=True)
    centred = rows - average
    inverse = lax.rsqrt(jnp.mean(centred * centred, axis=-1, keepdims=True) + EPSILON)
    unit_rows = centred * inverse
    return (unit_rows * gain + shift, unit_rows, inverse)


def norm_back(incoming, unit_rows, inverse, gain):
    scaled = incoming * gain
    inner = (
        scaled
        - jnp.mean(scaled, axis=-1, keepdims=True)
        - unit_rows * jnp.mean(scaled * unit_rows, axis=-1, keepdims=True)
    )
    return (inner * inverse, jnp.sum(incoming * unit_rows, axis=0), jnp.sum(incoming, axis=0))


def angle_tables():
    freqs = 1.0 / ANGLE_BASE ** (jnp.arange(0, ROTARY, 2).astype(jnp.float32) / ROTARY)
    angles = jnp.arange(SEQ_LEN).astype(jnp.float32)[:, None] * freqs[None, :]
    return (jnp.cos(angles), jnp.sin(angles))


def rotate(heads, cosine, sine, sign):
    half_rot = ROTARY // 2
    first = heads[..., :half_rot]
    latter = heads[..., half_rot:ROTARY]
    cos_part = cosine[:, None, :]
    sin_part = sine[:, None, :] * sign
    return jnp.concatenate(
        [
            first * cos_part - latter * sin_part,
            latter * cos_part + first * sin_part,
            heads[..., ROTARY:],
        ],
        axis=-1,
    )


def causal_scores(queries, key_rows, positions):
    scaling = 1.0 / math.sqrt(HD)
    scores = scaling * jnp.einsum(
        "qhd,khd->hqk", queries, key_rows, preferred_element_type=jnp.float32
    )
    causal = positions[:, None] >= positions[None, :]
    return jnp.where(causal[None], scores, NEGATIVE)


def attend_forward(pieces, positions):
    queries, key_rows, value_rows = pieces
    scores = causal_scores(queries, key_rows, positions)
    row_top = jnp.max(scores, axis=-1, keepdims=True)
    exponent = jnp.exp(scores - row_top)
    totals = jnp.sum(exponent, axis=-1, keepdims=True)
    weights = (exponent / totals).astype(jnp.bfloat16)
    mixed = jnp.einsum("hqk,khd->qhd", weights, value_rows, preferred_element_type=jnp.float32)
    return (mixed.astype(jnp.bfloat16), (row_top + jnp.log(totals))[..., 0])


def attend_back(pieces, positions):
    queries, key_rows, value_rows, grad_mixed, log_totals = pieces
    scaling = 1.0 / math.sqrt(HD)
    scores = causal_scores(queries, key_rows, positions)
    weights = jnp.exp(scores - log_totals[..., None])
    grad_values = jnp.einsum(
        "hqk,qhd->khd", weights.astype(jnp.bfloat16), grad_mixed, preferred_element_type=jnp.float32
    )
    grad_weights = jnp.einsum(
        "qhd,khd->hqk", grad_mixed, value_rows, preferred_element_type=jnp.float32
    )
    grad_scores = weights * (grad_weights - jnp.sum(weights * grad_weights, axis=-1, keepdims=True))
    grad_scores = grad_scores.astype(jnp.bfloat16)
    grad_queries = scaling * jnp.einsum(
        "hqk,khd->qhd", grad_scores, key_rows, preferred_element_type=jnp.float32
    )
    grad_keys = scaling * jnp.einsum(
        "hqk,qhd->khd", grad_scores, queries, preferred_element_type=jnp.float32
    )
    return (grad_queries, grad_keys, grad_values)


def scatter_sum(terms, axis, dimension):
    owned = lax.psum_scatter(
        terms.astype(jnp.bfloat16), axis, scatter_dimension=dimension, tiled=True
    )
    return owned.astype(jnp.float32)


def local(
    inputs,
    gain_first,
    shift_first,
    projections,
    biases,
    output_weight,
    gain_second,
    shift_second,
    gate_up,
    down_weight,
    cotangent,
):
    tensor_ways = lax.axis_size("tensor")
    row_count = inputs.shape[0]
    group_rows = row_count * tensor_ways
    sequences = group_rows // SEQ_LEN
    head_width = output_weight.shape[0]
    local_heads = head_width // HD
    head_shape = (sequences, SEQ_LEN, local_heads, HD)
    cosine, sine = angle_tables()
    positions = jnp.arange(SEQ_LEN)
    proj_full, out_full, gain_one, shift_one = (
        lax.all_gather(projections, "dp", axis=1, tiled=True),
        lax.all_gather(output_weight, "dp", axis=1, tiled=True),
        lax.all_gather(gain_first, "dp", axis=0, tiled=True),
        lax.all_gather(shift_first, "dp", axis=0, tiled=True),
    )
    gain_one = gain_one.astype(jnp.float32)
    residual = inputs.astype(jnp.float32)
    normed_one, unit_one, inverse_one = norm_rows(residual, gain_one, shift_one.astype(jnp.float32))
    gathered_one = lax.all_gather(normed_one.astype(jnp.bfloat16), "tensor", axis=0, tiled=True)
    pre_all = jnp.einsum("gd,jde->jge", gathered_one, proj_full, preferred_element_type=jnp.float32)
    pre_all = pre_all + biases.astype(jnp.float32)[:, None, :]
    queries = rotate(pre_all[0].reshape(head_shape), cosine, sine, 1.0).astype(jnp.bfloat16)
    key_rows = rotate(pre_all[1].reshape(head_shape), cosine, sine, 1.0).astype(jnp.bfloat16)
    value_rows = pre_all[2].reshape(head_shape).astype(jnp.bfloat16)
    mixed, log_totals = lax.map(
        lambda pieces: attend_forward(pieces, positions), (queries, key_rows, value_rows)
    )
    mixed_rows = mixed.reshape(group_rows, head_width)
    part = mixed_rows
    middle = residual + scatter_sum(
        jnp.dot(part, out_full, preferred_element_type=jnp.float32), "tensor", 0
    )
    gu_full, down_full, gain_two, shift_two = (
        lax.all_gather(gate_up, "dp", axis=1, tiled=True),
        lax.all_gather(down_weight, "dp", axis=1, tiled=True),
        lax.all_gather(gain_second, "dp", axis=0, tiled=True),
        lax.all_gather(shift_second, "dp", axis=0, tiled=True),
    )
    gain_two = gain_two.astype(jnp.float32)
    normed_two, unit_two, inverse_two = norm_rows(middle, gain_two, shift_two.astype(jnp.float32))
    gathered_two = lax.all_gather(normed_two.astype(jnp.bfloat16), "tensor", axis=0, tiled=True)
    gate_act = jnp.dot(gathered_two, gu_full[0], preferred_element_type=jnp.float32)
    up_act = jnp.dot(gathered_two, gu_full[1], preferred_element_type=jnp.float32)
    sigmoid_gate = jax.nn.sigmoid(gate_act)
    hidden = (gate_act * sigmoid_gate * up_act).astype(jnp.bfloat16)
    part = hidden
    outputs = (
        middle
        + scatter_sum(jnp.dot(part, down_full, preferred_element_type=jnp.float32), "tensor", 0)
    ).astype(jnp.bfloat16)
    gu_back, down_back, gain_two_back = (
        lax.all_gather(gate_up, "dp", axis=1, tiled=True),
        lax.all_gather(down_weight, "dp", axis=1, tiled=True),
        lax.all_gather(gain_second, "dp", axis=0, tiled=True),
    )
    gain_two_back = gain_two_back.astype(jnp.float32)
    gathered_cot = lax.all_gather(cotangent, "tensor", axis=0, tiled=True)
    grad_hidden = jnp.einsum(
        "gd,fd->gf", gathered_cot, down_back, preferred_element_type=jnp.float32
    )
    down_grad = jnp.einsum("gf,gd->fd", hidden, gathered_cot, preferred_element_type=jnp.float32)
    grad_up = (grad_hidden * gate_act * sigmoid_gate).astype(jnp.bfloat16)
    grad_gate = (
        grad_hidden * up_act * sigmoid_gate * (1.0 + gate_act * (1.0 - sigmoid_gate))
    ).astype(jnp.bfloat16)
    gu_grad = jnp.stack(
        [
            jnp.einsum("gd,gf->df", gathered_two, grad_gate, preferred_element_type=jnp.float32),
            jnp.einsum("gd,gf->df", gathered_two, grad_up, preferred_element_type=jnp.float32),
        ]
    )
    first_term = jnp.einsum("gf,df->gd", grad_gate, gu_back[0], preferred_element_type=jnp.float32)
    grad_second = scatter_sum(
        first_term
        + jnp.einsum("gf,df->gd", grad_up, gu_back[1], preferred_element_type=jnp.float32),
        "tensor",
        0,
    )
    gu_owned, down_owned = (
        scatter_sum(gu_grad, "dp", 1),
        scatter_sum(down_grad, "dp", 1),
    )
    grad_mid_norm, gain_two_part, shift_two_part = norm_back(
        grad_second, unit_two, inverse_two, gain_two_back
    )
    grad_middle = cotangent.astype(jnp.float32) + grad_mid_norm
    proj_back, out_back, gain_one_back = (
        lax.all_gather(projections, "dp", axis=1, tiled=True),
        lax.all_gather(output_weight, "dp", axis=1, tiled=True),
        lax.all_gather(gain_first, "dp", axis=0, tiled=True),
    )
    gain_one_back = gain_one_back.astype(jnp.float32)
    gathered_branch = lax.all_gather(grad_middle.astype(jnp.bfloat16), "tensor", axis=0, tiled=True)
    out_grad = jnp.einsum(
        "ge,gd->ed", mixed_rows, gathered_branch, preferred_element_type=jnp.float32
    )
    grad_mixed = jnp.einsum(
        "gd,ed->ge", gathered_branch, out_back, preferred_element_type=jnp.float32
    ).astype(jnp.bfloat16)
    grad_queries, grad_keys, grad_values = lax.map(
        lambda pieces: attend_back(pieces, positions),
        (queries, key_rows, value_rows, grad_mixed.reshape(head_shape), log_totals),
    )
    grad_queries = rotate(grad_queries, cosine, sine, -1.0)
    grad_keys = rotate(grad_keys, cosine, sine, -1.0)
    grad_pre = (
        jnp.stack([grad_queries, grad_keys, grad_values])
        .reshape(3, group_rows, head_width)
        .astype(jnp.bfloat16)
    )
    bias_part = jnp.sum(grad_pre, axis=1, dtype=jnp.float32)
    proj_grad = jnp.einsum(
        "gd,jge->jde", gathered_one, grad_pre, preferred_element_type=jnp.float32
    )
    part = grad_pre
    grad_normed = scatter_sum(
        jnp.einsum("jge,jde->gd", part, proj_back, preferred_element_type=jnp.float32),
        "tensor",
        0,
    )
    proj_owned, out_owned = (
        scatter_sum(proj_grad, "dp", 1),
        scatter_sum(out_grad, "dp", 1),
    )
    grad_in_norm, gain_one_part, shift_one_part = norm_back(
        grad_normed, unit_one, inverse_one, gain_one_back
    )
    input_grads = grad_middle + grad_in_norm
    one_hot = (jnp.arange(tensor_ways) == lax.axis_index("tensor")).astype(jnp.float32)
    spread_bias = (bias_part[:, None, :] * one_hot[None, :, None]).reshape(
        3, tensor_ways * head_width
    )
    summed = lax.psum(
        (gain_one_part, shift_one_part, gain_two_part, shift_two_part, spread_bias),
        ("dp", "tensor"),
    )
    own_width = gain_first.shape[0]
    own_offset = lax.axis_index("dp") * own_width

    def own_part(vector):
        return lax.dynamic_slice_in_dim(vector, own_offset, own_width, 0)

    bias_grad = jnp.sum(
        summed[4].reshape(3, tensor_ways, head_width) * one_hot[None, :, None], axis=1
    )
    return (
        outputs,
        input_grads,
        own_part(summed[0]),
        own_part(summed[1]),
        proj_owned,
        bias_grad,
        out_owned,
        own_part(summed[2]),
        own_part(summed[3]),
        gu_owned,
        down_owned,
    )


ORDER = ((1, 0, 0), (1, 1, 0), (0, 1, 1), (1, 1, 1), (0, 0, 0), (0, 1, 0), (0, 0, 1), (1, 0, 1))
EVEN_Y, EVEN_XY, ODD_X, ODD_XY, EVEN, EVEN_X, ODD, ODD_Y = range(8)
ANY = pl.BlockSpec(memory_space=pl.ANY)
VMEM_BYTES = 63 * 1024 * 1024


class Place:
    def __init__(self, send_sems, recv_sems, local_sems):
        self.dp, self.tensor = lax.axis_index("dp"), lax.axis_index("tensor")
        self.core = lax.rem(self.dp, 2)
        self.x = lax.rem(self.dp // 2, 2)
        self.y = self.dp // 4
        self.pools = {"send": send_sems, "recv": recv_sems, "local": local_sems}
        self.used = {"send": 0, "recv": 0, "local": 0}

    def take(self, kind):
        self.used[kind] += 1
        return self.pools[kind].at[self.used[kind] - 1]

    def at(self, x=0, y=0, core=0, near=0, far=0):
        dp = self.dp
        dp = dp + x * (2 - 4 * self.x) + y * (4 - 8 * self.y) + core * (1 - 2 * self.core)
        tensor = self.tensor
        tensor = tensor + near * (1 - 2 * lax.rem(tensor, 2)) + far * (2 - 4 * (tensor // 2))
        return (dp, tensor)

    def column(self, key):
        dy, dx, core = key
        y = self.y + dy * (1 - 2 * self.y)
        x = self.x + dx * (1 - 2 * self.x)
        return pl.multiple_of((y * 4 + x * 2 + core) * EIGHTH, EIGHTH)

    def greet(self):
        barrier = pltpu.get_barrier_semaphore()
        partners = [
            self.at(x=x, y=y, core=core)
            for x in (0, 1)
            for y in (0, 1)
            for core in (0, 1)
            if x or y or core
        ] + [self.at(near=1), self.at(far=1), self.at(far=1, core=1)]
        for partner in partners:
            pl.semaphore_signal(
                barrier, inc=1, device_id=partner, device_id_type=pl.DeviceIdType.MESH
            )
        pl.semaphore_wait(barrier, len(partners))

    def send(self, source, target, device, recv_sem=None, when=None):
        return Sent(
            pltpu.make_async_remote_copy(
                src_ref=source,
                dst_ref=target,
                send_sem=self.take("send"),
                recv_sem=self.take("recv") if recv_sem is None else recv_sem,
                device_id=device,
                device_id_type=pl.DeviceIdType.MESH,
            ),
            when,
        )

    def copy(self, source, target, when=None):
        return Copied(pltpu.make_async_copy(source, target, self.take("local")), when)


def guarded(when, action):
    if when is None:
        action()
    else:
        pl.when(when)(action)


class Sent:
    def __init__(self, copy, when):
        self.copy, self.when = copy, when

    def start(self):
        guarded(self.when, self.copy.start)
        return self

    def arrived(self, when=None):
        guarded(when, self.copy.wait_recv)

    def left(self):
        guarded(self.when, self.copy.wait_send)


class Copied:
    def __init__(self, copy, when):
        self.copy, self.when = copy, when

    def start(self):
        guarded(self.when, self.copy.start)
        return self

    def wait(self):
        guarded(self.when, self.copy.wait)


class GatherWeight:
    def __init__(self, place, shard, block, pair=None):
        self.place, self.shard, self.block = place, shard, block
        self.sent = []
        self.pair = pair

    def fetch(self, even=None, odd=None):
        p = self.place
        even = self.block(EVEN) if even is None else even
        odd = self.block(ODD) if odd is None else odd
        first, second = p.core == 0, p.core == 1
        self.own = p.copy(self.shard, even, first).start()
        even_sem, odd_sem = p.take("recv"), p.take("recv")
        self.to_far_even = p.send(self.shard, even, p.at(core=1, far=1), even_sem, first).start()
        self.to_sibling = p.send(self.shard, odd, p.at(core=1), odd_sem, second).start()
        self.to_far_odd = p.send(self.shard, odd, p.at(far=1), odd_sem, second).start()
        return self

    def fetched(self):
        p = self.place
        self.own.wait()
        self.to_far_even.arrived(p.core == 1)
        self.to_sibling.arrived()
        return self

    def fetch_left(self):
        self.to_far_even.left()
        self.to_sibling.left()
        self.to_far_odd.left()

    def spread(self, even=None, odd=None):
        p, block = self.place, self.block
        even = block(EVEN) if even is None else even
        odd = block(ODD) if odd is None else odd
        self.even_x = p.send(even, block(EVEN_X), p.at(x=1)).start()
        self.odd_y = p.send(odd, block(ODD_Y), p.at(y=1)).start()
        self.odd_x = p.send(odd, block(ODD_X), p.at(x=1)).start()
        self.even_y = p.send(even, block(EVEN_Y), p.at(y=1)).start()
        return self

    def relay(self):
        p, block = self.place, self.block
        self.even_x.arrived()
        self.even_xy = p.send(block(EVEN_X), block(EVEN_XY), p.at(y=1)).start()
        self.odd_y.arrived()
        self.odd_xy = p.send(block(ODD_Y), block(ODD_XY), p.at(x=1)).start()
        return self

    def finish(self):
        for copy in (self.odd_x, self.even_y, self.even_xy, self.odd_xy):
            copy.arrived()
        for copy in (
            self.even_x, self.odd_y, self.odd_x, self.even_y, self.even_xy, self.odd_xy,
        ):
            copy.left()


class GatherRows:
    def __init__(self, place, own, rows):
        self.place, self.own, self.rows = place, own, rows
        self.count = own.shape[0]

    def slot(self, k):
        return self.rows.at[pl.ds(k * self.count, self.count)]

    def start(self):
        p = self.place
        self.beside = p.send(self.own, self.slot(1), p.at(near=1)).start()
        self.sibling = p.send(self.own, self.slot(2), p.at(core=1)).start()
        self.here = p.copy(self.own, self.slot(0)).start()
        return self

    def relay(self):
        p = self.place
        self.beside.arrived()
        self.across = p.send(self.slot(1), self.slot(3), p.at(core=1)).start()
        return self

    def finish(self):
        self.sibling.arrived()
        self.across.arrived()
        self.here.wait()
        for copy in (self.beside, self.sibling, self.across):
            copy.left()


def combine(target, terms, chunk):
    @pl.loop(0, target.shape[0] // chunk)
    def _(i):
        rows = pl.ds(pl.multiple_of(i * chunk, chunk), chunk)
        total = terms[0][rows].astype(jnp.float32)
        for term in terms[1:]:
            total = total + term[rows].astype(jnp.float32)
        target[rows] = total.astype(target.dtype)


class ScatterRows:
    def __init__(self, place, far, near, got, got_beside):
        self.place, self.far, self.near = place, far, near
        self.got, self.got_beside = got, got_beside
        self.count = near.shape[0] // 2

    def start(self):
        self.sibling = self.place.send(self.far, self.got, self.place.at(core=1)).start()
        return self

    def relay(self):
        p, n = self.place, self.count
        self.sibling.arrived()
        late = pl.ds(n, n)
        combine(self.near.at[late], [self.near.at[late], self.got.at[late]], 32)
        self.beside = p.send(self.near.at[late], self.got_beside, p.at(near=1)).start()
        return self

    def total(self, rows):
        return (
            self.near[rows].astype(jnp.float32)
            + self.got[rows].astype(jnp.float32)
            + self.got_beside[rows].astype(jnp.float32)
        )

    def arrived(self):
        self.beside.arrived()

    def finish(self):
        self.sibling.left()
        self.beside.left()


class ScatterWeight:
    def __init__(self, place, send, keep, rows, got, last, home, result):
        self.place, self.parts, self.keep, self.rows = place, send, keep, rows
        self.got, self.last, self.home, self.result = got, last, home, result
        self.loads = []

    def half(self, ref, k):
        if self.rows:
            size = ref.shape[0] // 2
            return ref.at[pl.ds(k * size, size)]
        size = ref.shape[1] // 2
        return ref.at[:, pl.ds(k * size, size)]

    def load(self, sources):
        self.loads = [self.place.copy(a, b).start() for a, b in zip(sources, self.keep)]
        return self

    def start_even(self):
        p = self.place
        self.even = p.send(self.parts[0], self.got.at[0], p.at(y=1)).start()
        return self

    def start_odd(self):
        p = self.place
        self.odd = p.send(self.parts[1], self.got.at[1], p.at(x=1)).start()
        return self

    def start(self):
        return self.start_even().start_odd()

    def relay(self):
        p = self.place
        wait_all(self.loads)
        self.second = []
        for k, arrival in enumerate((self.even, self.odd)):
            arrival.arrived()
            there = self.half(self.keep[k], 1)
            combine(there, [there, self.half(self.got.at[k], 1)], 64)
            device = p.at(x=1) if k == 0 else p.at(y=1)
            self.second.append(p.send(there, self.last.at[k], device).start())
        return self

    def settle(self):
        p = self.place

        def terms(k):
            return [self.half(self.keep[k], 0), self.half(self.got.at[k], 0), self.last.at[k]]

        even_out, odd_out = self.half(self.keep[0], 0), self.half(self.keep[1], 0)
        first, second = p.core == 0, p.core == 1
        near_sem, far_sem = p.take("recv"), p.take("recv")
        self.second[1].arrived()
        combine(odd_out, terms(1), 64)
        self.to_sibling = p.send(odd_out, self.home.at[0], p.at(core=1), near_sem, first).start()
        self.to_far = p.send(odd_out, self.home.at[1], p.at(far=1), far_sem, second).start()
        self.second[0].arrived()
        pl.when(first)(lambda: combine(self.result, terms(0), 64))
        pl.when(second)(lambda: combine(even_out, terms(0), 64))
        self.to_first = p.send(
            even_out, self.home.at[0], p.at(core=1, far=1), near_sem, second
        ).start()
        return self

    def finish(self, output):
        p = self.place
        first, second = p.core == 0, p.core == 1
        self.to_sibling.arrived()
        self.to_far.arrived(second)
        pl.when(first)(lambda: combine(self.result, [self.result, self.home.at[0]], 64))
        pl.when(second)(lambda: combine(self.result, [self.home.at[0], self.home.at[1]], 64))
        self.store = p.copy(self.result, output).start()
        for copy in (self.even, self.odd, *self.second, self.to_sibling, self.to_first, self.to_far):
            copy.left()

    def stored(self):
        self.store.wait()


def load_local(place, source, target):
    return [
        place.copy(
            source.at[:, pl.ds(place.column(key), EIGHTH)], target.at[:, pl.ds(j * EIGHTH, EIGHTH)]
        ).start()
        for j, key in enumerate(ORDER)
    ]


def store_natural(place, source, target):
    return [
        place.copy(
            source.at[:, pl.ds(j * EIGHTH, EIGHTH)], target.at[:, pl.ds(place.column(key), EIGHTH)]
        ).start()
        for j, key in enumerate(ORDER)
    ]


def wait_all(copies):
    for copy in copies:
        copy.wait()


CHUNK = 32


def norm_into(count, rows_of, gain, shift, target):
    @pl.loop(0, count // CHUNK)
    def _(i):
        rows = pl.ds(pl.multiple_of(i * CHUNK, CHUNK), CHUNK)
        target[rows] = norm_rows(rows_of(rows), gain, shift)[0].astype(target.dtype)


def tiles(count, tile, body):
    @pl.loop(0, count // tile)
    def _(i):
        body(pl.ds(pl.multiple_of(i * tile, tile), tile))


def shifted(rows, offset):
    return pl.ds(pl.multiple_of(rows.start + offset, 256), rows.size)


def dot(left, right, contract):
    return lax.dot_general(
        left, right, (((contract[0],), (contract[1],)), ((), ())), preferred_element_type=jnp.float32
    )


def turned(pre, tables, rows, sign):
    cosine, sine_first, sine_latter = (table[rows] for table in tables)
    return (
        pre * cosine
        + pltpu.roll(pre, 128 - ROTARY // 2, 1) * (sine_first * sign)
        + pltpu.roll(pre, ROTARY // 2, 1) * (sine_latter * sign)
    )


def swapped_half(index, late):
    sequence, half = index // 2, lax.rem(index, 2)
    half = half + late * (1 - 2 * half)
    return half, pl.ds(pl.multiple_of(sequence * SEQ_LEN + half * HALF, HALF), HALF)


HALF = SEQ_LEN // 2


def head_lanes(array, head):
    lanes = lax.broadcasted_iota(jnp.int32, array.shape, 1)
    mine = (lanes < HD) if head == 0 else (lanes >= HD)
    return jnp.where(mine, array, jnp.zeros_like(array))


def side_by_side(first, second):
    lanes = lax.broadcasted_iota(jnp.int32, first.shape, 1)
    return jnp.where(lanes < HD, first, second)


def probabilities(queries, key_rows, half):
    scores = dot(queries, key_rows, (1, 1))
    row = lax.broadcasted_iota(jnp.int32, scores.shape, 0) + half * HALF
    column = lax.broadcasted_iota(jnp.int32, scores.shape, 1)
    scores = jnp.where(row >= column, scores, NEGATIVE)
    exponent = jnp.exp(scores - jnp.max(scores, axis=-1, keepdims=True))
    return exponent * (1.0 / jnp.sum(exponent, axis=-1, keepdims=True))


def attend_pair(heads, mixed, late):
    @pl.loop(0, 2 * heads.shape[2] // 128)
    def _(step):
        pairs = heads.shape[2] // 128
        sequence, lanes = step // pairs, pl.ds(pl.multiple_of(lax.rem(step, pairs) * 128, 128), 128)
        start = pl.multiple_of(sequence * SEQ_LEN, SEQ_LEN)
        for half in (0, 1):
            past = pl.ds(start, HALF * (half + 1))
            queries = heads[0, pl.ds(start + half * HALF, HALF), lanes]
            results = []
            for head in (0, 1):
                probs = probabilities(head_lanes(queries, head), heads[1, past, lanes], half)
                results.append(dot(probs.astype(jnp.bfloat16), heads[2, past, lanes], (1, 0)))
            _, rows = swapped_half(sequence * 2 + half, late)
            mixed[rows, lanes] = side_by_side(*results).astype(mixed.dtype)


def attend_pair_back(heads, grad_mixed, grad_pre, tables, late):
    @pl.loop(0, 2 * heads.shape[2] // 128)
    def _(step):
        pairs = heads.shape[2] // 128
        sequence, lanes = step // pairs, pl.ds(pl.multiple_of(lax.rem(step, pairs) * 128, 128), 128)
        start = pl.multiple_of(sequence * SEQ_LEN, SEQ_LEN)
        grads = [[None, None], [None, None]]
        for half in (0, 1):
            past = pl.ds(start, HALF * (half + 1))
            here = pl.ds(start + half * HALF, HALF)
            queries, incoming = heads[0, here, lanes], grad_mixed[here, lanes]
            key_rows, value_rows = heads[1, past, lanes], heads[2, past, lanes]
            found = []
            for head in (0, 1):
                probs = probabilities(head_lanes(queries, head), key_rows, half)
                grad_values = dot(probs.astype(jnp.bfloat16), incoming, (0, 0))
                grad_probs = dot(head_lanes(incoming, head), value_rows, (1, 1))
                product = probs * grad_probs
                grad_scores = product - probs * jnp.sum(product, axis=-1, keepdims=True)
                grad_scores = grad_scores.astype(jnp.bfloat16)
                grad_queries = dot(grad_scores, key_rows, (1, 0))
                grad_keys = dot(grad_scores, queries, (0, 0))
                found.append((grad_queries, grad_keys, grad_values))
            grad_queries, grad_keys, grad_values = (side_by_side(*two) for two in zip(*found))
            at_half = pl.ds(half * HALF, HALF)
            _, rows = swapped_half(sequence * 2 + half, late)
            grad_queries = turned(grad_queries * (1.0 / math.sqrt(HD)), tables, at_half, -1.0)
            grad_pre[0, rows, lanes] = grad_queries.astype(grad_pre.dtype)
            if half == 0:
                early = (grad_keys, grad_values)
            else:
                whole = [grad_keys[:HALF] + early[0], grad_keys[HALF:]]
                whole_values = [grad_values[:HALF] + early[1], grad_values[HALF:]]
                for k in (0, 1):
                    _, rows = swapped_half(sequence * 2 + k, late)
                    turned_keys = turned(whole[k], tables, pl.ds(k * HALF, HALF), -1.0)
                    grad_pre[1, rows, lanes] = turned_keys.astype(grad_pre.dtype)
                    grad_pre[2, rows, lanes] = whole_values[k].astype(grad_pre.dtype)


def forward_kernel(
    inputs, cotangent, vectors, biases, cosine, sine_first, sine_latter,
    projections, output_weight, gate_up, down_weight,
    proj_full, out_full, gu_full, down_full, vectors_full, rows_one, rows_cot, heads_out, mixed_out,
    middle, rows_two, hidden_out, gate_out, up_out,
    own, normed, own_cot, vectors_here, biases_here, proj_here, out_here, rows_here, heads, mixed,
    near, far, got, got_beside, total, rows_later, gu_here, gate_wide, hidden, gate_act, up_act,
    send_sems, recv_sems, local_sems,
):
    p = Place(send_sems, recv_sems, local_sems)
    count = own.shape[0]
    late = lax.rem(p.tensor, 2)
    tables = (cosine, sine_first, sine_latter)
    loads = load_local(p, inputs, own)
    cot_loads = load_local(p, cotangent, own_cot)
    p.greet()
    slots = {key: j for j, key in enumerate(ORDER)}
    vector_base = p.used["recv"]
    p.used["recv"] += len(ORDER)

    def vector_copy(dy, dx, core):
        here, there = slots[(dy, dx, 0)], slots[(dy, dx, 1)]
        slot = here + p.core * (there - here)
        columns = pl.ds(pl.multiple_of(slot * EIGHTH, EIGHTH), EIGHTH)
        return p.send(
            vectors, vectors_here.at[:, columns], p.at(x=dx, y=dy, core=core),
            recv_sems.at[vector_base + slot],
        )

    vector_sends = [
        vector_copy(dy, dx, core).start()
        for dy in (0, 1) for dx in (0, 1) for core in (0, 1) if dy or dx or core
    ]
    own_slot = slots[(0, 0, 0)] + p.core * (slots[(0, 0, 1)] - slots[(0, 0, 0)])
    own_vectors = p.copy(
        vectors, vectors_here.at[:, pl.ds(pl.multiple_of(own_slot * EIGHTH, EIGHTH), EIGHTH)]
    ).start()
    own_biases = p.copy(biases, biases_here, p.core == 0).start()
    far_biases = p.send(biases, biases_here, p.at(core=1, far=1), when=p.core == 0).start()

    def third(j):
        return GatherWeight(
            p, projections.at[j], lambda k: proj_here.at[j, pl.ds(k * EIGHTH, EIGHTH)]
        )

    def gu_block(j):
        return lambda k: gu_here.at[j, pl.ds(k * EIGHTH, EIGHTH)]

    thirds = [third(0), third(1), third(2)]
    out = GatherWeight(p, output_weight, lambda k: out_here.at[:, pl.ds(k * EIGHTH, EIGHTH)])
    gate = GatherWeight(p, gate_up.at[0], gu_block(0))
    up = GatherWeight(p, gate_up.at[1], gu_block(1))
    down = GatherWeight(p, down_weight, lambda k: down_full.at[:, pl.ds(k * EIGHTH, EIGHTH)])
    thirds[0].fetch()
    thirds[1].fetch()
    wait_all(cot_loads)
    wait_all(loads)
    own_vectors.wait()
    sibling_slot = slots[(0, 0, 1)] + p.core * (slots[(0, 0, 0)] - slots[(0, 0, 1)])
    for dy in (0, 1):
        for dx in (0, 1):
            for core in (0, 1):
                if dy or dx:
                    slot = slots[(dy, dx, core)]
                elif core:
                    slot = sibling_slot
                else:
                    continue
                pltpu.make_async_copy(
                    vectors, vectors_here.at[:, pl.ds(0, EIGHTH)], recv_sems.at[vector_base + slot]
                ).wait()
    gain_one, shift_one = vectors_here[0:1], vectors_here[1:2]
    norm_into(count, lambda rows: own[rows].astype(jnp.float32), gain_one, shift_one, normed)
    gather_one = GatherRows(p, normed, rows_here).start()
    gather_cot = GatherRows(p, own_cot, rows_cot)
    stores = [p.copy(vectors_here, vectors_full).start()]

    thirds[0].fetched().spread()
    thirds[2].fetch()
    thirds[1].fetched().spread()
    out.fetch()
    thirds[0].relay()
    thirds[2].fetched().spread()
    gate.fetch()
    gather_one.relay()
    gather_cot.start()
    thirds[1].relay()
    out.fetched().spread()
    thirds[2].relay()
    up.fetch()
    own_biases.wait()
    far_biases.arrived(p.core == 1)
    far_biases.left()

    def project(j):
        thirds[j].finish()
        stores.append(p.copy(proj_here.at[j], proj_full.at[j]).start())

        @pl.loop(0, 4)
        def _(index):
            rows = pl.ds(pl.multiple_of(index * HALF, HALF), HALF)
            half, target = swapped_half(index, late)
            positions = pl.ds(pl.multiple_of(half * HALF, HALF), HALF)
            pre = dot(rows_here[rows], proj_here[j], (1, 0)) + biases_here[j : j + 1]
            for k in range(pre.shape[1] // 128):
                lanes = slice(k * 128, (k + 1) * 128)
                part = pre[:, lanes]
                if j < 2:
                    part = turned(part, tables, positions, 1.0)
                if j == 0:
                    part = part * (1.0 / math.sqrt(HD))
                heads[j, target, lanes] = part.astype(heads.dtype)

    gather_one.finish()
    stores.append(p.copy(rows_here, rows_one).start())
    project(0)
    gate.fetched().spread()
    project(1)
    out.relay()
    project(2)
    gather_cot.relay()
    stores.append(p.copy(heads, heads_out).start())
    attend_pair(heads, mixed, late)
    out.finish()
    stores += [p.copy(out_here, out_full).start(), p.copy(mixed, mixed_out).start()]

    def out_rows(target, offset):
        def part(rows):
            target[rows] = dot(mixed[shifted(rows, offset)], out_here[...], (1, 0)).astype(target.dtype)

        return part

    scatter = ScatterRows(p, far, near, got, got_beside)
    tiles(2 * count, 256, out_rows(far, 2 * count))
    scatter.start()
    tiles(2 * count, 256, out_rows(near, 0))
    scatter.relay()
    gate.relay()
    up.fetched().spread()
    scatter.arrived()
    gain_two, shift_two = vectors_here[2:3], vectors_here[3:4]

    def norm(rows):
        value = own[rows].astype(jnp.float32) + scatter.total(rows)
        total[rows] = value
        normed[rows] = norm_rows(value, gain_two, shift_two)[0].astype(normed.dtype)

    tiles(count, CHUNK, norm)
    gather = GatherRows(p, normed, rows_later).start()
    stores.append(p.copy(total, middle).start())
    down.fetch()
    gather_cot.finish()
    gather.relay()
    up.relay()
    down.fetched().spread()
    gate.finish()
    gather.finish()
    stores.append(p.copy(rows_later, rows_two).start())
    stores.append(p.copy(gu_here.at[0], gu_full.at[0]).start())

    def gate_rows(rows):
        gate_wide[rows] = dot(rows_later[rows], gu_here[0], (1, 0))

    tiles(4 * count, 256, gate_rows)
    up.finish()
    stores.append(p.copy(gu_here.at[1], gu_full.at[1]).start())

    def up_rows(rows):
        wide_up = dot(rows_later[rows], gu_here[1], (1, 0))
        wide_gate = gate_wide[rows]
        hidden[rows] = (wide_gate * jax.nn.sigmoid(wide_gate) * wide_up).astype(hidden.dtype)
        gate_act[rows] = wide_gate.astype(gate_act.dtype)
        up_act[rows] = wide_up.astype(up_act.dtype)

    tiles(2 * count, 256, up_rows)
    down.relay()
    tiles(2 * count, 256, lambda rows: up_rows(shifted(rows, 2 * count)))
    stores.append(p.copy(hidden, hidden_out).start())
    stores.append(p.copy(gate_act, gate_out).start())
    stores.append(p.copy(up_act, up_out).start())
    down.finish()
    for weight in (*thirds, out, gate, up, down):
        weight.fetch_left()
    for sent in vector_sends:
        sent.left()
    scatter.finish()
    wait_all(stores)


def norm_back_rows(value, incoming, gain):
    average = jnp.mean(value, axis=-1, keepdims=True)
    centred = value - average
    inverse = lax.rsqrt(jnp.mean(centred * centred, axis=-1, keepdims=True) + EPSILON)
    unit = centred * inverse
    scaled = incoming * gain
    inner = (
        scaled
        - jnp.mean(scaled, axis=-1, keepdims=True)
        - unit * jnp.mean(scaled * unit, axis=-1, keepdims=True)
    )
    return inner * inverse, incoming * unit


def fold(array):
    return jnp.sum(array.reshape(array.shape[0] // 8, 8, array.shape[1]), axis=0)


def back_kernel(
    hidden_in, gate_in, up_in, cot_rows, rows_two, gu_full, down_full, middle, vectors,
    outputs, grad_middle, rows_branch, sums, down_owned, gate_owned, up_parts, down_parts, gate_parts,
    hidden, gate_act, up_act, cot, rows_here, gate, up, down, value, near, got, got_beside,
    got_out, got_out_beside, gain_sum, shift_sum, staging,
    down_got, down_last, down_home, down_result, gate_got, gate_last, gate_home,
    send_sems, recv_sems, local_sems,
):
    p = Place(send_sems, recv_sems, local_sems)
    count, width = value.shape
    hidden_width = hidden.shape[1]
    quarter = width // 4
    first_loads = [p.copy(hidden_in, hidden).start(), p.copy(cot_rows, cot).start()]
    second_loads = [
        p.copy(down_full, down).start(), p.copy(gate_in, gate_act).start(), p.copy(up_in, up_act).start(),
    ]
    third_loads = [p.copy(gu_full.at[0], gate).start(), p.copy(gu_full.at[1], up).start()]
    last_loads = [p.copy(rows_two, rows_here).start(), p.copy(middle, value).start()]
    p.greet()
    down_sum = ScatterWeight(
        p, [down_parts.at[0], down_parts.at[1]], [staging.at[0], staging.at[1]], False,
        down_got, down_last, down_home, down_result,
    )
    gate_sum = ScatterWeight(
        p, [gate_parts.at[0], gate_parts.at[1]],
        [gate.at[pl.ds(k * quarter, quarter)] for k in (2, 3)], True,
        gate_got, gate_last, gate_home, value.at[:, pl.ds(0, hidden_width)],
    )
    far = cot.at[pl.ds(2 * count, 2 * count)]
    scatter = ScatterRows(p, far, near, got, got_beside)
    out_scatter = ScatterRows(p, far, near, got_out, got_out_beside)

    def down_part(k):
        columns = pl.ds(k * quarter, quarter)
        staging[k % 2] = dot(hidden[...], cot[:, columns], (0, 0)).astype(staging.dtype)

    wait_all(first_loads)
    down_part(0)
    store_even = p.copy(staging.at[0], down_parts.at[0]).start()
    down_part(1)
    store_odd = p.copy(staging.at[1], down_parts.at[1]).start()
    store_even.wait()
    down_sum.start_even()
    down_part(2)
    store_odd.wait()
    down_sum.start_odd()
    down_part(3)
    wait_all(second_loads)

    def hidden_back(rows):
        grad = dot(cot[rows], down[...], (1, 1))
        gate_value = gate_act[rows].astype(jnp.float32)
        up_value = up_act[rows].astype(jnp.float32)
        sigmoid = jax.nn.sigmoid(gate_value)
        scaled = grad * sigmoid
        up_act[rows] = (scaled * gate_value).astype(up_act.dtype)
        gate_act[rows] = (
            scaled * up_value * (1.0 + gate_value * (1.0 - sigmoid))
        ).astype(gate_act.dtype)

    tiles(4 * count, 256, hidden_back)
    wait_all(third_loads)

    def second_rows(target, offset):
        def part(rows):
            here = shifted(rows, offset)
            target[rows] = (
                dot(gate_act[here], gate[...], (1, 1)) + dot(up_act[here], up[...], (1, 1))
            ).astype(target.dtype)

        return part

    tiles(2 * count, 256, second_rows(far, 2 * count))
    scatter.start()
    tiles(2 * count, 256, second_rows(near, 0))
    scatter.relay()
    wait_all(last_loads)

    def weight_part(target, grads, k):
        here = pl.ds(k * quarter, quarter)
        target[here] = dot(rows_here[:, here], grads[...], (0, 0)).astype(target.dtype)

    weight_part(gate, gate_act, 0)
    even_store = p.copy(gate.at[pl.ds(0, quarter)], gate_parts.at[0]).start()
    down_sum.relay()
    weight_part(gate, gate_act, 1)
    odd_store = p.copy(gate.at[pl.ds(quarter, quarter)], gate_parts.at[1]).start()
    even_store.wait()
    gate_sum.start_even()
    scatter.arrived()
    odd_store.wait()
    gate_sum.start_odd()
    gain = vectors[2:3]
    gain_sum[...] = jnp.zeros_like(gain_sum)
    shift_sum[...] = jnp.zeros_like(shift_sum)

    def middle_back(rows):
        incoming = scatter.total(rows)
        back, product = norm_back_rows(value[rows], incoming, gain)
        gain_sum[...] += fold(product)
        shift_sum[...] += fold(incoming)
        grad = cot[rows].astype(jnp.float32) + back
        value[rows] = grad
        cot[rows] = grad.astype(cot.dtype)

    tiles(count, CHUNK, middle_back)
    gather = GatherRows(p, cot.at[pl.ds(0, count)], rows_branch).start()
    grad_store = p.copy(value, grad_middle).start()
    gain_sum[0:1] = jnp.sum(gain_sum[...], axis=0, keepdims=True)
    gain_sum[1:2] = jnp.sum(shift_sum[...], axis=0, keepdims=True)
    stores = [p.copy(gain_sum, sums).start()]
    scatter.finish()

    def out_rows(target, offset):
        def part(rows):
            target[rows] = dot(hidden[shifted(rows, offset)], down[...], (1, 0)).astype(target.dtype)

        return part

    tiles(2 * count, 256, out_rows(far, 2 * count))
    out_scatter.start()
    tiles(2 * count, 256, out_rows(near, 0))
    down_sum.settle()
    grad_store.wait()
    middle_load = p.copy(middle, value).start()
    weight_part(gate, gate_act, 2)
    out_scatter.relay()
    weight_part(gate, gate_act, 3)
    gather.relay()
    weight_part(up, up_act, 0)
    weight_part(up, up_act, 1)
    gate_sum.relay()
    weight_part(up, up_act, 2)
    weight_part(up, up_act, 3)
    stores.append(p.copy(up, up_parts).start())
    out_scatter.arrived()
    middle_load.wait()
    own_out = cot.at[pl.ds(count, count)]

    def out_total(rows):
        own_out[rows] = (value[rows] + out_scatter.total(rows)).astype(own_out.dtype)

    tiles(count, CHUNK, out_total)
    stores += store_natural(p, own_out, outputs)
    down_sum.finish(down_owned)
    gate_sum.settle()
    gate_sum.finish(gate_owned)
    down_sum.stored()
    gate_sum.stored()
    out_scatter.finish()
    gather.finish()
    wait_all(stores)


def last_kernel(
    rows_branch, out_full, heads_in, mixed_in, rows_one, proj_full, inputs, vectors,
    cosine, sine_first, sine_latter, grad_middle, sums, up_parts,
    input_grads, proj_owned, out_owned, vector_grads, bias_grad, up_owned,
    branch, out_here, heads, mixed, grad_mixed, grad_pre, rows_here, proj_here, out_send, proj_send,
    own, got, got_beside, result, all_sums, shift_sum, vector_got, vector_total, z_got,
    bias_here, bias_got, *rest,
):
    weight_refs = [rest[5 * k : 5 * k + 5] for k in range(5)]
    p = Place(*rest[25:])
    count, width = own.shape
    quarter = width // 4
    late = lax.rem(p.tensor, 2)
    tables = (cosine, sine_first, sine_latter)
    first, second = p.core == 0, p.core == 1
    first_loads = [p.copy(rows_branch, branch).start(), p.copy(out_full, out_here).start()]
    head_load = p.copy(heads_in, heads).start()
    mixed_load = p.copy(mixed_in, mixed).start()
    later_loads = [p.copy(proj_full, proj_here).start(), p.copy(rows_one, rows_here).start()]
    loads = load_local(p, inputs, own)
    loads.append(p.copy(grad_middle, result).start())
    p.greet()

    def weight_sum(send, rows, refs):
        keep, got_quarters, last, home, total = refs
        return ScatterWeight(
            p, send, [keep.at[0], keep.at[1]], rows, got_quarters, last, home, total
        )

    up_quarters = [up_parts.at[pl.ds(k * quarter, quarter)] for k in range(4)]
    up = weight_sum(up_quarters[:2], True, weight_refs[0]).load(up_quarters[2:]).start()
    out = weight_sum([out_send.at[0], out_send.at[1]], False, weight_refs[1])
    thirds = [
        weight_sum([proj_send.at[j, 0], proj_send.at[j, 1]], True, weight_refs[2 + j])
        for j in range(3)
    ]
    wait_all(first_loads)

    @pl.loop(0, 4)
    def _(index):
        rows = pl.ds(pl.multiple_of(index * HALF, HALF), HALF)
        _, target = swapped_half(index, late)
        grad_mixed[target] = dot(branch[rows], out_here[...], (1, 1)).astype(grad_mixed.dtype)

    mixed_load.wait()

    def out_part(k):
        target = out_send.at[k] if k < 2 else weight_refs[1][0].at[k - 2]
        target[...] = dot(
            mixed[...], branch[:, pl.ds(k * quarter, quarter)], (0, 0)
        ).astype(target.dtype)

    for k in range(4):
        out_part(k)
    out.start()
    head_load.wait()
    attend_pair_back(heads, grad_mixed, grad_pre, tables, late)
    wait_all(later_loads)
    up.relay()
    near, far = branch.at[pl.ds(0, 2 * count)], branch.at[pl.ds(2 * count, 2 * count)]
    scatter = ScatterRows(p, far, near, got, got_beside)

    def term_rows(target, offset):
        def part(rows):
            here = shifted(rows, offset)
            total = dot(grad_pre[0, here], proj_here[0], (1, 1))
            for j in (1, 2):
                total = total + dot(grad_pre[j, here], proj_here[j], (1, 1))
            target[rows] = total.astype(target.dtype)

        return part

    def proj_part(j, k):
        target = proj_send.at[j, k] if k < 2 else weight_refs[2 + j][0].at[k - 2]
        target[...] = dot(
            rows_here[:, pl.ds(k * quarter, quarter)], grad_pre[j], (0, 0)
        ).astype(target.dtype)

    tiles(2 * count, 256, term_rows(far, 2 * count))
    scatter.start()
    out.relay()
    for j in range(3):
        proj_part(j, 0)
        thirds[j].start_even()
        proj_part(j, 1)
        thirds[j].start_odd()
    tiles(2 * count, 256, term_rows(near, 0))
    scatter.relay()

    bias_here[...] = jnp.zeros_like(bias_here)
    for j in range(3):
        def bias_rows(rows):
            bias_here[j : j + 1] += jnp.sum(
                grad_pre[j, rows].astype(jnp.float32), axis=0, keepdims=True
            )

        tiles(4 * count, 256, bias_rows)
    bias_x = p.send(bias_here, bias_got.at[0], p.at(x=1)).start()
    for j in range(3):
        proj_part(j, 2)
        proj_part(j, 3)
    bias_x.arrived()
    bias_x.left()
    bias_here[...] += bias_got[0]
    bias_y = p.send(bias_here, bias_got.at[1], p.at(y=1)).start()
    up.settle()
    bias_y.arrived()
    bias_y.left()
    bias_here[...] += bias_got[1]
    near_sem, far_sem = p.take("recv"), p.take("recv")
    bias_home = [
        p.send(bias_here, bias_got.at[2], p.at(core=1), near_sem, first).start(),
        p.send(bias_here, bias_got.at[2], p.at(core=1, far=1), near_sem, second).start(),
        p.send(bias_here, bias_got.at[3], p.at(far=1), far_sem, second).start(),
    ]
    wait_all(loads)
    thirds[0].relay()
    scatter.arrived()
    gain = vectors[0:1]
    all_sums[...] = jnp.zeros_like(all_sums)
    shift_sum[...] = jnp.zeros_like(shift_sum)

    def first_back(rows):
        incoming = scatter.total(rows)
        back, product = norm_back_rows(own[rows].astype(jnp.float32), incoming, gain)
        all_sums[...] += fold(product)
        shift_sum[...] += fold(incoming)
        result[rows] = result[rows] + back

    tiles(count, CHUNK, first_back)
    stores = store_natural(p, result, input_grads)
    all_sums[0:1] = jnp.sum(all_sums[...], axis=0, keepdims=True)
    all_sums[1:2] = jnp.sum(shift_sum[...], axis=0, keepdims=True)
    all_sums[2:4] = sums[0:2]
    slots = {key: j for j, key in enumerate(ORDER)}
    vector_sends = []
    for dy in (0, 1):
        for dx in (0, 1):
            for core in (0, 1):
                if not (dy or dx or core):
                    continue
                straight, crossed = slots[(dy, dx, core)], slots[(dy, dx, 1 - core)]
                slot = straight + p.core * (crossed - straight)
                columns = pl.ds(pl.multiple_of(slot * EIGHTH, EIGHTH), EIGHTH)
                vector_sends.append(
                    p.send(
                        all_sums.at[:, columns], vector_got.at[len(vector_sends)],
                        p.at(x=dx, y=dy, core=core),
                    ).start()
                )
    out.settle()
    thirds[1].relay()
    own_slot = slots[(0, 0, 0)] + p.core * (slots[(0, 0, 1)] - slots[(0, 0, 0)])
    total = all_sums[:, pl.ds(pl.multiple_of(own_slot * EIGHTH, EIGHTH), EIGHTH)]
    for k, sent in enumerate(vector_sends):
        sent.arrived()
        total = total + vector_got[k]
    vector_total[0] = total
    z_near = p.send(vector_total.at[0], z_got.at[0], p.at(near=1)).start()
    thirds[0].settle()
    thirds[2].relay()
    z_near.arrived()
    vector_total[1] = vector_total[0] + z_got[0]
    z_far = p.send(vector_total.at[1], z_got.at[1], p.at(far=1)).start()
    thirds[1].settle()
    z_far.arrived()
    z_near.left()
    z_far.left()
    vector_total[0] = vector_total[1] + z_got[1]
    vector_store = p.copy(vector_total.at[0], vector_grads).start()
    bias_home[0].arrived()
    bias_home[2].arrived(second)
    for sent in bias_home:
        sent.left()
    pl.when(second)(lambda: combine(bias_got.at[2], [bias_got.at[2], bias_got.at[3]], 8))
    pl.when(first)(lambda: combine(bias_got.at[2], [bias_got.at[2], bias_here], 8))
    bias_store = p.copy(bias_got.at[2], bias_grad).start()
    thirds[2].settle()
    up.finish(up_owned)
    out.finish(out_owned)
    for j in range(3):
        thirds[j].finish(proj_owned.at[j])
    for weight in (up, out, *thirds):
        weight.stored()
    scatter.finish()
    for sent in vector_sends:
        sent.left()
    wait_all(stores)
    vector_store.wait()
    bias_store.wait()


def call(body, name, collective, inputs, in_specs, outs, scratch, counts):
    bf16_bytes = sum(math.prod(o.shape) * o.dtype.itemsize for o in outs)
    return pl.pallas_call(
        body,
        out_shape=outs,
        in_specs=in_specs,
        out_specs=[ANY] * len(outs),
        scratch_shapes=[
            *scratch,
            pltpu.SemaphoreType.DMA((counts[0],)),
            pltpu.SemaphoreType.DMA((counts[1],)),
            pltpu.SemaphoreType.DMA((counts[2],)),
        ],
        compiler_params=pltpu.CompilerParams(
            collective_id=collective, has_side_effects=True, vmem_limit_bytes=VMEM_BYTES
        ),
        cost_estimate=pl.CostEstimate(
            flops=0, bytes_accessed=2 * bf16_bytes, transcendentals=0
        ),
        name=name,
    )(*inputs)


def bf16(*shape):
    return jax.ShapeDtypeStruct(shape, jnp.bfloat16)


def f32(*shape):
    return jax.ShapeDtypeStruct(shape, jnp.float32)


def held(shape_struct):
    return pltpu.VMEM(shape_struct.shape, shape_struct.dtype)


def weight_scratch(quarter, eighth):
    return [
        held(bf16(2, *quarter)), held(bf16(2, *quarter)), held(bf16(2, *eighth)),
        held(bf16(2, *eighth)), held(f32(*eighth)),
    ]


WHOLE = pl.BlockSpec(memory_space=pltpu.VMEM)
EIGHTH = 256


def local_pairs(
    inputs,
    gain_first,
    shift_first,
    projections,
    biases,
    output_weight,
    gain_second,
    shift_second,
    gate_up,
    down_weight,
    cotangent,
):
    count, width = inputs.shape
    rows = 4 * count
    heads_width = output_weight.shape[0]
    hidden_width = down_weight.shape[0]
    cosine, sine = angle_tables()
    rest = ((0, 0), (0, HD - ROTARY))
    cosine_table, sine_first, sine_latter = (
        jnp.tile(jnp.pad(table, rest, constant_values=fill), (1, 128 // HD))
        for table, fill in (
            (jnp.concatenate([cosine, cosine], axis=1), 1.0),
            (jnp.concatenate([-sine, jnp.zeros_like(sine)], axis=1), 0.0),
            (jnp.concatenate([jnp.zeros_like(sine), sine], axis=1), 0.0),
        )
    )
    vectors = jnp.pad(
        jnp.stack([gain_first, shift_first, gain_second, shift_second]).astype(jnp.float32),
        ((0, 4), (0, 0)),
    )
    wide_biases = jnp.pad(biases.astype(jnp.float32), ((0, 5), (0, 0)))
    wide = bf16(rows, width)
    inner = bf16(rows, hidden_width)
    own = bf16(count, width)
    half_rows = bf16(2 * count, width)
    (
        proj_full, out_full, gu_full, down_full, vectors, gathered_one, gathered_cot, heads, mixed_rows,
        middle, gathered_two, hidden, gate_act, up_act,
    ) = call(
        forward_kernel, "forward", 1,
        (
            inputs, cotangent, vectors, wide_biases, cosine_table, sine_first, sine_latter,
            projections, output_weight, gate_up, down_weight,
        ),
        [ANY] * 4 + [WHOLE] * 3 + [ANY] * 4,
        [
            bf16(3, width, heads_width), bf16(heads_width, width), bf16(2, width, hidden_width),
            bf16(hidden_width, width), f32(8, width), wide, wide, bf16(3, rows, heads_width),
            bf16(rows, heads_width), f32(count, width), wide, inner, inner, inner,
        ],
        [
            held(own), held(own), held(own), held(f32(8, width)), held(f32(8, heads_width)),
            held(bf16(3, width, heads_width)), held(bf16(heads_width, width)), held(wide),
            held(bf16(3, rows, heads_width)), held(bf16(rows, heads_width)),
            held(half_rows), held(half_rows), held(half_rows), held(own), held(f32(count, width)),
            held(wide), held(bf16(2, width, hidden_width)), held(f32(rows, hidden_width)),
            held(inner), held(inner), held(inner),
        ],
        (96, 96, 64),
    )

    by_rows = ((2 * EIGHTH, hidden_width), (EIGHTH, hidden_width))
    by_columns = ((hidden_width, 2 * EIGHTH), (hidden_width, EIGHTH))
    (
        outputs, grad_middle, gathered_branch, sums, down_owned, gate_owned, up_parts, *_,
    ) = call(
        back_kernel, "scatter_first", 3,
        (
            hidden, gate_act, up_act, gathered_cot, gathered_two, gu_full, down_full, middle, vectors,
        ),
        [ANY] * 8 + [WHOLE],
        [
            bf16(count, width), f32(count, width), bf16(rows, width), f32(8, width),
            f32(hidden_width, EIGHTH), f32(EIGHTH, hidden_width), bf16(width, hidden_width),
            bf16(2, hidden_width, 2 * EIGHTH), bf16(2, 2 * EIGHTH, hidden_width),
        ],
        [
            *[held(bf16(rows, hidden_width))] * 3, held(bf16(rows, width)), held(bf16(rows, width)),
            held(bf16(width, hidden_width)), held(bf16(width, hidden_width)),
            held(bf16(hidden_width, width)), held(f32(count, width)),
            held(bf16(2 * count, width)), held(bf16(2 * count, width)),
            held(bf16(count, width)), held(bf16(2 * count, width)), held(bf16(count, width)),
            held(f32(8, width)), held(f32(8, width)), held(bf16(2, hidden_width, 2 * EIGHTH)),
            *weight_scratch(*by_columns)[1:], *weight_scratch(*by_rows)[1:4],
        ],
        (64, 64, 48),
    )

    third = ((2 * EIGHTH, heads_width), (EIGHTH, heads_width))
    input_grads, proj_owned, out_owned, vector_grads, bias_grad, up_owned = call(
        last_kernel, "scatter_second", 4,
        (
            gathered_branch, out_full, heads, mixed_rows, gathered_one, proj_full, inputs, vectors,
            cosine_table, sine_first, sine_latter, grad_middle, sums, up_parts,
        ),
        [ANY] * 7 + [WHOLE] * 4 + [ANY, WHOLE, ANY],
        [
            f32(count, width), f32(3, EIGHTH, heads_width), f32(heads_width, EIGHTH),
            f32(8, EIGHTH), f32(8, heads_width), f32(EIGHTH, hidden_width),
        ],
        [
            held(wide), held(bf16(heads_width, width)), held(bf16(3, rows, heads_width)),
            held(bf16(rows, heads_width)), held(bf16(rows, heads_width)),
            held(bf16(3, rows, heads_width)), held(wide), held(bf16(3, width, heads_width)),
            held(bf16(2, heads_width, 2 * EIGHTH)), held(bf16(3, 2, 2 * EIGHTH, heads_width)),
            held(own), held(half_rows), held(own), held(f32(count, width)),
            held(f32(8, width)), held(f32(8, width)),
            held(f32(7, 8, EIGHTH)), held(f32(2, 8, EIGHTH)), held(f32(2, 8, EIGHTH)),
            held(f32(8, heads_width)), held(f32(4, 8, heads_width)),
            *weight_scratch(*by_rows),
            *weight_scratch((heads_width, 2 * EIGHTH), (heads_width, EIGHTH)),
            *weight_scratch(*third), *weight_scratch(*third), *weight_scratch(*third),
        ],
        (64, 64, 48),
    )
    return (
        outputs,
        input_grads,
        vector_grads[0],
        vector_grads[1],
        proj_owned,
        bias_grad[:3],
        out_owned,
        vector_grads[2],
        vector_grads[3],
        jnp.stack([gate_owned, up_owned]),
        down_owned,
    )


def solution(mesh):
    whole_pairs = dict(mesh.shape) == {"dp": 8, "tensor": 4}
    return jax.shard_map(
        local_pairs if whole_pairs else local,
        mesh=mesh,
        in_specs=(
            P(("dp", "tensor"), None),
            P("dp"),
            P("dp"),
            P(None, "dp", "tensor"),
            P(None, "tensor"),
            P("tensor", "dp"),
            P("dp"),
            P("dp"),
            P(None, "dp", "tensor"),
            P("tensor", "dp"),
            P(("dp", "tensor"), None),
        ),
        out_specs=(
            P(("dp", "tensor"), None),
            P(("dp", "tensor"), None),
            P("dp"),
            P("dp"),
            P(None, "dp", "tensor"),
            P(None, "tensor"),
            P("tensor", "dp"),
            P("dp"),
            P("dp"),
            P(None, "dp", "tensor"),
            P("tensor", "dp"),
        ),
        check_vma=False,
    )
```

```python
import math

import jax
import jax.numpy as jnp
from jax import lax
from jax.experimental import pallas as pl
from jax.experimental.pallas import tpu as pltpu
from jax.sharding import PartitionSpec as P

HD = 64
ROTARY = 16
SEQ_LEN = 512


EPSILON = 1e-05
ANGLE_BASE = 10000.0
NEGATIVE = -1e30


def norm_rows(rows, gain, shift):
    average = jnp.mean(rows, axis=-1, keepdims=True)
    centred = rows - average
    inverse = lax.rsqrt(jnp.mean(centred * centred, axis=-1, keepdims=True) + EPSILON)
    unit_rows = centred * inverse
    return (unit_rows * gain + shift, unit_rows, inverse)


def norm_back(incoming, unit_rows, inverse, gain):
    scaled = incoming * gain
    inner = (
        scaled
        - jnp.mean(scaled, axis=-1, keepdims=True)
        - unit_rows * jnp.mean(scaled * unit_rows, axis=-1, keepdims=True)
    )
    return (inner * inverse, jnp.sum(incoming * unit_rows, axis=0), jnp.sum(incoming, axis=0))


def angle_tables():
    freqs = 1.0 / ANGLE_BASE ** (jnp.arange(0, ROTARY, 2).astype(jnp.float32) / ROTARY)
    angles = jnp.arange(SEQ_LEN).astype(jnp.float32)[:, None] * freqs[None, :]
    return (jnp.cos(angles), jnp.sin(angles))


def rotate(heads, cosine, sine, sign):
    half_rot = ROTARY // 2
    first = heads[..., :half_rot]
    latter = heads[..., half_rot:ROTARY]
    cos_part = cosine[:, None, :]
    sin_part = sine[:, None, :] * sign
    return jnp.concatenate(
        [
            first * cos_part - latter * sin_part,
            latter * cos_part + first * sin_part,
            heads[..., ROTARY:],
        ],
        axis=-1,
    )


def causal_scores(queries, key_rows, positions):
    scaling = 1.0 / math.sqrt(HD)
    scores = scaling * jnp.einsum(
        "qhd,khd->hqk", queries, key_rows, preferred_element_type=jnp.float32
    )
    causal = positions[:, None] >= positions[None, :]
    return jnp.where(causal[None], scores, NEGATIVE)


def attend_forward(pieces, positions):
    queries, key_rows, value_rows = pieces
    scores = causal_scores(queries, key_rows, positions)
    row_top = jnp.max(scores, axis=-1, keepdims=True)
    exponent = jnp.exp(scores - row_top)
    totals = jnp.sum(exponent, axis=-1, keepdims=True)
    weights = (exponent / totals).astype(jnp.bfloat16)
    mixed = jnp.einsum("hqk,khd->qhd", weights, value_rows, preferred_element_type=jnp.float32)
    return (mixed.astype(jnp.bfloat16), (row_top + jnp.log(totals))[..., 0])


def attend_back(pieces, positions):
    queries, key_rows, value_rows, grad_mixed, log_totals = pieces
    scaling = 1.0 / math.sqrt(HD)
    scores = causal_scores(queries, key_rows, positions)
    weights = jnp.exp(scores - log_totals[..., None])
    grad_values = jnp.einsum(
        "hqk,qhd->khd", weights.astype(jnp.bfloat16), grad_mixed, preferred_element_type=jnp.float32
    )
    grad_weights = jnp.einsum(
        "qhd,khd->hqk", grad_mixed, value_rows, preferred_element_type=jnp.float32
    )
    grad_scores = weights * (grad_weights - jnp.sum(weights * grad_weights, axis=-1, keepdims=True))
    grad_scores = grad_scores.astype(jnp.bfloat16)
    grad_queries = scaling * jnp.einsum(
        "hqk,khd->qhd", grad_scores, key_rows, preferred_element_type=jnp.float32
    )
    grad_keys = scaling * jnp.einsum(
        "hqk,qhd->khd", grad_scores, queries, preferred_element_type=jnp.float32
    )
    return (grad_queries, grad_keys, grad_values)


def scatter_sum(terms, axis, dimension):
    owned = lax.psum_scatter(
        terms.astype(jnp.bfloat16), axis, scatter_dimension=dimension, tiled=True
    )
    return owned.astype(jnp.float32)


def local(
    inputs,
    gain_first,
    shift_first,
    projections,
    biases,
    output_weight,
    gain_second,
    shift_second,
    gate_up,
    down_weight,
    cotangent,
):
    tensor_ways = lax.axis_size("tensor")
    row_count = inputs.shape[0]
    group_rows = row_count * tensor_ways
    sequences = group_rows // SEQ_LEN
    head_width = output_weight.shape[0]
    local_heads = head_width // HD
    head_shape = (sequences, SEQ_LEN, local_heads, HD)
    cosine, sine = angle_tables()
    positions = jnp.arange(SEQ_LEN)
    proj_full, out_full, gain_one, shift_one = (
        lax.all_gather(projections, "dp", axis=1, tiled=True),
        lax.all_gather(output_weight, "dp", axis=1, tiled=True),
        lax.all_gather(gain_first, "dp", axis=0, tiled=True),
        lax.all_gather(shift_first, "dp", axis=0, tiled=True),
    )
    gain_one = gain_one.astype(jnp.float32)
    residual = inputs.astype(jnp.float32)
    normed_one, unit_one, inverse_one = norm_rows(residual, gain_one, shift_one.astype(jnp.float32))
    gathered_one = lax.all_gather(normed_one.astype(jnp.bfloat16), "tensor", axis=0, tiled=True)
    pre_all = jnp.einsum("gd,jde->jge", gathered_one, proj_full, preferred_element_type=jnp.float32)
    pre_all = pre_all + biases.astype(jnp.float32)[:, None, :]
    queries = rotate(pre_all[0].reshape(head_shape), cosine, sine, 1.0).astype(jnp.bfloat16)
    key_rows = rotate(pre_all[1].reshape(head_shape), cosine, sine, 1.0).astype(jnp.bfloat16)
    value_rows = pre_all[2].reshape(head_shape).astype(jnp.bfloat16)
    mixed, log_totals = lax.map(
        lambda pieces: attend_forward(pieces, positions), (queries, key_rows, value_rows)
    )
    mixed_rows = mixed.reshape(group_rows, head_width)
    part = mixed_rows
    middle = residual + scatter_sum(
        jnp.dot(part, out_full, preferred_element_type=jnp.float32), "tensor", 0
    )
    gu_full, down_full, gain_two, shift_two = (
        lax.all_gather(gate_up, "dp", axis=1, tiled=True),
        lax.all_gather(down_weight, "dp", axis=1, tiled=True),
        lax.all_gather(gain_second, "dp", axis=0, tiled=True),
        lax.all_gather(shift_second, "dp", axis=0, tiled=True),
    )
    gain_two = gain_two.astype(jnp.float32)
    normed_two, unit_two, inverse_two = norm_rows(middle, gain_two, shift_two.astype(jnp.float32))
    gathered_two = lax.all_gather(normed_two.astype(jnp.bfloat16), "tensor", axis=0, tiled=True)
    gate_act = jnp.dot(gathered_two, gu_full[0], preferred_element_type=jnp.float32)
    up_act = jnp.dot(gathered_two, gu_full[1], preferred_element_type=jnp.float32)
    sigmoid_gate = jax.nn.sigmoid(gate_act)
    hidden = (gate_act * sigmoid_gate * up_act).astype(jnp.bfloat16)
    part = hidden
    outputs = (
        middle
        + scatter_sum(jnp.dot(part, down_full, preferred_element_type=jnp.float32), "tensor", 0)
    ).astype(jnp.bfloat16)
    gu_back, down_back, gain_two_back = (
        lax.all_gather(gate_up, "dp", axis=1, tiled=True),
        lax.all_gather(down_weight, "dp", axis=1, tiled=True),
        lax.all_gather(gain_second, "dp", axis=0, tiled=True),
    )
    gain_two_back = gain_two_back.astype(jnp.float32)
    gathered_cot = lax.all_gather(cotangent, "tensor", axis=0, tiled=True)
    grad_hidden = jnp.einsum(
        "gd,fd->gf", gathered_cot, down_back, preferred_element_type=jnp.float32
    )
    down_grad = jnp.einsum("gf,gd->fd", hidden, gathered_cot, preferred_element_type=jnp.float32)
    grad_up = (grad_hidden * gate_act * sigmoid_gate).astype(jnp.bfloat16)
    grad_gate = (
        grad_hidden * up_act * sigmoid_gate * (1.0 + gate_act * (1.0 - sigmoid_gate))
    ).astype(jnp.bfloat16)
    gu_grad = jnp.stack(
        [
            jnp.einsum("gd,gf->df", gathered_two, grad_gate, preferred_element_type=jnp.float32),
            jnp.einsum("gd,gf->df", gathered_two, grad_up, preferred_element_type=jnp.float32),
        ]
    )
    first_term = jnp.einsum("gf,df->gd", grad_gate, gu_back[0], preferred_element_type=jnp.float32)
    grad_second = scatter_sum(
        first_term
        + jnp.einsum("gf,df->gd", grad_up, gu_back[1], preferred_element_type=jnp.float32),
        "tensor",
        0,
    )
    gu_owned, down_owned = (
        scatter_sum(gu_grad, "dp", 1),
        scatter_sum(down_grad, "dp", 1),
    )
    grad_mid_norm, gain_two_part, shift_two_part = norm_back(
        grad_second, unit_two, inverse_two, gain_two_back
    )
    grad_middle = cotangent.astype(jnp.float32) + grad_mid_norm
    proj_back, out_back, gain_one_back = (
        lax.all_gather(projections, "dp", axis=1, tiled=True),
        lax.all_gather(output_weight, "dp", axis=1, tiled=True),
        lax.all_gather(gain_first, "dp", axis=0, tiled=True),
    )
    gain_one_back = gain_one_back.astype(jnp.float32)
    gathered_branch = lax.all_gather(grad_middle.astype(jnp.bfloat16), "tensor", axis=0, tiled=True)
    out_grad = jnp.einsum(
        "ge,gd->ed", mixed_rows, gathered_branch, preferred_element_type=jnp.float32
    )
    grad_mixed = jnp.einsum(
        "gd,ed->ge", gathered_branch, out_back, preferred_element_type=jnp.float32
    ).astype(jnp.bfloat16)
    grad_queries, grad_keys, grad_values = lax.map(
        lambda pieces: attend_back(pieces, positions),
        (queries, key_rows, value_rows, grad_mixed.reshape(head_shape), log_totals),
    )
    grad_queries = rotate(grad_queries, cosine, sine, -1.0)
    grad_keys = rotate(grad_keys, cosine, sine, -1.0)
    grad_pre = (
        jnp.stack([grad_queries, grad_keys, grad_values])
        .reshape(3, group_rows, head_width)
        .astype(jnp.bfloat16)
    )
    bias_part = jnp.sum(grad_pre, axis=1, dtype=jnp.float32)
    proj_grad = jnp.einsum(
        "gd,jge->jde", gathered_one, grad_pre, preferred_element_type=jnp.float32
    )
    part = grad_pre
    grad_normed = scatter_sum(
        jnp.einsum("jge,jde->gd", part, proj_back, preferred_element_type=jnp.float32),
        "tensor",
        0,
    )
    proj_owned, out_owned = (
        scatter_sum(proj_grad, "dp", 1),
        scatter_sum(out_grad, "dp", 1),
    )
    grad_in_norm, gain_one_part, shift_one_part = norm_back(
        grad_normed, unit_one, inverse_one, gain_one_back
    )
    input_grads = grad_middle + grad_in_norm
    one_hot = (jnp.arange(tensor_ways) == lax.axis_index("tensor")).astype(jnp.float32)
    spread_bias = (bias_part[:, None, :] * one_hot[None, :, None]).reshape(
        3, tensor_ways * head_width
    )
    summed = lax.psum(
        (gain_one_part, shift_one_part, gain_two_part, shift_two_part, spread_bias),
        ("dp", "tensor"),
    )
    own_width = gain_first.shape[0]
    own_offset = lax.axis_index("dp") * own_width

    def own_part(vector):
        return lax.dynamic_slice_in_dim(vector, own_offset, own_width, 0)

    bias_grad = jnp.sum(
        summed[4].reshape(3, tensor_ways, head_width) * one_hot[None, :, None], axis=1
    )
    return (
        outputs,
        input_grads,
        own_part(summed[0]),
        own_part(summed[1]),
        proj_owned,
        bias_grad,
        out_owned,
        own_part(summed[2]),
        own_part(summed[3]),
        gu_owned,
        down_owned,
    )


ORDER = ((1, 0, 0), (1, 1, 0), (0, 1, 1), (1, 1, 1), (0, 0, 0), (0, 1, 0), (0, 0, 1), (1, 0, 1))
EVEN_Y, EVEN_XY, ODD_X, ODD_XY, EVEN, EVEN_X, ODD, ODD_Y = range(8)
ANY = pl.BlockSpec(memory_space=pl.ANY)
VMEM_BYTES = 63 * 1024 * 1024


class Place:
    def __init__(self, send_sems, recv_sems, local_sems):
        self.dp, self.tensor = lax.axis_index("dp"), lax.axis_index("tensor")
        self.core = lax.rem(self.dp, 2)
        self.x = lax.rem(self.dp // 2, 2)
        self.y = self.dp // 4
        self.pools = {"send": send_sems, "recv": recv_sems, "local": local_sems}
        self.used = {"send": 0, "recv": 0, "local": 0}

    def take(self, kind):
        self.used[kind] += 1
        return self.pools[kind].at[self.used[kind] - 1]

    def at(self, x=0, y=0, core=0, near=0, far=0):
        dp = self.dp
        dp = dp + x * (2 - 4 * self.x) + y * (4 - 8 * self.y) + core * (1 - 2 * self.core)
        tensor = self.tensor
        tensor = tensor + near * (1 - 2 * lax.rem(tensor, 2)) + far * (2 - 4 * (tensor // 2))
        return (dp, tensor)

    def column(self, key):
        dy, dx, core = key
        y = self.y + dy * (1 - 2 * self.y)
        x = self.x + dx * (1 - 2 * self.x)
        return pl.multiple_of((y * 4 + x * 2 + core) * EIGHTH, EIGHTH)

    def greet(self):
        barrier = pltpu.get_barrier_semaphore()
        partners = [
            self.at(x=x, y=y, core=core)
            for x in (0, 1)
            for y in (0, 1)
            for core in (0, 1)
            if x or y or core
        ] + [self.at(near=1), self.at(far=1), self.at(far=1, core=1)]
        for partner in partners:
            pl.semaphore_signal(
                barrier, inc=1, device_id=partner, device_id_type=pl.DeviceIdType.MESH
            )
        pl.semaphore_wait(barrier, len(partners))

    def send(self, source, target, device, recv_sem=None, when=None):
        return Sent(
            pltpu.make_async_remote_copy(
                src_ref=source,
                dst_ref=target,
                send_sem=self.take("send"),
                recv_sem=self.take("recv") if recv_sem is None else recv_sem,
                device_id=device,
                device_id_type=pl.DeviceIdType.MESH,
            ),
            when,
        )

    def copy(self, source, target, when=None):
        return Copied(pltpu.make_async_copy(source, target, self.take("local")), when)


def guarded(when, action):
    if when is None:
        action()
    else:
        pl.when(when)(action)


class Sent:
    def __init__(self, copy, when):
        self.copy, self.when = copy, when

    def start(self):
        guarded(self.when, self.copy.start)
        return self

    def arrived(self, when=None):
        guarded(when, self.copy.wait_recv)

    def left(self):
        guarded(self.when, self.copy.wait_send)


class Copied:
    def __init__(self, copy, when):
        self.copy, self.when = copy, when

    def start(self):
        guarded(self.when, self.copy.start)
        return self

    def wait(self):
        guarded(self.when, self.copy.wait)


class GatherWeight:
    def __init__(self, place, shard, block, pair=None):
        self.place, self.shard, self.block = place, shard, block
        self.sent = []
        self.pair = pair

    def fetch(self, even=None, odd=None):
        p = self.place
        even = self.block(EVEN) if even is None else even
        odd = self.block(ODD) if odd is None else odd
        first, second = p.core == 0, p.core == 1
        self.own = p.copy(self.shard, even, first).start()
        even_sem, odd_sem = p.take("recv"), p.take("recv")
        self.to_far_even = p.send(self.shard, even, p.at(core=1, far=1), even_sem, first).start()
        self.to_sibling = p.send(self.shard, odd, p.at(core=1), odd_sem, second).start()
        self.to_far_odd = p.send(self.shard, odd, p.at(far=1), odd_sem, second).start()
        return self

    def fetched(self):
        p = self.place
        self.own.wait()
        self.to_far_even.arrived(p.core == 1)
        self.to_sibling.arrived()
        return self

    def fetch_left(self):
        self.to_far_even.left()
        self.to_sibling.left()
        self.to_far_odd.left()

    def spread(self, even=None, odd=None):
        p, block = self.place, self.block
        even = block(EVEN) if even is None else even
        odd = block(ODD) if odd is None else odd
        self.even_x = p.send(even, block(EVEN_X), p.at(x=1)).start()
        self.odd_y = p.send(odd, block(ODD_Y), p.at(y=1)).start()
        self.odd_x = p.send(odd, block(ODD_X), p.at(x=1)).start()
        self.even_y = p.send(even, block(EVEN_Y), p.at(y=1)).start()
        return self

    def relay(self):
        p, block = self.place, self.block
        self.even_x.arrived()
        self.even_xy = p.send(block(EVEN_X), block(EVEN_XY), p.at(y=1)).start()
        self.odd_y.arrived()
        self.odd_xy = p.send(block(ODD_Y), block(ODD_XY), p.at(x=1)).start()
        return self

    def finish(self):
        for copy in (self.odd_x, self.even_y, self.even_xy, self.odd_xy):
            copy.arrived()
        for copy in (
            self.even_x, self.odd_y, self.odd_x, self.even_y, self.even_xy, self.odd_xy,
        ):
            copy.left()


class GatherRows:
    def __init__(self, place, own, rows):
        self.place, self.own, self.rows = place, own, rows
        self.count = own.shape[0]

    def slot(self, k):
        return self.rows.at[pl.ds(k * self.count, self.count)]

    def start(self):
        p = self.place
        self.beside = p.send(self.own, self.slot(1), p.at(near=1)).start()
        self.sibling = p.send(self.own, self.slot(2), p.at(core=1)).start()
        self.here = p.copy(self.own, self.slot(0)).start()
        return self

    def relay(self):
        p = self.place
        self.beside.arrived()
        self.across = p.send(self.slot(1), self.slot(3), p.at(core=1)).start()
        return self

    def finish(self):
        self.sibling.arrived()
        self.across.arrived()
        self.here.wait()
        for copy in (self.beside, self.sibling, self.across):
            copy.left()


def combine(target, terms, chunk):
    @pl.loop(0, target.shape[0] // chunk)
    def _(i):
        rows = pl.ds(pl.multiple_of(i * chunk, chunk), chunk)
        total = terms[0][rows].astype(jnp.float32)
        for term in terms[1:]:
            total = total + term[rows].astype(jnp.float32)
        target[rows] = total.astype(target.dtype)


class ScatterRows:
    def __init__(self, place, far, near, got, got_beside):
        self.place, self.far, self.near = place, far, near
        self.got, self.got_beside = got, got_beside
        self.count = near.shape[0] // 2

    def start(self):
        self.sibling = self.place.send(self.far, self.got, self.place.at(core=1)).start()
        return self

    def relay(self):
        p, n = self.place, self.count
        self.sibling.arrived()
        late = pl.ds(n, n)
        combine(self.near.at[late], [self.near.at[late], self.got.at[late]], 32)
        self.beside = p.send(self.near.at[late], self.got_beside, p.at(near=1)).start()
        return self

    def total(self, rows):
        return (
            self.near[rows].astype(jnp.float32)
            + self.got[rows].astype(jnp.float32)
            + self.got_beside[rows].astype(jnp.float32)
        )

    def arrived(self):
        self.beside.arrived()

    def finish(self):
        self.sibling.left()
        self.beside.left()


class ScatterWeight:
    def __init__(self, place, send, keep, rows, got, last, home, result):
        self.place, self.parts, self.keep, self.rows = place, send, keep, rows
        self.got, self.last, self.home, self.result = got, last, home, result
        self.loads = []

    def half(self, ref, k):
        if self.rows:
            size = ref.shape[0] // 2
            return ref.at[pl.ds(k * size, size)]
        size = ref.shape[1] // 2
        return ref.at[:, pl.ds(k * size, size)]

    def load(self, sources):
        self.loads = [self.place.copy(a, b).start() for a, b in zip(sources, self.keep)]
        return self

    def start_even(self):
        p = self.place
        self.even = p.send(self.parts[0], self.got.at[0], p.at(y=1)).start()
        return self

    def start_odd(self):
        p = self.place
        self.odd = p.send(self.parts[1], self.got.at[1], p.at(x=1)).start()
        return self

    def start(self):
        return self.start_even().start_odd()

    def relay(self):
        p = self.place
        wait_all(self.loads)
        self.second = []
        for k, arrival in enumerate((self.even, self.odd)):
            arrival.arrived()
            there = self.half(self.keep[k], 1)
            combine(there, [there, self.half(self.got.at[k], 1)], 64)
            device = p.at(x=1) if k == 0 else p.at(y=1)
            self.second.append(p.send(there, self.last.at[k], device).start())
        return self

    def gather(self):
        for k in (1, 0):
            self.second[k].arrived()
            here = self.half(self.keep[k], 0)
            combine(here, [here, self.half(self.got.at[k], 0), self.last.at[k]], 64)
        return self

    def settle(self):
        self.gather()
        even, odd = self.half(self.keep[0], 0), self.half(self.keep[1], 0)
        self.way_home = HomeSum(self.place, even, odd, even, self.home, self.result).start()
        return self

    def finish(self, output):
        self.way_home.finish(output)
        self.left()

    def left(self):
        for copy in (self.even, self.odd, *self.second):
            copy.left()

    def stored(self):
        self.way_home.stored()


class HomeSum:
    def __init__(self, place, even, odd, here, home, result):
        self.place, self.even, self.odd, self.here = place, even, odd, here
        self.home, self.result = home, result

    def start(self):
        p = self.place
        first, second = p.core == 0, p.core == 1
        near_sem, far_sem = p.take("recv"), p.take("recv")
        home = self.home
        self.to_sibling = p.send(self.odd, home.at[0], p.at(core=1), near_sem, first).start()
        self.to_first = p.send(self.even, home.at[0], p.at(core=1, far=1), near_sem, second).start()
        self.to_far = p.send(self.odd, home.at[1], p.at(far=1), far_sem, second).start()
        return self

    def finish(self, output):
        p, home = self.place, self.home
        first, second = p.core == 0, p.core == 1
        self.to_sibling.arrived()
        self.to_far.arrived(second)
        pl.when(first)(lambda: combine(self.result, [self.here, home.at[0]], 64))
        pl.when(second)(lambda: combine(self.result, [home.at[0], home.at[1]], 64))
        self.store = p.copy(self.result, output).start()
        for copy in (self.to_sibling, self.to_first, self.to_far):
            copy.left()

    def stored(self):
        self.store.wait()


def load_local(place, source, target):
    return [
        place.copy(
            source.at[:, pl.ds(place.column(key), EIGHTH)], target.at[:, pl.ds(j * EIGHTH, EIGHTH)]
        ).start()
        for j, key in enumerate(ORDER)
    ]


def store_natural(place, source, target):
    return [
        place.copy(
            source.at[:, pl.ds(j * EIGHTH, EIGHTH)], target.at[:, pl.ds(place.column(key), EIGHTH)]
        ).start()
        for j, key in enumerate(ORDER)
    ]


def wait_all(copies):
    for copy in copies:
        copy.wait()


CHUNK = 32


def norm_into(count, rows_of, gain, shift, target):
    @pl.loop(0, count // CHUNK)
    def _(i):
        rows = pl.ds(pl.multiple_of(i * CHUNK, CHUNK), CHUNK)
        target[rows] = norm_rows(rows_of(rows), gain, shift)[0].astype(target.dtype)


def tiles(count, tile, body):
    @pl.loop(0, count // tile)
    def _(i):
        body(pl.ds(pl.multiple_of(i * tile, tile), tile))


def shifted(rows, offset):
    return pl.ds(pl.multiple_of(rows.start + offset, 256), rows.size)


def dot(left, right, contract):
    return lax.dot_general(
        left, right, (((contract[0],), (contract[1],)), ((), ())), preferred_element_type=jnp.float32
    )


def turned(pre, tables, rows, sign):
    cosine, sine_first, sine_latter = (table[rows] for table in tables)
    return (
        pre * cosine
        + pltpu.roll(pre, 128 - ROTARY // 2, 1) * (sine_first * sign)
        + pltpu.roll(pre, ROTARY // 2, 1) * (sine_latter * sign)
    )


def swapped_half(index, late):
    sequence, half = index // 2, lax.rem(index, 2)
    half = half + late * (1 - 2 * half)
    return half, pl.ds(pl.multiple_of(sequence * SEQ_LEN + half * HALF, HALF), HALF)


HALF = SEQ_LEN // 2


def head_lanes(array, head):
    lanes = lax.broadcasted_iota(jnp.int32, array.shape, 1)
    mine = (lanes < HD) if head == 0 else (lanes >= HD)
    return jnp.where(mine, array, jnp.zeros_like(array))


def side_by_side(first, second):
    lanes = lax.broadcasted_iota(jnp.int32, first.shape, 1)
    return jnp.where(lanes < HD, first, second)


def probabilities(queries, key_rows, half):
    scores = dot(queries, key_rows, (1, 1))
    row = lax.broadcasted_iota(jnp.int32, scores.shape, 0) + half * HALF
    column = lax.broadcasted_iota(jnp.int32, scores.shape, 1)
    scores = jnp.where(row >= column, scores, NEGATIVE)
    exponent = jnp.exp(scores - jnp.max(scores, axis=-1, keepdims=True))
    return exponent * (1.0 / jnp.sum(exponent, axis=-1, keepdims=True))


def attend_pair(heads, mixed, late):
    @pl.loop(0, 2 * heads.shape[2] // 128)
    def _(step):
        pairs = heads.shape[2] // 128
        sequence, lanes = step // pairs, pl.ds(pl.multiple_of(lax.rem(step, pairs) * 128, 128), 128)
        start = pl.multiple_of(sequence * SEQ_LEN, SEQ_LEN)
        for half in (0, 1):
            past = pl.ds(start, HALF * (half + 1))
            queries = heads[0, pl.ds(start + half * HALF, HALF), lanes]
            results = []
            for head in (0, 1):
                probs = probabilities(head_lanes(queries, head), heads[1, past, lanes], half)
                results.append(dot(probs.astype(jnp.bfloat16), heads[2, past, lanes], (1, 0)))
            _, rows = swapped_half(sequence * 2 + half, late)
            mixed[rows, lanes] = side_by_side(*results).astype(mixed.dtype)


def attend_pair_back(heads, grad_mixed, grad_pre, tables, late):
    @pl.loop(0, 2 * heads.shape[2] // 128)
    def _(step):
        pairs = heads.shape[2] // 128
        sequence, lanes = step // pairs, pl.ds(pl.multiple_of(lax.rem(step, pairs) * 128, 128), 128)
        start = pl.multiple_of(sequence * SEQ_LEN, SEQ_LEN)
        grads = [[None, None], [None, None]]
        for half in (0, 1):
            past = pl.ds(start, HALF * (half + 1))
            here = pl.ds(start + half * HALF, HALF)
            queries, incoming = heads[0, here, lanes], grad_mixed[here, lanes]
            key_rows, value_rows = heads[1, past, lanes], heads[2, past, lanes]
            found = []
            for head in (0, 1):
                probs = probabilities(head_lanes(queries, head), key_rows, half)
                grad_values = dot(probs.astype(jnp.bfloat16), incoming, (0, 0))
                grad_probs = dot(head_lanes(incoming, head), value_rows, (1, 1))
                product = probs * grad_probs
                grad_scores = product - probs * jnp.sum(product, axis=-1, keepdims=True)
                grad_scores = grad_scores.astype(jnp.bfloat16)
                grad_queries = dot(grad_scores, key_rows, (1, 0))
                grad_keys = dot(grad_scores, queries, (0, 0))
                found.append((grad_queries, grad_keys, grad_values))
            grad_queries, grad_keys, grad_values = (side_by_side(*two) for two in zip(*found))
            at_half = pl.ds(half * HALF, HALF)
            _, rows = swapped_half(sequence * 2 + half, late)
            grad_queries = turned(grad_queries * (1.0 / math.sqrt(HD)), tables, at_half, -1.0)
            grad_pre[0, rows, lanes] = grad_queries.astype(grad_pre.dtype)
            if half == 0:
                early = (grad_keys, grad_values)
            else:
                whole = [grad_keys[:HALF] + early[0], grad_keys[HALF:]]
                whole_values = [grad_values[:HALF] + early[1], grad_values[HALF:]]
                for k in (0, 1):
                    _, rows = swapped_half(sequence * 2 + k, late)
                    turned_keys = turned(whole[k], tables, pl.ds(k * HALF, HALF), -1.0)
                    grad_pre[1, rows, lanes] = turned_keys.astype(grad_pre.dtype)
                    grad_pre[2, rows, lanes] = whole_values[k].astype(grad_pre.dtype)


def forward_kernel(
    inputs, cotangent, vectors, biases, cosine, sine_first, sine_latter,
    projections, output_weight, gate_up, down_weight,
    proj_full, out_full, gu_full, down_full, vectors_full, rows_one, rows_cot, heads_out, mixed_out,
    middle, rows_two, hidden_out, gate_out, up_out,
    own, normed, own_cot, vectors_here, biases_here, proj_here, out_here, rows_here, heads, mixed,
    near, far, got, got_beside, total, rows_later, gu_here, gate_wide, hidden, gate_act, up_act,
    send_sems, recv_sems, local_sems,
):
    p = Place(send_sems, recv_sems, local_sems)
    count = own.shape[0]
    late = lax.rem(p.tensor, 2)
    tables = (cosine, sine_first, sine_latter)
    loads = load_local(p, inputs, own)
    cot_loads = load_local(p, cotangent, own_cot)
    p.greet()
    slots = {key: j for j, key in enumerate(ORDER)}
    vector_base = p.used["recv"]
    p.used["recv"] += len(ORDER)

    def vector_copy(dy, dx, core):
        here, there = slots[(dy, dx, 0)], slots[(dy, dx, 1)]
        slot = here + p.core * (there - here)
        columns = pl.ds(pl.multiple_of(slot * EIGHTH, EIGHTH), EIGHTH)
        return p.send(
            vectors, vectors_here.at[:, columns], p.at(x=dx, y=dy, core=core),
            recv_sems.at[vector_base + slot],
        )

    vector_sends = [
        vector_copy(dy, dx, core).start()
        for dy in (0, 1) for dx in (0, 1) for core in (0, 1) if dy or dx or core
    ]
    own_slot = slots[(0, 0, 0)] + p.core * (slots[(0, 0, 1)] - slots[(0, 0, 0)])
    own_vectors = p.copy(
        vectors, vectors_here.at[:, pl.ds(pl.multiple_of(own_slot * EIGHTH, EIGHTH), EIGHTH)]
    ).start()
    own_biases = p.copy(biases, biases_here, p.core == 0).start()
    far_biases = p.send(biases, biases_here, p.at(core=1, far=1), when=p.core == 0).start()

    def third(j):
        return GatherWeight(
            p, projections.at[j], lambda k: proj_here.at[j, pl.ds(k * EIGHTH, EIGHTH)]
        )

    def gu_block(j):
        return lambda k: gu_here.at[j, pl.ds(k * EIGHTH, EIGHTH)]

    thirds = [third(0), third(1), third(2)]
    out = GatherWeight(p, output_weight, lambda k: out_here.at[:, pl.ds(k * EIGHTH, EIGHTH)])
    gate = GatherWeight(p, gate_up.at[0], gu_block(0))
    up = GatherWeight(p, gate_up.at[1], gu_block(1))
    down = GatherWeight(p, down_weight, lambda k: down_full.at[:, pl.ds(k * EIGHTH, EIGHTH)])
    thirds[0].fetch()
    thirds[1].fetch()
    wait_all(cot_loads)
    wait_all(loads)
    own_vectors.wait()
    sibling_slot = slots[(0, 0, 1)] + p.core * (slots[(0, 0, 0)] - slots[(0, 0, 1)])
    for dy in (0, 1):
        for dx in (0, 1):
            for core in (0, 1):
                if dy or dx:
                    slot = slots[(dy, dx, core)]
                elif core:
                    slot = sibling_slot
                else:
                    continue
                pltpu.make_async_copy(
                    vectors, vectors_here.at[:, pl.ds(0, EIGHTH)], recv_sems.at[vector_base + slot]
                ).wait()
    gain_one, shift_one = vectors_here[0:1], vectors_here[1:2]
    norm_into(count, lambda rows: own[rows].astype(jnp.float32), gain_one, shift_one, normed)
    gather_one = GatherRows(p, normed, rows_here).start()
    gather_cot = GatherRows(p, own_cot, rows_cot)
    stores = [p.copy(vectors_here, vectors_full).start()]

    thirds[0].fetched().spread()
    thirds[2].fetch()
    thirds[1].fetched().spread()
    out.fetch()
    thirds[0].relay()
    thirds[2].fetched().spread()
    gate.fetch()
    thirds[1].relay()
    out.fetched().spread()
    thirds[2].relay()
    gather_one.relay()
    gather_cot.start()
    up.fetch()
    own_biases.wait()
    far_biases.arrived(p.core == 1)
    far_biases.left()

    def project(j):
        thirds[j].finish()
        stores.append(p.copy(proj_here.at[j], proj_full.at[j]).start())

        @pl.loop(0, 4)
        def _(index):
            rows = pl.ds(pl.multiple_of(index * HALF, HALF), HALF)
            half, target = swapped_half(index, late)
            positions = pl.ds(pl.multiple_of(half * HALF, HALF), HALF)
            pre = dot(rows_here[rows], proj_here[j], (1, 0)) + biases_here[j : j + 1]
            for k in range(pre.shape[1] // 128):
                lanes = slice(k * 128, (k + 1) * 128)
                part = pre[:, lanes]
                if j < 2:
                    part = turned(part, tables, positions, 1.0)
                if j == 0:
                    part = part * (1.0 / math.sqrt(HD))
                heads[j, target, lanes] = part.astype(heads.dtype)

    gather_one.finish()
    stores.append(p.copy(rows_here, rows_one).start())
    project(0)
    gate.fetched().spread()
    project(1)
    out.relay()
    project(2)
    gather_cot.relay()
    stores.append(p.copy(heads, heads_out).start())
    attend_pair(heads, mixed, late)
    out.finish()
    stores += [p.copy(out_here, out_full).start(), p.copy(mixed, mixed_out).start()]

    def out_rows(target, offset):
        def part(rows):
            target[rows] = dot(mixed[shifted(rows, offset)], out_here[...], (1, 0)).astype(target.dtype)

        return part

    scatter = ScatterRows(p, far, near, got, got_beside)
    tiles(2 * count, 256, out_rows(far, 2 * count))
    scatter.start()
    tiles(2 * count, 256, out_rows(near, 0))
    scatter.relay()
    gate.relay()
    up.fetched().spread()
    scatter.arrived()
    gain_two, shift_two = vectors_here[2:3], vectors_here[3:4]

    def norm(rows):
        value = own[rows].astype(jnp.float32) + scatter.total(rows)
        total[rows] = value
        normed[rows] = norm_rows(value, gain_two, shift_two)[0].astype(normed.dtype)

    tiles(count, CHUNK, norm)
    gather = GatherRows(p, normed, rows_later).start()
    stores.append(p.copy(total, middle).start())
    down.fetch()
    gather_cot.finish()
    gather.relay()
    up.relay()
    down.fetched().spread()
    gate.finish()
    gather.finish()
    stores.append(p.copy(rows_later, rows_two).start())
    stores.append(p.copy(gu_here.at[0], gu_full.at[0]).start())

    def gate_rows(rows):
        gate_wide[rows] = dot(rows_later[rows], gu_here[0], (1, 0))

    tiles(4 * count, 256, gate_rows)
    up.finish()
    stores.append(p.copy(gu_here.at[1], gu_full.at[1]).start())

    def up_rows(rows):
        wide_up = dot(rows_later[rows], gu_here[1], (1, 0))
        wide_gate = gate_wide[rows]
        hidden[rows] = (wide_gate * jax.nn.sigmoid(wide_gate) * wide_up).astype(hidden.dtype)
        gate_act[rows] = wide_gate.astype(gate_act.dtype)
        up_act[rows] = wide_up.astype(up_act.dtype)

    tiles(2 * count, 256, up_rows)
    down.relay()
    tiles(2 * count, 256, lambda rows: up_rows(shifted(rows, 2 * count)))
    stores.append(p.copy(hidden, hidden_out).start())
    stores.append(p.copy(gate_act, gate_out).start())
    stores.append(p.copy(up_act, up_out).start())
    down.finish()
    for weight in (*thirds, out, gate, up, down):
        weight.fetch_left()
    for sent in vector_sends:
        sent.left()
    scatter.finish()
    wait_all(stores)


def norm_back_rows(value, incoming, gain):
    average = jnp.mean(value, axis=-1, keepdims=True)
    centred = value - average
    inverse = lax.rsqrt(jnp.mean(centred * centred, axis=-1, keepdims=True) + EPSILON)
    unit = centred * inverse
    scaled = incoming * gain
    inner = (
        scaled
        - jnp.mean(scaled, axis=-1, keepdims=True)
        - unit * jnp.mean(scaled * unit, axis=-1, keepdims=True)
    )
    return inner * inverse, incoming * unit


def fold(array):
    return jnp.sum(array.reshape(array.shape[0] // 8, 8, array.shape[1]), axis=0)


def back_kernel(
    hidden_in, gate_in, up_in, cot_rows, rows_two, gu_full, down_full, middle, vectors,
    outputs, grad_middle, rows_branch, sums, down_owned, gate_sums, up_parts, down_parts,
    hidden, gate_act, up_act, cot, rows_here, gate, up, down, value, near, got, got_beside,
    got_out, got_out_beside, gain_sum, shift_sum, staging,
    down_got, down_last, down_home, down_result, gate_got, gate_last,
    send_sems, recv_sems, local_sems,
):
    p = Place(send_sems, recv_sems, local_sems)
    count, width = value.shape
    hidden_width = hidden.shape[1]
    quarter = width // 4
    first_loads = [p.copy(hidden_in, hidden).start(), p.copy(cot_rows, cot).start()]
    p.greet()
    down_sum = ScatterWeight(
        p, [down_parts.at[0], down_parts.at[1]], [staging.at[0], staging.at[1]], False,
        down_got, down_last, down_home, down_result,
    )
    gate_quarters = [gate.at[pl.ds(k * quarter, quarter)] for k in range(4)]
    gate_sum = ScatterWeight(
        p, gate_quarters[:2], gate_quarters[2:], True, gate_got, gate_last, None, None
    )
    far = cot.at[pl.ds(2 * count, 2 * count)]
    scatter = ScatterRows(p, far, near, got, got_beside)
    near_out = rows_here.at[pl.ds(0, 2 * count)]
    out_scatter = ScatterRows(p, far, near_out, got_out, got_out_beside)

    def down_part(k):
        columns = pl.ds(k * quarter, quarter)
        staging[k % 2] = dot(hidden[...], cot[:, columns], (0, 0)).astype(staging.dtype)

    wait_all(first_loads)
    second_loads = [
        p.copy(down_full, down).start(), p.copy(gate_in, gate_act).start(), p.copy(up_in, up_act).start(),
    ]
    down_part(0)
    store_even = p.copy(staging.at[0], down_parts.at[0]).start()
    down_part(1)
    store_odd = p.copy(staging.at[1], down_parts.at[1]).start()
    store_even.wait()
    down_sum.start_even()
    down_part(2)
    store_odd.wait()
    down_sum.start_odd()
    down_part(3)
    wait_all(second_loads)
    third_loads = [p.copy(gu_full.at[0], gate).start(), p.copy(gu_full.at[1], up).start()]

    def hidden_back(rows):
        grad = dot(cot[rows], down[...], (1, 1))
        gate_value = gate_act[rows].astype(jnp.float32)
        up_value = up_act[rows].astype(jnp.float32)
        sigmoid = jax.nn.sigmoid(gate_value)
        scaled = grad * sigmoid
        up_act[rows] = (scaled * gate_value).astype(up_act.dtype)
        gate_act[rows] = (
            scaled * up_value * (1.0 + gate_value * (1.0 - sigmoid))
        ).astype(gate_act.dtype)

    tiles(4 * count, 256, hidden_back)
    wait_all(third_loads)
    last_loads = [p.copy(rows_two, rows_here).start(), p.copy(middle, value).start()]

    def second_rows(target, offset):
        def part(rows):
            here = shifted(rows, offset)
            target[rows] = (
                dot(gate_act[here], gate[...], (1, 1)) + dot(up_act[here], up[...], (1, 1))
            ).astype(target.dtype)

        return part

    tiles(2 * count, 256, second_rows(far, 2 * count))
    scatter.start()
    tiles(2 * count, 256, second_rows(near, 0))
    scatter.relay()
    wait_all(last_loads)

    def weight_part(target, grads, k):
        here = pl.ds(k * quarter, quarter)
        target[here] = dot(rows_here[:, here], grads[...], (0, 0)).astype(target.dtype)

    weight_part(gate, gate_act, 0)
    weight_part(gate, gate_act, 1)
    down_sum.relay()
    gate_sum.start()
    weight_part(gate, gate_act, 2)
    weight_part(gate, gate_act, 3)

    def out_rows(target, offset):
        def part(rows):
            target[rows] = dot(hidden[shifted(rows, offset)], down[...], (1, 0)).astype(target.dtype)

        return part

    for k in range(4):
        weight_part(up, up_act, k)
    stores = [p.copy(up, up_parts).start()]
    scatter.sibling.left()
    tiles(2 * count, 256, out_rows(far, 2 * count))
    out_scatter.start()
    tiles(2 * count, 256, out_rows(near_out, 0))
    scatter.arrived()
    gain = vectors[2:3]
    gain_sum[...] = jnp.zeros_like(gain_sum)
    shift_sum[...] = jnp.zeros_like(shift_sum)

    def middle_back(rows):
        incoming = scatter.total(rows)
        back, product = norm_back_rows(value[rows], incoming, gain)
        gain_sum[...] += fold(product)
        shift_sum[...] += fold(incoming)
        grad = cot[rows].astype(jnp.float32) + back
        value[rows] = grad
        cot[rows] = grad.astype(cot.dtype)

    tiles(count, CHUNK, middle_back)
    gather = GatherRows(p, cot.at[pl.ds(0, count)], rows_branch).start()
    grad_store = p.copy(value, grad_middle).start()
    gain_sum[0:1] = jnp.sum(gain_sum[...], axis=0, keepdims=True)
    gain_sum[1:2] = jnp.sum(shift_sum[...], axis=0, keepdims=True)
    stores.append(p.copy(gain_sum, sums).start())
    scatter.beside.left()
    grad_store.wait()
    middle_load = p.copy(middle, value).start()
    down_sum.settle()
    gather.relay()
    out_scatter.relay()
    gate_sum.relay()
    middle_load.wait()
    out_scatter.arrived()
    own_out = near_out.at[pl.ds(0, count)]

    def out_total(rows):
        own_out[rows] = (value[rows] + out_scatter.total(rows)).astype(own_out.dtype)

    tiles(count, CHUNK, out_total)
    stores += store_natural(p, own_out, outputs)
    down_sum.finish(down_owned)
    gate_sum.gather()
    for k in (0, 1):
        stores.append(p.copy(gate_sum.half(gate_quarters[2 + k], 0), gate_sums.at[k]).start())
    gate_sum.left()
    down_sum.stored()
    gather.finish()
    out_scatter.finish()
    wait_all(stores)


def last_kernel(
    rows_branch, out_full, heads_in, mixed_in, rows_one, proj_full, inputs, vectors,
    cosine, sine_first, sine_latter, grad_middle, sums, up_parts, gate_sums,
    input_grads, proj_owned, out_owned, vector_grads, bias_grad, gu_owned,
    branch, out_here, heads, mixed, grad_mixed, grad_pre, rows_here, proj_here, out_send,
    own, got, got_beside, result, all_sums, shift_sum, vector_got, vector_total, z_got,
    bias_here, bias_got, gate_home, gate_even, up_result, out_result, third_result, *rest,
):
    weight_refs = [rest[4 * k : 4 * k + 4] for k in range(5)]
    p = Place(*rest[20:])
    count, width = own.shape
    quarter = width // 4
    late = lax.rem(p.tensor, 2)
    tables = (cosine, sine_first, sine_latter)
    first, second = p.core == 0, p.core == 1
    first_loads = [p.copy(rows_branch, branch).start(), p.copy(out_full, out_here).start()]
    p.greet()

    def weight_sum(send, rows, refs, total):
        keep, got_quarters, last, home = refs
        return ScatterWeight(
            p, send, [keep.at[0], keep.at[1]], rows, got_quarters, last, home, total
        )

    up_quarters = [up_parts.at[pl.ds(k * quarter, quarter)] for k in range(4)]
    up = weight_sum(up_quarters[:2], True, weight_refs[0], up_result).start()
    gate = HomeSum(p, gate_sums.at[0], gate_sums.at[1], gate_even, gate_home, up_result).start()
    out = weight_sum([out_send.at[0], out_send.at[1]], False, weight_refs[1], out_result)
    proj_send = [[heads.at[j, pl.ds(k * quarter, quarter)] for k in (0, 1)] for j in range(3)]
    thirds = [
        weight_sum(proj_send[j], True, weight_refs[2 + j], third_result.at[j]) for j in range(3)
    ]
    wait_all(first_loads)
    mixed_load = p.copy(mixed_in, mixed).start()
    head_load = p.copy(heads_in, heads).start()

    @pl.loop(0, 4)
    def _(index):
        rows = pl.ds(pl.multiple_of(index * HALF, HALF), HALF)
        _, target = swapped_half(index, late)
        grad_mixed[target] = dot(branch[rows], out_here[...], (1, 1)).astype(grad_mixed.dtype)

    mixed_load.wait()

    def out_part(k):
        target = out_send.at[k] if k < 2 else weight_refs[1][0].at[k - 2]
        target[...] = dot(
            mixed[...], branch[:, pl.ds(k * quarter, quarter)], (0, 0)
        ).astype(target.dtype)

    for k in range(4):
        out_part(k)
    head_load.wait()
    later_loads = [p.copy(proj_full, proj_here).start(), p.copy(rows_one, rows_here).start()]
    loads = load_local(p, inputs, own)
    loads.append(p.copy(grad_middle, result).start())
    gate_load = p.copy(gate_sums.at[0], gate_even).start()
    up.load(up_quarters[2:])
    attend_pair_back(heads, grad_mixed, grad_pre, tables, late)
    wait_all(later_loads)
    up.relay()
    near, far = branch.at[pl.ds(0, 2 * count)], branch.at[pl.ds(2 * count, 2 * count)]
    scatter = ScatterRows(p, far, near, got, got_beside)

    def term_rows(target, offset):
        def part(rows):
            here = shifted(rows, offset)
            total = dot(grad_pre[0, here], proj_here[0], (1, 1))
            for j in (1, 2):
                total = total + dot(grad_pre[j, here], proj_here[j], (1, 1))
            target[rows] = total.astype(target.dtype)

        return part

    def proj_part(j, k):
        target = proj_send[j][k] if k < 2 else weight_refs[2 + j][0].at[k - 2]
        target[...] = dot(
            rows_here[:, pl.ds(k * quarter, quarter)], grad_pre[j], (0, 0)
        ).astype(target.dtype)

    tiles(2 * count, 256, term_rows(far, 2 * count))
    scatter.start()
    tiles(2 * count, 256, term_rows(near, 0))
    scatter.relay()
    out.start()
    for j in range(3):
        proj_part(j, 0)
        proj_part(j, 1)
    up.settle()
    thirds[0].start()
    for j in range(3):
        proj_part(j, 2)
        proj_part(j, 3)
    out.relay()
    thirds[1].start()

    bias_here[...] = jnp.zeros_like(bias_here)
    for j in range(3):
        def bias_rows(rows):
            bias_here[j : j + 1] += jnp.sum(
                grad_pre[j, rows].astype(jnp.float32), axis=0, keepdims=True
            )

        tiles(4 * count, 256, bias_rows)
    bias_x = p.send(bias_here, bias_got.at[0], p.at(x=1)).start()
    bias_x.arrived()
    bias_x.left()
    bias_here[...] += bias_got[0]
    bias_y = p.send(bias_here, bias_got.at[1], p.at(y=1)).start()
    gate_load.wait()
    gate.finish(gu_owned.at[0])
    bias_y.arrived()
    bias_y.left()
    bias_here[...] += bias_got[1]
    near_sem, far_sem = p.take("recv"), p.take("recv")
    bias_home = [
        p.send(bias_here, bias_got.at[2], p.at(core=1), near_sem, first).start(),
        p.send(bias_here, bias_got.at[2], p.at(core=1, far=1), near_sem, second).start(),
        p.send(bias_here, bias_got.at[3], p.at(far=1), far_sem, second).start(),
    ]
    thirds[0].relay()
    thirds[2].start()
    out.settle()
    wait_all(loads)
    scatter.arrived()
    gain = vectors[0:1]
    all_sums[...] = jnp.zeros_like(all_sums)
    shift_sum[...] = jnp.zeros_like(shift_sum)

    def first_back(rows):
        incoming = scatter.total(rows)
        back, product = norm_back_rows(own[rows].astype(jnp.float32), incoming, gain)
        all_sums[...] += fold(product)
        shift_sum[...] += fold(incoming)
        result[rows] = result[rows] + back

    tiles(count, CHUNK, first_back)
    stores = store_natural(p, result, input_grads)
    all_sums[0:1] = jnp.sum(all_sums[...], axis=0, keepdims=True)
    all_sums[1:2] = jnp.sum(shift_sum[...], axis=0, keepdims=True)
    all_sums[2:4] = sums[0:2]
    slots = {key: j for j, key in enumerate(ORDER)}
    vector_sends = []
    for dy in (0, 1):
        for dx in (0, 1):
            for core in (0, 1):
                if not (dy or dx or core):
                    continue
                straight, crossed = slots[(dy, dx, core)], slots[(dy, dx, 1 - core)]
                slot = straight + p.core * (crossed - straight)
                columns = pl.ds(pl.multiple_of(slot * EIGHTH, EIGHTH), EIGHTH)
                vector_sends.append(
                    p.send(
                        all_sums.at[:, columns], vector_got.at[len(vector_sends)],
                        p.at(x=dx, y=dy, core=core),
                    ).start()
                )
    thirds[1].relay()
    thirds[0].settle()
    own_slot = slots[(0, 0, 0)] + p.core * (slots[(0, 0, 1)] - slots[(0, 0, 0)])
    total = all_sums[:, pl.ds(pl.multiple_of(own_slot * EIGHTH, EIGHTH), EIGHTH)]
    for k, sent in enumerate(vector_sends):
        sent.arrived()
        total = total + vector_got[k]
    vector_total[0] = total
    z_near = p.send(vector_total.at[0], z_got.at[0], p.at(near=1)).start()
    thirds[2].relay()
    thirds[1].settle()
    z_near.arrived()
    vector_total[1] = vector_total[0] + z_got[0]
    z_far = p.send(vector_total.at[1], z_got.at[1], p.at(far=1)).start()
    thirds[2].settle()
    z_far.arrived()
    z_near.left()
    z_far.left()
    vector_total[0] = vector_total[1] + z_got[1]
    vector_store = p.copy(vector_total.at[0], vector_grads).start()
    bias_home[0].arrived()
    bias_home[2].arrived(second)
    for sent in bias_home:
        sent.left()
    pl.when(second)(lambda: combine(bias_got.at[2], [bias_got.at[2], bias_got.at[3]], 8))
    pl.when(first)(lambda: combine(bias_got.at[2], [bias_got.at[2], bias_here], 8))
    bias_store = p.copy(bias_got.at[2], bias_grad).start()
    gate.stored()
    up.finish(gu_owned.at[1])
    out.finish(out_owned)
    for j in range(3):
        thirds[j].finish(proj_owned.at[j])
    for weight in (up, out, *thirds):
        weight.stored()
    scatter.finish()
    for sent in vector_sends:
        sent.left()
    wait_all(stores)
    vector_store.wait()
    bias_store.wait()


def call(body, name, collective, inputs, in_specs, outs, scratch, counts):
    bf16_bytes = sum(math.prod(o.shape) * o.dtype.itemsize for o in outs)
    return pl.pallas_call(
        body,
        out_shape=outs,
        in_specs=in_specs,
        out_specs=[ANY] * len(outs),
        scratch_shapes=[
            *scratch,
            pltpu.SemaphoreType.DMA((counts[0],)),
            pltpu.SemaphoreType.DMA((counts[1],)),
            pltpu.SemaphoreType.DMA((counts[2],)),
        ],
        compiler_params=pltpu.CompilerParams(
            collective_id=collective, has_side_effects=True, vmem_limit_bytes=VMEM_BYTES
        ),
        cost_estimate=pl.CostEstimate(
            flops=0, bytes_accessed=2 * bf16_bytes, transcendentals=0
        ),
        name=name,
    )(*inputs)


def bf16(*shape):
    return jax.ShapeDtypeStruct(shape, jnp.bfloat16)


def f32(*shape):
    return jax.ShapeDtypeStruct(shape, jnp.float32)


def held(shape_struct):
    return pltpu.VMEM(shape_struct.shape, shape_struct.dtype)


def weight_scratch(quarter, eighth):
    return [
        held(bf16(2, *quarter)), held(bf16(2, *quarter)), held(bf16(2, *eighth)),
        held(bf16(2, *eighth)),
    ]


WHOLE = pl.BlockSpec(memory_space=pltpu.VMEM)
EIGHTH = 256


def local_pairs(
    inputs,
    gain_first,
    shift_first,
    projections,
    biases,
    output_weight,
    gain_second,
    shift_second,
    gate_up,
    down_weight,
    cotangent,
):
    count, width = inputs.shape
    rows = 4 * count
    heads_width = output_weight.shape[0]
    hidden_width = down_weight.shape[0]
    cosine, sine = angle_tables()
    rest = ((0, 0), (0, HD - ROTARY))
    cosine_table, sine_first, sine_latter = (
        jnp.tile(jnp.pad(table, rest, constant_values=fill), (1, 128 // HD))
        for table, fill in (
            (jnp.concatenate([cosine, cosine], axis=1), 1.0),
            (jnp.concatenate([-sine, jnp.zeros_like(sine)], axis=1), 0.0),
            (jnp.concatenate([jnp.zeros_like(sine), sine], axis=1), 0.0),
        )
    )
    vectors = jnp.pad(
        jnp.stack([gain_first, shift_first, gain_second, shift_second]).astype(jnp.float32),
        ((0, 4), (0, 0)),
    )
    wide_biases = jnp.pad(biases.astype(jnp.float32), ((0, 5), (0, 0)))
    wide = bf16(rows, width)
    inner = bf16(rows, hidden_width)
    own = bf16(count, width)
    half_rows = bf16(2 * count, width)
    (
        proj_full, out_full, gu_full, down_full, vectors, gathered_one, gathered_cot, heads, mixed_rows,
        middle, gathered_two, hidden, gate_act, up_act,
    ) = call(
        forward_kernel, "forward", 1,
        (
            inputs, cotangent, vectors, wide_biases, cosine_table, sine_first, sine_latter,
            projections, output_weight, gate_up, down_weight,
        ),
        [ANY] * 4 + [WHOLE] * 3 + [ANY] * 4,
        [
            bf16(3, width, heads_width), bf16(heads_width, width), bf16(2, width, hidden_width),
            bf16(hidden_width, width), f32(8, width), wide, wide, bf16(3, rows, heads_width),
            bf16(rows, heads_width), f32(count, width), wide, inner, inner, inner,
        ],
        [
            held(own), held(own), held(own), held(f32(8, width)), held(f32(8, heads_width)),
            held(bf16(3, width, heads_width)), held(bf16(heads_width, width)), held(wide),
            held(bf16(3, rows, heads_width)), held(bf16(rows, heads_width)),
            held(half_rows), held(half_rows), held(half_rows), held(own), held(f32(count, width)),
            held(wide), held(bf16(2, width, hidden_width)), held(f32(rows, hidden_width)),
            held(inner), held(inner), held(inner),
        ],
        (96, 96, 64),
    )

    by_rows = ((2 * EIGHTH, hidden_width), (EIGHTH, hidden_width))
    by_columns = ((hidden_width, 2 * EIGHTH), (hidden_width, EIGHTH))
    (
        outputs, grad_middle, gathered_branch, sums, down_owned, gate_sums, up_parts, _,
    ) = call(
        back_kernel, "backward_first", 2,
        (
            hidden, gate_act, up_act, gathered_cot, gathered_two, gu_full, down_full, middle, vectors,
        ),
        [ANY] * 8 + [WHOLE],
        [
            own, f32(count, width), wide, f32(8, width), f32(hidden_width, EIGHTH),
            bf16(2, EIGHTH, hidden_width), bf16(width, hidden_width),
            bf16(2, hidden_width, 2 * EIGHTH),
        ],
        [
            held(inner), held(inner), held(inner), held(wide), held(wide),
            held(bf16(width, hidden_width)), held(bf16(width, hidden_width)),
            held(bf16(hidden_width, width)), held(f32(count, width)),
            held(half_rows), held(half_rows), held(own), held(half_rows), held(own),
            held(f32(8, width)), held(f32(8, width)), held(bf16(2, hidden_width, 2 * EIGHTH)),
            *weight_scratch(*by_columns)[1:], held(f32(hidden_width, EIGHTH)),
            *weight_scratch(*by_rows)[1:3],
        ],
        (64, 64, 48),
    )
    third = ((2 * EIGHTH, heads_width), (EIGHTH, heads_width))
    input_grads, proj_owned, out_owned, vector_grads, bias_grad, gu_owned = call(
        last_kernel, "backward_last", 3,
        (
            gathered_branch, out_full, heads, mixed_rows, gathered_one, proj_full, inputs, vectors,
            cosine_table, sine_first, sine_latter, grad_middle, sums, up_parts, gate_sums,
        ),
        [ANY] * 7 + [WHOLE] * 4 + [ANY, WHOLE, ANY, ANY],
        [
            f32(count, width), f32(3, EIGHTH, heads_width), f32(heads_width, EIGHTH),
            f32(8, EIGHTH), f32(8, heads_width), f32(2, EIGHTH, hidden_width),
        ],
        [
            held(wide), held(bf16(heads_width, width)), held(bf16(3, rows, heads_width)),
            held(bf16(rows, heads_width)), held(bf16(rows, heads_width)),
            held(bf16(3, rows, heads_width)), held(wide), held(bf16(3, width, heads_width)),
            held(bf16(2, heads_width, 2 * EIGHTH)),
            held(own), held(half_rows), held(own), held(f32(count, width)),
            held(f32(8, width)), held(f32(8, width)),
            held(f32(7, 8, EIGHTH)), held(f32(2, 8, EIGHTH)), held(f32(2, 8, EIGHTH)),
            held(f32(8, heads_width)), held(f32(4, 8, heads_width)),
            held(bf16(2, EIGHTH, hidden_width)), held(bf16(EIGHTH, hidden_width)),
            held(f32(EIGHTH, hidden_width)), held(f32(heads_width, EIGHTH)),
            held(f32(3, EIGHTH, heads_width)),
            *weight_scratch(*by_rows),
            *weight_scratch((heads_width, 2 * EIGHTH), (heads_width, EIGHTH)),
            *weight_scratch(*third), *weight_scratch(*third), *weight_scratch(*third),
        ],
        (64, 64, 48),
    )
    return (
        outputs,
        input_grads,
        vector_grads[0],
        vector_grads[1],
        proj_owned,
        bias_grad[:3],
        out_owned,
        vector_grads[2],
        vector_grads[3],
        gu_owned,
        down_owned,
    )


def solution(mesh):
    whole_pairs = dict(mesh.shape) == {"dp": 8, "tensor": 4}
    return jax.shard_map(
        local_pairs if whole_pairs else local,
        mesh=mesh,
        in_specs=(
            P(("dp", "tensor"), None),
            P("dp"),
            P("dp"),
            P(None, "dp", "tensor"),
            P(None, "tensor"),
            P("tensor", "dp"),
            P("dp"),
            P("dp"),
            P(None, "dp", "tensor"),
            P("tensor", "dp"),
            P(("dp", "tensor"), None),
        ),
        out_specs=(
            P(("dp", "tensor"), None),
            P(("dp", "tensor"), None),
            P("dp"),
            P("dp"),
            P(None, "dp", "tensor"),
            P(None, "tensor"),
            P("tensor", "dp"),
            P("dp"),
            P("dp"),
            P(None, "dp", "tensor"),
            P("tensor", "dp"),
        ),
        check_vma=False,
    )
```

```python
import math

import jax
import jax.numpy as jnp
from jax import lax
from jax.experimental import pallas as pl
from jax.experimental.pallas import tpu as pltpu
from jax.sharding import PartitionSpec as P

HD = 64
ROTARY = 16
SEQ_LEN = 512


EPSILON = 1e-05
ANGLE_BASE = 10000.0
NEGATIVE = -1e30


def norm_rows(rows, gain, shift):
    average = jnp.mean(rows, axis=-1, keepdims=True)
    centred = rows - average
    inverse = lax.rsqrt(jnp.mean(centred * centred, axis=-1, keepdims=True) + EPSILON)
    unit_rows = centred * inverse
    return (unit_rows * gain + shift, unit_rows, inverse)


def norm_back(incoming, unit_rows, inverse, gain):
    scaled = incoming * gain
    inner = (
        scaled
        - jnp.mean(scaled, axis=-1, keepdims=True)
        - unit_rows * jnp.mean(scaled * unit_rows, axis=-1, keepdims=True)
    )
    return (inner * inverse, jnp.sum(incoming * unit_rows, axis=0), jnp.sum(incoming, axis=0))


def angle_tables():
    freqs = 1.0 / ANGLE_BASE ** (jnp.arange(0, ROTARY, 2).astype(jnp.float32) / ROTARY)
    angles = jnp.arange(SEQ_LEN).astype(jnp.float32)[:, None] * freqs[None, :]
    return (jnp.cos(angles), jnp.sin(angles))


def rotate(heads, cosine, sine, sign):
    half_rot = ROTARY // 2
    first = heads[..., :half_rot]
    latter = heads[..., half_rot:ROTARY]
    cos_part = cosine[:, None, :]
    sin_part = sine[:, None, :] * sign
    return jnp.concatenate(
        [
            first * cos_part - latter * sin_part,
            latter * cos_part + first * sin_part,
            heads[..., ROTARY:],
        ],
        axis=-1,
    )


def causal_scores(queries, key_rows, positions):
    scaling = 1.0 / math.sqrt(HD)
    scores = scaling * jnp.einsum(
        "qhd,khd->hqk", queries, key_rows, preferred_element_type=jnp.float32
    )
    causal = positions[:, None] >= positions[None, :]
    return jnp.where(causal[None], scores, NEGATIVE)


def attend_forward(pieces, positions):
    queries, key_rows, value_rows = pieces
    scores = causal_scores(queries, key_rows, positions)
    row_top = jnp.max(scores, axis=-1, keepdims=True)
    exponent = jnp.exp(scores - row_top)
    totals = jnp.sum(exponent, axis=-1, keepdims=True)
    weights = (exponent / totals).astype(jnp.bfloat16)
    mixed = jnp.einsum("hqk,khd->qhd", weights, value_rows, preferred_element_type=jnp.float32)
    return (mixed.astype(jnp.bfloat16), (row_top + jnp.log(totals))[..., 0])


def attend_back(pieces, positions):
    queries, key_rows, value_rows, grad_mixed, log_totals = pieces
    scaling = 1.0 / math.sqrt(HD)
    scores = causal_scores(queries, key_rows, positions)
    weights = jnp.exp(scores - log_totals[..., None])
    grad_values = jnp.einsum(
        "hqk,qhd->khd", weights.astype(jnp.bfloat16), grad_mixed, preferred_element_type=jnp.float32
    )
    grad_weights = jnp.einsum(
        "qhd,khd->hqk", grad_mixed, value_rows, preferred_element_type=jnp.float32
    )
    grad_scores = weights * (grad_weights - jnp.sum(weights * grad_weights, axis=-1, keepdims=True))
    grad_scores = grad_scores.astype(jnp.bfloat16)
    grad_queries = scaling * jnp.einsum(
        "hqk,khd->qhd", grad_scores, key_rows, preferred_element_type=jnp.float32
    )
    grad_keys = scaling * jnp.einsum(
        "hqk,qhd->khd", grad_scores, queries, preferred_element_type=jnp.float32
    )
    return (grad_queries, grad_keys, grad_values)


def scatter_sum(terms, axis, dimension):
    owned = lax.psum_scatter(
        terms.astype(jnp.bfloat16), axis, scatter_dimension=dimension, tiled=True
    )
    return owned.astype(jnp.float32)


def local(
    inputs,
    gain_first,
    shift_first,
    projections,
    biases,
    output_weight,
    gain_second,
    shift_second,
    gate_up,
    down_weight,
    cotangent,
):
    tensor_ways = lax.axis_size("tensor")
    row_count = inputs.shape[0]
    group_rows = row_count * tensor_ways
    sequences = group_rows // SEQ_LEN
    head_width = output_weight.shape[0]
    local_heads = head_width // HD
    head_shape = (sequences, SEQ_LEN, local_heads, HD)
    cosine, sine = angle_tables()
    positions = jnp.arange(SEQ_LEN)
    proj_full, out_full, gain_one, shift_one = (
        lax.all_gather(projections, "dp", axis=1, tiled=True),
        lax.all_gather(output_weight, "dp", axis=1, tiled=True),
        lax.all_gather(gain_first, "dp", axis=0, tiled=True),
        lax.all_gather(shift_first, "dp", axis=0, tiled=True),
    )
    gain_one = gain_one.astype(jnp.float32)
    residual = inputs.astype(jnp.float32)
    normed_one, unit_one, inverse_one = norm_rows(residual, gain_one, shift_one.astype(jnp.float32))
    gathered_one = lax.all_gather(normed_one.astype(jnp.bfloat16), "tensor", axis=0, tiled=True)
    pre_all = jnp.einsum("gd,jde->jge", gathered_one, proj_full, preferred_element_type=jnp.float32)
    pre_all = pre_all + biases.astype(jnp.float32)[:, None, :]
    queries = rotate(pre_all[0].reshape(head_shape), cosine, sine, 1.0).astype(jnp.bfloat16)
    key_rows = rotate(pre_all[1].reshape(head_shape), cosine, sine, 1.0).astype(jnp.bfloat16)
    value_rows = pre_all[2].reshape(head_shape).astype(jnp.bfloat16)
    mixed, log_totals = lax.map(
        lambda pieces: attend_forward(pieces, positions), (queries, key_rows, value_rows)
    )
    mixed_rows = mixed.reshape(group_rows, head_width)
    part = mixed_rows
    middle = residual + scatter_sum(
        jnp.dot(part, out_full, preferred_element_type=jnp.float32), "tensor", 0
    )
    gu_full, down_full, gain_two, shift_two = (
        lax.all_gather(gate_up, "dp", axis=1, tiled=True),
        lax.all_gather(down_weight, "dp", axis=1, tiled=True),
        lax.all_gather(gain_second, "dp", axis=0, tiled=True),
        lax.all_gather(shift_second, "dp", axis=0, tiled=True),
    )
    gain_two = gain_two.astype(jnp.float32)
    normed_two, unit_two, inverse_two = norm_rows(middle, gain_two, shift_two.astype(jnp.float32))
    gathered_two = lax.all_gather(normed_two.astype(jnp.bfloat16), "tensor", axis=0, tiled=True)
    gate_act = jnp.dot(gathered_two, gu_full[0], preferred_element_type=jnp.float32)
    up_act = jnp.dot(gathered_two, gu_full[1], preferred_element_type=jnp.float32)
    sigmoid_gate = jax.nn.sigmoid(gate_act)
    hidden = (gate_act * sigmoid_gate * up_act).astype(jnp.bfloat16)
    part = hidden
    outputs = (
        middle
        + scatter_sum(jnp.dot(part, down_full, preferred_element_type=jnp.float32), "tensor", 0)
    ).astype(jnp.bfloat16)
    gu_back, down_back, gain_two_back = (
        lax.all_gather(gate_up, "dp", axis=1, tiled=True),
        lax.all_gather(down_weight, "dp", axis=1, tiled=True),
        lax.all_gather(gain_second, "dp", axis=0, tiled=True),
    )
    gain_two_back = gain_two_back.astype(jnp.float32)
    gathered_cot = lax.all_gather(cotangent, "tensor", axis=0, tiled=True)
    grad_hidden = jnp.einsum(
        "gd,fd->gf", gathered_cot, down_back, preferred_element_type=jnp.float32
    )
    down_grad = jnp.einsum("gf,gd->fd", hidden, gathered_cot, preferred_element_type=jnp.float32)
    grad_up = (grad_hidden * gate_act * sigmoid_gate).astype(jnp.bfloat16)
    grad_gate = (
        grad_hidden * up_act * sigmoid_gate * (1.0 + gate_act * (1.0 - sigmoid_gate))
    ).astype(jnp.bfloat16)
    gu_grad = jnp.stack(
        [
            jnp.einsum("gd,gf->df", gathered_two, grad_gate, preferred_element_type=jnp.float32),
            jnp.einsum("gd,gf->df", gathered_two, grad_up, preferred_element_type=jnp.float32),
        ]
    )
    first_term = jnp.einsum("gf,df->gd", grad_gate, gu_back[0], preferred_element_type=jnp.float32)
    grad_second = scatter_sum(
        first_term
        + jnp.einsum("gf,df->gd", grad_up, gu_back[1], preferred_element_type=jnp.float32),
        "tensor",
        0,
    )
    gu_owned, down_owned = (
        scatter_sum(gu_grad, "dp", 1),
        scatter_sum(down_grad, "dp", 1),
    )
    grad_mid_norm, gain_two_part, shift_two_part = norm_back(
        grad_second, unit_two, inverse_two, gain_two_back
    )
    grad_middle = cotangent.astype(jnp.float32) + grad_mid_norm
    proj_back, out_back, gain_one_back = (
        lax.all_gather(projections, "dp", axis=1, tiled=True),
        lax.all_gather(output_weight, "dp", axis=1, tiled=True),
        lax.all_gather(gain_first, "dp", axis=0, tiled=True),
    )
    gain_one_back = gain_one_back.astype(jnp.float32)
    gathered_branch = lax.all_gather(grad_middle.astype(jnp.bfloat16), "tensor", axis=0, tiled=True)
    out_grad = jnp.einsum(
        "ge,gd->ed", mixed_rows, gathered_branch, preferred_element_type=jnp.float32
    )
    grad_mixed = jnp.einsum(
        "gd,ed->ge", gathered_branch, out_back, preferred_element_type=jnp.float32
    ).astype(jnp.bfloat16)
    grad_queries, grad_keys, grad_values = lax.map(
        lambda pieces: attend_back(pieces, positions),
        (queries, key_rows, value_rows, grad_mixed.reshape(head_shape), log_totals),
    )
    grad_queries = rotate(grad_queries, cosine, sine, -1.0)
    grad_keys = rotate(grad_keys, cosine, sine, -1.0)
    grad_pre = (
        jnp.stack([grad_queries, grad_keys, grad_values])
        .reshape(3, group_rows, head_width)
        .astype(jnp.bfloat16)
    )
    bias_part = jnp.sum(grad_pre, axis=1, dtype=jnp.float32)
    proj_grad = jnp.einsum(
        "gd,jge->jde", gathered_one, grad_pre, preferred_element_type=jnp.float32
    )
    part = grad_pre
    grad_normed = scatter_sum(
        jnp.einsum("jge,jde->gd", part, proj_back, preferred_element_type=jnp.float32),
        "tensor",
        0,
    )
    proj_owned, out_owned = (
        scatter_sum(proj_grad, "dp", 1),
        scatter_sum(out_grad, "dp", 1),
    )
    grad_in_norm, gain_one_part, shift_one_part = norm_back(
        grad_normed, unit_one, inverse_one, gain_one_back
    )
    input_grads = grad_middle + grad_in_norm
    one_hot = (jnp.arange(tensor_ways) == lax.axis_index("tensor")).astype(jnp.float32)
    spread_bias = (bias_part[:, None, :] * one_hot[None, :, None]).reshape(
        3, tensor_ways * head_width
    )
    summed = lax.psum(
        (gain_one_part, shift_one_part, gain_two_part, shift_two_part, spread_bias),
        ("dp", "tensor"),
    )
    own_width = gain_first.shape[0]
    own_offset = lax.axis_index("dp") * own_width

    def own_part(vector):
        return lax.dynamic_slice_in_dim(vector, own_offset, own_width, 0)

    bias_grad = jnp.sum(
        summed[4].reshape(3, tensor_ways, head_width) * one_hot[None, :, None], axis=1
    )
    return (
        outputs,
        input_grads,
        own_part(summed[0]),
        own_part(summed[1]),
        proj_owned,
        bias_grad,
        out_owned,
        own_part(summed[2]),
        own_part(summed[3]),
        gu_owned,
        down_owned,
    )


ORDER = ((1, 0, 0), (1, 1, 0), (0, 1, 1), (1, 1, 1), (0, 0, 0), (0, 1, 0), (0, 0, 1), (1, 0, 1))
EVEN_Y, EVEN_XY, ODD_X, ODD_XY, EVEN, EVEN_X, ODD, ODD_Y = range(8)
ANY = pl.BlockSpec(memory_space=pl.ANY)
VMEM_BYTES = 63 * 1024 * 1024


class Place:
    def __init__(self, send_sems, recv_sems, local_sems):
        self.dp, self.tensor = lax.axis_index("dp"), lax.axis_index("tensor")
        self.core = lax.rem(self.dp, 2)
        self.x = lax.rem(self.dp // 2, 2)
        self.y = self.dp // 4
        self.pools = {"send": send_sems, "recv": recv_sems, "local": local_sems}
        self.used = {"send": 0, "recv": 0, "local": 0}

    def take(self, kind):
        self.used[kind] += 1
        return self.pools[kind].at[self.used[kind] - 1]

    def at(self, x=0, y=0, core=0, near=0, far=0):
        dp = self.dp
        dp = dp + x * (2 - 4 * self.x) + y * (4 - 8 * self.y) + core * (1 - 2 * self.core)
        tensor = self.tensor
        tensor = tensor + near * (1 - 2 * lax.rem(tensor, 2)) + far * (3 - 2 * tensor)
        return (dp, tensor)

    def column(self, key):
        dy, dx, core = key
        y = self.y + dy * (1 - 2 * self.y)
        x = self.x + dx * (1 - 2 * self.x)
        return pl.multiple_of((y * 4 + x * 2 + core) * EIGHTH, EIGHTH)

    def greet(self):
        barrier = pltpu.get_barrier_semaphore()
        partners = [
            self.at(x=x, y=y, core=core)
            for x in (0, 1)
            for y in (0, 1)
            for core in (0, 1)
            if x or y or core
        ] + [self.at(near=1), self.at(far=1), self.at(far=1, core=1)]
        for partner in partners:
            pl.semaphore_signal(
                barrier, inc=1, device_id=partner, device_id_type=pl.DeviceIdType.MESH
            )
        pl.semaphore_wait(barrier, len(partners))

    def send(self, source, target, device, recv_sem=None, when=None):
        return Sent(
            pltpu.make_async_remote_copy(
                src_ref=source,
                dst_ref=target,
                send_sem=self.take("send"),
                recv_sem=self.take("recv") if recv_sem is None else recv_sem,
                device_id=device,
                device_id_type=pl.DeviceIdType.MESH,
            ),
            when,
        )

    def copy(self, source, target, when=None):
        return Copied(pltpu.make_async_copy(source, target, self.take("local")), when)


def guarded(when, action):
    if when is None:
        action()
    else:
        pl.when(when)(action)


class Sent:
    def __init__(self, copy, when):
        self.copy, self.when = copy, when

    def start(self):
        guarded(self.when, self.copy.start)
        return self

    def arrived(self, when=None):
        guarded(when, self.copy.wait_recv)

    def left(self):
        guarded(self.when, self.copy.wait_send)


class Copied:
    def __init__(self, copy, when):
        self.copy, self.when = copy, when

    def start(self):
        guarded(self.when, self.copy.start)
        return self

    def wait(self):
        guarded(self.when, self.copy.wait)


class GatherWeight:
    def __init__(self, place, shard, block):
        self.place, self.shard, self.block = place, shard, block
        self.spreads, self.arrivals = [], {}

    def fetch(self):
        p = self.place
        even, odd = self.block(EVEN), self.block(ODD)
        first, second = p.core == 0, p.core == 1
        self.own = p.copy(self.shard, even, first).start()
        even_sem, odd_sem = p.take("recv"), p.take("recv")
        self.to_far_even = p.send(self.shard, even, p.at(core=1, far=1), even_sem, first).start()
        self.to_sibling = p.send(self.shard, odd, p.at(core=1), odd_sem, second).start()
        self.to_far_odd = p.send(self.shard, odd, p.at(far=1), odd_sem, second).start()
        return self

    def spread(self, core):
        p, block = self.place, self.block
        here = p.core == core
        if core:
            self.to_far_even.arrived(here)
        self.to_sibling.arrived(here)
        even = block(EVEN) if core else self.shard
        routes = (
            (even, EVEN_X, p.at(x=1)), (block(ODD), ODD_Y, p.at(y=1)),
            (block(ODD), ODD_X, p.at(x=1)), (even, EVEN_Y, p.at(y=1)),
        )
        for source, target, device in routes:
            if target not in self.arrivals:
                self.arrivals[target] = p.take("recv")
            self.spreads.append(
                p.send(source, block(target), device, self.arrivals[target], here).start()
            )
        return self

    def relay(self):
        p, block = self.place, self.block
        even_x, odd_y, self.odd_x, self.even_y = self.spreads[:4]
        even_x.arrived()
        self.even_xy = p.send(block(EVEN_X), block(EVEN_XY), p.at(y=1)).start()
        odd_y.arrived()
        self.odd_xy = p.send(block(ODD_Y), block(ODD_XY), p.at(x=1)).start()
        return self

    def finish(self):
        self.own.wait()
        for copy in (self.odd_x, self.even_y, self.even_xy, self.odd_xy):
            copy.arrived()

    def left(self):
        for copy in (
            *self.spreads, self.even_xy, self.odd_xy,
            self.to_far_even, self.to_sibling, self.to_far_odd,
        ):
            copy.left()


class GatherRows:
    def __init__(self, place, own, rows):
        self.place, self.own, self.rows = place, own, rows
        self.count = own.shape[0]

    def slot(self, k):
        return self.rows.at[pl.ds(k * self.count, self.count)]

    def start(self):
        p = self.place
        self.beside = p.send(self.own, self.slot(1), p.at(near=1)).start()
        self.sibling = p.send(self.own, self.slot(2), p.at(core=1)).start()
        self.here = p.copy(self.own, self.slot(0)).start()
        return self

    def relay(self):
        p = self.place
        self.beside.arrived()
        self.across = p.send(self.slot(1), self.slot(3), p.at(core=1)).start()
        return self

    def finish(self):
        self.sibling.arrived()
        self.across.arrived()
        self.here.wait()
        for copy in (self.beside, self.sibling, self.across):
            copy.left()


def combine(target, terms, chunk):
    @pl.loop(0, target.shape[0] // chunk)
    def _(i):
        rows = pl.ds(pl.multiple_of(i * chunk, chunk), chunk)
        total = terms[0][rows].astype(jnp.float32)
        for term in terms[1:]:
            total = total + term[rows].astype(jnp.float32)
        target[rows] = total.astype(target.dtype)


class ScatterRows:
    def __init__(self, place, far, near, got, got_beside):
        self.place, self.far, self.near = place, far, near
        self.got, self.got_beside = got, got_beside
        self.count = near.shape[0] // 2

    def start(self):
        self.sibling = self.place.send(self.far, self.got, self.place.at(core=1)).start()
        return self

    def relay(self):
        p, n = self.place, self.count
        self.sibling.arrived()
        late = pl.ds(n, n)
        combine(self.near.at[late], [self.near.at[late], self.got.at[late]], 32)
        self.beside = p.send(self.near.at[late], self.got_beside, p.at(near=1)).start()
        return self

    def total(self, rows):
        return (
            self.near[rows].astype(jnp.float32)
            + self.got[rows].astype(jnp.float32)
            + self.got_beside[rows].astype(jnp.float32)
        )

    def arrived(self):
        self.beside.arrived()

    def finish(self):
        self.sibling.left()
        self.beside.left()


class ScatterWeight:
    def __init__(self, place, send, keep, rows, got, last, home, result):
        self.place, self.parts, self.keep, self.rows = place, send, keep, rows
        self.got, self.last, self.home, self.result = got, last, home, result
        self.loads = []

    def half(self, ref, k):
        if self.rows:
            size = ref.shape[0] // 2
            return ref.at[pl.ds(k * size, size)]
        size = ref.shape[1] // 2
        return ref.at[:, pl.ds(k * size, size)]

    def load(self, sources):
        self.loads = [self.place.copy(a, b).start() for a, b in zip(sources, self.keep)]
        return self

    def start_even(self):
        p = self.place
        self.even = p.send(self.parts[0], self.got.at[0], p.at(y=1)).start()
        return self

    def start_odd(self):
        p = self.place
        self.odd = p.send(self.parts[1], self.got.at[1], p.at(x=1)).start()
        return self

    def start(self):
        return self.start_even().start_odd()

    def relay(self):
        p = self.place
        wait_all(self.loads)
        self.second = []
        for k, arrival in enumerate((self.even, self.odd)):
            arrival.arrived()
            there = self.half(self.keep[k], 1)
            combine(there, [there, self.half(self.got.at[k], 1)], 64)
            device = p.at(x=1) if k == 0 else p.at(y=1)
            self.second.append(p.send(there, self.last.at[k], device).start())
        return self

    def gather(self):
        for k in (1, 0):
            self.second[k].arrived()
            here = self.half(self.keep[k], 0)
            combine(here, [here, self.half(self.got.at[k], 0), self.last.at[k]], 64)
        return self

    def settle(self):
        self.gather()
        even, odd = self.half(self.keep[0], 0), self.half(self.keep[1], 0)
        self.way_home = HomeSum(self.place, even, odd, even, self.home, self.result).start()
        return self

    def finish(self, output):
        self.way_home.finish(output)
        self.left()

    def left(self):
        for copy in (self.even, self.odd, *self.second):
            copy.left()

    def stored(self):
        self.way_home.stored()


class HomeSum:
    def __init__(self, place, even, odd, here, home, result):
        self.place, self.even, self.odd, self.here = place, even, odd, here
        self.home, self.result = home, result

    def start(self):
        p = self.place
        first, second = p.core == 0, p.core == 1
        near_sem, far_sem = p.take("recv"), p.take("recv")
        home = self.home
        self.to_sibling = p.send(self.odd, home.at[0], p.at(core=1), near_sem, first).start()
        self.to_first = p.send(self.even, home.at[0], p.at(core=1, far=1), near_sem, second).start()
        self.to_far = p.send(self.odd, home.at[1], p.at(far=1), far_sem, second).start()
        return self

    def finish(self, output):
        p, home = self.place, self.home
        first, second = p.core == 0, p.core == 1
        self.to_sibling.arrived()
        self.to_far.arrived(second)
        pl.when(first)(lambda: combine(self.result, [self.here, home.at[0]], 64))
        pl.when(second)(lambda: combine(self.result, [home.at[0], home.at[1]], 64))
        self.store = p.copy(self.result, output).start()
        for copy in (self.to_sibling, self.to_first, self.to_far):
            copy.left()

    def stored(self):
        self.store.wait()


def load_local(place, source, target):
    return [
        place.copy(
            source.at[:, pl.ds(place.column(key), EIGHTH)], target.at[:, pl.ds(j * EIGHTH, EIGHTH)]
        ).start()
        for j, key in enumerate(ORDER)
    ]


def store_natural(place, source, target):
    return [
        place.copy(
            source.at[:, pl.ds(j * EIGHTH, EIGHTH)], target.at[:, pl.ds(place.column(key), EIGHTH)]
        ).start()
        for j, key in enumerate(ORDER)
    ]


def wait_all(copies):
    for copy in copies:
        copy.wait()


CHUNK = 32


def norm_into(count, rows_of, gain, shift, target):
    @pl.loop(0, count // CHUNK)
    def _(i):
        rows = pl.ds(pl.multiple_of(i * CHUNK, CHUNK), CHUNK)
        target[rows] = norm_rows(rows_of(rows), gain, shift)[0].astype(target.dtype)


def tiles(count, tile, body):
    @pl.loop(0, count // tile)
    def _(i):
        body(pl.ds(pl.multiple_of(i * tile, tile), tile))


def shifted(rows, offset):
    return pl.ds(pl.multiple_of(rows.start + offset, 256), rows.size)


def dot(left, right, contract):
    return lax.dot_general(
        left, right, (((contract[0],), (contract[1],)), ((), ())), preferred_element_type=jnp.float32
    )


def turned(pre, tables, rows, sign):
    cosine, sine_first, sine_latter = (table[rows] for table in tables)
    return (
        pre * cosine
        + pltpu.roll(pre, 128 - ROTARY // 2, 1) * (sine_first * sign)
        + pltpu.roll(pre, ROTARY // 2, 1) * (sine_latter * sign)
    )


def swapped_half(index, late):
    sequence, half = index // 2, lax.rem(index, 2)
    half = half + late * (1 - 2 * half)
    return half, pl.ds(pl.multiple_of(sequence * SEQ_LEN + half * HALF, HALF), HALF)


HALF = SEQ_LEN // 2


def head_lanes(array, head):
    lanes = lax.broadcasted_iota(jnp.int32, array.shape, 1)
    mine = (lanes < HD) if head == 0 else (lanes >= HD)
    return jnp.where(mine, array, jnp.zeros_like(array))


def side_by_side(first, second):
    lanes = lax.broadcasted_iota(jnp.int32, first.shape, 1)
    return jnp.where(lanes < HD, first, second)


def probabilities(queries, key_rows, half):
    scores = dot(queries, key_rows, (1, 1))
    row = lax.broadcasted_iota(jnp.int32, scores.shape, 0) + half * HALF
    column = lax.broadcasted_iota(jnp.int32, scores.shape, 1)
    scores = jnp.where(row >= column, scores, NEGATIVE)
    exponent = jnp.exp(scores - jnp.max(scores, axis=-1, keepdims=True))
    return exponent * (1.0 / jnp.sum(exponent, axis=-1, keepdims=True))


def attend_pair(heads, mixed, late):
    @pl.loop(0, 2 * heads.shape[2] // 128)
    def _(step):
        pairs = heads.shape[2] // 128
        sequence, lanes = step // pairs, pl.ds(pl.multiple_of(lax.rem(step, pairs) * 128, 128), 128)
        start = pl.multiple_of(sequence * SEQ_LEN, SEQ_LEN)
        for half in (0, 1):
            past = pl.ds(start, HALF * (half + 1))
            queries = heads[0, pl.ds(start + half * HALF, HALF), lanes]
            results = []
            for head in (0, 1):
                probs = probabilities(head_lanes(queries, head), heads[1, past, lanes], half)
                results.append(dot(probs.astype(jnp.bfloat16), heads[2, past, lanes], (1, 0)))
            _, rows = swapped_half(sequence * 2 + half, late)
            mixed[rows, lanes] = side_by_side(*results).astype(mixed.dtype)


def attend_pair_back(heads, grad_mixed, grad_pre, tables, late):
    @pl.loop(0, 2 * heads.shape[2] // 128)
    def _(step):
        pairs = heads.shape[2] // 128
        sequence, lanes = step // pairs, pl.ds(pl.multiple_of(lax.rem(step, pairs) * 128, 128), 128)
        start = pl.multiple_of(sequence * SEQ_LEN, SEQ_LEN)
        grads = [[None, None], [None, None]]
        for half in (0, 1):
            past = pl.ds(start, HALF * (half + 1))
            here = pl.ds(start + half * HALF, HALF)
            queries, incoming = heads[0, here, lanes], grad_mixed[here, lanes]
            key_rows, value_rows = heads[1, past, lanes], heads[2, past, lanes]
            found = []
            for head in (0, 1):
                probs = probabilities(head_lanes(queries, head), key_rows, half)
                grad_values = dot(probs.astype(jnp.bfloat16), incoming, (0, 0))
                grad_probs = dot(head_lanes(incoming, head), value_rows, (1, 1))
                product = probs * grad_probs
                grad_scores = product - probs * jnp.sum(product, axis=-1, keepdims=True)
                grad_scores = grad_scores.astype(jnp.bfloat16)
                grad_queries = dot(grad_scores, key_rows, (1, 0))
                grad_keys = dot(grad_scores, queries, (0, 0))
                found.append((grad_queries, grad_keys, grad_values))
            grad_queries, grad_keys, grad_values = (side_by_side(*two) for two in zip(*found))
            at_half = pl.ds(half * HALF, HALF)
            _, rows = swapped_half(sequence * 2 + half, late)
            grad_queries = turned(grad_queries * (1.0 / math.sqrt(HD)), tables, at_half, -1.0)
            grad_pre[0, rows, lanes] = grad_queries.astype(grad_pre.dtype)
            if half == 0:
                early = (grad_keys, grad_values)
            else:
                whole = [grad_keys[:HALF] + early[0], grad_keys[HALF:]]
                whole_values = [grad_values[:HALF] + early[1], grad_values[HALF:]]
                for k in (0, 1):
                    _, rows = swapped_half(sequence * 2 + k, late)
                    turned_keys = turned(whole[k], tables, pl.ds(k * HALF, HALF), -1.0)
                    grad_pre[1, rows, lanes] = turned_keys.astype(grad_pre.dtype)
                    grad_pre[2, rows, lanes] = whole_values[k].astype(grad_pre.dtype)


def forward_kernel(
    inputs, cotangent, gain_first, shift_first, gain_second, shift_second, biases, turns,
    projections, output_weight, gate_up, down_weight,
    proj_full, out_full, gu_full, down_full, vectors_full, rows_one, rows_cot, heads_out, mixed_out,
    middle, rows_two, hidden_out, gate_out, up_out,
    own, normed, own_cot, vectors_here, biases_here, proj_here, out_here, rows_here, heads, mixed,
    near, far, got, got_beside, total, rows_later, gu_here, gate_wide, hidden, gate_act, up_act,
    vectors, own_bias, turns_here, send_sems, recv_sems, local_sems,
):
    p = Place(send_sems, recv_sems, local_sems)
    count = own.shape[0]
    late = lax.rem(p.tensor, 2)
    tables = [turns_here.at[k] for k in range(3)]
    loads = load_local(p, inputs, own)
    loads.append(p.copy(turns, turns_here).start())
    vectors[...] = jnp.zeros_like(vectors)
    for k, vector in enumerate((gain_first, shift_first, gain_second, shift_second)):
        vectors[k : k + 1] = vector[...].astype(jnp.float32)
    own_bias[...] = jnp.zeros_like(own_bias)
    own_bias[0:3] = biases[...].astype(jnp.float32)
    cot_loads = load_local(p, cotangent, own_cot)
    p.greet()
    slots = {key: j for j, key in enumerate(ORDER)}
    vector_base = p.used["recv"]
    p.used["recv"] += len(ORDER)

    def vector_copy(dy, dx, core):
        here, there = slots[(dy, dx, 0)], slots[(dy, dx, 1)]
        slot = here + p.core * (there - here)
        columns = pl.ds(pl.multiple_of(slot * EIGHTH, EIGHTH), EIGHTH)
        return p.send(
            vectors, vectors_here.at[:, columns], p.at(x=dx, y=dy, core=core),
            recv_sems.at[vector_base + slot],
        )

    vector_sends = [
        vector_copy(dy, dx, core).start()
        for dy in (0, 1) for dx in (0, 1) for core in (0, 1) if dy or dx or core
    ]
    own_slot = slots[(0, 0, 0)] + p.core * (slots[(0, 0, 1)] - slots[(0, 0, 0)])
    own_vectors = p.copy(
        vectors, vectors_here.at[:, pl.ds(pl.multiple_of(own_slot * EIGHTH, EIGHTH), EIGHTH)]
    ).start()
    own_biases = p.copy(own_bias, biases_here, p.core == 0).start()
    far_biases = p.send(own_bias, biases_here, p.at(core=1, far=1), when=p.core == 0).start()

    def third(j):
        return GatherWeight(
            p, projections.at[j], lambda k: proj_here.at[j, pl.ds(k * EIGHTH, EIGHTH)]
        )

    def gu_block(j):
        return lambda k: gu_here.at[j, pl.ds(k * EIGHTH, EIGHTH)]

    thirds = [third(0), third(1), third(2)]
    out = GatherWeight(p, output_weight, lambda k: out_here.at[:, pl.ds(k * EIGHTH, EIGHTH)])
    gate = GatherWeight(p, gate_up.at[0], gu_block(0))
    up = GatherWeight(p, gate_up.at[1], gu_block(1))
    down = GatherWeight(p, down_weight, lambda k: down_full.at[:, pl.ds(k * EIGHTH, EIGHTH)])
    thirds[0].fetch()
    thirds[1].fetch()
    thirds[0].spread(0)
    thirds[1].spread(0)
    wait_all(cot_loads)
    wait_all(loads)
    own_vectors.wait()
    sibling_slot = slots[(0, 0, 1)] + p.core * (slots[(0, 0, 0)] - slots[(0, 0, 1)])
    for dy in (0, 1):
        for dx in (0, 1):
            for core in (0, 1):
                if dy or dx:
                    slot = slots[(dy, dx, core)]
                elif core:
                    slot = sibling_slot
                else:
                    continue
                pltpu.make_async_copy(
                    vectors, vectors_here.at[:, pl.ds(0, EIGHTH)], recv_sems.at[vector_base + slot]
                ).wait()
    gain_one, shift_one = vectors_here[0:1], vectors_here[1:2]
    norm_into(count, lambda rows: own[rows].astype(jnp.float32), gain_one, shift_one, normed)
    gather_one = GatherRows(p, normed, rows_here).start()
    gather_cot = GatherRows(p, own_cot, rows_cot)
    stores = [p.copy(vectors_here, vectors_full).start()]

    thirds[0].spread(1)
    thirds[2].fetch().spread(0)
    thirds[1].spread(1)
    out.fetch().spread(0)
    thirds[0].relay()
    thirds[2].spread(1)
    gate.fetch()
    thirds[1].relay()
    out.spread(1)
    gate.spread(0)
    thirds[2].relay()
    gather_one.relay()
    gather_cot.start()
    up.fetch()
    own_biases.wait()
    far_biases.arrived(p.core == 1)
    far_biases.left()

    def project(j):
        thirds[j].finish()
        stores.append(p.copy(proj_here.at[j], proj_full.at[j]).start())

        @pl.loop(0, 4)
        def _(index):
            rows = pl.ds(pl.multiple_of(index * HALF, HALF), HALF)
            half, target = swapped_half(index, late)
            positions = pl.ds(pl.multiple_of(half * HALF, HALF), HALF)
            pre = dot(rows_here[rows], proj_here[j], (1, 0)) + biases_here[j : j + 1]
            for k in range(pre.shape[1] // 128):
                lanes = slice(k * 128, (k + 1) * 128)
                part = pre[:, lanes]
                if j < 2:
                    part = turned(part, tables, positions, 1.0)
                if j == 0:
                    part = part * (1.0 / math.sqrt(HD))
                heads[j, target, lanes] = part.astype(heads.dtype)

    gather_one.finish()
    stores.append(p.copy(rows_here, rows_one).start())
    project(0)
    gate.spread(1)
    project(1)
    out.relay()
    project(2)
    up.spread(0)
    gather_cot.relay()
    stores.append(p.copy(heads, heads_out).start())
    attend_pair(heads, mixed, late)
    out.finish()
    stores += [p.copy(out_here, out_full).start(), p.copy(mixed, mixed_out).start()]

    def out_rows(target, offset):
        def part(rows):
            target[rows] = dot(mixed[shifted(rows, offset)], out_here[...], (1, 0)).astype(target.dtype)

        return part

    scatter = ScatterRows(p, far, near, got, got_beside)
    tiles(2 * count, 256, out_rows(far, 2 * count))
    scatter.start()
    tiles(2 * count, 256, out_rows(near, 0))
    scatter.relay()
    down.fetch()
    gate.relay()
    up.spread(1)
    down.spread(0)
    scatter.arrived()
    gain_two, shift_two = vectors_here[2:3], vectors_here[3:4]

    def norm(rows):
        value = own[rows].astype(jnp.float32) + scatter.total(rows)
        total[rows] = value
        normed[rows] = norm_rows(value, gain_two, shift_two)[0].astype(normed.dtype)

    tiles(count, CHUNK, norm)
    gather = GatherRows(p, normed, rows_later).start()
    stores.append(p.copy(total, middle).start())
    gather_cot.finish()
    gather.relay()
    up.relay()
    down.spread(1)
    gate.finish()
    gather.finish()
    stores.append(p.copy(rows_later, rows_two).start())
    stores.append(p.copy(gu_here.at[0], gu_full.at[0]).start())

    def gate_rows(rows):
        gate_wide[rows] = dot(rows_later[rows], gu_here[0], (1, 0))

    tiles(4 * count, 256, gate_rows)
    up.finish()
    stores.append(p.copy(gu_here.at[1], gu_full.at[1]).start())

    def up_rows(rows):
        wide_up = dot(rows_later[rows], gu_here[1], (1, 0))
        wide_gate = gate_wide[rows]
        hidden[rows] = (wide_gate * jax.nn.sigmoid(wide_gate) * wide_up).astype(hidden.dtype)
        gate_act[rows] = wide_gate.astype(gate_act.dtype)
        up_act[rows] = wide_up.astype(up_act.dtype)

    tiles(2 * count, 256, up_rows)
    down.relay()
    tiles(2 * count, 256, lambda rows: up_rows(shifted(rows, 2 * count)))
    stores.append(p.copy(hidden, hidden_out).start())
    stores.append(p.copy(gate_act, gate_out).start())
    stores.append(p.copy(up_act, up_out).start())
    down.finish()
    for weight in (*thirds, out, gate, up, down):
        weight.left()
    for sent in vector_sends:
        sent.left()
    scatter.finish()
    wait_all(stores)


def norm_back_rows(value, incoming, gain):
    average = jnp.mean(value, axis=-1, keepdims=True)
    centred = value - average
    inverse = lax.rsqrt(jnp.mean(centred * centred, axis=-1, keepdims=True) + EPSILON)
    unit = centred * inverse
    scaled = incoming * gain
    inner = (
        scaled
        - jnp.mean(scaled, axis=-1, keepdims=True)
        - unit * jnp.mean(scaled * unit, axis=-1, keepdims=True)
    )
    return inner * inverse, incoming * unit


def fold(array):
    return jnp.sum(array.reshape(array.shape[0] // 8, 8, array.shape[1]), axis=0)


def back_kernel(
    hidden_in, gate_in, up_in, cot_rows, rows_two, gu_full, down_full, middle, vectors,
    out_half, grad_middle, rows_branch, sums, down_owned, gate_sums, up_parts, down_parts,
    hidden, gate_act, up_act, cot, rows_here, gate, up, down, value, near, got, got_beside,
    got_out, gain_sum, shift_sum, staging,
    down_got, down_last, down_home, down_result, gate_got, gate_last,
    send_sems, recv_sems, local_sems,
):
    p = Place(send_sems, recv_sems, local_sems)
    count, width = value.shape
    hidden_width = hidden.shape[1]
    quarter = width // 4
    first_loads = [p.copy(hidden_in, hidden).start(), p.copy(cot_rows, cot).start()]
    p.greet()
    down_sum = ScatterWeight(
        p, [down_parts.at[0], down_parts.at[1]], [staging.at[0], staging.at[1]], False,
        down_got, down_last, down_home, down_result,
    )
    gate_quarters = [gate.at[pl.ds(k * quarter, quarter)] for k in range(4)]
    gate_sum = ScatterWeight(
        p, gate_quarters[:2], gate_quarters[2:], True, gate_got, gate_last, None, None
    )
    far = cot.at[pl.ds(2 * count, 2 * count)]
    scatter = ScatterRows(p, far, near, got, got_beside)
    near_out = rows_here.at[pl.ds(0, 2 * count)]
    out_scatter = ScatterRows(p, far, near_out, got_out, None)

    def down_part(k):
        columns = pl.ds(k * quarter, quarter)
        staging[k % 2] = dot(hidden[...], cot[:, columns], (0, 0)).astype(staging.dtype)

    wait_all(first_loads)
    second_loads = [
        p.copy(down_full, down).start(), p.copy(gate_in, gate_act).start(), p.copy(up_in, up_act).start(),
    ]
    down_part(0)
    store_even = p.copy(staging.at[0], down_parts.at[0]).start()
    down_part(1)
    store_odd = p.copy(staging.at[1], down_parts.at[1]).start()
    store_even.wait()
    down_sum.start_even()
    down_part(2)
    store_odd.wait()
    down_sum.start_odd()
    down_part(3)
    wait_all(second_loads)
    third_loads = [p.copy(gu_full.at[0], gate).start(), p.copy(gu_full.at[1], up).start()]

    def hidden_back(rows):
        grad = dot(cot[rows], down[...], (1, 1))
        gate_value = gate_act[rows].astype(jnp.float32)
        up_value = up_act[rows].astype(jnp.float32)
        sigmoid = jax.nn.sigmoid(gate_value)
        scaled = grad * sigmoid
        up_act[rows] = (scaled * gate_value).astype(up_act.dtype)
        gate_act[rows] = (
            scaled * up_value * (1.0 + gate_value * (1.0 - sigmoid))
        ).astype(gate_act.dtype)

    tiles(4 * count, 256, hidden_back)
    wait_all(third_loads)
    last_loads = [p.copy(rows_two, rows_here).start(), p.copy(middle, value).start()]

    def second_rows(target, offset):
        def part(rows):
            here = shifted(rows, offset)
            target[rows] = (
                dot(gate_act[here], gate[...], (1, 1)) + dot(up_act[here], up[...], (1, 1))
            ).astype(target.dtype)

        return part

    tiles(2 * count, 256, second_rows(far, 2 * count))
    scatter.start()
    tiles(2 * count, 256, second_rows(near, 0))
    scatter.relay()
    wait_all(last_loads)

    def weight_part(target, grads, k):
        here = pl.ds(k * quarter, quarter)
        target[here] = dot(rows_here[:, here], grads[...], (0, 0)).astype(target.dtype)

    weight_part(gate, gate_act, 0)
    weight_part(gate, gate_act, 1)
    down_sum.relay()
    weight_part(gate, gate_act, 2)
    weight_part(gate, gate_act, 3)

    def out_rows(target, offset):
        def part(rows):
            target[rows] = dot(hidden[shifted(rows, offset)], down[...], (1, 0)).astype(target.dtype)

        return part

    for k in range(4):
        weight_part(up, up_act, k)
    stores = [p.copy(up, up_parts).start()]
    scatter.sibling.left()
    tiles(2 * count, 256, out_rows(far, 2 * count))
    out_scatter.start()
    down_sum.settle()
    gate_sum.start()
    tiles(2 * count, 256, out_rows(near_out, 0))
    scatter.arrived()
    gain = vectors[2:3]
    gain_sum[...] = jnp.zeros_like(gain_sum)
    shift_sum[...] = jnp.zeros_like(shift_sum)

    def middle_back(rows):
        incoming = scatter.total(rows)
        back, product = norm_back_rows(value[rows], incoming, gain)
        gain_sum[...] += fold(product)
        shift_sum[...] += fold(incoming)
        grad = cot[rows].astype(jnp.float32) + back
        value[rows] = grad
        cot[rows] = grad.astype(cot.dtype)

    tiles(count, CHUNK, middle_back)
    gather = GatherRows(p, cot.at[pl.ds(0, count)], rows_branch).start()
    stores.append(p.copy(value, grad_middle).start())
    gain_sum[0:1] = jnp.sum(gain_sum[...], axis=0, keepdims=True)
    gain_sum[1:2] = jnp.sum(shift_sum[...], axis=0, keepdims=True)
    stores.append(p.copy(gain_sum, sums).start())
    scatter.beside.left()
    out_scatter.sibling.arrived()
    combine(near_out, [near_out, got_out], 32)
    stores.append(p.copy(near_out, out_half).start())
    gather.relay()
    gate_sum.relay()
    down_sum.finish(down_owned)
    gate_sum.gather()
    for k in (0, 1):
        stores.append(p.copy(gate_sum.half(gate_quarters[2 + k], 0), gate_sums.at[k]).start())
    gate_sum.left()
    down_sum.stored()
    gather.finish()
    out_scatter.sibling.left()
    wait_all(stores)


def last_kernel(
    rows_branch, out_full, heads_in, mixed_in, rows_one, proj_full, inputs, vectors,
    turns, grad_middle, sums, up_parts, gate_sums, out_half, middle,
    outputs, input_grads, proj_owned, out_owned, vector_grads, bias_grad, gu_owned,
    branch, out_here, heads, mixed, grad_mixed, grad_pre, rows_here, proj_here, out_send,
    own, got, got_beside, result, all_sums, shift_sum, vector_got, vector_total, z_got,
    bias_here, bias_got, turns_here, got_out, gate_home, gate_even, up_result, out_result, third_result, *rest,
):
    weight_refs = [rest[4 * k : 4 * k + 4] for k in range(5)]
    p = Place(*rest[20:])
    count, width = own.shape
    quarter = width // 4
    late = lax.rem(p.tensor, 2)
    tables = [turns_here.at[k] for k in range(3)]
    first, second = p.core == 0, p.core == 1
    first_loads = [p.copy(rows_branch, branch).start(), p.copy(out_full, out_here).start()]
    p.greet()

    def weight_sum(send, rows, refs, total):
        keep, got_quarters, last, home = refs
        return ScatterWeight(
            p, send, [keep.at[0], keep.at[1]], rows, got_quarters, last, home, total
        )

    up_quarters = [up_parts.at[pl.ds(k * quarter, quarter)] for k in range(4)]
    up = weight_sum(up_quarters[:2], True, weight_refs[0], up_result).start()
    gate = HomeSum(p, gate_sums.at[0], gate_sums.at[1], gate_even, gate_home, up_result).start()
    out = weight_sum([out_send.at[0], out_send.at[1]], False, weight_refs[1], out_result)
    proj_send = [[heads.at[j, pl.ds(k * quarter, quarter)] for k in (0, 1)] for j in range(3)]
    thirds = [
        weight_sum(proj_send[j], True, weight_refs[2 + j], third_result.at[j]) for j in range(3)
    ]
    out_beside = p.send(out_half.at[pl.ds(count, count)], got_out, p.at(near=1)).start()
    out_loads = [p.copy(out_half.at[pl.ds(0, count)], own).start(), p.copy(middle, result).start()]
    wait_all(first_loads)
    mixed_load = p.copy(mixed_in, mixed).start()
    head_load = p.copy(heads_in, heads).start()
    out_loads.append(p.copy(turns, turns_here).start())

    @pl.loop(0, 4)
    def _(index):
        rows = pl.ds(pl.multiple_of(index * HALF, HALF), HALF)
        _, target = swapped_half(index, late)
        grad_mixed[target] = dot(branch[rows], out_here[...], (1, 1)).astype(grad_mixed.dtype)

    mixed_load.wait()

    def out_part(k):
        target = out_send.at[k] if k < 2 else weight_refs[1][0].at[k - 2]
        target[...] = dot(
            mixed[...], branch[:, pl.ds(k * quarter, quarter)], (0, 0)
        ).astype(target.dtype)

    for k in range(4):
        out_part(k)
    head_load.wait()
    later_loads = [p.copy(proj_full, proj_here).start(), p.copy(rows_one, rows_here).start()]
    wait_all(out_loads)
    gate_load = p.copy(gate_sums.at[0], gate_even).start()
    up.load(up_quarters[2:])
    attend_pair_back(heads, grad_mixed, grad_pre, tables, late)
    wait_all(later_loads)
    up.relay()
    near, far = branch.at[pl.ds(0, 2 * count)], branch.at[pl.ds(2 * count, 2 * count)]
    scatter = ScatterRows(p, far, near, got, got_beside)

    def term_rows(target, offset):
        def part(rows):
            here = shifted(rows, offset)
            total = dot(grad_pre[0, here], proj_here[0], (1, 1))
            for j in (1, 2):
                total = total + dot(grad_pre[j, here], proj_here[j], (1, 1))
            target[rows] = total.astype(target.dtype)

        return part

    def proj_part(j, k):
        target = proj_send[j][k] if k < 2 else weight_refs[2 + j][0].at[k - 2]
        target[...] = dot(
            rows_here[:, pl.ds(k * quarter, quarter)], grad_pre[j], (0, 0)
        ).astype(target.dtype)

    tiles(2 * count, 256, term_rows(far, 2 * count))
    scatter.start()
    tiles(2 * count, 256, term_rows(near, 0))
    scatter.relay()
    out_beside.arrived()

    def out_total(rows):
        total = result[rows] + own[rows].astype(jnp.float32) + got_out[rows].astype(jnp.float32)
        own[rows] = total.astype(own.dtype)

    tiles(count, CHUNK, out_total)
    stores = store_natural(p, own, outputs)
    for j in range(3):
        proj_part(j, 0)
        proj_part(j, 1)
    up.settle()
    out.start()
    thirds[0].start()
    thirds[1].start()
    wait_all(stores)
    loads = load_local(p, inputs, own)
    loads.append(p.copy(grad_middle, result).start())
    for j in range(3):
        proj_part(j, 2)
        proj_part(j, 3)
    out.relay()

    bias_here[...] = jnp.zeros_like(bias_here)
    for j in range(3):
        def bias_rows(rows):
            bias_here[j : j + 1] += jnp.sum(
                grad_pre[j, rows].astype(jnp.float32), axis=0, keepdims=True
            )

        tiles(4 * count, 256, bias_rows)
    bias_x = p.send(bias_here, bias_got.at[0], p.at(x=1)).start()
    bias_x.arrived()
    bias_x.left()
    bias_here[...] += bias_got[0]
    bias_y = p.send(bias_here, bias_got.at[1], p.at(y=1)).start()
    gate_load.wait()
    gate.finish(gu_owned.at[0])
    bias_y.arrived()
    bias_y.left()
    bias_here[...] += bias_got[1]
    near_sem, far_sem = p.take("recv"), p.take("recv")
    bias_home = [
        p.send(bias_here, bias_got.at[2], p.at(core=1), near_sem, first).start(),
        p.send(bias_here, bias_got.at[2], p.at(core=1, far=1), near_sem, second).start(),
        p.send(bias_here, bias_got.at[3], p.at(far=1), far_sem, second).start(),
    ]
    thirds[0].relay()
    thirds[2].start()
    out.settle()
    wait_all(loads)
    scatter.arrived()
    gain = vectors[0:1]
    all_sums[...] = jnp.zeros_like(all_sums)
    shift_sum[...] = jnp.zeros_like(shift_sum)

    def first_back(rows):
        incoming = scatter.total(rows)
        back, product = norm_back_rows(own[rows].astype(jnp.float32), incoming, gain)
        all_sums[...] += fold(product)
        shift_sum[...] += fold(incoming)
        result[rows] = result[rows] + back

    tiles(count, CHUNK, first_back)
    stores = store_natural(p, result, input_grads)
    all_sums[0:1] = jnp.sum(all_sums[...], axis=0, keepdims=True)
    all_sums[1:2] = jnp.sum(shift_sum[...], axis=0, keepdims=True)
    all_sums[2:4] = sums[0:2]
    slots = {key: j for j, key in enumerate(ORDER)}
    vector_sends = []
    for dy in (0, 1):
        for dx in (0, 1):
            for core in (0, 1):
                if not (dy or dx or core):
                    continue
                straight, crossed = slots[(dy, dx, core)], slots[(dy, dx, 1 - core)]
                slot = straight + p.core * (crossed - straight)
                columns = pl.ds(pl.multiple_of(slot * EIGHTH, EIGHTH), EIGHTH)
                vector_sends.append(
                    p.send(
                        all_sums.at[:, columns], vector_got.at[len(vector_sends)],
                        p.at(x=dx, y=dy, core=core),
                    ).start()
                )
    thirds[1].relay()
    thirds[0].settle()
    own_slot = slots[(0, 0, 0)] + p.core * (slots[(0, 0, 1)] - slots[(0, 0, 0)])
    total = all_sums[:, pl.ds(pl.multiple_of(own_slot * EIGHTH, EIGHTH), EIGHTH)]
    for k, sent in enumerate(vector_sends):
        sent.arrived()
        total = total + vector_got[k]
    vector_total[0] = total
    z_near = p.send(vector_total.at[0], z_got.at[0], p.at(near=1)).start()
    thirds[2].relay()
    thirds[1].settle()
    z_near.arrived()
    vector_total[1] = vector_total[0] + z_got[0]
    z_far = p.send(vector_total.at[1], z_got.at[1], p.at(far=1)).start()
    thirds[2].settle()
    z_far.arrived()
    z_near.left()
    z_far.left()
    vector_total[0] = vector_total[1] + z_got[1]
    vector_store = p.copy(vector_total.at[0], vector_grads).start()
    bias_home[0].arrived()
    bias_home[2].arrived(second)
    for sent in bias_home:
        sent.left()
    pl.when(second)(lambda: combine(bias_got.at[2], [bias_got.at[2], bias_got.at[3]], 8))
    pl.when(first)(lambda: combine(bias_got.at[2], [bias_got.at[2], bias_here], 8))
    bias_store = p.copy(bias_got.at[2], bias_grad).start()
    gate.stored()
    up.finish(gu_owned.at[1])
    out.finish(out_owned)
    for j in range(3):
        thirds[j].finish(proj_owned.at[j])
    for weight in (up, out, *thirds):
        weight.stored()
    scatter.finish()
    for sent in vector_sends:
        sent.left()
    out_beside.left()
    wait_all(stores)
    vector_store.wait()
    bias_store.wait()


def call(body, name, collective, inputs, in_specs, outs, scratch, counts):
    bf16_bytes = sum(math.prod(o.shape) * o.dtype.itemsize for o in outs)
    return pl.pallas_call(
        body,
        out_shape=outs,
        in_specs=in_specs,
        out_specs=[ANY] * len(outs),
        scratch_shapes=[
            *scratch,
            pltpu.SemaphoreType.DMA((counts[0],)),
            pltpu.SemaphoreType.DMA((counts[1],)),
            pltpu.SemaphoreType.DMA((counts[2],)),
        ],
        compiler_params=pltpu.CompilerParams(
            collective_id=collective, has_side_effects=True, vmem_limit_bytes=VMEM_BYTES
        ),
        cost_estimate=pl.CostEstimate(
            flops=0, bytes_accessed=2 * bf16_bytes, transcendentals=0
        ),
        name=name,
    )(*inputs)


def bf16(*shape):
    return jax.ShapeDtypeStruct(shape, jnp.bfloat16)


def f32(*shape):
    return jax.ShapeDtypeStruct(shape, jnp.float32)


def held(shape_struct):
    return pltpu.VMEM(shape_struct.shape, shape_struct.dtype)


def weight_scratch(quarter, eighth):
    return [
        held(bf16(2, *quarter)), held(bf16(2, *quarter)), held(bf16(2, *eighth)),
        held(bf16(2, *eighth)),
    ]


WHOLE = pl.BlockSpec(memory_space=pltpu.VMEM)
EIGHTH = 256


def local_pairs(
    inputs,
    gain_first,
    shift_first,
    projections,
    biases,
    output_weight,
    gain_second,
    shift_second,
    gate_up,
    down_weight,
    cotangent,
):
    count, width = inputs.shape
    rows = 4 * count
    heads_width = output_weight.shape[0]
    hidden_width = down_weight.shape[0]
    cosine, sine = angle_tables()
    rest = ((0, 0), (0, HD - ROTARY))
    turns = jnp.stack([
        jnp.tile(jnp.pad(table, rest, constant_values=fill), (1, 128 // HD))
        for table, fill in (
            (jnp.concatenate([cosine, cosine], axis=1), 1.0),
            (jnp.concatenate([-sine, jnp.zeros_like(sine)], axis=1), 0.0),
            (jnp.concatenate([jnp.zeros_like(sine), sine], axis=1), 0.0),
        )
    ])
    wide = bf16(rows, width)
    inner = bf16(rows, hidden_width)
    own = bf16(count, width)
    half_rows = bf16(2 * count, width)
    (
        proj_full, out_full, gu_full, down_full, vectors, gathered_one, gathered_cot, heads, mixed_rows,
        middle, gathered_two, hidden, gate_act, up_act,
    ) = call(
        forward_kernel, "forward", 1,
        (
            inputs, cotangent,
            *(v[None] for v in (gain_first, shift_first, gain_second, shift_second)), biases, turns,
            projections, output_weight, gate_up, down_weight,
        ),
        [ANY] * 2 + [WHOLE] * 5 + [ANY] * 5,
        [
            bf16(3, width, heads_width), bf16(heads_width, width), bf16(2, width, hidden_width),
            bf16(hidden_width, width), f32(8, width), wide, wide, bf16(3, rows, heads_width),
            bf16(rows, heads_width), f32(count, width), wide, inner, inner, inner,
        ],
        [
            held(own), held(own), held(own), held(f32(8, width)), held(f32(8, heads_width)),
            held(bf16(3, width, heads_width)), held(bf16(heads_width, width)), held(wide),
            held(bf16(3, rows, heads_width)), held(bf16(rows, heads_width)),
            held(half_rows), held(half_rows), held(half_rows), held(own), held(f32(count, width)),
            held(wide), held(bf16(2, width, hidden_width)), held(f32(rows, hidden_width)),
            held(inner), held(inner), held(inner), held(f32(8, EIGHTH)), held(f32(8, heads_width)),
            held(f32(*turns.shape)),
        ],
        (128, 96, 64),
    )

    by_rows = ((2 * EIGHTH, hidden_width), (EIGHTH, hidden_width))
    by_columns = ((hidden_width, 2 * EIGHTH), (hidden_width, EIGHTH))
    (
        out_half, grad_middle, gathered_branch, sums, down_owned, gate_sums, up_parts, _,
    ) = call(
        back_kernel, "backward_first", 2,
        (
            hidden, gate_act, up_act, gathered_cot, gathered_two, gu_full, down_full, middle, vectors,
        ),
        [ANY] * 8 + [WHOLE],
        [
            half_rows, f32(count, width), wide, f32(8, width), f32(hidden_width, EIGHTH),
            bf16(2, EIGHTH, hidden_width), bf16(width, hidden_width),
            bf16(2, hidden_width, 2 * EIGHTH),
        ],
        [
            held(inner), held(inner), held(inner), held(wide), held(wide),
            held(bf16(width, hidden_width)), held(bf16(width, hidden_width)),
            held(bf16(hidden_width, width)), held(f32(count, width)),
            held(half_rows), held(half_rows), held(own), held(half_rows),
            held(f32(8, width)), held(f32(8, width)), held(bf16(2, hidden_width, 2 * EIGHTH)),
            *weight_scratch(*by_columns)[1:], held(f32(hidden_width, EIGHTH)),
            *weight_scratch(*by_rows)[1:3],
        ],
        (64, 64, 48),
    )
    third = ((2 * EIGHTH, heads_width), (EIGHTH, heads_width))
    outputs, input_grads, proj_owned, out_owned, vector_grads, bias_grad, gu_owned = call(
        last_kernel, "backward_last", 3,
        (
            gathered_branch, out_full, heads, mixed_rows, gathered_one, proj_full, inputs, vectors,
            turns, grad_middle, sums, up_parts, gate_sums,
            out_half, middle,
        ),
        [ANY] * 7 + [WHOLE] + [ANY] * 2 + [WHOLE] + [ANY] * 4,
        [
            own, f32(count, width), f32(3, EIGHTH, heads_width), f32(heads_width, EIGHTH),
            f32(8, EIGHTH), f32(8, heads_width), f32(2, EIGHTH, hidden_width),
        ],
        [
            held(wide), held(bf16(heads_width, width)), held(bf16(3, rows, heads_width)),
            held(bf16(rows, heads_width)), held(bf16(rows, heads_width)),
            held(bf16(3, rows, heads_width)), held(wide), held(bf16(3, width, heads_width)),
            held(bf16(2, heads_width, 2 * EIGHTH)),
            held(own), held(half_rows), held(own), held(f32(count, width)),
            held(f32(8, width)), held(f32(8, width)),
            held(f32(7, 8, EIGHTH)), held(f32(2, 8, EIGHTH)), held(f32(2, 8, EIGHTH)),
            held(f32(8, heads_width)), held(f32(4, 8, heads_width)), held(f32(*turns.shape)),
            held(own),
            held(bf16(2, EIGHTH, hidden_width)), held(bf16(EIGHTH, hidden_width)),
            held(f32(EIGHTH, hidden_width)), held(f32(heads_width, EIGHTH)),
            held(f32(3, EIGHTH, heads_width)),
            *weight_scratch(*by_rows),
            *weight_scratch((heads_width, 2 * EIGHTH), (heads_width, EIGHTH)),
            *weight_scratch(*third), *weight_scratch(*third), *weight_scratch(*third),
        ],
        (64, 64, 48),
    )
    return (
        outputs,
        input_grads,
        vector_grads[0],
        vector_grads[1],
        proj_owned,
        bias_grad[:3],
        out_owned,
        vector_grads[2],
        vector_grads[3],
        gu_owned,
        down_owned,
    )


def solution(mesh):
    whole_pairs = dict(mesh.shape) == {"dp": 8, "tensor": 4}
    return jax.shard_map(
        local_pairs if whole_pairs else local,
        mesh=mesh,
        in_specs=(
            P(("dp", "tensor"), None),
            P("dp"),
            P("dp"),
            P(None, "dp", "tensor"),
            P(None, "tensor"),
            P("tensor", "dp"),
            P("dp"),
            P("dp"),
            P(None, "dp", "tensor"),
            P("tensor", "dp"),
            P(("dp", "tensor"), None),
        ),
        out_specs=(
            P(("dp", "tensor"), None),
            P(("dp", "tensor"), None),
            P("dp"),
            P("dp"),
            P(None, "dp", "tensor"),
            P(None, "tensor"),
            P("tensor", "dp"),
            P("dp"),
            P("dp"),
            P(None, "dp", "tensor"),
            P("tensor", "dp"),
        ),
        check_vma=False,
    )
```

```python
import math

import jax
import jax.numpy as jnp
from jax import lax
from jax.experimental import pallas as pl
from jax.experimental.pallas import tpu as pltpu
from jax.sharding import PartitionSpec as P

HD = 64
ROTARY = 16
SEQ_LEN = 512


EPSILON = 1e-05
ANGLE_BASE = 10000.0
NEGATIVE = -1e30


def norm_rows(rows, gain, shift):
    average = jnp.mean(rows, axis=-1, keepdims=True)
    centred = rows - average
    inverse = lax.rsqrt(jnp.mean(centred * centred, axis=-1, keepdims=True) + EPSILON)
    unit_rows = centred * inverse
    return (unit_rows * gain + shift, unit_rows, inverse)


def norm_back(incoming, unit_rows, inverse, gain):
    scaled = incoming * gain
    inner = (
        scaled
        - jnp.mean(scaled, axis=-1, keepdims=True)
        - unit_rows * jnp.mean(scaled * unit_rows, axis=-1, keepdims=True)
    )
    return (inner * inverse, jnp.sum(incoming * unit_rows, axis=0), jnp.sum(incoming, axis=0))


def angle_tables():
    freqs = 1.0 / ANGLE_BASE ** (jnp.arange(0, ROTARY, 2).astype(jnp.float32) / ROTARY)
    angles = jnp.arange(SEQ_LEN).astype(jnp.float32)[:, None] * freqs[None, :]
    return (jnp.cos(angles), jnp.sin(angles))


def rotate(heads, cosine, sine, sign):
    half_rot = ROTARY // 2
    first = heads[..., :half_rot]
    latter = heads[..., half_rot:ROTARY]
    cos_part = cosine[:, None, :]
    sin_part = sine[:, None, :] * sign
    return jnp.concatenate(
        [
            first * cos_part - latter * sin_part,
            latter * cos_part + first * sin_part,
            heads[..., ROTARY:],
        ],
        axis=-1,
    )


def causal_scores(queries, key_rows, positions):
    scaling = 1.0 / math.sqrt(HD)
    scores = scaling * jnp.einsum(
        "qhd,khd->hqk", queries, key_rows, preferred_element_type=jnp.float32
    )
    causal = positions[:, None] >= positions[None, :]
    return jnp.where(causal[None], scores, NEGATIVE)


def attend_forward(pieces, positions):
    queries, key_rows, value_rows = pieces
    scores = causal_scores(queries, key_rows, positions)
    row_top = jnp.max(scores, axis=-1, keepdims=True)
    exponent = jnp.exp(scores - row_top)
    totals = jnp.sum(exponent, axis=-1, keepdims=True)
    weights = (exponent / totals).astype(jnp.bfloat16)
    mixed = jnp.einsum("hqk,khd->qhd", weights, value_rows, preferred_element_type=jnp.float32)
    return (mixed.astype(jnp.bfloat16), (row_top + jnp.log(totals))[..., 0])


def attend_back(pieces, positions):
    queries, key_rows, value_rows, grad_mixed, log_totals = pieces
    scaling = 1.0 / math.sqrt(HD)
    scores = causal_scores(queries, key_rows, positions)
    weights = jnp.exp(scores - log_totals[..., None])
    grad_values = jnp.einsum(
        "hqk,qhd->khd", weights.astype(jnp.bfloat16), grad_mixed, preferred_element_type=jnp.float32
    )
    grad_weights = jnp.einsum(
        "qhd,khd->hqk", grad_mixed, value_rows, preferred_element_type=jnp.float32
    )
    grad_scores = weights * (grad_weights - jnp.sum(weights * grad_weights, axis=-1, keepdims=True))
    grad_scores = grad_scores.astype(jnp.bfloat16)
    grad_queries = scaling * jnp.einsum(
        "hqk,khd->qhd", grad_scores, key_rows, preferred_element_type=jnp.float32
    )
    grad_keys = scaling * jnp.einsum(
        "hqk,qhd->khd", grad_scores, queries, preferred_element_type=jnp.float32
    )
    return (grad_queries, grad_keys, grad_values)


def scatter_sum(terms, axis, dimension):
    owned = lax.psum_scatter(
        terms.astype(jnp.bfloat16), axis, scatter_dimension=dimension, tiled=True
    )
    return owned.astype(jnp.float32)


def local(
    inputs,
    gain_first,
    shift_first,
    projections,
    biases,
    output_weight,
    gain_second,
    shift_second,
    gate_up,
    down_weight,
    cotangent,
):
    tensor_ways = lax.axis_size("tensor")
    row_count = inputs.shape[0]
    group_rows = row_count * tensor_ways
    sequences = group_rows // SEQ_LEN
    head_width = output_weight.shape[0]
    local_heads = head_width // HD
    head_shape = (sequences, SEQ_LEN, local_heads, HD)
    cosine, sine = angle_tables()
    positions = jnp.arange(SEQ_LEN)
    proj_full, out_full, gain_one, shift_one = (
        lax.all_gather(projections, "dp", axis=1, tiled=True),
        lax.all_gather(output_weight, "dp", axis=1, tiled=True),
        lax.all_gather(gain_first, "dp", axis=0, tiled=True),
        lax.all_gather(shift_first, "dp", axis=0, tiled=True),
    )
    gain_one = gain_one.astype(jnp.float32)
    residual = inputs.astype(jnp.float32)
    normed_one, unit_one, inverse_one = norm_rows(residual, gain_one, shift_one.astype(jnp.float32))
    gathered_one = lax.all_gather(normed_one.astype(jnp.bfloat16), "tensor", axis=0, tiled=True)
    pre_all = jnp.einsum("gd,jde->jge", gathered_one, proj_full, preferred_element_type=jnp.float32)
    pre_all = pre_all + biases.astype(jnp.float32)[:, None, :]
    queries = rotate(pre_all[0].reshape(head_shape), cosine, sine, 1.0).astype(jnp.bfloat16)
    key_rows = rotate(pre_all[1].reshape(head_shape), cosine, sine, 1.0).astype(jnp.bfloat16)
    value_rows = pre_all[2].reshape(head_shape).astype(jnp.bfloat16)
    mixed, log_totals = lax.map(
        lambda pieces: attend_forward(pieces, positions), (queries, key_rows, value_rows)
    )
    mixed_rows = mixed.reshape(group_rows, head_width)
    part = mixed_rows
    middle = residual + scatter_sum(
        jnp.dot(part, out_full, preferred_element_type=jnp.float32), "tensor", 0
    )
    gu_full, down_full, gain_two, shift_two = (
        lax.all_gather(gate_up, "dp", axis=1, tiled=True),
        lax.all_gather(down_weight, "dp", axis=1, tiled=True),
        lax.all_gather(gain_second, "dp", axis=0, tiled=True),
        lax.all_gather(shift_second, "dp", axis=0, tiled=True),
    )
    gain_two = gain_two.astype(jnp.float32)
    normed_two, unit_two, inverse_two = norm_rows(middle, gain_two, shift_two.astype(jnp.float32))
    gathered_two = lax.all_gather(normed_two.astype(jnp.bfloat16), "tensor", axis=0, tiled=True)
    gate_act = jnp.dot(gathered_two, gu_full[0], preferred_element_type=jnp.float32)
    up_act = jnp.dot(gathered_two, gu_full[1], preferred_element_type=jnp.float32)
    sigmoid_gate = jax.nn.sigmoid(gate_act)
    hidden = (gate_act * sigmoid_gate * up_act).astype(jnp.bfloat16)
    part = hidden
    outputs = (
        middle
        + scatter_sum(jnp.dot(part, down_full, preferred_element_type=jnp.float32), "tensor", 0)
    ).astype(jnp.bfloat16)
    gu_back, down_back, gain_two_back = (
        lax.all_gather(gate_up, "dp", axis=1, tiled=True),
        lax.all_gather(down_weight, "dp", axis=1, tiled=True),
        lax.all_gather(gain_second, "dp", axis=0, tiled=True),
    )
    gain_two_back = gain_two_back.astype(jnp.float32)
    gathered_cot = lax.all_gather(cotangent, "tensor", axis=0, tiled=True)
    grad_hidden = jnp.einsum(
        "gd,fd->gf", gathered_cot, down_back, preferred_element_type=jnp.float32
    )
    down_grad = jnp.einsum("gf,gd->fd", hidden, gathered_cot, preferred_element_type=jnp.float32)
    grad_up = (grad_hidden * gate_act * sigmoid_gate).astype(jnp.bfloat16)
    grad_gate = (
        grad_hidden * up_act * sigmoid_gate * (1.0 + gate_act * (1.0 - sigmoid_gate))
    ).astype(jnp.bfloat16)
    gu_grad = jnp.stack(
        [
            jnp.einsum("gd,gf->df", gathered_two, grad_gate, preferred_element_type=jnp.float32),
            jnp.einsum("gd,gf->df", gathered_two, grad_up, preferred_element_type=jnp.float32),
        ]
    )
    first_term = jnp.einsum("gf,df->gd", grad_gate, gu_back[0], preferred_element_type=jnp.float32)
    grad_second = scatter_sum(
        first_term
        + jnp.einsum("gf,df->gd", grad_up, gu_back[1], preferred_element_type=jnp.float32),
        "tensor",
        0,
    )
    gu_owned, down_owned = (
        scatter_sum(gu_grad, "dp", 1),
        scatter_sum(down_grad, "dp", 1),
    )
    grad_mid_norm, gain_two_part, shift_two_part = norm_back(
        grad_second, unit_two, inverse_two, gain_two_back
    )
    grad_middle = cotangent.astype(jnp.float32) + grad_mid_norm
    proj_back, out_back, gain_one_back = (
        lax.all_gather(projections, "dp", axis=1, tiled=True),
        lax.all_gather(output_weight, "dp", axis=1, tiled=True),
        lax.all_gather(gain_first, "dp", axis=0, tiled=True),
    )
    gain_one_back = gain_one_back.astype(jnp.float32)
    gathered_branch = lax.all_gather(grad_middle.astype(jnp.bfloat16), "tensor", axis=0, tiled=True)
    out_grad = jnp.einsum(
        "ge,gd->ed", mixed_rows, gathered_branch, preferred_element_type=jnp.float32
    )
    grad_mixed = jnp.einsum(
        "gd,ed->ge", gathered_branch, out_back, preferred_element_type=jnp.float32
    ).astype(jnp.bfloat16)
    grad_queries, grad_keys, grad_values = lax.map(
        lambda pieces: attend_back(pieces, positions),
        (queries, key_rows, value_rows, grad_mixed.reshape(head_shape), log_totals),
    )
    grad_queries = rotate(grad_queries, cosine, sine, -1.0)
    grad_keys = rotate(grad_keys, cosine, sine, -1.0)
    grad_pre = (
        jnp.stack([grad_queries, grad_keys, grad_values])
        .reshape(3, group_rows, head_width)
        .astype(jnp.bfloat16)
    )
    bias_part = jnp.sum(grad_pre, axis=1, dtype=jnp.float32)
    proj_grad = jnp.einsum(
        "gd,jge->jde", gathered_one, grad_pre, preferred_element_type=jnp.float32
    )
    part = grad_pre
    grad_normed = scatter_sum(
        jnp.einsum("jge,jde->gd", part, proj_back, preferred_element_type=jnp.float32),
        "tensor",
        0,
    )
    proj_owned, out_owned = (
        scatter_sum(proj_grad, "dp", 1),
        scatter_sum(out_grad, "dp", 1),
    )
    grad_in_norm, gain_one_part, shift_one_part = norm_back(
        grad_normed, unit_one, inverse_one, gain_one_back
    )
    input_grads = grad_middle + grad_in_norm
    one_hot = (jnp.arange(tensor_ways) == lax.axis_index("tensor")).astype(jnp.float32)
    spread_bias = (bias_part[:, None, :] * one_hot[None, :, None]).reshape(
        3, tensor_ways * head_width
    )
    summed = lax.psum(
        (gain_one_part, shift_one_part, gain_two_part, shift_two_part, spread_bias),
        ("dp", "tensor"),
    )
    own_width = gain_first.shape[0]
    own_offset = lax.axis_index("dp") * own_width

    def own_part(vector):
        return lax.dynamic_slice_in_dim(vector, own_offset, own_width, 0)

    bias_grad = jnp.sum(
        summed[4].reshape(3, tensor_ways, head_width) * one_hot[None, :, None], axis=1
    )
    return (
        outputs,
        input_grads,
        own_part(summed[0]),
        own_part(summed[1]),
        proj_owned,
        bias_grad,
        out_owned,
        own_part(summed[2]),
        own_part(summed[3]),
        gu_owned,
        down_owned,
    )


ORDER = ((1, 0, 0), (1, 1, 0), (0, 1, 1), (1, 1, 1), (0, 0, 0), (0, 1, 0), (0, 0, 1), (1, 0, 1))
EVEN_Y, EVEN_XY, ODD_X, ODD_XY, EVEN, EVEN_X, ODD, ODD_Y = range(8)
ANY = pl.BlockSpec(memory_space=pl.ANY)
VMEM_BYTES = 63 * 1024 * 1024


class Place:
    def __init__(self, send_sems, recv_sems, local_sems):
        self.dp, self.tensor = lax.axis_index("dp"), lax.axis_index("tensor")
        self.core = lax.rem(self.dp, 2)
        self.x = lax.rem(self.dp // 2, 2)
        self.y = self.dp // 4
        self.pools = {"send": send_sems, "recv": recv_sems, "local": local_sems}
        self.used = {"send": 0, "recv": 0, "local": 0}

    def take(self, kind):
        self.used[kind] += 1
        return self.pools[kind].at[self.used[kind] - 1]

    def at(self, x=0, y=0, core=0, near=0, far=0):
        dp = self.dp
        dp = dp + x * (2 - 4 * self.x) + y * (4 - 8 * self.y) + core * (1 - 2 * self.core)
        tensor = self.tensor
        tensor = tensor + near * (1 - 2 * lax.rem(tensor, 2)) + far * (3 - 2 * tensor)
        return (dp, tensor)

    def column(self, key):
        dy, dx, core = key
        y = self.y + dy * (1 - 2 * self.y)
        x = self.x + dx * (1 - 2 * self.x)
        return pl.multiple_of((y * 4 + x * 2 + core) * EIGHTH, EIGHTH)

    def greet(self):
        barrier = pltpu.get_barrier_semaphore()
        partners = [
            self.at(x=x, y=y, core=core)
            for x in (0, 1)
            for y in (0, 1)
            for core in (0, 1)
            if x or y or core
        ] + [self.at(near=1), self.at(far=1), self.at(far=1, core=1)]
        for partner in partners:
            pl.semaphore_signal(
                barrier, inc=1, device_id=partner, device_id_type=pl.DeviceIdType.MESH
            )
        pl.semaphore_wait(barrier, len(partners))

    def send(self, source, target, device, recv_sem=None, when=None):
        return Sent(
            pltpu.make_async_remote_copy(
                src_ref=source,
                dst_ref=target,
                send_sem=self.take("send"),
                recv_sem=self.take("recv") if recv_sem is None else recv_sem,
                device_id=device,
                device_id_type=pl.DeviceIdType.MESH,
            ),
            when,
        )

    def copy(self, source, target, when=None):
        return Copied(pltpu.make_async_copy(source, target, self.take("local")), when)


def guarded(when, action):
    if when is None:
        action()
    else:
        pl.when(when)(action)


class Sent:
    def __init__(self, copy, when):
        self.copy, self.when = copy, when

    def start(self):
        guarded(self.when, self.copy.start)
        return self

    def arrived(self, when=None):
        guarded(when, self.copy.wait_recv)

    def left(self):
        guarded(self.when, self.copy.wait_send)


class Copied:
    def __init__(self, copy, when):
        self.copy, self.when = copy, when

    def start(self):
        guarded(self.when, self.copy.start)
        return self

    def wait(self):
        guarded(self.when, self.copy.wait)


class GatherWeight:
    def __init__(self, place, shard, block):
        self.place, self.shard, self.block = place, shard, block
        self.spreads, self.arrivals = [], {}

    def fetch(self):
        p = self.place
        even, odd = self.block(EVEN), self.block(ODD)
        first, second = p.core == 0, p.core == 1
        self.own = p.copy(self.shard, even, first).start()
        even_sem, odd_sem = p.take("recv"), p.take("recv")
        self.to_far_even = p.send(self.shard, even, p.at(core=1, far=1), even_sem, first).start()
        self.to_sibling = p.send(self.shard, odd, p.at(core=1), odd_sem, second).start()
        self.to_far_odd = p.send(self.shard, odd, p.at(far=1), odd_sem, second).start()
        return self

    def spread(self, core):
        p, block = self.place, self.block
        here = p.core == core
        if core:
            self.to_far_even.arrived(here)
        self.to_sibling.arrived(here)
        even = block(EVEN) if core else self.shard
        routes = (
            (even, EVEN_X, p.at(x=1)), (block(ODD), ODD_Y, p.at(y=1)),
            (block(ODD), ODD_X, p.at(x=1)), (even, EVEN_Y, p.at(y=1)),
        )
        for source, target, device in routes:
            if target not in self.arrivals:
                self.arrivals[target] = p.take("recv")
            self.spreads.append(
                p.send(source, block(target), device, self.arrivals[target], here).start()
            )
        return self

    def relay(self):
        p, block = self.place, self.block
        even_x, odd_y, self.odd_x, self.even_y = self.spreads[:4]
        even_x.arrived()
        self.even_xy = p.send(block(EVEN_X), block(EVEN_XY), p.at(y=1)).start()
        odd_y.arrived()
        self.odd_xy = p.send(block(ODD_Y), block(ODD_XY), p.at(x=1)).start()
        return self

    def finish(self):
        self.own.wait()
        for copy in (self.odd_x, self.even_y, self.even_xy, self.odd_xy):
            copy.arrived()

    def left(self):
        for copy in (
            *self.spreads, self.even_xy, self.odd_xy,
            self.to_far_even, self.to_sibling, self.to_far_odd,
        ):
            copy.left()


class GatherRows:
    def __init__(self, place, own, rows):
        self.place, self.own, self.rows = place, own, rows
        self.count = own.shape[0]

    def slot(self, k):
        return self.rows.at[pl.ds(k * self.count, self.count)]

    def start(self):
        p = self.place
        self.beside = p.send(self.own, self.slot(1), p.at(near=1)).start()
        self.sibling = p.send(self.own, self.slot(2), p.at(core=1)).start()
        self.here = p.copy(self.own, self.slot(0)).start()
        return self

    def relay(self):
        p = self.place
        self.beside.arrived()
        self.across = p.send(self.slot(1), self.slot(3), p.at(core=1)).start()
        return self

    def finish(self):
        self.sibling.arrived()
        self.across.arrived()
        self.here.wait()
        for copy in (self.beside, self.sibling, self.across):
            copy.left()


def combine(target, terms, chunk):
    @pl.loop(0, target.shape[0] // chunk)
    def _(i):
        rows = pl.ds(pl.multiple_of(i * chunk, chunk), chunk)
        total = terms[0][rows].astype(jnp.float32)
        for term in terms[1:]:
            total = total + term[rows].astype(jnp.float32)
        target[rows] = total.astype(target.dtype)


class ScatterRows:
    def __init__(self, place, far, near, got, got_beside):
        self.place, self.far, self.near = place, far, near
        self.got, self.got_beside = got, got_beside
        self.count = near.shape[0] // 2

    def start(self):
        self.sibling = self.place.send(self.far, self.got, self.place.at(core=1)).start()
        return self

    def relay(self):
        p, n = self.place, self.count
        self.sibling.arrived()
        late = pl.ds(n, n)
        combine(self.near.at[late], [self.near.at[late], self.got.at[late]], 32)
        self.beside = p.send(self.near.at[late], self.got_beside, p.at(near=1)).start()
        return self

    def total(self, rows):
        return (
            self.near[rows].astype(jnp.float32)
            + self.got[rows].astype(jnp.float32)
            + self.got_beside[rows].astype(jnp.float32)
        )

    def arrived(self):
        self.beside.arrived()

    def finish(self):
        self.sibling.left()
        self.beside.left()


class ScatterWeight:
    def __init__(self, place, send, keep, rows, got, last, home, result):
        self.place, self.parts, self.keep, self.rows = place, send, keep, rows
        self.got, self.last, self.home, self.result = got, last, home, result
        self.loads = []

    def half(self, ref, k):
        if self.rows:
            size = ref.shape[0] // 2
            return ref.at[pl.ds(k * size, size)]
        size = ref.shape[1] // 2
        return ref.at[:, pl.ds(k * size, size)]

    def load(self, sources):
        self.loads = [self.place.copy(a, b).start() for a, b in zip(sources, self.keep)]
        return self

    def start_even(self):
        p = self.place
        self.even = p.send(self.parts[0], self.got.at[0], p.at(y=1)).start()
        return self

    def start_odd(self):
        p = self.place
        self.odd = p.send(self.parts[1], self.got.at[1], p.at(x=1)).start()
        return self

    def start(self):
        return self.start_even().start_odd()

    def relay(self):
        p = self.place
        wait_all(self.loads)
        self.second = []
        for k, arrival in enumerate((self.even, self.odd)):
            arrival.arrived()
            there = self.half(self.keep[k], 1)
            combine(there, [there, self.half(self.got.at[k], 1)], 64)
            device = p.at(x=1) if k == 0 else p.at(y=1)
            self.second.append(p.send(there, self.last.at[k], device).start())
        return self

    def gather(self):
        for k in (1, 0):
            self.second[k].arrived()
            here = self.half(self.keep[k], 0)
            combine(here, [here, self.half(self.got.at[k], 0), self.last.at[k]], 64)
        return self

    def settle(self):
        self.gather()
        even, odd = self.half(self.keep[0], 0), self.half(self.keep[1], 0)
        self.way_home = HomeSum(self.place, even, odd, even, self.home, self.result).start()
        return self

    def finish(self, output):
        self.way_home.finish(output)
        self.left()

    def left(self):
        for copy in (self.even, self.odd, *self.second):
            copy.left()

    def stored(self):
        self.way_home.stored()


class HomeSum:
    def __init__(self, place, even, odd, here, home, result):
        self.place, self.even, self.odd, self.here = place, even, odd, here
        self.home, self.result = home, result

    def start(self):
        p = self.place
        first, second = p.core == 0, p.core == 1
        near_sem, far_sem = p.take("recv"), p.take("recv")
        home = self.home
        self.to_sibling = p.send(self.odd, home.at[0], p.at(core=1), near_sem, first).start()
        self.to_first = p.send(self.even, home.at[0], p.at(core=1, far=1), near_sem, second).start()
        self.to_far = p.send(self.odd, home.at[1], p.at(far=1), far_sem, second).start()
        return self

    def finish(self, output):
        p, home = self.place, self.home
        first, second = p.core == 0, p.core == 1
        self.to_sibling.arrived()
        self.to_far.arrived(second)
        pl.when(first)(lambda: combine(self.result, [self.here, home.at[0]], 64))
        pl.when(second)(lambda: combine(self.result, [home.at[0], home.at[1]], 64))
        self.store = p.copy(self.result, output).start()
        for copy in (self.to_sibling, self.to_first, self.to_far):
            copy.left()

    def stored(self):
        self.store.wait()


def load_local(place, source, target):
    return [
        place.copy(
            source.at[:, pl.ds(place.column(key), EIGHTH)], target.at[:, pl.ds(j * EIGHTH, EIGHTH)]
        ).start()
        for j, key in enumerate(ORDER)
    ]


def store_natural(place, source, target):
    return [
        place.copy(
            source.at[:, pl.ds(j * EIGHTH, EIGHTH)], target.at[:, pl.ds(place.column(key), EIGHTH)]
        ).start()
        for j, key in enumerate(ORDER)
    ]


def wait_all(copies):
    for copy in copies:
        copy.wait()


CHUNK = 32


def norm_into(count, rows_of, gain, shift, target):
    @pl.loop(0, count // CHUNK)
    def _(i):
        rows = pl.ds(pl.multiple_of(i * CHUNK, CHUNK), CHUNK)
        target[rows] = norm_rows(rows_of(rows), gain, shift)[0].astype(target.dtype)


def tiles(count, tile, body):
    @pl.loop(0, count // tile)
    def _(i):
        body(pl.ds(pl.multiple_of(i * tile, tile), tile))


def shifted(rows, offset):
    return pl.ds(pl.multiple_of(rows.start + offset, 256), rows.size)


def dot(left, right, contract):
    return lax.dot_general(
        left, right, (((contract[0],), (contract[1],)), ((), ())), preferred_element_type=jnp.float32
    )


def turned(pre, tables, rows, sign):
    cosine, sine_first, sine_latter = (table[rows] for table in tables)
    return (
        pre * cosine
        + pltpu.roll(pre, 128 - ROTARY // 2, 1) * (sine_first * sign)
        + pltpu.roll(pre, ROTARY // 2, 1) * (sine_latter * sign)
    )


def swapped_half(index, late):
    sequence, half = index // 2, lax.rem(index, 2)
    half = half + late * (1 - 2 * half)
    return half, pl.ds(pl.multiple_of(sequence * SEQ_LEN + half * HALF, HALF), HALF)


HALF = SEQ_LEN // 2


def head_lanes(array, head):
    lanes = lax.broadcasted_iota(jnp.int32, array.shape, 1)
    mine = (lanes < HD) if head == 0 else (lanes >= HD)
    return jnp.where(mine, array, jnp.zeros_like(array))


def side_by_side(first, second):
    lanes = lax.broadcasted_iota(jnp.int32, first.shape, 1)
    return jnp.where(lanes < HD, first, second)


def probabilities(queries, key_rows, half):
    scores = dot(queries, key_rows, (1, 1))
    row = lax.broadcasted_iota(jnp.int32, scores.shape, 0) + half * HALF
    column = lax.broadcasted_iota(jnp.int32, scores.shape, 1)
    scores = jnp.where(row >= column, scores, NEGATIVE)
    exponent = jnp.exp(scores - jnp.max(scores, axis=-1, keepdims=True))
    return exponent * (1.0 / jnp.sum(exponent, axis=-1, keepdims=True))


def attend_pair(heads, mixed, late):
    @pl.loop(0, 2 * heads.shape[2] // 128)
    def _(step):
        pairs = heads.shape[2] // 128
        sequence, lanes = step // pairs, pl.ds(pl.multiple_of(lax.rem(step, pairs) * 128, 128), 128)
        start = pl.multiple_of(sequence * SEQ_LEN, SEQ_LEN)
        for half in (0, 1):
            past = pl.ds(start, HALF * (half + 1))
            queries = heads[0, pl.ds(start + half * HALF, HALF), lanes]
            results = []
            for head in (0, 1):
                probs = probabilities(head_lanes(queries, head), heads[1, past, lanes], half)
                results.append(dot(probs.astype(jnp.bfloat16), heads[2, past, lanes], (1, 0)))
            _, rows = swapped_half(sequence * 2 + half, late)
            mixed[rows, lanes] = side_by_side(*results).astype(mixed.dtype)


def attend_pair_back(heads, grad_mixed, grad_pre, tables, late):
    @pl.loop(0, 2 * heads.shape[2] // 128)
    def _(step):
        pairs = heads.shape[2] // 128
        sequence, lanes = step // pairs, pl.ds(pl.multiple_of(lax.rem(step, pairs) * 128, 128), 128)
        start = pl.multiple_of(sequence * SEQ_LEN, SEQ_LEN)
        grads = [[None, None], [None, None]]
        for half in (0, 1):
            past = pl.ds(start, HALF * (half + 1))
            here = pl.ds(start + half * HALF, HALF)
            queries, incoming = heads[0, here, lanes], grad_mixed[here, lanes]
            key_rows, value_rows = heads[1, past, lanes], heads[2, past, lanes]
            found = []
            for head in (0, 1):
                probs = probabilities(head_lanes(queries, head), key_rows, half)
                grad_values = dot(probs.astype(jnp.bfloat16), incoming, (0, 0))
                grad_probs = dot(head_lanes(incoming, head), value_rows, (1, 1))
                product = probs * grad_probs
                grad_scores = product - probs * jnp.sum(product, axis=-1, keepdims=True)
                grad_scores = grad_scores.astype(jnp.bfloat16)
                grad_queries = dot(grad_scores, key_rows, (1, 0))
                grad_keys = dot(grad_scores, queries, (0, 0))
                found.append((grad_queries, grad_keys, grad_values))
            grad_queries, grad_keys, grad_values = (side_by_side(*two) for two in zip(*found))
            at_half = pl.ds(half * HALF, HALF)
            _, rows = swapped_half(sequence * 2 + half, late)
            grad_queries = turned(grad_queries * (1.0 / math.sqrt(HD)), tables, at_half, -1.0)
            grad_pre[0, rows, lanes] = grad_queries.astype(grad_pre.dtype)
            if half == 0:
                early = (grad_keys, grad_values)
            else:
                whole = [grad_keys[:HALF] + early[0], grad_keys[HALF:]]
                whole_values = [grad_values[:HALF] + early[1], grad_values[HALF:]]
                for k in (0, 1):
                    _, rows = swapped_half(sequence * 2 + k, late)
                    turned_keys = turned(whole[k], tables, pl.ds(k * HALF, HALF), -1.0)
                    grad_pre[1, rows, lanes] = turned_keys.astype(grad_pre.dtype)
                    grad_pre[2, rows, lanes] = whole_values[k].astype(grad_pre.dtype)


def forward_kernel(
    inputs, cotangent, parameters, biases, turns,
    projections, output_weight, gate_up, down_weight,
    proj_full, out_full, gu_full, down_full, vectors_full, rows_one, rows_cot, heads_out, mixed_out,
    middle, rows_two, hidden_out, gate_out, up_out, down_parts,
    own, normed, own_cot, vectors_here, biases_here, proj_here, out_here, rows_here, heads, mixed,
    near, far, got, got_beside, total, rows_later, gu_here, gate_wide, hidden, gate_act, up_act,
    vectors, own_bias, turns_here, send_sems, recv_sems, local_sems,
):
    p = Place(send_sems, recv_sems, local_sems)
    count = own.shape[0]
    late = lax.rem(p.tensor, 2)
    tables = [turns_here.at[k] for k in range(3)]
    loads = load_local(p, inputs, own)
    loads.append(p.copy(turns, turns_here).start())
    vectors[...] = jnp.zeros_like(vectors)
    vectors[0:4] = parameters[...].astype(jnp.float32)
    own_bias[...] = jnp.zeros_like(own_bias)
    own_bias[0:3] = biases[...].astype(jnp.float32)
    cot_loads = load_local(p, cotangent, own_cot)
    p.greet()
    slots = {key: j for j, key in enumerate(ORDER)}
    vector_base = p.used["recv"]
    p.used["recv"] += len(ORDER)

    def vector_copy(dy, dx, core):
        here, there = slots[(dy, dx, 0)], slots[(dy, dx, 1)]
        slot = here + p.core * (there - here)
        columns = pl.ds(pl.multiple_of(slot * EIGHTH, EIGHTH), EIGHTH)
        return p.send(
            vectors, vectors_here.at[:, columns], p.at(x=dx, y=dy, core=core),
            recv_sems.at[vector_base + slot],
        )

    vector_sends = [
        vector_copy(dy, dx, core).start()
        for dy in (0, 1) for dx in (0, 1) for core in (0, 1) if dy or dx or core
    ]
    own_slot = slots[(0, 0, 0)] + p.core * (slots[(0, 0, 1)] - slots[(0, 0, 0)])
    own_vectors = p.copy(
        vectors, vectors_here.at[:, pl.ds(pl.multiple_of(own_slot * EIGHTH, EIGHTH), EIGHTH)]
    ).start()
    own_biases = p.copy(own_bias, biases_here, p.core == 0).start()
    far_biases = p.send(own_bias, biases_here, p.at(core=1, far=1), when=p.core == 0).start()

    def third(j):
        return GatherWeight(
            p, projections.at[j], lambda k: proj_here.at[j, pl.ds(k * EIGHTH, EIGHTH)]
        )

    def gu_block(j):
        return lambda k: gu_here.at[j, pl.ds(k * EIGHTH, EIGHTH)]

    thirds = [third(0), third(1), third(2)]
    out = GatherWeight(p, output_weight, lambda k: out_here.at[:, pl.ds(k * EIGHTH, EIGHTH)])
    gate = GatherWeight(p, gate_up.at[0], gu_block(0))
    up = GatherWeight(p, gate_up.at[1], gu_block(1))
    down = GatherWeight(p, down_weight, lambda k: down_full.at[:, pl.ds(k * EIGHTH, EIGHTH)])
    thirds[0].fetch()
    thirds[1].fetch()
    thirds[0].spread(0)
    thirds[1].spread(0)
    wait_all(cot_loads)
    wait_all(loads)
    own_vectors.wait()
    sibling_slot = slots[(0, 0, 1)] + p.core * (slots[(0, 0, 0)] - slots[(0, 0, 1)])
    for dy in (0, 1):
        for dx in (0, 1):
            for core in (0, 1):
                if dy or dx:
                    slot = slots[(dy, dx, core)]
                elif core:
                    slot = sibling_slot
                else:
                    continue
                pltpu.make_async_copy(
                    vectors, vectors_here.at[:, pl.ds(0, EIGHTH)], recv_sems.at[vector_base + slot]
                ).wait()
    gain_one, shift_one = vectors_here[0:1], vectors_here[1:2]
    norm_into(count, lambda rows: own[rows].astype(jnp.float32), gain_one, shift_one, normed)
    gather_one = GatherRows(p, normed, rows_here).start()
    gather_cot = GatherRows(p, own_cot, rows_cot)
    stores = [p.copy(vectors_here, vectors_full).start()]

    thirds[0].spread(1)
    thirds[2].fetch().spread(0)
    thirds[1].spread(1)
    out.fetch().spread(0)
    thirds[0].relay()
    thirds[2].spread(1)
    gate.fetch()
    thirds[1].relay()
    out.spread(1)
    gate.spread(0)
    thirds[2].relay()
    gather_one.relay()
    gather_cot.start()
    up.fetch()
    own_biases.wait()
    far_biases.arrived(p.core == 1)
    far_biases.left()

    def project(j):
        thirds[j].finish()
        stores.append(p.copy(proj_here.at[j], proj_full.at[j]).start())

        @pl.loop(0, 4)
        def _(index):
            rows = pl.ds(pl.multiple_of(index * HALF, HALF), HALF)
            half, target = swapped_half(index, late)
            positions = pl.ds(pl.multiple_of(half * HALF, HALF), HALF)
            pre = dot(rows_here[rows], proj_here[j], (1, 0)) + biases_here[j : j + 1]
            for k in range(pre.shape[1] // 128):
                lanes = slice(k * 128, (k + 1) * 128)
                part = pre[:, lanes]
                if j < 2:
                    part = turned(part, tables, positions, 1.0)
                if j == 0:
                    part = part * (1.0 / math.sqrt(HD))
                heads[j, target, lanes] = part.astype(heads.dtype)

    gather_one.finish()
    rows_store = p.copy(rows_here, rows_one).start()
    project(0)
    gate.spread(1)
    project(1)
    out.relay()
    project(2)
    up.spread(0)
    gather_cot.relay()
    stores.append(p.copy(heads, heads_out).start())
    attend_pair(heads, mixed, late)
    out.finish()
    stores += [p.copy(out_here, out_full).start(), p.copy(mixed, mixed_out).start()]

    def out_rows(target, offset):
        def part(rows):
            target[rows] = dot(mixed[shifted(rows, offset)], out_here[...], (1, 0)).astype(target.dtype)

        return part

    scatter = ScatterRows(p, far, near, got, got_beside)
    tiles(2 * count, 256, out_rows(far, 2 * count))
    scatter.start()
    tiles(2 * count, 256, out_rows(near, 0))
    scatter.relay()
    down.fetch()
    gate.relay()
    up.spread(1)
    down.spread(0)
    scatter.arrived()
    gain_two, shift_two = vectors_here[2:3], vectors_here[3:4]

    def norm(rows):
        value = own[rows].astype(jnp.float32) + scatter.total(rows)
        total[rows] = value
        normed[rows] = norm_rows(value, gain_two, shift_two)[0].astype(normed.dtype)

    tiles(count, CHUNK, norm)
    gather = GatherRows(p, normed, rows_later).start()
    stores.append(p.copy(total, middle).start())
    gather_cot.finish()
    gather.relay()
    up.relay()
    down.spread(1)
    gate.finish()
    gather.finish()
    stores.append(p.copy(rows_later, rows_two).start())
    gate_store = p.copy(gu_here.at[0], gu_full.at[0]).start()
    rows_store.wait()
    cot_load = p.copy(rows_cot, rows_here).start()

    def gate_rows(rows):
        gate_wide[rows] = dot(rows_later[rows], gu_here[0], (1, 0))

    tiles(4 * count, 256, gate_rows)
    up.finish()
    up_store = p.copy(gu_here.at[1], gu_full.at[1]).start()

    def up_rows(rows):
        wide_up = dot(rows_later[rows], gu_here[1], (1, 0))
        wide_gate = gate_wide[rows]
        hidden[rows] = (wide_gate * jax.nn.sigmoid(wide_gate) * wide_up).astype(hidden.dtype)
        gate_act[rows] = wide_gate.astype(gate_act.dtype)
        up_act[rows] = wide_up.astype(up_act.dtype)

    tiles(2 * count, 256, up_rows)
    down.relay()
    tiles(2 * count, 256, lambda rows: up_rows(shifted(rows, 2 * count)))
    stores.append(p.copy(hidden, hidden_out).start())
    stores.append(p.copy(gate_act, gate_out).start())
    stores.append(p.copy(up_act, up_out).start())
    cot_load.wait()
    gate_store.wait()
    gate.left()
    quarter = down_parts.shape[2]
    for k in range(4):
        if k == 2:
            up_store.wait()
            up.left()
        columns = pl.ds((k % 2) * quarter, quarter)
        part = gu_here.at[k // 2, pl.ds(0, hidden.shape[1]), columns]
        part[...] = dot(hidden[...], rows_here[:, pl.ds(k * quarter, quarter)], (0, 0)).astype(part.dtype)
        stores.append(p.copy(part, down_parts.at[k]).start())
    down.finish()
    for weight in (*thirds, out, down):
        weight.left()
    for sent in vector_sends:
        sent.left()
    scatter.finish()
    wait_all(stores)


def norm_back_rows(value, incoming, gain):
    average = jnp.mean(value, axis=-1, keepdims=True)
    centred = value - average
    inverse = lax.rsqrt(jnp.mean(centred * centred, axis=-1, keepdims=True) + EPSILON)
    unit = centred * inverse
    scaled = incoming * gain
    inner = (
        scaled
        - jnp.mean(scaled, axis=-1, keepdims=True)
        - unit * jnp.mean(scaled * unit, axis=-1, keepdims=True)
    )
    return inner * inverse, incoming * unit


def fold(array):
    return jnp.sum(array.reshape(array.shape[0] // 8, 8, array.shape[1]), axis=0)


def back_kernel(
    hidden_in, gate_in, up_in, cot_rows, rows_two, gu_full, down_full, down_parts, middle, vectors,
    out_half, grad_middle, rows_branch, sums, down_owned, gate_sums, up_parts,
    hidden, gate_act, up_act, cot, rows_here, gate, up, down, value, near, got, got_beside,
    got_out, gain_sum, shift_sum, staging,
    down_got, down_last, down_home, down_result, gate_got, gate_last,
    send_sems, recv_sems, local_sems,
):
    p = Place(send_sems, recv_sems, local_sems)
    count, width = value.shape
    hidden_width = hidden.shape[1]
    quarter = width // 4
    first_loads = [
        p.copy(cot_rows, cot).start(), p.copy(down_full, down).start(),
        p.copy(gate_in, gate_act).start(), p.copy(up_in, up_act).start(),
    ]
    p.greet()
    down_sum = ScatterWeight(
        p, [down_parts.at[0], down_parts.at[1]], [staging.at[0], staging.at[1]], False,
        down_got, down_last, down_home, down_result,
    )
    gate_quarters = [gate.at[pl.ds(k * quarter, quarter)] for k in range(4)]
    gate_sum = ScatterWeight(
        p, gate_quarters[:2], gate_quarters[2:], True, gate_got, gate_last, None, None
    )
    far = cot.at[pl.ds(2 * count, 2 * count)]
    scatter = ScatterRows(p, far, near, got, got_beside)
    near_out = rows_here.at[pl.ds(0, 2 * count)]
    out_scatter = ScatterRows(p, far, near_out, got_out, None)

    down_sum.start()
    wait_all(first_loads)
    third_loads = [p.copy(gu_full.at[0], gate).start(), p.copy(gu_full.at[1], up).start()]

    def hidden_back(rows):
        grad = dot(cot[rows], down[...], (1, 1))
        gate_value = gate_act[rows].astype(jnp.float32)
        up_value = up_act[rows].astype(jnp.float32)
        sigmoid = jax.nn.sigmoid(gate_value)
        scaled = grad * sigmoid
        up_act[rows] = (scaled * gate_value).astype(up_act.dtype)
        gate_act[rows] = (
            scaled * up_value * (1.0 + gate_value * (1.0 - sigmoid))
        ).astype(gate_act.dtype)

    tiles(4 * count, 256, hidden_back)
    wait_all(third_loads)
    last_loads = [
        p.copy(rows_two, rows_here).start(), p.copy(middle, value).start(),
        p.copy(hidden_in, hidden).start(),
    ]
    down_sum.load([down_parts.at[2], down_parts.at[3]])

    def second_rows(target, offset):
        def part(rows):
            here = shifted(rows, offset)
            target[rows] = (
                dot(gate_act[here], gate[...], (1, 1)) + dot(up_act[here], up[...], (1, 1))
            ).astype(target.dtype)

        return part

    tiles(2 * count, 256, second_rows(far, 2 * count))
    scatter.start()
    tiles(2 * count, 256, second_rows(near, 0))
    scatter.relay()
    wait_all(last_loads)

    def weight_part(target, grads, k):
        here = pl.ds(k * quarter, quarter)
        target[here] = dot(rows_here[:, here], grads[...], (0, 0)).astype(target.dtype)

    weight_part(gate, gate_act, 0)
    weight_part(gate, gate_act, 1)
    down_sum.relay()
    weight_part(gate, gate_act, 2)
    weight_part(gate, gate_act, 3)

    def out_rows(target, offset):
        def part(rows):
            target[rows] = dot(hidden[shifted(rows, offset)], down[...], (1, 0)).astype(target.dtype)

        return part

    for k in range(4):
        weight_part(up, up_act, k)
    stores = [p.copy(up, up_parts).start()]
    scatter.sibling.left()
    tiles(2 * count, 256, out_rows(far, 2 * count))
    out_scatter.start()
    down_sum.settle()
    gate_sum.start()
    tiles(2 * count, 256, out_rows(near_out, 0))
    scatter.arrived()
    gain = vectors[2:3]
    gain_sum[...] = jnp.zeros_like(gain_sum)
    shift_sum[...] = jnp.zeros_like(shift_sum)

    def middle_back(rows):
        incoming = scatter.total(rows)
        back, product = norm_back_rows(value[rows], incoming, gain)
        gain_sum[...] += fold(product)
        shift_sum[...] += fold(incoming)
        grad = cot[rows].astype(jnp.float32) + back
        value[rows] = grad
        cot[rows] = grad.astype(cot.dtype)

    tiles(count, CHUNK, middle_back)
    gather = GatherRows(p, cot.at[pl.ds(0, count)], rows_branch).start()
    stores.append(p.copy(value, grad_middle).start())
    gain_sum[0:1] = jnp.sum(gain_sum[...], axis=0, keepdims=True)
    gain_sum[1:2] = jnp.sum(shift_sum[...], axis=0, keepdims=True)
    stores.append(p.copy(gain_sum, sums).start())
    scatter.beside.left()
    out_scatter.sibling.arrived()
    combine(near_out, [near_out, got_out], 32)
    stores.append(p.copy(near_out, out_half).start())
    gather.relay()
    gate_sum.relay()
    down_sum.finish(down_owned)
    gate_sum.gather()
    for k in (0, 1):
        stores.append(p.copy(gate_sum.half(gate_quarters[2 + k], 0), gate_sums.at[k]).start())
    gate_sum.left()
    down_sum.stored()
    gather.finish()
    out_scatter.sibling.left()
    wait_all(stores)


def last_kernel(
    rows_branch, out_full, heads_in, mixed_in, rows_one, proj_full, inputs, vectors,
    turns, grad_middle, sums, up_parts, gate_sums, out_half, middle,
    outputs, input_grads, proj_owned, out_owned, vector_grads, bias_grad, gu_owned,
    branch, out_here, heads, mixed, grad_mixed, grad_pre, rows_here, proj_here, out_send,
    own, got, got_beside, result, all_sums, shift_sum, vector_got, vector_total, z_got,
    bias_here, bias_got, turns_here, got_out, gate_home, gate_even, up_result, out_result, third_result, *rest,
):
    weight_refs = [rest[4 * k : 4 * k + 4] for k in range(5)]
    p = Place(*rest[20:])
    count, width = own.shape
    quarter = width // 4
    late = lax.rem(p.tensor, 2)
    tables = [turns_here.at[k] for k in range(3)]
    first, second = p.core == 0, p.core == 1
    first_loads = [p.copy(rows_branch, branch).start(), p.copy(out_full, out_here).start()]
    p.greet()

    def weight_sum(send, rows, refs, total):
        keep, got_quarters, last, home = refs
        return ScatterWeight(
            p, send, [keep.at[0], keep.at[1]], rows, got_quarters, last, home, total
        )

    up_quarters = [up_parts.at[pl.ds(k * quarter, quarter)] for k in range(4)]
    up = weight_sum(up_quarters[:2], True, weight_refs[0], up_result).start()
    gate = HomeSum(p, gate_sums.at[0], gate_sums.at[1], gate_even, gate_home, up_result).start()
    out = weight_sum([out_send.at[0], out_send.at[1]], False, weight_refs[1], out_result)
    proj_send = [[heads.at[j, pl.ds(k * quarter, quarter)] for k in (0, 1)] for j in range(3)]
    thirds = [
        weight_sum(proj_send[j], True, weight_refs[2 + j], third_result.at[j]) for j in range(3)
    ]
    out_beside = p.send(out_half.at[pl.ds(count, count)], got_out, p.at(near=1)).start()
    out_loads = [p.copy(out_half.at[pl.ds(0, count)], own).start(), p.copy(middle, result).start()]
    wait_all(first_loads)
    mixed_load = p.copy(mixed_in, mixed).start()
    head_load = p.copy(heads_in, heads).start()
    out_loads.append(p.copy(turns, turns_here).start())

    @pl.loop(0, 4)
    def _(index):
        rows = pl.ds(pl.multiple_of(index * HALF, HALF), HALF)
        _, target = swapped_half(index, late)
        grad_mixed[target] = dot(branch[rows], out_here[...], (1, 1)).astype(grad_mixed.dtype)

    mixed_load.wait()

    def out_part(k):
        target = out_send.at[k] if k < 2 else weight_refs[1][0].at[k - 2]
        target[...] = dot(
            mixed[...], branch[:, pl.ds(k * quarter, quarter)], (0, 0)
        ).astype(target.dtype)

    for k in range(4):
        out_part(k)
    head_load.wait()
    later_loads = [p.copy(proj_full, proj_here).start(), p.copy(rows_one, rows_here).start()]
    wait_all(out_loads)
    gate_load = p.copy(gate_sums.at[0], gate_even).start()
    up.load(up_quarters[2:])
    attend_pair_back(heads, grad_mixed, grad_pre, tables, late)
    wait_all(later_loads)
    up.relay()
    near, far = branch.at[pl.ds(0, 2 * count)], branch.at[pl.ds(2 * count, 2 * count)]
    scatter = ScatterRows(p, far, near, got, got_beside)

    def term_rows(target, offset):
        def part(rows):
            here = shifted(rows, offset)
            total = dot(grad_pre[0, here], proj_here[0], (1, 1))
            for j in (1, 2):
                total = total + dot(grad_pre[j, here], proj_here[j], (1, 1))
            target[rows] = total.astype(target.dtype)

        return part

    def proj_part(j, k):
        target = proj_send[j][k] if k < 2 else weight_refs[2 + j][0].at[k - 2]
        target[...] = dot(
            rows_here[:, pl.ds(k * quarter, quarter)], grad_pre[j], (0, 0)
        ).astype(target.dtype)

    tiles(2 * count, 256, term_rows(far, 2 * count))
    scatter.start()
    tiles(2 * count, 256, term_rows(near, 0))
    scatter.relay()
    out_beside.arrived()

    def out_total(rows):
        total = result[rows] + own[rows].astype(jnp.float32) + got_out[rows].astype(jnp.float32)
        own[rows] = total.astype(own.dtype)

    tiles(count, CHUNK, out_total)
    stores = store_natural(p, own, outputs)
    for j in range(3):
        proj_part(j, 0)
        proj_part(j, 1)
    up.settle()
    out.start()
    thirds[0].start()
    thirds[1].start()
    wait_all(stores)
    loads = load_local(p, inputs, own)
    loads.append(p.copy(grad_middle, result).start())
    for j in range(3):
        proj_part(j, 2)
        proj_part(j, 3)
    out.relay()

    bias_here[...] = jnp.zeros_like(bias_here)
    for j in range(3):
        def bias_rows(rows):
            bias_here[j : j + 1] += jnp.sum(
                grad_pre[j, rows].astype(jnp.float32), axis=0, keepdims=True
            )

        tiles(4 * count, 256, bias_rows)
    bias_x = p.send(bias_here, bias_got.at[0], p.at(x=1)).start()
    bias_x.arrived()
    bias_x.left()
    bias_here[...] += bias_got[0]
    bias_y = p.send(bias_here, bias_got.at[1], p.at(y=1)).start()
    gate_load.wait()
    gate.finish(gu_owned.at[0])
    bias_y.arrived()
    bias_y.left()
    bias_here[...] += bias_got[1]
    near_sem, far_sem = p.take("recv"), p.take("recv")
    bias_home = [
        p.send(bias_here, bias_got.at[2], p.at(core=1), near_sem, first).start(),
        p.send(bias_here, bias_got.at[2], p.at(core=1, far=1), near_sem, second).start(),
        p.send(bias_here, bias_got.at[3], p.at(far=1), far_sem, second).start(),
    ]
    thirds[0].relay()
    thirds[2].start()
    out.settle()
    wait_all(loads)
    scatter.arrived()
    gain = vectors[0:1]
    all_sums[...] = jnp.zeros_like(all_sums)
    shift_sum[...] = jnp.zeros_like(shift_sum)

    def first_back(rows):
        incoming = scatter.total(rows)
        back, product = norm_back_rows(own[rows].astype(jnp.float32), incoming, gain)
        all_sums[...] += fold(product)
        shift_sum[...] += fold(incoming)
        result[rows] = result[rows] + back

    tiles(count, CHUNK, first_back)
    stores = store_natural(p, result, input_grads)
    all_sums[0:1] = jnp.sum(all_sums[...], axis=0, keepdims=True)
    all_sums[1:2] = jnp.sum(shift_sum[...], axis=0, keepdims=True)
    all_sums[2:4] = sums[0:2]
    slots = {key: j for j, key in enumerate(ORDER)}
    vector_sends = []
    for dy in (0, 1):
        for dx in (0, 1):
            for core in (0, 1):
                if not (dy or dx or core):
                    continue
                straight, crossed = slots[(dy, dx, core)], slots[(dy, dx, 1 - core)]
                slot = straight + p.core * (crossed - straight)
                columns = pl.ds(pl.multiple_of(slot * EIGHTH, EIGHTH), EIGHTH)
                vector_sends.append(
                    p.send(
                        all_sums.at[:, columns], vector_got.at[len(vector_sends)],
                        p.at(x=dx, y=dy, core=core),
                    ).start()
                )
    thirds[1].relay()
    thirds[0].settle()
    own_slot = slots[(0, 0, 0)] + p.core * (slots[(0, 0, 1)] - slots[(0, 0, 0)])
    total = all_sums[:, pl.ds(pl.multiple_of(own_slot * EIGHTH, EIGHTH), EIGHTH)]
    for k, sent in enumerate(vector_sends):
        sent.arrived()
        total = total + vector_got[k]
    vector_total[0] = total
    z_near = p.send(vector_total.at[0], z_got.at[0], p.at(near=1)).start()
    thirds[2].relay()
    thirds[1].settle()
    z_near.arrived()
    vector_total[1] = vector_total[0] + z_got[0]
    z_far = p.send(vector_total.at[1], z_got.at[1], p.at(far=1)).start()
    thirds[2].settle()
    z_far.arrived()
    z_near.left()
    z_far.left()
    vector_total[0] = vector_total[1] + z_got[1]
    vector_store = p.copy(vector_total.at[0], vector_grads).start()
    bias_home[0].arrived()
    bias_home[2].arrived(second)
    for sent in bias_home:
        sent.left()
    pl.when(second)(lambda: combine(bias_got.at[2], [bias_got.at[2], bias_got.at[3]], 8))
    pl.when(first)(lambda: combine(bias_got.at[2], [bias_got.at[2], bias_here], 8))
    bias_store = p.copy(bias_got.at[2], bias_grad).start()
    gate.stored()
    up.finish(gu_owned.at[1])
    out.finish(out_owned)
    for j in range(3):
        thirds[j].finish(proj_owned.at[j])
    for weight in (up, out, *thirds):
        weight.stored()
    scatter.finish()
    for sent in vector_sends:
        sent.left()
    out_beside.left()
    wait_all(stores)
    vector_store.wait()
    bias_store.wait()


def call(body, name, collective, inputs, in_specs, outs, scratch, counts):
    bf16_bytes = sum(math.prod(o.shape) * o.dtype.itemsize for o in outs)
    return pl.pallas_call(
        body,
        out_shape=outs,
        in_specs=in_specs,
        out_specs=[ANY] * len(outs),
        scratch_shapes=[
            *scratch,
            pltpu.SemaphoreType.DMA((counts[0],)),
            pltpu.SemaphoreType.DMA((counts[1],)),
            pltpu.SemaphoreType.DMA((counts[2],)),
        ],
        compiler_params=pltpu.CompilerParams(
            collective_id=collective, has_side_effects=True, vmem_limit_bytes=VMEM_BYTES
        ),
        cost_estimate=pl.CostEstimate(
            flops=0, bytes_accessed=2 * bf16_bytes, transcendentals=0
        ),
        name=name,
    )(*inputs)


def bf16(*shape):
    return jax.ShapeDtypeStruct(shape, jnp.bfloat16)


def f32(*shape):
    return jax.ShapeDtypeStruct(shape, jnp.float32)


def held(shape_struct):
    return pltpu.VMEM(shape_struct.shape, shape_struct.dtype)


def weight_scratch(quarter, eighth):
    return [
        held(bf16(2, *quarter)), held(bf16(2, *quarter)), held(bf16(2, *eighth)),
        held(bf16(2, *eighth)),
    ]


WHOLE = pl.BlockSpec(memory_space=pltpu.VMEM)
EIGHTH = 256


def local_pairs(
    inputs,
    gain_first,
    shift_first,
    projections,
    biases,
    output_weight,
    gain_second,
    shift_second,
    gate_up,
    down_weight,
    cotangent,
):
    count, width = inputs.shape
    rows = 4 * count
    heads_width = output_weight.shape[0]
    hidden_width = down_weight.shape[0]
    cosine, sine = angle_tables()
    rest = ((0, 0), (0, HD - ROTARY))
    turns = jnp.stack([
        jnp.tile(jnp.pad(table, rest, constant_values=fill), (1, 128 // HD))
        for table, fill in (
            (jnp.concatenate([cosine, cosine], axis=1), 1.0),
            (jnp.concatenate([-sine, jnp.zeros_like(sine)], axis=1), 0.0),
            (jnp.concatenate([jnp.zeros_like(sine), sine], axis=1), 0.0),
        )
    ])
    wide = bf16(rows, width)
    inner = bf16(rows, hidden_width)
    own = bf16(count, width)
    half_rows = bf16(2 * count, width)
    (
        proj_full, out_full, gu_full, down_full, vectors, gathered_one, gathered_cot, heads, mixed_rows,
        middle, gathered_two, hidden, gate_act, up_act, down_parts,
    ) = call(
        forward_kernel, "forward", 1,
        (
            inputs, cotangent,
            jnp.concatenate([gain_first, shift_first, gain_second, shift_second]).reshape(4, -1),
            biases, turns,
            projections, output_weight, gate_up, down_weight,
        ),
        [ANY] * 2 + [WHOLE] * 2 + [ANY] * 5,
        [
            bf16(3, width, heads_width), bf16(heads_width, width), bf16(2, width, hidden_width),
            bf16(hidden_width, width), f32(8, width), wide, wide, bf16(3, rows, heads_width),
            bf16(rows, heads_width), f32(count, width), wide, inner, inner, inner,
            bf16(4, hidden_width, 2 * EIGHTH),
        ],
        [
            held(own), held(own), held(own), held(f32(8, width)), held(f32(8, heads_width)),
            held(bf16(3, width, heads_width)), held(bf16(heads_width, width)), held(wide),
            held(bf16(3, rows, heads_width)), held(bf16(rows, heads_width)),
            held(half_rows), held(half_rows), held(half_rows), held(own), held(f32(count, width)),
            held(wide), held(bf16(2, width, hidden_width)), held(f32(rows, hidden_width)),
            held(inner), held(inner), held(inner), held(f32(8, EIGHTH)), held(f32(8, heads_width)),
            held(f32(*turns.shape)),
        ],
        (128, 96, 64),
    )

    by_rows = ((2 * EIGHTH, hidden_width), (EIGHTH, hidden_width))
    by_columns = ((hidden_width, 2 * EIGHTH), (hidden_width, EIGHTH))
    (
        out_half, grad_middle, gathered_branch, sums, down_owned, gate_sums, up_parts,
    ) = call(
        back_kernel, "backward_first", 2,
        (
            hidden, gate_act, up_act, gathered_cot, gathered_two, gu_full, down_full, down_parts,
            middle, vectors,
        ),
        [ANY] * 9 + [WHOLE],
        [
            half_rows, f32(count, width), wide, f32(8, width), f32(hidden_width, EIGHTH),
            bf16(2, EIGHTH, hidden_width), bf16(width, hidden_width),
        ],
        [
            held(inner), held(inner), held(inner), held(wide), held(wide),
            held(bf16(width, hidden_width)), held(bf16(width, hidden_width)),
            held(bf16(hidden_width, width)), held(f32(count, width)),
            held(half_rows), held(half_rows), held(own), held(half_rows),
            held(f32(8, width)), held(f32(8, width)), held(bf16(2, hidden_width, 2 * EIGHTH)),
            *weight_scratch(*by_columns)[1:], held(f32(hidden_width, EIGHTH)),
            *weight_scratch(*by_rows)[1:3],
        ],
        (64, 64, 48),
    )
    third = ((2 * EIGHTH, heads_width), (EIGHTH, heads_width))
    outputs, input_grads, proj_owned, out_owned, vector_grads, bias_grad, gu_owned = call(
        last_kernel, "backward_last", 3,
        (
            gathered_branch, out_full, heads, mixed_rows, gathered_one, proj_full, inputs, vectors,
            turns, grad_middle, sums, up_parts, gate_sums,
            out_half, middle,
        ),
        [ANY] * 7 + [WHOLE] + [ANY] * 2 + [WHOLE] + [ANY] * 4,
        [
            own, f32(count, width), f32(3, EIGHTH, heads_width), f32(heads_width, EIGHTH),
            f32(8, EIGHTH), f32(8, heads_width), f32(2, EIGHTH, hidden_width),
        ],
        [
            held(wide), held(bf16(heads_width, width)), held(bf16(3, rows, heads_width)),
            held(bf16(rows, heads_width)), held(bf16(rows, heads_width)),
            held(bf16(3, rows, heads_width)), held(wide), held(bf16(3, width, heads_width)),
            held(bf16(2, heads_width, 2 * EIGHTH)),
            held(own), held(half_rows), held(own), held(f32(count, width)),
            held(f32(8, width)), held(f32(8, width)),
            held(f32(7, 8, EIGHTH)), held(f32(2, 8, EIGHTH)), held(f32(2, 8, EIGHTH)),
            held(f32(8, heads_width)), held(f32(4, 8, heads_width)), held(f32(*turns.shape)),
            held(own),
            held(bf16(2, EIGHTH, hidden_width)), held(bf16(EIGHTH, hidden_width)),
            held(f32(EIGHTH, hidden_width)), held(f32(heads_width, EIGHTH)),
            held(f32(3, EIGHTH, heads_width)),
            *weight_scratch(*by_rows),
            *weight_scratch((heads_width, 2 * EIGHTH), (heads_width, EIGHTH)),
            *weight_scratch(*third), *weight_scratch(*third), *weight_scratch(*third),
        ],
        (64, 64, 48),
    )
    return (
        outputs,
        input_grads,
        vector_grads[0],
        vector_grads[1],
        proj_owned,
        bias_grad[:3],
        out_owned,
        vector_grads[2],
        vector_grads[3],
        gu_owned,
        down_owned,
    )


def solution(mesh):
    whole_pairs = dict(mesh.shape) == {"dp": 8, "tensor": 4}
    return jax.shard_map(
        local_pairs if whole_pairs else local,
        mesh=mesh,
        in_specs=(
            P(("dp", "tensor"), None),
            P("dp"),
            P("dp"),
            P(None, "dp", "tensor"),
            P(None, "tensor"),
            P("tensor", "dp"),
            P("dp"),
            P("dp"),
            P(None, "dp", "tensor"),
            P("tensor", "dp"),
            P(("dp", "tensor"), None),
        ),
        out_specs=(
            P(("dp", "tensor"), None),
            P(("dp", "tensor"), None),
            P("dp"),
            P("dp"),
            P(None, "dp", "tensor"),
            P(None, "tensor"),
            P("tensor", "dp"),
            P("dp"),
            P("dp"),
            P(None, "dp", "tensor"),
            P("tensor", "dp"),
        ),
        check_vma=False,
    )
```

```python
import math

import jax
import jax.numpy as jnp
from jax import lax
from jax.experimental import pallas as pl
from jax.experimental.pallas import tpu as pltpu
from jax.sharding import PartitionSpec as P

HD = 64
ROTARY = 16
SEQ_LEN = 512


EPSILON = 1e-05
ANGLE_BASE = 10000.0
NEGATIVE = -1e30


def norm_rows(rows, gain, shift):
    average = jnp.mean(rows, axis=-1, keepdims=True)
    centred = rows - average
    inverse = lax.rsqrt(jnp.mean(centred * centred, axis=-1, keepdims=True) + EPSILON)
    unit_rows = centred * inverse
    return (unit_rows * gain + shift, unit_rows, inverse)


def norm_back(incoming, unit_rows, inverse, gain):
    scaled = incoming * gain
    inner = (
        scaled
        - jnp.mean(scaled, axis=-1, keepdims=True)
        - unit_rows * jnp.mean(scaled * unit_rows, axis=-1, keepdims=True)
    )
    return (inner * inverse, jnp.sum(incoming * unit_rows, axis=0), jnp.sum(incoming, axis=0))


def angle_tables():
    freqs = 1.0 / ANGLE_BASE ** (jnp.arange(0, ROTARY, 2).astype(jnp.float32) / ROTARY)
    angles = jnp.arange(SEQ_LEN).astype(jnp.float32)[:, None] * freqs[None, :]
    return (jnp.cos(angles), jnp.sin(angles))


def rotate(heads, cosine, sine, sign):
    half_rot = ROTARY // 2
    first = heads[..., :half_rot]
    latter = heads[..., half_rot:ROTARY]
    cos_part = cosine[:, None, :]
    sin_part = sine[:, None, :] * sign
    return jnp.concatenate(
        [
            first * cos_part - latter * sin_part,
            latter * cos_part + first * sin_part,
            heads[..., ROTARY:],
        ],
        axis=-1,
    )


def causal_scores(queries, key_rows, positions):
    scaling = 1.0 / math.sqrt(HD)
    scores = scaling * jnp.einsum(
        "qhd,khd->hqk", queries, key_rows, preferred_element_type=jnp.float32
    )
    causal = positions[:, None] >= positions[None, :]
    return jnp.where(causal[None], scores, NEGATIVE)


def attend_forward(pieces, positions):
    queries, key_rows, value_rows = pieces
    scores = causal_scores(queries, key_rows, positions)
    row_top = jnp.max(scores, axis=-1, keepdims=True)
    exponent = jnp.exp(scores - row_top)
    totals = jnp.sum(exponent, axis=-1, keepdims=True)
    weights = (exponent / totals).astype(jnp.bfloat16)
    mixed = jnp.einsum("hqk,khd->qhd", weights, value_rows, preferred_element_type=jnp.float32)
    return (mixed.astype(jnp.bfloat16), (row_top + jnp.log(totals))[..., 0])


def attend_back(pieces, positions):
    queries, key_rows, value_rows, grad_mixed, log_totals = pieces
    scaling = 1.0 / math.sqrt(HD)
    scores = causal_scores(queries, key_rows, positions)
    weights = jnp.exp(scores - log_totals[..., None])
    grad_values = jnp.einsum(
        "hqk,qhd->khd", weights.astype(jnp.bfloat16), grad_mixed, preferred_element_type=jnp.float32
    )
    grad_weights = jnp.einsum(
        "qhd,khd->hqk", grad_mixed, value_rows, preferred_element_type=jnp.float32
    )
    grad_scores = weights * (grad_weights - jnp.sum(weights * grad_weights, axis=-1, keepdims=True))
    grad_scores = grad_scores.astype(jnp.bfloat16)
    grad_queries = scaling * jnp.einsum(
        "hqk,khd->qhd", grad_scores, key_rows, preferred_element_type=jnp.float32
    )
    grad_keys = scaling * jnp.einsum(
        "hqk,qhd->khd", grad_scores, queries, preferred_element_type=jnp.float32
    )
    return (grad_queries, grad_keys, grad_values)


def scatter_sum(terms, axis, dimension):
    owned = lax.psum_scatter(
        terms.astype(jnp.bfloat16), axis, scatter_dimension=dimension, tiled=True
    )
    return owned.astype(jnp.float32)


def local(
    inputs,
    gain_first,
    shift_first,
    projections,
    biases,
    output_weight,
    gain_second,
    shift_second,
    gate_up,
    down_weight,
    cotangent,
):
    tensor_ways = lax.axis_size("tensor")
    row_count = inputs.shape[0]
    group_rows = row_count * tensor_ways
    sequences = group_rows // SEQ_LEN
    head_width = output_weight.shape[0]
    local_heads = head_width // HD
    head_shape = (sequences, SEQ_LEN, local_heads, HD)
    cosine, sine = angle_tables()
    positions = jnp.arange(SEQ_LEN)
    proj_full, out_full, gain_one, shift_one = (
        lax.all_gather(projections, "dp", axis=1, tiled=True),
        lax.all_gather(output_weight, "dp", axis=1, tiled=True),
        lax.all_gather(gain_first, "dp", axis=0, tiled=True),
        lax.all_gather(shift_first, "dp", axis=0, tiled=True),
    )
    gain_one = gain_one.astype(jnp.float32)
    residual = inputs.astype(jnp.float32)
    normed_one, unit_one, inverse_one = norm_rows(residual, gain_one, shift_one.astype(jnp.float32))
    gathered_one = lax.all_gather(normed_one.astype(jnp.bfloat16), "tensor", axis=0, tiled=True)
    pre_all = jnp.einsum("gd,jde->jge", gathered_one, proj_full, preferred_element_type=jnp.float32)
    pre_all = pre_all + biases.astype(jnp.float32)[:, None, :]
    queries = rotate(pre_all[0].reshape(head_shape), cosine, sine, 1.0).astype(jnp.bfloat16)
    key_rows = rotate(pre_all[1].reshape(head_shape), cosine, sine, 1.0).astype(jnp.bfloat16)
    value_rows = pre_all[2].reshape(head_shape).astype(jnp.bfloat16)
    mixed, log_totals = lax.map(
        lambda pieces: attend_forward(pieces, positions), (queries, key_rows, value_rows)
    )
    mixed_rows = mixed.reshape(group_rows, head_width)
    part = mixed_rows
    middle = residual + scatter_sum(
        jnp.dot(part, out_full, preferred_element_type=jnp.float32), "tensor", 0
    )
    gu_full, down_full, gain_two, shift_two = (
        lax.all_gather(gate_up, "dp", axis=1, tiled=True),
        lax.all_gather(down_weight, "dp", axis=1, tiled=True),
        lax.all_gather(gain_second, "dp", axis=0, tiled=True),
        lax.all_gather(shift_second, "dp", axis=0, tiled=True),
    )
    gain_two = gain_two.astype(jnp.float32)
    normed_two, unit_two, inverse_two = norm_rows(middle, gain_two, shift_two.astype(jnp.float32))
    gathered_two = lax.all_gather(normed_two.astype(jnp.bfloat16), "tensor", axis=0, tiled=True)
    gate_act = jnp.dot(gathered_two, gu_full[0], preferred_element_type=jnp.float32)
    up_act = jnp.dot(gathered_two, gu_full[1], preferred_element_type=jnp.float32)
    sigmoid_gate = jax.nn.sigmoid(gate_act)
    hidden = (gate_act * sigmoid_gate * up_act).astype(jnp.bfloat16)
    part = hidden
    outputs = (
        middle
        + scatter_sum(jnp.dot(part, down_full, preferred_element_type=jnp.float32), "tensor", 0)
    ).astype(jnp.bfloat16)
    gu_back, down_back, gain_two_back = (
        lax.all_gather(gate_up, "dp", axis=1, tiled=True),
        lax.all_gather(down_weight, "dp", axis=1, tiled=True),
        lax.all_gather(gain_second, "dp", axis=0, tiled=True),
    )
    gain_two_back = gain_two_back.astype(jnp.float32)
    gathered_cot = lax.all_gather(cotangent, "tensor", axis=0, tiled=True)
    grad_hidden = jnp.einsum(
        "gd,fd->gf", gathered_cot, down_back, preferred_element_type=jnp.float32
    )
    down_grad = jnp.einsum("gf,gd->fd", hidden, gathered_cot, preferred_element_type=jnp.float32)
    grad_up = (grad_hidden * gate_act * sigmoid_gate).astype(jnp.bfloat16)
    grad_gate = (
        grad_hidden * up_act * sigmoid_gate * (1.0 + gate_act * (1.0 - sigmoid_gate))
    ).astype(jnp.bfloat16)
    gu_grad = jnp.stack(
        [
            jnp.einsum("gd,gf->df", gathered_two, grad_gate, preferred_element_type=jnp.float32),
            jnp.einsum("gd,gf->df", gathered_two, grad_up, preferred_element_type=jnp.float32),
        ]
    )
    first_term = jnp.einsum("gf,df->gd", grad_gate, gu_back[0], preferred_element_type=jnp.float32)
    grad_second = scatter_sum(
        first_term
        + jnp.einsum("gf,df->gd", grad_up, gu_back[1], preferred_element_type=jnp.float32),
        "tensor",
        0,
    )
    gu_owned, down_owned = (
        scatter_sum(gu_grad, "dp", 1),
        scatter_sum(down_grad, "dp", 1),
    )
    grad_mid_norm, gain_two_part, shift_two_part = norm_back(
        grad_second, unit_two, inverse_two, gain_two_back
    )
    grad_middle = cotangent.astype(jnp.float32) + grad_mid_norm
    proj_back, out_back, gain_one_back = (
        lax.all_gather(projections, "dp", axis=1, tiled=True),
        lax.all_gather(output_weight, "dp", axis=1, tiled=True),
        lax.all_gather(gain_first, "dp", axis=0, tiled=True),
    )
    gain_one_back = gain_one_back.astype(jnp.float32)
    gathered_branch = lax.all_gather(grad_middle.astype(jnp.bfloat16), "tensor", axis=0, tiled=True)
    out_grad = jnp.einsum(
        "ge,gd->ed", mixed_rows, gathered_branch, preferred_element_type=jnp.float32
    )
    grad_mixed = jnp.einsum(
        "gd,ed->ge", gathered_branch, out_back, preferred_element_type=jnp.float32
    ).astype(jnp.bfloat16)
    grad_queries, grad_keys, grad_values = lax.map(
        lambda pieces: attend_back(pieces, positions),
        (queries, key_rows, value_rows, grad_mixed.reshape(head_shape), log_totals),
    )
    grad_queries = rotate(grad_queries, cosine, sine, -1.0)
    grad_keys = rotate(grad_keys, cosine, sine, -1.0)
    grad_pre = (
        jnp.stack([grad_queries, grad_keys, grad_values])
        .reshape(3, group_rows, head_width)
        .astype(jnp.bfloat16)
    )
    bias_part = jnp.sum(grad_pre, axis=1, dtype=jnp.float32)
    proj_grad = jnp.einsum(
        "gd,jge->jde", gathered_one, grad_pre, preferred_element_type=jnp.float32
    )
    part = grad_pre
    grad_normed = scatter_sum(
        jnp.einsum("jge,jde->gd", part, proj_back, preferred_element_type=jnp.float32),
        "tensor",
        0,
    )
    proj_owned, out_owned = (
        scatter_sum(proj_grad, "dp", 1),
        scatter_sum(out_grad, "dp", 1),
    )
    grad_in_norm, gain_one_part, shift_one_part = norm_back(
        grad_normed, unit_one, inverse_one, gain_one_back
    )
    input_grads = grad_middle + grad_in_norm
    one_hot = (jnp.arange(tensor_ways) == lax.axis_index("tensor")).astype(jnp.float32)
    spread_bias = (bias_part[:, None, :] * one_hot[None, :, None]).reshape(
        3, tensor_ways * head_width
    )
    summed = lax.psum(
        (gain_one_part, shift_one_part, gain_two_part, shift_two_part, spread_bias),
        ("dp", "tensor"),
    )
    own_width = gain_first.shape[0]
    own_offset = lax.axis_index("dp") * own_width

    def own_part(vector):
        return lax.dynamic_slice_in_dim(vector, own_offset, own_width, 0)

    bias_grad = jnp.sum(
        summed[4].reshape(3, tensor_ways, head_width) * one_hot[None, :, None], axis=1
    )
    return (
        outputs,
        input_grads,
        own_part(summed[0]),
        own_part(summed[1]),
        proj_owned,
        bias_grad,
        out_owned,
        own_part(summed[2]),
        own_part(summed[3]),
        gu_owned,
        down_owned,
    )


ORDER = ((1, 0, 0), (1, 1, 0), (0, 1, 1), (1, 1, 1), (0, 0, 0), (0, 1, 0), (0, 0, 1), (1, 0, 1))
EVEN_Y, EVEN_XY, ODD_X, ODD_XY, EVEN, EVEN_X, ODD, ODD_Y = range(8)
ANY = pl.BlockSpec(memory_space=pl.ANY)
VMEM_BYTES = 63 * 1024 * 1024


class Place:
    def __init__(self, send_sems, recv_sems, local_sems):
        self.dp, self.tensor = lax.axis_index("dp"), lax.axis_index("tensor")
        self.core = lax.rem(self.dp, 2)
        self.x = lax.rem(self.dp // 2, 2)
        self.y = self.dp // 4
        self.pools = {"send": send_sems, "recv": recv_sems, "local": local_sems}
        self.used = {"send": 0, "recv": 0, "local": 0}

    def take(self, kind):
        self.used[kind] += 1
        return self.pools[kind].at[self.used[kind] - 1]

    def at(self, x=0, y=0, core=0, near=0, far=0):
        dp = self.dp
        dp = dp + x * (2 - 4 * self.x) + y * (4 - 8 * self.y) + core * (1 - 2 * self.core)
        tensor = self.tensor
        tensor = tensor + near * (1 - 2 * lax.rem(tensor, 2)) + far * (3 - 2 * tensor)
        return (dp, tensor)

    def column(self, key):
        dy, dx, core = key
        y = self.y + dy * (1 - 2 * self.y)
        x = self.x + dx * (1 - 2 * self.x)
        return pl.multiple_of((y * 4 + x * 2 + core) * EIGHTH, EIGHTH)

    def greet(self):
        barrier = pltpu.get_barrier_semaphore()
        partners = [
            self.at(x=x, y=y, core=core)
            for x in (0, 1)
            for y in (0, 1)
            for core in (0, 1)
            if x or y or core
        ] + [self.at(near=1), self.at(far=1), self.at(far=1, core=1)]
        for partner in partners:
            pl.semaphore_signal(
                barrier, inc=1, device_id=partner, device_id_type=pl.DeviceIdType.MESH
            )
        pl.semaphore_wait(barrier, len(partners))

    def send(self, source, target, device, recv_sem=None, when=None):
        return Sent(
            pltpu.make_async_remote_copy(
                src_ref=source,
                dst_ref=target,
                send_sem=self.take("send"),
                recv_sem=self.take("recv") if recv_sem is None else recv_sem,
                device_id=device,
                device_id_type=pl.DeviceIdType.MESH,
            ),
            when,
        )

    def copy(self, source, target, when=None):
        return Copied(pltpu.make_async_copy(source, target, self.take("local")), when)


def guarded(when, action):
    if when is None:
        action()
    else:
        pl.when(when)(action)


class Sent:
    def __init__(self, copy, when):
        self.copy, self.when = copy, when

    def start(self):
        guarded(self.when, self.copy.start)
        return self

    def arrived(self, when=None):
        guarded(when, self.copy.wait_recv)

    def left(self):
        guarded(self.when, self.copy.wait_send)


class Copied:
    def __init__(self, copy, when):
        self.copy, self.when = copy, when

    def start(self):
        guarded(self.when, self.copy.start)
        return self

    def wait(self):
        guarded(self.when, self.copy.wait)


class GatherWeight:
    def __init__(self, place, shard, block):
        self.place, self.shard, self.block = place, shard, block
        self.spreads, self.arrivals = [], {}

    def fetch(self):
        p = self.place
        even, odd = self.block(EVEN), self.block(ODD)
        first, second = p.core == 0, p.core == 1
        self.own = p.copy(self.shard, even, first).start()
        even_sem, odd_sem = p.take("recv"), p.take("recv")
        self.to_far_even = p.send(self.shard, even, p.at(core=1, far=1), even_sem, first).start()
        self.to_sibling = p.send(self.shard, odd, p.at(core=1), odd_sem, second).start()
        self.to_far_odd = p.send(self.shard, odd, p.at(far=1), odd_sem, second).start()
        return self

    def spread(self, core):
        p, block = self.place, self.block
        here = p.core == core
        if core:
            self.to_far_even.arrived(here)
        self.to_sibling.arrived(here)
        even = block(EVEN) if core else self.shard
        routes = (
            (even, EVEN_X, p.at(x=1)), (block(ODD), ODD_Y, p.at(y=1)),
            (block(ODD), ODD_X, p.at(x=1)), (even, EVEN_Y, p.at(y=1)),
        )
        for source, target, device in routes:
            if target not in self.arrivals:
                self.arrivals[target] = p.take("recv")
            self.spreads.append(
                p.send(source, block(target), device, self.arrivals[target], here).start()
            )
        return self

    def relay(self):
        p, block = self.place, self.block
        even_x, odd_y, self.odd_x, self.even_y = self.spreads[:4]
        even_x.arrived()
        self.even_xy = p.send(block(EVEN_X), block(EVEN_XY), p.at(y=1)).start()
        odd_y.arrived()
        self.odd_xy = p.send(block(ODD_Y), block(ODD_XY), p.at(x=1)).start()
        return self

    def finish(self):
        self.own.wait()
        for copy in (self.odd_x, self.even_y, self.even_xy, self.odd_xy):
            copy.arrived()

    def left(self):
        for copy in (
            *self.spreads, self.even_xy, self.odd_xy,
            self.to_far_even, self.to_sibling, self.to_far_odd,
        ):
            copy.left()


class GatherRows:
    def __init__(self, place, own, rows):
        self.place, self.own, self.rows = place, own, rows
        self.count = own.shape[0]

    def slot(self, k):
        return self.rows.at[pl.ds(k * self.count, self.count)]

    def start(self):
        p = self.place
        self.beside = p.send(self.own, self.slot(1), p.at(near=1)).start()
        self.sibling = p.send(self.own, self.slot(2), p.at(core=1)).start()
        self.here = p.copy(self.own, self.slot(0)).start()
        return self

    def relay(self):
        p = self.place
        self.beside.arrived()
        self.across = p.send(self.slot(1), self.slot(3), p.at(core=1)).start()
        return self

    def finish(self):
        self.sibling.arrived()
        self.across.arrived()
        self.here.wait()
        for copy in (self.beside, self.sibling, self.across):
            copy.left()


def combine(target, terms, chunk):
    @pl.loop(0, target.shape[0] // chunk)
    def _(i):
        rows = pl.ds(pl.multiple_of(i * chunk, chunk), chunk)
        total = terms[0][rows].astype(jnp.float32)
        for term in terms[1:]:
            total = total + term[rows].astype(jnp.float32)
        target[rows] = total.astype(target.dtype)


class ScatterRows:
    def __init__(self, place, far, near, got, got_beside):
        self.place, self.far, self.near = place, far, near
        self.got, self.got_beside = got, got_beside
        self.count = near.shape[0] // 2

    def start(self):
        self.sibling = self.place.send(self.far, self.got, self.place.at(core=1)).start()
        return self

    def relay(self):
        p, n = self.place, self.count
        self.sibling.arrived()
        late = pl.ds(n, n)
        combine(self.near.at[late], [self.near.at[late], self.got.at[late]], 32)
        self.beside = p.send(self.near.at[late], self.got_beside, p.at(near=1)).start()
        return self

    def total(self, rows):
        return (
            self.near[rows].astype(jnp.float32)
            + self.got[rows].astype(jnp.float32)
            + self.got_beside[rows].astype(jnp.float32)
        )

    def arrived(self):
        self.beside.arrived()

    def finish(self):
        self.sibling.left()
        self.beside.left()


class ScatterWeight:
    def __init__(self, place, send, keep, rows, got, last, home, result):
        self.place, self.parts, self.keep, self.rows = place, send, keep, rows
        self.got, self.last, self.home, self.result = got, last, home, result
        self.loads = []

    def half(self, ref, k):
        if self.rows:
            size = ref.shape[0] // 2
            return ref.at[pl.ds(k * size, size)]
        size = ref.shape[1] // 2
        return ref.at[:, pl.ds(k * size, size)]

    def load(self, sources):
        self.loads = [self.place.copy(a, b).start() for a, b in zip(sources, self.keep)]
        return self

    def start_even(self):
        p = self.place
        self.even = p.send(self.parts[0], self.got.at[0], p.at(y=1)).start()
        return self

    def start_odd(self):
        p = self.place
        self.odd = p.send(self.parts[1], self.got.at[1], p.at(x=1)).start()
        return self

    def start(self):
        return self.start_even().start_odd()

    def relay(self):
        p = self.place
        wait_all(self.loads)
        self.second = []
        for k, arrival in enumerate((self.even, self.odd)):
            arrival.arrived()
            there = self.half(self.keep[k], 1)
            combine(there, [there, self.half(self.got.at[k], 1)], 64)
            device = p.at(x=1) if k == 0 else p.at(y=1)
            self.second.append(p.send(there, self.last.at[k], device).start())
        return self

    def gather(self):
        for k in (1, 0):
            self.second[k].arrived()
            here = self.half(self.keep[k], 0)
            combine(here, [here, self.half(self.got.at[k], 0), self.last.at[k]], 64)
        return self

    def settle(self):
        self.gather()
        even, odd = self.half(self.keep[0], 0), self.half(self.keep[1], 0)
        self.way_home = HomeSum(self.place, even, odd, even, self.home, self.result).start()
        return self

    def finish(self, output):
        self.way_home.finish(output)
        self.left()

    def left(self):
        for copy in (self.even, self.odd, *self.second):
            copy.left()

    def stored(self):
        self.way_home.stored()


class HomeSum:
    def __init__(self, place, even, odd, here, home, result):
        self.place, self.even, self.odd, self.here = place, even, odd, here
        self.home, self.result = home, result

    def start(self):
        p = self.place
        first, second = p.core == 0, p.core == 1
        near_sem, far_sem = p.take("recv"), p.take("recv")
        home = self.home
        self.to_sibling = p.send(self.odd, home.at[0], p.at(core=1), near_sem, first).start()
        self.to_first = p.send(self.even, home.at[0], p.at(core=1, far=1), near_sem, second).start()
        self.to_far = p.send(self.odd, home.at[1], p.at(far=1), far_sem, second).start()
        return self

    def finish(self, output):
        p, home = self.place, self.home
        first, second = p.core == 0, p.core == 1
        self.to_sibling.arrived()
        self.to_far.arrived(second)
        pl.when(first)(lambda: combine(self.result, [self.here, home.at[0]], 64))
        pl.when(second)(lambda: combine(self.result, [home.at[0], home.at[1]], 64))
        self.store = p.copy(self.result, output).start()
        for copy in (self.to_sibling, self.to_first, self.to_far):
            copy.left()

    def stored(self):
        self.store.wait()


def load_local(place, source, target):
    return [
        place.copy(
            source.at[:, pl.ds(place.column(key), EIGHTH)], target.at[:, pl.ds(j * EIGHTH, EIGHTH)]
        ).start()
        for j, key in enumerate(ORDER)
    ]


def store_natural(place, source, target):
    return [
        place.copy(
            source.at[:, pl.ds(j * EIGHTH, EIGHTH)], target.at[:, pl.ds(place.column(key), EIGHTH)]
        ).start()
        for j, key in enumerate(ORDER)
    ]


def wait_all(copies):
    for copy in copies:
        copy.wait()


CHUNK = 32


def norm_into(count, rows_of, gain, shift, target):
    @pl.loop(0, count // CHUNK)
    def _(i):
        rows = pl.ds(pl.multiple_of(i * CHUNK, CHUNK), CHUNK)
        target[rows] = norm_rows(rows_of(rows), gain, shift)[0].astype(target.dtype)


def tiles(count, tile, body):
    @pl.loop(0, count // tile)
    def _(i):
        body(pl.ds(pl.multiple_of(i * tile, tile), tile))


def shifted(rows, offset):
    return pl.ds(pl.multiple_of(rows.start + offset, 256), rows.size)


def dot(left, right, contract):
    return lax.dot_general(
        left, right, (((contract[0],), (contract[1],)), ((), ())), preferred_element_type=jnp.float32
    )


def turned(pre, tables, rows, sign):
    cosine, sine_first, sine_latter = (table[rows] for table in tables)
    return (
        pre * cosine
        + pltpu.roll(pre, 128 - ROTARY // 2, 1) * (sine_first * sign)
        + pltpu.roll(pre, ROTARY // 2, 1) * (sine_latter * sign)
    )


def swapped_half(index, late):
    sequence, half = index // 2, lax.rem(index, 2)
    half = half + late * (1 - 2 * half)
    return half, pl.ds(pl.multiple_of(sequence * SEQ_LEN + half * HALF, HALF), HALF)


HALF = SEQ_LEN // 2


def head_lanes(array, head):
    lanes = lax.broadcasted_iota(jnp.int32, array.shape, 1)
    mine = (lanes < HD) if head == 0 else (lanes >= HD)
    return jnp.where(mine, array, jnp.zeros_like(array))


def side_by_side(first, second):
    lanes = lax.broadcasted_iota(jnp.int32, first.shape, 1)
    return jnp.where(lanes < HD, first, second)


def probabilities(queries, key_rows, half):
    scores = dot(queries, key_rows, (1, 1))
    row = lax.broadcasted_iota(jnp.int32, scores.shape, 0) + half * HALF
    column = lax.broadcasted_iota(jnp.int32, scores.shape, 1)
    scores = jnp.where(row >= column, scores, NEGATIVE)
    exponent = jnp.exp(scores - jnp.max(scores, axis=-1, keepdims=True))
    return exponent * (1.0 / jnp.sum(exponent, axis=-1, keepdims=True))


def attend_pair(heads, mixed, late):
    @pl.loop(0, 2 * heads.shape[2] // 128)
    def _(step):
        pairs = heads.shape[2] // 128
        sequence, lanes = step // pairs, pl.ds(pl.multiple_of(lax.rem(step, pairs) * 128, 128), 128)
        start = pl.multiple_of(sequence * SEQ_LEN, SEQ_LEN)
        for half in (0, 1):
            past = pl.ds(start, HALF * (half + 1))
            queries = heads[0, pl.ds(start + half * HALF, HALF), lanes]
            results = []
            for head in (0, 1):
                probs = probabilities(head_lanes(queries, head), heads[1, past, lanes], half)
                results.append(dot(probs.astype(jnp.bfloat16), heads[2, past, lanes], (1, 0)))
            _, rows = swapped_half(sequence * 2 + half, late)
            mixed[rows, lanes] = side_by_side(*results).astype(mixed.dtype)


def attend_pair_back(heads, grad_mixed, grad_pre, tables, late):
    @pl.loop(0, 2 * heads.shape[2] // 128)
    def _(step):
        pairs = heads.shape[2] // 128
        sequence, lanes = step // pairs, pl.ds(pl.multiple_of(lax.rem(step, pairs) * 128, 128), 128)
        start = pl.multiple_of(sequence * SEQ_LEN, SEQ_LEN)
        grads = [[None, None], [None, None]]
        for half in (0, 1):
            past = pl.ds(start, HALF * (half + 1))
            here = pl.ds(start + half * HALF, HALF)
            queries, incoming = heads[0, here, lanes], grad_mixed[here, lanes]
            key_rows, value_rows = heads[1, past, lanes], heads[2, past, lanes]
            found = []
            for head in (0, 1):
                probs = probabilities(head_lanes(queries, head), key_rows, half)
                grad_values = dot(probs.astype(jnp.bfloat16), incoming, (0, 0))
                grad_probs = dot(head_lanes(incoming, head), value_rows, (1, 1))
                product = probs * grad_probs
                grad_scores = product - probs * jnp.sum(product, axis=-1, keepdims=True)
                grad_scores = grad_scores.astype(jnp.bfloat16)
                grad_queries = dot(grad_scores, key_rows, (1, 0))
                grad_keys = dot(grad_scores, queries, (0, 0))
                found.append((grad_queries, grad_keys, grad_values))
            grad_queries, grad_keys, grad_values = (side_by_side(*two) for two in zip(*found))
            at_half = pl.ds(half * HALF, HALF)
            _, rows = swapped_half(sequence * 2 + half, late)
            grad_queries = turned(grad_queries * (1.0 / math.sqrt(HD)), tables, at_half, -1.0)
            grad_pre[0, rows, lanes] = grad_queries.astype(grad_pre.dtype)
            if half == 0:
                early = (grad_keys, grad_values)
            else:
                whole = [grad_keys[:HALF] + early[0], grad_keys[HALF:]]
                whole_values = [grad_values[:HALF] + early[1], grad_values[HALF:]]
                for k in (0, 1):
                    _, rows = swapped_half(sequence * 2 + k, late)
                    turned_keys = turned(whole[k], tables, pl.ds(k * HALF, HALF), -1.0)
                    grad_pre[1, rows, lanes] = turned_keys.astype(grad_pre.dtype)
                    grad_pre[2, rows, lanes] = whole_values[k].astype(grad_pre.dtype)


def forward_kernel(
    inputs, cotangent, parameters, biases, turns,
    projections, output_weight, gate_up, down_weight,
    proj_full, out_full, gu_full, down_full, vectors_full, rows_one, rows_cot, heads_out, mixed_out,
    middle, rows_two, hidden_out, gate_out, up_out, down_parts,
    own, normed, own_cot, vectors_here, biases_here, proj_here, out_here, rows_here, heads, mixed,
    near, far, got, got_beside, total, rows_later, gu_here, gate_wide, hidden, gate_act, up_act,
    vectors, own_bias, turns_here, send_sems, recv_sems, local_sems,
):
    p = Place(send_sems, recv_sems, local_sems)
    count = own.shape[0]
    late = lax.rem(p.tensor, 2)
    tables = [turns_here.at[k] for k in range(3)]
    loads = load_local(p, inputs, own)
    loads.append(p.copy(turns, turns_here).start())
    vectors[...] = jnp.zeros_like(vectors)
    vectors[0:4] = parameters[...].astype(jnp.float32)
    own_bias[...] = jnp.zeros_like(own_bias)
    own_bias[0:3] = biases[...].astype(jnp.float32)
    cot_loads = load_local(p, cotangent, own_cot)
    p.greet()
    slots = {key: j for j, key in enumerate(ORDER)}
    vector_base = p.used["recv"]
    p.used["recv"] += len(ORDER)

    def vector_copy(dy, dx, core):
        here, there = slots[(dy, dx, 0)], slots[(dy, dx, 1)]
        slot = here + p.core * (there - here)
        columns = pl.ds(pl.multiple_of(slot * EIGHTH, EIGHTH), EIGHTH)
        return p.send(
            vectors, vectors_here.at[:, columns], p.at(x=dx, y=dy, core=core),
            recv_sems.at[vector_base + slot],
        )

    vector_sends = [
        vector_copy(dy, dx, core).start()
        for dy in (0, 1) for dx in (0, 1) for core in (0, 1) if dy or dx or core
    ]
    own_slot = slots[(0, 0, 0)] + p.core * (slots[(0, 0, 1)] - slots[(0, 0, 0)])
    own_vectors = p.copy(
        vectors, vectors_here.at[:, pl.ds(pl.multiple_of(own_slot * EIGHTH, EIGHTH), EIGHTH)]
    ).start()
    own_biases = p.copy(own_bias, biases_here, p.core == 0).start()
    far_biases = p.send(own_bias, biases_here, p.at(core=1, far=1), when=p.core == 0).start()

    def third(j):
        return GatherWeight(
            p, projections.at[j], lambda k: proj_here.at[j, pl.ds(k * EIGHTH, EIGHTH)]
        )

    def gu_block(j):
        return lambda k: gu_here.at[j, pl.ds(k * EIGHTH, EIGHTH)]

    thirds = [third(0), third(1), third(2)]
    out = GatherWeight(p, output_weight, lambda k: out_here.at[:, pl.ds(k * EIGHTH, EIGHTH)])
    gate = GatherWeight(p, gate_up.at[0], gu_block(0))
    up = GatherWeight(p, gate_up.at[1], gu_block(1))
    down = GatherWeight(p, down_weight, lambda k: down_full.at[:, pl.ds(k * EIGHTH, EIGHTH)])
    thirds[0].fetch()
    thirds[1].fetch()
    thirds[0].spread(0)
    thirds[1].spread(0)
    wait_all(cot_loads)
    wait_all(loads)
    own_vectors.wait()
    sibling_slot = slots[(0, 0, 1)] + p.core * (slots[(0, 0, 0)] - slots[(0, 0, 1)])
    for dy in (0, 1):
        for dx in (0, 1):
            for core in (0, 1):
                if dy or dx:
                    slot = slots[(dy, dx, core)]
                elif core:
                    slot = sibling_slot
                else:
                    continue
                pltpu.make_async_copy(
                    vectors, vectors_here.at[:, pl.ds(0, EIGHTH)], recv_sems.at[vector_base + slot]
                ).wait()
    gain_one, shift_one = vectors_here[0:1], vectors_here[1:2]
    norm_into(count, lambda rows: own[rows].astype(jnp.float32), gain_one, shift_one, normed)
    gather_one = GatherRows(p, normed, rows_here).start()
    gather_cot = GatherRows(p, own_cot, rows_cot)
    stores = [p.copy(vectors_here, vectors_full).start()]

    thirds[0].spread(1)
    thirds[2].fetch().spread(0)
    thirds[1].spread(1)
    out.fetch().spread(0)
    thirds[0].relay()
    thirds[2].spread(1)
    gate.fetch()
    thirds[1].relay()
    out.spread(1)
    gate.spread(0)
    thirds[2].relay()
    out.relay()
    gather_one.relay()
    gather_cot.start()
    up.fetch()
    own_biases.wait()
    far_biases.arrived(p.core == 1)
    far_biases.left()

    def project(j):
        thirds[j].finish()
        stores.append(p.copy(proj_here.at[j], proj_full.at[j]).start())

        @pl.loop(0, 4)
        def _(index):
            rows = pl.ds(pl.multiple_of(index * HALF, HALF), HALF)
            half, target = swapped_half(index, late)
            positions = pl.ds(pl.multiple_of(half * HALF, HALF), HALF)
            pre = dot(rows_here[rows], proj_here[j], (1, 0)) + biases_here[j : j + 1]
            for k in range(pre.shape[1] // 128):
                lanes = slice(k * 128, (k + 1) * 128)
                part = pre[:, lanes]
                if j < 2:
                    part = turned(part, tables, positions, 1.0)
                if j == 0:
                    part = part * (1.0 / math.sqrt(HD))
                heads[j, target, lanes] = part.astype(heads.dtype)

    gather_one.finish()
    rows_store = p.copy(rows_here, rows_one).start()
    project(0)
    gate.spread(1)
    project(1)
    project(2)
    up.spread(0)
    gather_cot.relay()
    stores.append(p.copy(heads, heads_out).start())
    attend_pair(heads, mixed, late)
    out.finish()
    stores += [p.copy(out_here, out_full).start(), p.copy(mixed, mixed_out).start()]

    def out_rows(target, offset):
        def part(rows):
            target[rows] = dot(mixed[shifted(rows, offset)], out_here[...], (1, 0)).astype(target.dtype)

        return part

    scatter = ScatterRows(p, far, near, got, got_beside)
    tiles(2 * count, 256, out_rows(far, 2 * count))
    scatter.start()
    tiles(2 * count, 256, out_rows(near, 0))
    scatter.relay()
    gate.relay()
    up.spread(1)
    scatter.arrived()
    gain_two, shift_two = vectors_here[2:3], vectors_here[3:4]

    def norm(rows):
        value = own[rows].astype(jnp.float32) + scatter.total(rows)
        total[rows] = value
        normed[rows] = norm_rows(value, gain_two, shift_two)[0].astype(normed.dtype)

    tiles(count, CHUNK, norm)
    gather = GatherRows(p, normed, rows_later).start()
    down.fetch().spread(0)
    stores.append(p.copy(total, middle).start())
    gather_cot.finish()
    gather.relay()
    up.relay()
    down.spread(1)
    gate.finish()
    gather.finish()
    stores.append(p.copy(rows_later, rows_two).start())
    gate_store = p.copy(gu_here.at[0], gu_full.at[0]).start()
    rows_store.wait()
    cot_load = p.copy(rows_cot, rows_here).start()

    def gate_rows(rows):
        gate_wide[rows] = dot(rows_later[rows], gu_here[0], (1, 0))

    tiles(4 * count, 256, gate_rows)
    up.finish()
    up_store = p.copy(gu_here.at[1], gu_full.at[1]).start()

    def up_rows(rows):
        wide_up = dot(rows_later[rows], gu_here[1], (1, 0))
        wide_gate = gate_wide[rows]
        hidden[rows] = (wide_gate * jax.nn.sigmoid(wide_gate) * wide_up).astype(hidden.dtype)
        gate_act[rows] = wide_gate.astype(gate_act.dtype)
        up_act[rows] = wide_up.astype(up_act.dtype)

    tiles(2 * count, 256, up_rows)
    down.relay()
    tiles(2 * count, 256, lambda rows: up_rows(shifted(rows, 2 * count)))
    stores.append(p.copy(hidden, hidden_out).start())
    stores.append(p.copy(gate_act, gate_out).start())
    stores.append(p.copy(up_act, up_out).start())
    cot_load.wait()
    gate_store.wait()
    gate.left()
    quarter = down_parts.shape[2]
    for k in range(4):
        if k == 2:
            up_store.wait()
            up.left()
        columns = pl.ds((k % 2) * quarter, quarter)
        part = gu_here.at[k // 2, pl.ds(0, hidden.shape[1]), columns]
        part[...] = dot(hidden[...], rows_here[:, pl.ds(k * quarter, quarter)], (0, 0)).astype(part.dtype)
        stores.append(p.copy(part, down_parts.at[k]).start())
    down.finish()
    for weight in (*thirds, out, down):
        weight.left()
    for sent in vector_sends:
        sent.left()
    scatter.finish()
    wait_all(stores)


def norm_back_rows(value, incoming, gain):
    average = jnp.mean(value, axis=-1, keepdims=True)
    centred = value - average
    inverse = lax.rsqrt(jnp.mean(centred * centred, axis=-1, keepdims=True) + EPSILON)
    unit = centred * inverse
    scaled = incoming * gain
    inner = (
        scaled
        - jnp.mean(scaled, axis=-1, keepdims=True)
        - unit * jnp.mean(scaled * unit, axis=-1, keepdims=True)
    )
    return inner * inverse, incoming * unit


def fold(array):
    return jnp.sum(array.reshape(array.shape[0] // 8, 8, array.shape[1]), axis=0)


def back_kernel(
    hidden_in, gate_in, up_in, cot_rows, rows_two, gu_full, down_full, down_parts, middle, vectors,
    out_half, grad_middle, rows_branch, sums, down_owned, gate_sums, up_parts,
    hidden, gate_act, up_act, cot, rows_here, gate, up, down, value, near, got, got_beside,
    got_out, gain_sum, shift_sum, staging,
    down_got, down_last, down_home, down_result, gate_got, gate_last,
    send_sems, recv_sems, local_sems,
):
    p = Place(send_sems, recv_sems, local_sems)
    count, width = value.shape
    hidden_width = hidden.shape[1]
    quarter = width // 4
    first_loads = [
        p.copy(cot_rows, cot).start(), p.copy(down_full, down).start(),
        p.copy(gate_in, gate_act).start(), p.copy(up_in, up_act).start(),
    ]
    p.greet()
    down_sum = ScatterWeight(
        p, [down_parts.at[0], down_parts.at[1]], [staging.at[0], staging.at[1]], False,
        down_got, down_last, down_home, down_result,
    )
    gate_quarters = [gate.at[pl.ds(k * quarter, quarter)] for k in range(4)]
    gate_sum = ScatterWeight(
        p, gate_quarters[:2], gate_quarters[2:], True, gate_got, gate_last, None, None
    )
    far = cot.at[pl.ds(2 * count, 2 * count)]
    scatter = ScatterRows(p, far, near, got, got_beside)
    near_out = rows_here.at[pl.ds(0, 2 * count)]
    out_scatter = ScatterRows(p, far, near_out, got_out, None)

    down_sum.start()
    wait_all(first_loads)
    third_loads = [p.copy(gu_full.at[0], gate).start(), p.copy(gu_full.at[1], up).start()]

    def hidden_back(rows):
        grad = dot(cot[rows], down[...], (1, 1))
        gate_value = gate_act[rows].astype(jnp.float32)
        up_value = up_act[rows].astype(jnp.float32)
        sigmoid = jax.nn.sigmoid(gate_value)
        scaled = grad * sigmoid
        up_act[rows] = (scaled * gate_value).astype(up_act.dtype)
        gate_act[rows] = (
            scaled * up_value * (1.0 + gate_value * (1.0 - sigmoid))
        ).astype(gate_act.dtype)

    tiles(4 * count, 256, hidden_back)
    wait_all(third_loads)
    last_loads = [
        p.copy(rows_two, rows_here).start(), p.copy(middle, value).start(),
        p.copy(hidden_in, hidden).start(),
    ]
    down_sum.load([down_parts.at[2], down_parts.at[3]])

    def second_rows(target, offset):
        def part(rows):
            here = shifted(rows, offset)
            target[rows] = (
                dot(gate_act[here], gate[...], (1, 1)) + dot(up_act[here], up[...], (1, 1))
            ).astype(target.dtype)

        return part

    tiles(2 * count, 256, second_rows(far, 2 * count))
    scatter.start()
    tiles(2 * count, 256, second_rows(near, 0))
    scatter.relay()
    wait_all(last_loads)

    def weight_part(target, grads, k):
        here = pl.ds(k * quarter, quarter)
        target[here] = dot(rows_here[:, here], grads[...], (0, 0)).astype(target.dtype)

    weight_part(gate, gate_act, 0)
    weight_part(gate, gate_act, 1)
    down_sum.relay()
    weight_part(gate, gate_act, 2)
    weight_part(gate, gate_act, 3)

    def out_rows(target, offset):
        def part(rows):
            target[rows] = dot(hidden[shifted(rows, offset)], down[...], (1, 0)).astype(target.dtype)

        return part

    for k in range(4):
        weight_part(up, up_act, k)
    stores = [p.copy(up, up_parts).start()]
    scatter.sibling.left()
    tiles(2 * count, 256, out_rows(far, 2 * count))
    out_scatter.start()
    down_sum.settle()
    gate_sum.start()
    tiles(2 * count, 256, out_rows(near_out, 0))
    scatter.arrived()
    gain = vectors[2:3]
    gain_sum[...] = jnp.zeros_like(gain_sum)
    shift_sum[...] = jnp.zeros_like(shift_sum)

    def middle_back(rows):
        incoming = scatter.total(rows)
        back, product = norm_back_rows(value[rows], incoming, gain)
        gain_sum[...] += fold(product)
        shift_sum[...] += fold(incoming)
        grad = cot[rows].astype(jnp.float32) + back
        value[rows] = grad
        cot[rows] = grad.astype(cot.dtype)

    tiles(count, CHUNK, middle_back)
    gather = GatherRows(p, cot.at[pl.ds(0, count)], rows_branch).start()
    stores.append(p.copy(value, grad_middle).start())
    gain_sum[0:1] = jnp.sum(gain_sum[...], axis=0, keepdims=True)
    gain_sum[1:2] = jnp.sum(shift_sum[...], axis=0, keepdims=True)
    stores.append(p.copy(gain_sum, sums).start())
    scatter.beside.left()
    out_scatter.sibling.arrived()
    combine(near_out, [near_out, got_out], 32)
    stores.append(p.copy(near_out, out_half).start())
    gather.relay()
    gate_sum.relay()
    down_sum.finish(down_owned)
    gate_sum.gather()
    for k in (0, 1):
        stores.append(p.copy(gate_sum.half(gate_quarters[2 + k], 0), gate_sums.at[k]).start())
    gate_sum.left()
    down_sum.stored()
    gather.finish()
    out_scatter.sibling.left()
    wait_all(stores)


def last_kernel(
    rows_branch, out_full, heads_in, mixed_in, rows_one, proj_full, inputs, vectors,
    turns, grad_middle, sums, up_parts, gate_sums, out_half, middle,
    outputs, input_grads, proj_owned, out_owned, vector_grads, bias_grad, gu_owned,
    branch, out_here, heads, mixed, grad_mixed, grad_pre, rows_here, proj_here, out_send,
    own, got, got_beside, result, all_sums, shift_sum, vector_got, vector_total, z_got,
    bias_here, bias_got, turns_here, got_out, gate_home, gate_even, up_result, out_result, third_result, *rest,
):
    weight_refs = [rest[4 * k : 4 * k + 4] for k in range(5)]
    p = Place(*rest[20:])
    count, width = own.shape
    quarter = width // 4
    late = lax.rem(p.tensor, 2)
    tables = [turns_here.at[k] for k in range(3)]
    first, second = p.core == 0, p.core == 1
    first_loads = [p.copy(rows_branch, branch).start(), p.copy(out_full, out_here).start()]
    p.greet()

    def weight_sum(send, rows, refs, total):
        keep, got_quarters, last, home = refs
        return ScatterWeight(
            p, send, [keep.at[0], keep.at[1]], rows, got_quarters, last, home, total
        )

    up_quarters = [up_parts.at[pl.ds(k * quarter, quarter)] for k in range(4)]
    up = weight_sum(up_quarters[:2], True, weight_refs[0], up_result).start()
    gate = HomeSum(p, gate_sums.at[0], gate_sums.at[1], gate_even, gate_home, up_result).start()
    out = weight_sum([out_send.at[0], out_send.at[1]], False, weight_refs[1], out_result)
    proj_send = [[heads.at[j, pl.ds(k * quarter, quarter)] for k in (0, 1)] for j in range(3)]
    thirds = [
        weight_sum(proj_send[j], True, weight_refs[2 + j], third_result.at[j]) for j in range(3)
    ]
    out_beside = p.send(out_half.at[pl.ds(count, count)], got_out, p.at(near=1)).start()
    out_loads = [p.copy(out_half.at[pl.ds(0, count)], own).start(), p.copy(middle, result).start()]
    wait_all(first_loads)
    mixed_load = p.copy(mixed_in, mixed).start()
    head_load = p.copy(heads_in, heads).start()
    out_loads.append(p.copy(turns, turns_here).start())

    @pl.loop(0, 4)
    def _(index):
        rows = pl.ds(pl.multiple_of(index * HALF, HALF), HALF)
        _, target = swapped_half(index, late)
        grad_mixed[target] = dot(branch[rows], out_here[...], (1, 1)).astype(grad_mixed.dtype)

    mixed_load.wait()

    def out_part(k):
        target = out_send.at[k] if k < 2 else weight_refs[1][0].at[k - 2]
        target[...] = dot(
            mixed[...], branch[:, pl.ds(k * quarter, quarter)], (0, 0)
        ).astype(target.dtype)

    for k in range(4):
        out_part(k)
    head_load.wait()
    later_loads = [p.copy(proj_full, proj_here).start(), p.copy(rows_one, rows_here).start()]
    wait_all(out_loads)
    gate_load = p.copy(gate_sums.at[0], gate_even).start()
    up.load(up_quarters[2:])
    attend_pair_back(heads, grad_mixed, grad_pre, tables, late)
    wait_all(later_loads)
    up.relay()
    near, far = branch.at[pl.ds(0, 2 * count)], branch.at[pl.ds(2 * count, 2 * count)]
    scatter = ScatterRows(p, far, near, got, got_beside)

    def term_rows(target, offset):
        def part(rows):
            here = shifted(rows, offset)
            total = dot(grad_pre[0, here], proj_here[0], (1, 1))
            for j in (1, 2):
                total = total + dot(grad_pre[j, here], proj_here[j], (1, 1))
            target[rows] = total.astype(target.dtype)

        return part

    def proj_part(j, k):
        target = proj_send[j][k] if k < 2 else weight_refs[2 + j][0].at[k - 2]
        target[...] = dot(
            rows_here[:, pl.ds(k * quarter, quarter)], grad_pre[j], (0, 0)
        ).astype(target.dtype)

    tiles(2 * count, 256, term_rows(far, 2 * count))
    scatter.start()
    tiles(2 * count, 256, term_rows(near, 0))
    scatter.relay()
    out_beside.arrived()

    def out_total(rows):
        total = result[rows] + own[rows].astype(jnp.float32) + got_out[rows].astype(jnp.float32)
        own[rows] = total.astype(own.dtype)

    tiles(count, CHUNK, out_total)
    stores = store_natural(p, own, outputs)
    for j in range(3):
        proj_part(j, 0)
        proj_part(j, 1)
    up.settle()
    out.start()
    thirds[0].start()
    thirds[1].start()
    wait_all(stores)
    loads = load_local(p, inputs, own)
    loads.append(p.copy(grad_middle, result).start())
    for j in range(3):
        proj_part(j, 2)
        proj_part(j, 3)
    out.relay()

    bias_here[...] = jnp.zeros_like(bias_here)
    for j in range(3):
        def bias_rows(rows):
            bias_here[j : j + 1] += jnp.sum(
                grad_pre[j, rows].astype(jnp.float32), axis=0, keepdims=True
            )

        tiles(4 * count, 256, bias_rows)
    bias_x = p.send(bias_here, bias_got.at[0], p.at(x=1)).start()
    bias_x.arrived()
    bias_x.left()
    bias_here[...] += bias_got[0]
    bias_y = p.send(bias_here, bias_got.at[1], p.at(y=1)).start()
    gate_load.wait()
    gate.finish(gu_owned.at[0])
    bias_y.arrived()
    bias_y.left()
    bias_here[...] += bias_got[1]
    near_sem, far_sem = p.take("recv"), p.take("recv")
    bias_home = [
        p.send(bias_here, bias_got.at[2], p.at(core=1), near_sem, first).start(),
        p.send(bias_here, bias_got.at[2], p.at(core=1, far=1), near_sem, second).start(),
        p.send(bias_here, bias_got.at[3], p.at(far=1), far_sem, second).start(),
    ]
    thirds[0].relay()
    thirds[2].start()
    out.settle()
    wait_all(loads)
    scatter.arrived()
    gain = vectors[0:1]
    all_sums[...] = jnp.zeros_like(all_sums)
    shift_sum[...] = jnp.zeros_like(shift_sum)

    def first_back(rows):
        incoming = scatter.total(rows)
        back, product = norm_back_rows(own[rows].astype(jnp.float32), incoming, gain)
        all_sums[...] += fold(product)
        shift_sum[...] += fold(incoming)
        result[rows] = result[rows] + back

    tiles(count, CHUNK, first_back)
    stores = store_natural(p, result, input_grads)
    all_sums[0:1] = jnp.sum(all_sums[...], axis=0, keepdims=True)
    all_sums[1:2] = jnp.sum(shift_sum[...], axis=0, keepdims=True)
    all_sums[2:4] = sums[0:2]
    slots = {key: j for j, key in enumerate(ORDER)}
    vector_sends = []
    for dy in (0, 1):
        for dx in (0, 1):
            for core in (0, 1):
                if not (dy or dx or core):
                    continue
                straight, crossed = slots[(dy, dx, core)], slots[(dy, dx, 1 - core)]
                slot = straight + p.core * (crossed - straight)
                columns = pl.ds(pl.multiple_of(slot * EIGHTH, EIGHTH), EIGHTH)
                vector_sends.append(
                    p.send(
                        all_sums.at[:, columns], vector_got.at[len(vector_sends)],
                        p.at(x=dx, y=dy, core=core),
                    ).start()
                )
    thirds[1].relay()
    thirds[0].settle()
    own_slot = slots[(0, 0, 0)] + p.core * (slots[(0, 0, 1)] - slots[(0, 0, 0)])
    total = all_sums[:, pl.ds(pl.multiple_of(own_slot * EIGHTH, EIGHTH), EIGHTH)]
    for k, sent in enumerate(vector_sends):
        sent.arrived()
        total = total + vector_got[k]
    vector_total[0] = total
    z_near = p.send(vector_total.at[0], z_got.at[0], p.at(near=1)).start()
    thirds[2].relay()
    thirds[1].settle()
    z_near.arrived()
    vector_total[1] = vector_total[0] + z_got[0]
    z_far = p.send(vector_total.at[1], z_got.at[1], p.at(far=1)).start()
    thirds[2].settle()
    z_far.arrived()
    z_near.left()
    z_far.left()
    vector_total[0] = vector_total[1] + z_got[1]
    vector_store = p.copy(vector_total.at[0], vector_grads).start()
    bias_home[0].arrived()
    bias_home[2].arrived(second)
    for sent in bias_home:
        sent.left()
    pl.when(second)(lambda: combine(bias_got.at[2], [bias_got.at[2], bias_got.at[3]], 8))
    pl.when(first)(lambda: combine(bias_got.at[2], [bias_got.at[2], bias_here], 8))
    bias_store = p.copy(bias_got.at[2], bias_grad).start()
    gate.stored()
    up.finish(gu_owned.at[1])
    out.finish(out_owned)
    for j in range(3):
        thirds[j].finish(proj_owned.at[j])
    for weight in (up, out, *thirds):
        weight.stored()
    scatter.finish()
    for sent in vector_sends:
        sent.left()
    out_beside.left()
    wait_all(stores)
    vector_store.wait()
    bias_store.wait()


def call(body, name, collective, inputs, in_specs, outs, scratch, counts):
    bf16_bytes = sum(math.prod(o.shape) * o.dtype.itemsize for o in outs)
    return pl.pallas_call(
        body,
        out_shape=outs,
        in_specs=in_specs,
        out_specs=[ANY] * len(outs),
        scratch_shapes=[
            *scratch,
            pltpu.SemaphoreType.DMA((counts[0],)),
            pltpu.SemaphoreType.DMA((counts[1],)),
            pltpu.SemaphoreType.DMA((counts[2],)),
        ],
        compiler_params=pltpu.CompilerParams(
            collective_id=collective, has_side_effects=True, vmem_limit_bytes=VMEM_BYTES
        ),
        cost_estimate=pl.CostEstimate(
            flops=0, bytes_accessed=2 * bf16_bytes, transcendentals=0
        ),
        name=name,
    )(*inputs)


def bf16(*shape):
    return jax.ShapeDtypeStruct(shape, jnp.bfloat16)


def f32(*shape):
    return jax.ShapeDtypeStruct(shape, jnp.float32)


def held(shape_struct):
    return pltpu.VMEM(shape_struct.shape, shape_struct.dtype)


def weight_scratch(quarter, eighth):
    return [
        held(bf16(2, *quarter)), held(bf16(2, *quarter)), held(bf16(2, *eighth)),
        held(bf16(2, *eighth)),
    ]


WHOLE = pl.BlockSpec(memory_space=pltpu.VMEM)
EIGHTH = 256


def local_pairs(
    inputs,
    gain_first,
    shift_first,
    projections,
    biases,
    output_weight,
    gain_second,
    shift_second,
    gate_up,
    down_weight,
    cotangent,
):
    count, width = inputs.shape
    rows = 4 * count
    heads_width = output_weight.shape[0]
    hidden_width = down_weight.shape[0]
    cosine, sine = angle_tables()
    rest = ((0, 0), (0, HD - ROTARY))
    turns = jnp.stack([
        jnp.tile(jnp.pad(table, rest, constant_values=fill), (1, 128 // HD))
        for table, fill in (
            (jnp.concatenate([cosine, cosine], axis=1), 1.0),
            (jnp.concatenate([-sine, jnp.zeros_like(sine)], axis=1), 0.0),
            (jnp.concatenate([jnp.zeros_like(sine), sine], axis=1), 0.0),
        )
    ])
    wide = bf16(rows, width)
    inner = bf16(rows, hidden_width)
    own = bf16(count, width)
    half_rows = bf16(2 * count, width)
    (
        proj_full, out_full, gu_full, down_full, vectors, gathered_one, gathered_cot, heads, mixed_rows,
        middle, gathered_two, hidden, gate_act, up_act, down_parts,
    ) = call(
        forward_kernel, "forward", 1,
        (
            inputs, cotangent,
            jnp.concatenate([gain_first, shift_first, gain_second, shift_second]).reshape(4, -1),
            biases, turns,
            projections, output_weight, gate_up, down_weight,
        ),
        [ANY] * 2 + [WHOLE] * 2 + [ANY] * 5,
        [
            bf16(3, width, heads_width), bf16(heads_width, width), bf16(2, width, hidden_width),
            bf16(hidden_width, width), f32(8, width), wide, wide, bf16(3, rows, heads_width),
            bf16(rows, heads_width), f32(count, width), wide, inner, inner, inner,
            bf16(4, hidden_width, 2 * EIGHTH),
        ],
        [
            held(own), held(own), held(own), held(f32(8, width)), held(f32(8, heads_width)),
            held(bf16(3, width, heads_width)), held(bf16(heads_width, width)), held(wide),
            held(bf16(3, rows, heads_width)), held(bf16(rows, heads_width)),
            held(half_rows), held(half_rows), held(half_rows), held(own), held(f32(count, width)),
            held(wide), held(bf16(2, width, hidden_width)), held(f32(rows, hidden_width)),
            held(inner), held(inner), held(inner), held(f32(8, EIGHTH)), held(f32(8, heads_width)),
            held(f32(*turns.shape)),
        ],
        (128, 96, 64),
    )

    by_rows = ((2 * EIGHTH, hidden_width), (EIGHTH, hidden_width))
    by_columns = ((hidden_width, 2 * EIGHTH), (hidden_width, EIGHTH))
    (
        out_half, grad_middle, gathered_branch, sums, down_owned, gate_sums, up_parts,
    ) = call(
        back_kernel, "backward_first", 2,
        (
            hidden, gate_act, up_act, gathered_cot, gathered_two, gu_full, down_full, down_parts,
            middle, vectors,
        ),
        [ANY] * 9 + [WHOLE],
        [
            half_rows, f32(count, width), wide, f32(8, width), f32(hidden_width, EIGHTH),
            bf16(2, EIGHTH, hidden_width), bf16(width, hidden_width),
        ],
        [
            held(inner), held(inner), held(inner), held(wide), held(wide),
            held(bf16(width, hidden_width)), held(bf16(width, hidden_width)),
            held(bf16(hidden_width, width)), held(f32(count, width)),
            held(half_rows), held(half_rows), held(own), held(half_rows),
            held(f32(8, width)), held(f32(8, width)), held(bf16(2, hidden_width, 2 * EIGHTH)),
            *weight_scratch(*by_columns)[1:], held(f32(hidden_width, EIGHTH)),
            *weight_scratch(*by_rows)[1:3],
        ],
        (64, 64, 48),
    )
    third = ((2 * EIGHTH, heads_width), (EIGHTH, heads_width))
    outputs, input_grads, proj_owned, out_owned, vector_grads, bias_grad, gu_owned = call(
        last_kernel, "backward_last", 3,
        (
            gathered_branch, out_full, heads, mixed_rows, gathered_one, proj_full, inputs, vectors,
            turns, grad_middle, sums, up_parts, gate_sums,
            out_half, middle,
        ),
        [ANY] * 7 + [WHOLE] + [ANY] * 2 + [WHOLE] + [ANY] * 4,
        [
            own, f32(count, width), f32(3, EIGHTH, heads_width), f32(heads_width, EIGHTH),
            f32(8, EIGHTH), f32(8, heads_width), f32(2, EIGHTH, hidden_width),
        ],
        [
            held(wide), held(bf16(heads_width, width)), held(bf16(3, rows, heads_width)),
            held(bf16(rows, heads_width)), held(bf16(rows, heads_width)),
            held(bf16(3, rows, heads_width)), held(wide), held(bf16(3, width, heads_width)),
            held(bf16(2, heads_width, 2 * EIGHTH)),
            held(own), held(half_rows), held(own), held(f32(count, width)),
            held(f32(8, width)), held(f32(8, width)),
            held(f32(7, 8, EIGHTH)), held(f32(2, 8, EIGHTH)), held(f32(2, 8, EIGHTH)),
            held(f32(8, heads_width)), held(f32(4, 8, heads_width)), held(f32(*turns.shape)),
            held(own),
            held(bf16(2, EIGHTH, hidden_width)), held(bf16(EIGHTH, hidden_width)),
            held(f32(EIGHTH, hidden_width)), held(f32(heads_width, EIGHTH)),
            held(f32(3, EIGHTH, heads_width)),
            *weight_scratch(*by_rows),
            *weight_scratch((heads_width, 2 * EIGHTH), (heads_width, EIGHTH)),
            *weight_scratch(*third), *weight_scratch(*third), *weight_scratch(*third),
        ],
        (64, 64, 48),
    )
    return (
        outputs,
        input_grads,
        vector_grads[0],
        vector_grads[1],
        proj_owned,
        bias_grad[:3],
        out_owned,
        vector_grads[2],
        vector_grads[3],
        gu_owned,
        down_owned,
    )


def solution(mesh):
    whole_pairs = dict(mesh.shape) == {"dp": 8, "tensor": 4}
    return jax.shard_map(
        local_pairs if whole_pairs else local,
        mesh=mesh,
        in_specs=(
            P(("dp", "tensor"), None),
            P("dp"),
            P("dp"),
            P(None, "dp", "tensor"),
            P(None, "tensor"),
            P("tensor", "dp"),
            P("dp"),
            P("dp"),
            P(None, "dp", "tensor"),
            P("tensor", "dp"),
            P(("dp", "tensor"), None),
        ),
        out_specs=(
            P(("dp", "tensor"), None),
            P(("dp", "tensor"), None),
            P("dp"),
            P("dp"),
            P(None, "dp", "tensor"),
            P(None, "tensor"),
            P("tensor", "dp"),
            P("dp"),
            P("dp"),
            P(None, "dp", "tensor"),
            P("tensor", "dp"),
        ),
        check_vma=False,
    )
```

```python
import math

import jax
import jax.numpy as jnp
from jax import lax
from jax.experimental import pallas as pl
from jax.experimental.pallas import tpu as pltpu
from jax.sharding import PartitionSpec as P

HD = 64
ROTARY = 16
SEQ_LEN = 512


EPSILON = 1e-05
ANGLE_BASE = 10000.0
NEGATIVE = -1e30


def norm_rows(rows, gain, shift):
    average = jnp.mean(rows, axis=-1, keepdims=True)
    centred = rows - average
    inverse = lax.rsqrt(jnp.mean(centred * centred, axis=-1, keepdims=True) + EPSILON)
    unit_rows = centred * inverse
    return (unit_rows * gain + shift, unit_rows, inverse)


def norm_back(incoming, unit_rows, inverse, gain):
    scaled = incoming * gain
    inner = (
        scaled
        - jnp.mean(scaled, axis=-1, keepdims=True)
        - unit_rows * jnp.mean(scaled * unit_rows, axis=-1, keepdims=True)
    )
    return (inner * inverse, jnp.sum(incoming * unit_rows, axis=0), jnp.sum(incoming, axis=0))


def angle_tables():
    freqs = 1.0 / ANGLE_BASE ** (jnp.arange(0, ROTARY, 2).astype(jnp.float32) / ROTARY)
    angles = jnp.arange(SEQ_LEN).astype(jnp.float32)[:, None] * freqs[None, :]
    return (jnp.cos(angles), jnp.sin(angles))


def rotate(heads, cosine, sine, sign):
    half_rot = ROTARY // 2
    first = heads[..., :half_rot]
    latter = heads[..., half_rot:ROTARY]
    cos_part = cosine[:, None, :]
    sin_part = sine[:, None, :] * sign
    return jnp.concatenate(
        [
            first * cos_part - latter * sin_part,
            latter * cos_part + first * sin_part,
            heads[..., ROTARY:],
        ],
        axis=-1,
    )


def causal_scores(queries, key_rows, positions):
    scaling = 1.0 / math.sqrt(HD)
    scores = scaling * jnp.einsum(
        "qhd,khd->hqk", queries, key_rows, preferred_element_type=jnp.float32
    )
    causal = positions[:, None] >= positions[None, :]
    return jnp.where(causal[None], scores, NEGATIVE)


def attend_forward(pieces, positions):
    queries, key_rows, value_rows = pieces
    scores = causal_scores(queries, key_rows, positions)
    row_top = jnp.max(scores, axis=-1, keepdims=True)
    exponent = jnp.exp(scores - row_top)
    totals = jnp.sum(exponent, axis=-1, keepdims=True)
    weights = (exponent / totals).astype(jnp.bfloat16)
    mixed = jnp.einsum("hqk,khd->qhd", weights, value_rows, preferred_element_type=jnp.float32)
    return (mixed.astype(jnp.bfloat16), (row_top + jnp.log(totals))[..., 0])


def attend_back(pieces, positions):
    queries, key_rows, value_rows, grad_mixed, log_totals = pieces
    scaling = 1.0 / math.sqrt(HD)
    scores = causal_scores(queries, key_rows, positions)
    weights = jnp.exp(scores - log_totals[..., None])
    grad_values = jnp.einsum(
        "hqk,qhd->khd", weights.astype(jnp.bfloat16), grad_mixed, preferred_element_type=jnp.float32
    )
    grad_weights = jnp.einsum(
        "qhd,khd->hqk", grad_mixed, value_rows, preferred_element_type=jnp.float32
    )
    grad_scores = weights * (grad_weights - jnp.sum(weights * grad_weights, axis=-1, keepdims=True))
    grad_scores = grad_scores.astype(jnp.bfloat16)
    grad_queries = scaling * jnp.einsum(
        "hqk,khd->qhd", grad_scores, key_rows, preferred_element_type=jnp.float32
    )
    grad_keys = scaling * jnp.einsum(
        "hqk,qhd->khd", grad_scores, queries, preferred_element_type=jnp.float32
    )
    return (grad_queries, grad_keys, grad_values)


def scatter_sum(terms, axis, dimension):
    owned = lax.psum_scatter(
        terms.astype(jnp.bfloat16), axis, scatter_dimension=dimension, tiled=True
    )
    return owned.astype(jnp.float32)


def local(
    inputs,
    gain_first,
    shift_first,
    projections,
    biases,
    output_weight,
    gain_second,
    shift_second,
    gate_up,
    down_weight,
    cotangent,
):
    tensor_ways = lax.axis_size("tensor")
    row_count = inputs.shape[0]
    group_rows = row_count * tensor_ways
    sequences = group_rows // SEQ_LEN
    head_width = output_weight.shape[0]
    local_heads = head_width // HD
    head_shape = (sequences, SEQ_LEN, local_heads, HD)
    cosine, sine = angle_tables()
    positions = jnp.arange(SEQ_LEN)
    proj_full, out_full, gain_one, shift_one = (
        lax.all_gather(projections, "dp", axis=1, tiled=True),
        lax.all_gather(output_weight, "dp", axis=1, tiled=True),
        lax.all_gather(gain_first, "dp", axis=0, tiled=True),
        lax.all_gather(shift_first, "dp", axis=0, tiled=True),
    )
    gain_one = gain_one.astype(jnp.float32)
    residual = inputs.astype(jnp.float32)
    normed_one, unit_one, inverse_one = norm_rows(residual, gain_one, shift_one.astype(jnp.float32))
    gathered_one = lax.all_gather(normed_one.astype(jnp.bfloat16), "tensor", axis=0, tiled=True)
    pre_all = jnp.einsum("gd,jde->jge", gathered_one, proj_full, preferred_element_type=jnp.float32)
    pre_all = pre_all + biases.astype(jnp.float32)[:, None, :]
    queries = rotate(pre_all[0].reshape(head_shape), cosine, sine, 1.0).astype(jnp.bfloat16)
    key_rows = rotate(pre_all[1].reshape(head_shape), cosine, sine, 1.0).astype(jnp.bfloat16)
    value_rows = pre_all[2].reshape(head_shape).astype(jnp.bfloat16)
    mixed, log_totals = lax.map(
        lambda pieces: attend_forward(pieces, positions), (queries, key_rows, value_rows)
    )
    mixed_rows = mixed.reshape(group_rows, head_width)
    part = mixed_rows
    middle = residual + scatter_sum(
        jnp.dot(part, out_full, preferred_element_type=jnp.float32), "tensor", 0
    )
    gu_full, down_full, gain_two, shift_two = (
        lax.all_gather(gate_up, "dp", axis=1, tiled=True),
        lax.all_gather(down_weight, "dp", axis=1, tiled=True),
        lax.all_gather(gain_second, "dp", axis=0, tiled=True),
        lax.all_gather(shift_second, "dp", axis=0, tiled=True),
    )
    gain_two = gain_two.astype(jnp.float32)
    normed_two, unit_two, inverse_two = norm_rows(middle, gain_two, shift_two.astype(jnp.float32))
    gathered_two = lax.all_gather(normed_two.astype(jnp.bfloat16), "tensor", axis=0, tiled=True)
    gate_act = jnp.dot(gathered_two, gu_full[0], preferred_element_type=jnp.float32)
    up_act = jnp.dot(gathered_two, gu_full[1], preferred_element_type=jnp.float32)
    sigmoid_gate = jax.nn.sigmoid(gate_act)
    hidden = (gate_act * sigmoid_gate * up_act).astype(jnp.bfloat16)
    part = hidden
    outputs = (
        middle
        + scatter_sum(jnp.dot(part, down_full, preferred_element_type=jnp.float32), "tensor", 0)
    ).astype(jnp.bfloat16)
    gu_back, down_back, gain_two_back = (
        lax.all_gather(gate_up, "dp", axis=1, tiled=True),
        lax.all_gather(down_weight, "dp", axis=1, tiled=True),
        lax.all_gather(gain_second, "dp", axis=0, tiled=True),
    )
    gain_two_back = gain_two_back.astype(jnp.float32)
    gathered_cot = lax.all_gather(cotangent, "tensor", axis=0, tiled=True)
    grad_hidden = jnp.einsum(
        "gd,fd->gf", gathered_cot, down_back, preferred_element_type=jnp.float32
    )
    down_grad = jnp.einsum("gf,gd->fd", hidden, gathered_cot, preferred_element_type=jnp.float32)
    grad_up = (grad_hidden * gate_act * sigmoid_gate).astype(jnp.bfloat16)
    grad_gate = (
        grad_hidden * up_act * sigmoid_gate * (1.0 + gate_act * (1.0 - sigmoid_gate))
    ).astype(jnp.bfloat16)
    gu_grad = jnp.stack(
        [
            jnp.einsum("gd,gf->df", gathered_two, grad_gate, preferred_element_type=jnp.float32),
            jnp.einsum("gd,gf->df", gathered_two, grad_up, preferred_element_type=jnp.float32),
        ]
    )
    first_term = jnp.einsum("gf,df->gd", grad_gate, gu_back[0], preferred_element_type=jnp.float32)
    grad_second = scatter_sum(
        first_term
        + jnp.einsum("gf,df->gd", grad_up, gu_back[1], preferred_element_type=jnp.float32),
        "tensor",
        0,
    )
    gu_owned, down_owned = (
        scatter_sum(gu_grad, "dp", 1),
        scatter_sum(down_grad, "dp", 1),
    )
    grad_mid_norm, gain_two_part, shift_two_part = norm_back(
        grad_second, unit_two, inverse_two, gain_two_back
    )
    grad_middle = cotangent.astype(jnp.float32) + grad_mid_norm
    proj_back, out_back, gain_one_back = (
        lax.all_gather(projections, "dp", axis=1, tiled=True),
        lax.all_gather(output_weight, "dp", axis=1, tiled=True),
        lax.all_gather(gain_first, "dp", axis=0, tiled=True),
    )
    gain_one_back = gain_one_back.astype(jnp.float32)
    gathered_branch = lax.all_gather(grad_middle.astype(jnp.bfloat16), "tensor", axis=0, tiled=True)
    out_grad = jnp.einsum(
        "ge,gd->ed", mixed_rows, gathered_branch, preferred_element_type=jnp.float32
    )
    grad_mixed = jnp.einsum(
        "gd,ed->ge", gathered_branch, out_back, preferred_element_type=jnp.float32
    ).astype(jnp.bfloat16)
    grad_queries, grad_keys, grad_values = lax.map(
        lambda pieces: attend_back(pieces, positions),
        (queries, key_rows, value_rows, grad_mixed.reshape(head_shape), log_totals),
    )
    grad_queries = rotate(grad_queries, cosine, sine, -1.0)
    grad_keys = rotate(grad_keys, cosine, sine, -1.0)
    grad_pre = (
        jnp.stack([grad_queries, grad_keys, grad_values])
        .reshape(3, group_rows, head_width)
        .astype(jnp.bfloat16)
    )
    bias_part = jnp.sum(grad_pre, axis=1, dtype=jnp.float32)
    proj_grad = jnp.einsum(
        "gd,jge->jde", gathered_one, grad_pre, preferred_element_type=jnp.float32
    )
    part = grad_pre
    grad_normed = scatter_sum(
        jnp.einsum("jge,jde->gd", part, proj_back, preferred_element_type=jnp.float32),
        "tensor",
        0,
    )
    proj_owned, out_owned = (
        scatter_sum(proj_grad, "dp", 1),
        scatter_sum(out_grad, "dp", 1),
    )
    grad_in_norm, gain_one_part, shift_one_part = norm_back(
        grad_normed, unit_one, inverse_one, gain_one_back
    )
    input_grads = grad_middle + grad_in_norm
    one_hot = (jnp.arange(tensor_ways) == lax.axis_index("tensor")).astype(jnp.float32)
    spread_bias = (bias_part[:, None, :] * one_hot[None, :, None]).reshape(
        3, tensor_ways * head_width
    )
    summed = lax.psum(
        (gain_one_part, shift_one_part, gain_two_part, shift_two_part, spread_bias),
        ("dp", "tensor"),
    )
    own_width = gain_first.shape[0]
    own_offset = lax.axis_index("dp") * own_width

    def own_part(vector):
        return lax.dynamic_slice_in_dim(vector, own_offset, own_width, 0)

    bias_grad = jnp.sum(
        summed[4].reshape(3, tensor_ways, head_width) * one_hot[None, :, None], axis=1
    )
    return (
        outputs,
        input_grads,
        own_part(summed[0]),
        own_part(summed[1]),
        proj_owned,
        bias_grad,
        out_owned,
        own_part(summed[2]),
        own_part(summed[3]),
        gu_owned,
        down_owned,
    )


ORDER = ((1, 0, 0), (1, 1, 0), (0, 1, 1), (1, 1, 1), (0, 0, 0), (0, 1, 0), (0, 0, 1), (1, 0, 1))
EVEN_Y, EVEN_XY, ODD_X, ODD_XY, EVEN, EVEN_X, ODD, ODD_Y = range(8)
ANY = pl.BlockSpec(memory_space=pl.ANY)
VMEM_BYTES = 63 * 1024 * 1024


class Place:
    def __init__(self, send_sems, recv_sems, local_sems):
        self.dp, self.tensor = lax.axis_index("dp"), lax.axis_index("tensor")
        self.core = lax.rem(self.dp, 2)
        self.x = lax.rem(self.dp // 2, 2)
        self.y = self.dp // 4
        self.pools = {"send": send_sems, "recv": recv_sems, "local": local_sems}
        self.used = {"send": 0, "recv": 0, "local": 0}

    def take(self, kind):
        self.used[kind] += 1
        return self.pools[kind].at[self.used[kind] - 1]

    def at(self, x=0, y=0, core=0, near=0, far=0):
        dp = self.dp
        dp = dp + x * (2 - 4 * self.x) + y * (4 - 8 * self.y) + core * (1 - 2 * self.core)
        tensor = self.tensor
        tensor = tensor + near * (1 - 2 * lax.rem(tensor, 2)) + far * (3 - 2 * tensor)
        return (dp, tensor)

    def column(self, key):
        dy, dx, core = key
        y = self.y + dy * (1 - 2 * self.y)
        x = self.x + dx * (1 - 2 * self.x)
        return pl.multiple_of((y * 4 + x * 2 + core) * EIGHTH, EIGHTH)

    def greet(self):
        barrier = pltpu.get_barrier_semaphore()
        partners = [
            self.at(x=x, y=y, core=core)
            for x in (0, 1)
            for y in (0, 1)
            for core in (0, 1)
            if x or y or core
        ] + [self.at(near=1), self.at(far=1), self.at(far=1, core=1)]
        for partner in partners:
            pl.semaphore_signal(
                barrier, inc=1, device_id=partner, device_id_type=pl.DeviceIdType.MESH
            )
        pl.semaphore_wait(barrier, len(partners))

    def send(self, source, target, device, recv_sem=None, when=None):
        return Sent(
            pltpu.make_async_remote_copy(
                src_ref=source,
                dst_ref=target,
                send_sem=self.take("send"),
                recv_sem=self.take("recv") if recv_sem is None else recv_sem,
                device_id=device,
                device_id_type=pl.DeviceIdType.MESH,
            ),
            when,
        )

    def copy(self, source, target, when=None):
        return Copied(pltpu.make_async_copy(source, target, self.take("local")), when)


def guarded(when, action):
    if when is None:
        action()
    else:
        pl.when(when)(action)


class Sent:
    def __init__(self, copy, when):
        self.copy, self.when = copy, when

    def start(self):
        guarded(self.when, self.copy.start)
        return self

    def arrived(self, when=None):
        guarded(when, self.copy.wait_recv)

    def left(self):
        guarded(self.when, self.copy.wait_send)


class Copied:
    def __init__(self, copy, when):
        self.copy, self.when = copy, when

    def start(self):
        guarded(self.when, self.copy.start)
        return self

    def wait(self):
        guarded(self.when, self.copy.wait)


class GatherWeight:
    def __init__(self, place, shard, block):
        self.place, self.shard, self.block = place, shard, block
        self.spreads, self.arrivals = [], {}

    def fetch(self):
        p = self.place
        even, odd = self.block(EVEN), self.block(ODD)
        first, second = p.core == 0, p.core == 1
        self.own = p.copy(self.shard, even, first).start()
        even_sem, odd_sem = p.take("recv"), p.take("recv")
        self.to_far_even = p.send(self.shard, even, p.at(core=1, far=1), even_sem, first).start()
        self.to_sibling = p.send(self.shard, odd, p.at(core=1), odd_sem, second).start()
        self.to_far_odd = p.send(self.shard, odd, p.at(far=1), odd_sem, second).start()
        return self

    def spread(self, core):
        p, block = self.place, self.block
        here = p.core == core
        if core:
            self.to_far_even.arrived(here)
        self.to_sibling.arrived(here)
        even = block(EVEN) if core else self.shard
        routes = (
            (even, EVEN_X, p.at(x=1)), (block(ODD), ODD_Y, p.at(y=1)),
            (block(ODD), ODD_X, p.at(x=1)), (even, EVEN_Y, p.at(y=1)),
        )
        for source, target, device in routes:
            if target not in self.arrivals:
                self.arrivals[target] = p.take("recv")
            self.spreads.append(
                p.send(source, block(target), device, self.arrivals[target], here).start()
            )
        return self

    def relay(self):
        p, block = self.place, self.block
        even_x, odd_y, self.odd_x, self.even_y = self.spreads[:4]
        even_x.arrived()
        self.even_xy = p.send(block(EVEN_X), block(EVEN_XY), p.at(y=1)).start()
        odd_y.arrived()
        self.odd_xy = p.send(block(ODD_Y), block(ODD_XY), p.at(x=1)).start()
        return self

    def finish(self):
        self.own.wait()
        for copy in (self.odd_x, self.even_y, self.even_xy, self.odd_xy):
            copy.arrived()

    def left(self):
        for copy in (
            *self.spreads, self.even_xy, self.odd_xy,
            self.to_far_even, self.to_sibling, self.to_far_odd,
        ):
            copy.left()


class GatherRows:
    def __init__(self, place, own, rows):
        self.place, self.own, self.rows = place, own, rows
        self.count = own.shape[0]

    def slot(self, k):
        return self.rows.at[pl.ds(k * self.count, self.count)]

    def start(self):
        p = self.place
        self.beside = p.send(self.own, self.slot(1), p.at(near=1)).start()
        self.sibling = p.send(self.own, self.slot(2), p.at(core=1)).start()
        self.here = p.copy(self.own, self.slot(0)).start()
        return self

    def relay(self):
        p = self.place
        self.beside.arrived()
        self.across = p.send(self.slot(1), self.slot(3), p.at(core=1)).start()
        return self

    def finish(self):
        self.sibling.arrived()
        self.across.arrived()
        self.here.wait()
        for copy in (self.beside, self.sibling, self.across):
            copy.left()


def combine(target, terms, chunk):
    @pl.loop(0, target.shape[0] // chunk)
    def _(i):
        rows = pl.ds(pl.multiple_of(i * chunk, chunk), chunk)
        total = terms[0][rows].astype(jnp.float32)
        for term in terms[1:]:
            total = total + term[rows].astype(jnp.float32)
        target[rows] = total.astype(target.dtype)


class ScatterRows:
    def __init__(self, place, far, near, got, got_beside):
        self.place, self.far, self.near = place, far, near
        self.got, self.got_beside = got, got_beside
        self.count = near.shape[0] // 2

    def start(self):
        self.sibling = self.place.send(self.far, self.got, self.place.at(core=1)).start()
        return self

    def relay(self):
        p, n = self.place, self.count
        self.sibling.arrived()
        late = pl.ds(n, n)
        combine(self.near.at[late], [self.near.at[late], self.got.at[late]], 32)
        self.beside = p.send(self.near.at[late], self.got_beside, p.at(near=1)).start()
        return self

    def total(self, rows):
        return (
            self.near[rows].astype(jnp.float32)
            + self.got[rows].astype(jnp.float32)
            + self.got_beside[rows].astype(jnp.float32)
        )

    def arrived(self):
        self.beside.arrived()

    def finish(self):
        self.sibling.left()
        self.beside.left()


class ScatterWeight:
    def __init__(self, place, send, keep, rows, got, last, home, result):
        self.place, self.parts, self.keep, self.rows = place, send, keep, rows
        self.got, self.last, self.home, self.result = got, last, home, result
        self.loads = []

    def half(self, ref, k):
        if self.rows:
            size = ref.shape[0] // 2
            return ref.at[pl.ds(k * size, size)]
        size = ref.shape[1] // 2
        return ref.at[:, pl.ds(k * size, size)]

    def load(self, sources):
        self.loads = [self.place.copy(a, b).start() for a, b in zip(sources, self.keep)]
        return self

    def start_even(self):
        p = self.place
        self.even = p.send(self.parts[0], self.got.at[0], p.at(y=1)).start()
        return self

    def start_odd(self):
        p = self.place
        self.odd = p.send(self.parts[1], self.got.at[1], p.at(x=1)).start()
        return self

    def start(self):
        return self.start_even().start_odd()

    def relay(self):
        p = self.place
        wait_all(self.loads)
        self.second = []
        for k, arrival in enumerate((self.even, self.odd)):
            arrival.arrived()
            there = self.half(self.keep[k], 1)
            combine(there, [there, self.half(self.got.at[k], 1)], 64)
            device = p.at(x=1) if k == 0 else p.at(y=1)
            self.second.append(p.send(there, self.last.at[k], device).start())
        return self

    def gather(self):
        for k in (1, 0):
            self.second[k].arrived()
            here = self.half(self.keep[k], 0)
            combine(here, [here, self.half(self.got.at[k], 0), self.last.at[k]], 64)
        return self

    def settle(self):
        self.gather()
        even, odd = self.half(self.keep[0], 0), self.half(self.keep[1], 0)
        self.way_home = HomeSum(self.place, even, odd, even, self.home, self.result).start()
        return self

    def finish(self, output):
        self.way_home.finish(output)
        self.left()

    def left(self):
        for copy in (self.even, self.odd, *self.second):
            copy.left()

    def stored(self):
        self.way_home.stored()


class HomeSum:
    def __init__(self, place, even, odd, here, home, result):
        self.place, self.even, self.odd, self.here = place, even, odd, here
        self.home, self.result = home, result

    def start(self):
        p = self.place
        first, second = p.core == 0, p.core == 1
        near_sem, far_sem = p.take("recv"), p.take("recv")
        home = self.home
        self.to_sibling = p.send(self.odd, home.at[0], p.at(core=1), near_sem, first).start()
        self.to_first = p.send(self.even, home.at[0], p.at(core=1, far=1), near_sem, second).start()
        self.to_far = p.send(self.odd, home.at[1], p.at(far=1), far_sem, second).start()
        return self

    def finish(self, output):
        p, home = self.place, self.home
        first, second = p.core == 0, p.core == 1
        self.to_sibling.arrived()
        self.to_far.arrived(second)
        pl.when(first)(lambda: combine(self.result, [self.here, home.at[0]], 64))
        pl.when(second)(lambda: combine(self.result, [home.at[0], home.at[1]], 64))
        self.store = p.copy(self.result, output).start()
        for copy in (self.to_sibling, self.to_first, self.to_far):
            copy.left()

    def stored(self):
        self.store.wait()


def load_local(place, source, target):
    return [
        place.copy(
            source.at[:, pl.ds(place.column(key), EIGHTH)], target.at[:, pl.ds(j * EIGHTH, EIGHTH)]
        ).start()
        for j, key in enumerate(ORDER)
    ]


def store_natural(place, source, target):
    return [
        place.copy(
            source.at[:, pl.ds(j * EIGHTH, EIGHTH)], target.at[:, pl.ds(place.column(key), EIGHTH)]
        ).start()
        for j, key in enumerate(ORDER)
    ]


def wait_all(copies):
    for copy in copies:
        copy.wait()


CHUNK = 32


def norm_into(count, rows_of, gain, shift, target):
    @pl.loop(0, count // CHUNK)
    def _(i):
        rows = pl.ds(pl.multiple_of(i * CHUNK, CHUNK), CHUNK)
        target[rows] = norm_rows(rows_of(rows), gain, shift)[0].astype(target.dtype)


def tiles(count, tile, body):
    @pl.loop(0, count // tile)
    def _(i):
        body(pl.ds(pl.multiple_of(i * tile, tile), tile))


def shifted(rows, offset):
    return pl.ds(pl.multiple_of(rows.start + offset, 256), rows.size)


def dot(left, right, contract):
    return lax.dot_general(
        left, right, (((contract[0],), (contract[1],)), ((), ())), preferred_element_type=jnp.float32
    )


def turned(pre, tables, rows, sign):
    cosine, sine_first, sine_latter = (table[rows] for table in tables)
    return (
        pre * cosine
        + pltpu.roll(pre, 128 - ROTARY // 2, 1) * (sine_first * sign)
        + pltpu.roll(pre, ROTARY // 2, 1) * (sine_latter * sign)
    )


def swapped_half(index, late):
    sequence, half = index // 2, lax.rem(index, 2)
    half = half + late * (1 - 2 * half)
    return half, pl.ds(pl.multiple_of(sequence * SEQ_LEN + half * HALF, HALF), HALF)


HALF = SEQ_LEN // 2


def head_lanes(array, head):
    lanes = lax.broadcasted_iota(jnp.int32, array.shape, 1)
    mine = (lanes < HD) if head == 0 else (lanes >= HD)
    return jnp.where(mine, array, jnp.zeros_like(array))


def side_by_side(first, second):
    lanes = lax.broadcasted_iota(jnp.int32, first.shape, 1)
    return jnp.where(lanes < HD, first, second)


def probabilities(queries, key_rows, half):
    scores = dot(queries, key_rows, (1, 1))
    row = lax.broadcasted_iota(jnp.int32, scores.shape, 0) + half * HALF
    column = lax.broadcasted_iota(jnp.int32, scores.shape, 1)
    scores = jnp.where(row >= column, scores, NEGATIVE)
    exponent = jnp.exp(scores - jnp.max(scores, axis=-1, keepdims=True))
    return exponent * (1.0 / jnp.sum(exponent, axis=-1, keepdims=True))


def attend_pair(heads, mixed, late):
    @pl.loop(0, 2 * heads.shape[2] // 128)
    def _(step):
        pairs = heads.shape[2] // 128
        sequence, lanes = step // pairs, pl.ds(pl.multiple_of(lax.rem(step, pairs) * 128, 128), 128)
        start = pl.multiple_of(sequence * SEQ_LEN, SEQ_LEN)
        for half in (0, 1):
            past = pl.ds(start, HALF * (half + 1))
            queries = heads[0, pl.ds(start + half * HALF, HALF), lanes]
            results = []
            for head in (0, 1):
                probs = probabilities(head_lanes(queries, head), heads[1, past, lanes], half)
                results.append(dot(probs.astype(jnp.bfloat16), heads[2, past, lanes], (1, 0)))
            _, rows = swapped_half(sequence * 2 + half, late)
            mixed[rows, lanes] = side_by_side(*results).astype(mixed.dtype)


def attend_pair_back(heads, grad_mixed, grad_pre, tables, late):
    @pl.loop(0, 2 * heads.shape[2] // 128)
    def _(step):
        pairs = heads.shape[2] // 128
        sequence, lanes = step // pairs, pl.ds(pl.multiple_of(lax.rem(step, pairs) * 128, 128), 128)
        start = pl.multiple_of(sequence * SEQ_LEN, SEQ_LEN)
        grads = [[None, None], [None, None]]
        for half in (0, 1):
            past = pl.ds(start, HALF * (half + 1))
            here = pl.ds(start + half * HALF, HALF)
            queries, incoming = heads[0, here, lanes], grad_mixed[here, lanes]
            key_rows, value_rows = heads[1, past, lanes], heads[2, past, lanes]
            found = []
            for head in (0, 1):
                probs = probabilities(head_lanes(queries, head), key_rows, half)
                grad_values = dot(probs.astype(jnp.bfloat16), incoming, (0, 0))
                grad_probs = dot(head_lanes(incoming, head), value_rows, (1, 1))
                product = probs * grad_probs
                grad_scores = product - probs * jnp.sum(product, axis=-1, keepdims=True)
                grad_scores = grad_scores.astype(jnp.bfloat16)
                grad_queries = dot(grad_scores, key_rows, (1, 0))
                grad_keys = dot(grad_scores, queries, (0, 0))
                found.append((grad_queries, grad_keys, grad_values))
            grad_queries, grad_keys, grad_values = (side_by_side(*two) for two in zip(*found))
            at_half = pl.ds(half * HALF, HALF)
            _, rows = swapped_half(sequence * 2 + half, late)
            grad_queries = turned(grad_queries * (1.0 / math.sqrt(HD)), tables, at_half, -1.0)
            grad_pre[0, rows, lanes] = grad_queries.astype(grad_pre.dtype)
            if half == 0:
                early = (grad_keys, grad_values)
            else:
                whole = [grad_keys[:HALF] + early[0], grad_keys[HALF:]]
                whole_values = [grad_values[:HALF] + early[1], grad_values[HALF:]]
                for k in (0, 1):
                    _, rows = swapped_half(sequence * 2 + k, late)
                    turned_keys = turned(whole[k], tables, pl.ds(k * HALF, HALF), -1.0)
                    grad_pre[1, rows, lanes] = turned_keys.astype(grad_pre.dtype)
                    grad_pre[2, rows, lanes] = whole_values[k].astype(grad_pre.dtype)


def forward_kernel(
    inputs, cotangent, parameters, biases, turns,
    projections, output_weight, gate_up, down_weight,
    proj_full, out_full, gu_full, down_full, vectors_full, rows_one, rows_cot, heads_out, mixed_out,
    middle, rows_two, hidden_out, gate_out, up_out, down_parts,
    own, normed, own_cot, vectors_here, biases_here, proj_here, out_here, rows_here, heads, mixed,
    near, far, got, got_beside, total, rows_later, gu_here, gate_wide, hidden, gate_act, up_act,
    vectors, own_bias, turns_here, send_sems, recv_sems, local_sems,
):
    p = Place(send_sems, recv_sems, local_sems)
    count = own.shape[0]
    late = lax.rem(p.tensor, 2)
    tables = [turns_here.at[k] for k in range(3)]
    loads = load_local(p, inputs, own)
    loads.append(p.copy(turns, turns_here).start())
    vectors[...] = jnp.zeros_like(vectors)
    vectors[0:4] = parameters[...].astype(jnp.float32)
    own_bias[...] = jnp.zeros_like(own_bias)
    own_bias[0:3] = biases[...].astype(jnp.float32)
    cot_loads = load_local(p, cotangent, own_cot)
    p.greet()
    slots = {key: j for j, key in enumerate(ORDER)}
    vector_base = p.used["recv"]
    p.used["recv"] += len(ORDER)

    def vector_copy(dy, dx, core):
        here, there = slots[(dy, dx, 0)], slots[(dy, dx, 1)]
        slot = here + p.core * (there - here)
        columns = pl.ds(pl.multiple_of(slot * EIGHTH, EIGHTH), EIGHTH)
        return p.send(
            vectors, vectors_here.at[:, columns], p.at(x=dx, y=dy, core=core),
            recv_sems.at[vector_base + slot],
        )

    vector_sends = [
        vector_copy(dy, dx, core).start()
        for dy in (0, 1) for dx in (0, 1) for core in (0, 1) if dy or dx or core
    ]
    own_slot = slots[(0, 0, 0)] + p.core * (slots[(0, 0, 1)] - slots[(0, 0, 0)])
    own_vectors = p.copy(
        vectors, vectors_here.at[:, pl.ds(pl.multiple_of(own_slot * EIGHTH, EIGHTH), EIGHTH)]
    ).start()
    own_biases = p.copy(own_bias, biases_here, p.core == 0).start()
    far_biases = p.send(own_bias, biases_here, p.at(core=1, far=1), when=p.core == 0).start()

    def third(j):
        return GatherWeight(
            p, projections.at[j], lambda k: proj_here.at[j, pl.ds(k * EIGHTH, EIGHTH)]
        )

    def gu_block(j):
        return lambda k: gu_here.at[j, pl.ds(k * EIGHTH, EIGHTH)]

    thirds = [third(0), third(1), third(2)]
    out = GatherWeight(p, output_weight, lambda k: out_here.at[:, pl.ds(k * EIGHTH, EIGHTH)])
    gate = GatherWeight(p, gate_up.at[0], gu_block(0))
    up = GatherWeight(p, gate_up.at[1], gu_block(1))
    down = GatherWeight(p, down_weight, lambda k: down_full.at[:, pl.ds(k * EIGHTH, EIGHTH)])
    thirds[0].fetch()
    thirds[1].fetch()
    thirds[0].spread(0)
    thirds[1].spread(0)
    wait_all(cot_loads)
    wait_all(loads)
    own_vectors.wait()
    sibling_slot = slots[(0, 0, 1)] + p.core * (slots[(0, 0, 0)] - slots[(0, 0, 1)])
    for dy in (0, 1):
        for dx in (0, 1):
            for core in (0, 1):
                if dy or dx:
                    slot = slots[(dy, dx, core)]
                elif core:
                    slot = sibling_slot
                else:
                    continue
                pltpu.make_async_copy(
                    vectors, vectors_here.at[:, pl.ds(0, EIGHTH)], recv_sems.at[vector_base + slot]
                ).wait()
    gain_one, shift_one = vectors_here[0:1], vectors_here[1:2]
    norm_into(count, lambda rows: own[rows].astype(jnp.float32), gain_one, shift_one, normed)
    gather_one = GatherRows(p, normed, rows_here).start()
    gather_cot = GatherRows(p, own_cot, rows_cot)
    stores = [p.copy(vectors_here, vectors_full).start()]

    thirds[0].spread(1)
    thirds[2].fetch().spread(0)
    thirds[1].spread(1)
    out.fetch().spread(0)
    thirds[0].relay()
    thirds[2].spread(1)
    gate.fetch()
    thirds[1].relay()
    out.spread(1)
    gate.spread(0)
    thirds[2].relay()
    out.relay()
    gather_one.relay()
    gather_cot.start()
    up.fetch()
    own_biases.wait()
    far_biases.arrived(p.core == 1)
    far_biases.left()

    def project(j):
        thirds[j].finish()
        stores.append(p.copy(proj_here.at[j], proj_full.at[j]).start())

        @pl.loop(0, 4)
        def _(index):
            rows = pl.ds(pl.multiple_of(index * HALF, HALF), HALF)
            half, target = swapped_half(index, late)
            positions = pl.ds(pl.multiple_of(half * HALF, HALF), HALF)
            pre = dot(rows_here[rows], proj_here[j], (1, 0)) + biases_here[j : j + 1]
            for k in range(pre.shape[1] // 128):
                lanes = slice(k * 128, (k + 1) * 128)
                part = pre[:, lanes]
                if j < 2:
                    part = turned(part, tables, positions, 1.0)
                if j == 0:
                    part = part * (1.0 / math.sqrt(HD))
                heads[j, target, lanes] = part.astype(heads.dtype)

    gather_one.finish()
    rows_store = p.copy(rows_here, rows_one).start()
    project(0)
    gate.spread(1)
    project(1)
    project(2)
    up.spread(0)
    gather_cot.relay()
    stores.append(p.copy(heads, heads_out).start())
    attend_pair(heads, mixed, late)
    out.finish()
    stores += [p.copy(out_here, out_full).start(), p.copy(mixed, mixed_out).start()]

    def out_rows(target, offset):
        def part(rows):
            target[rows] = dot(mixed[shifted(rows, offset)], out_here[...], (1, 0)).astype(target.dtype)

        return part

    scatter = ScatterRows(p, far, near, got, got_beside)
    tiles(2 * count, 256, out_rows(far, 2 * count))
    scatter.start()
    tiles(2 * count, 256, out_rows(near, 0))
    scatter.relay()
    gate.relay()
    up.spread(1)
    scatter.arrived()
    gain_two, shift_two = vectors_here[2:3], vectors_here[3:4]

    def norm(rows):
        value = own[rows].astype(jnp.float32) + scatter.total(rows)
        total[rows] = value
        normed[rows] = norm_rows(value, gain_two, shift_two)[0].astype(normed.dtype)

    tiles(count, CHUNK, norm)
    gather = GatherRows(p, normed, rows_later).start()
    stores.append(p.copy(total, middle).start())
    gather_cot.finish()
    gather.relay()
    down.fetch().spread(0)
    up.relay()
    down.spread(1)
    gate.finish()
    gather.finish()
    stores.append(p.copy(rows_later, rows_two).start())
    gate_store = p.copy(gu_here.at[0], gu_full.at[0]).start()
    rows_store.wait()
    cot_load = p.copy(rows_cot, rows_here).start()

    def gate_rows(rows):
        gate_wide[rows] = dot(rows_later[rows], gu_here[0], (1, 0))

    tiles(4 * count, 256, gate_rows)
    up.finish()
    up_store = p.copy(gu_here.at[1], gu_full.at[1]).start()

    def up_rows(rows):
        wide_up = dot(rows_later[rows], gu_here[1], (1, 0))
        wide_gate = gate_wide[rows]
        hidden[rows] = (wide_gate * jax.nn.sigmoid(wide_gate) * wide_up).astype(hidden.dtype)
        gate_act[rows] = wide_gate.astype(gate_act.dtype)
        up_act[rows] = wide_up.astype(up_act.dtype)

    tiles(2 * count, 256, up_rows)
    down.relay()
    tiles(2 * count, 256, lambda rows: up_rows(shifted(rows, 2 * count)))
    stores.append(p.copy(hidden, hidden_out).start())
    stores.append(p.copy(gate_act, gate_out).start())
    stores.append(p.copy(up_act, up_out).start())
    cot_load.wait()
    gate_store.wait()
    gate.left()
    quarter = down_parts.shape[2]
    for k in range(4):
        if k == 2:
            up_store.wait()
            up.left()
        columns = pl.ds((k % 2) * quarter, quarter)
        part = gu_here.at[k // 2, pl.ds(0, hidden.shape[1]), columns]
        part[...] = dot(hidden[...], rows_here[:, pl.ds(k * quarter, quarter)], (0, 0)).astype(part.dtype)
        stores.append(p.copy(part, down_parts.at[k]).start())
    down.finish()
    for weight in (*thirds, out, down):
        weight.left()
    for sent in vector_sends:
        sent.left()
    scatter.finish()
    wait_all(stores)


def norm_back_rows(value, incoming, gain):
    average = jnp.mean(value, axis=-1, keepdims=True)
    centred = value - average
    inverse = lax.rsqrt(jnp.mean(centred * centred, axis=-1, keepdims=True) + EPSILON)
    unit = centred * inverse
    scaled = incoming * gain
    inner = (
        scaled
        - jnp.mean(scaled, axis=-1, keepdims=True)
        - unit * jnp.mean(scaled * unit, axis=-1, keepdims=True)
    )
    return inner * inverse, incoming * unit


def fold(array):
    return jnp.sum(array.reshape(array.shape[0] // 8, 8, array.shape[1]), axis=0)


def back_kernel(
    hidden_in, gate_in, up_in, cot_rows, rows_two, gu_full, down_full, down_parts, middle, vectors,
    out_half, grad_middle, rows_branch, sums, down_owned, gate_sums, up_parts,
    hidden, gate_act, up_act, cot, rows_here, gate, up, down, value, near, got, got_beside,
    got_out, gain_sum, shift_sum, staging,
    down_got, down_last, down_home, down_result, gate_got, gate_last,
    send_sems, recv_sems, local_sems,
):
    p = Place(send_sems, recv_sems, local_sems)
    count, width = value.shape
    hidden_width = hidden.shape[1]
    quarter = width // 4
    first_loads = [
        p.copy(cot_rows, cot).start(), p.copy(down_full, down).start(),
        p.copy(gate_in, gate_act).start(), p.copy(up_in, up_act).start(),
    ]
    p.greet()
    down_sum = ScatterWeight(
        p, [down_parts.at[0], down_parts.at[1]], [staging.at[0], staging.at[1]], False,
        down_got, down_last, down_home, down_result,
    )
    gate_quarters = [gate.at[pl.ds(k * quarter, quarter)] for k in range(4)]
    gate_sum = ScatterWeight(
        p, gate_quarters[:2], gate_quarters[2:], True, gate_got, gate_last, None, None
    )
    far = cot.at[pl.ds(2 * count, 2 * count)]
    scatter = ScatterRows(p, far, near, got, got_beside)
    near_out = rows_here.at[pl.ds(0, 2 * count)]
    out_scatter = ScatterRows(p, far, near_out, got_out, None)

    down_sum.start()
    wait_all(first_loads)
    third_loads = [p.copy(gu_full.at[0], gate).start(), p.copy(gu_full.at[1], up).start()]

    def hidden_back(rows):
        grad = dot(cot[rows], down[...], (1, 1))
        gate_value = gate_act[rows].astype(jnp.float32)
        up_value = up_act[rows].astype(jnp.float32)
        sigmoid = jax.nn.sigmoid(gate_value)
        scaled = grad * sigmoid
        up_act[rows] = (scaled * gate_value).astype(up_act.dtype)
        gate_act[rows] = (
            scaled * up_value * (1.0 + gate_value * (1.0 - sigmoid))
        ).astype(gate_act.dtype)

    tiles(4 * count, 256, hidden_back)
    wait_all(third_loads)
    last_loads = [
        p.copy(rows_two, rows_here).start(), p.copy(middle, value).start(),
        p.copy(hidden_in, hidden).start(),
    ]
    down_sum.load([down_parts.at[2], down_parts.at[3]])

    def second_rows(target, offset):
        def part(rows):
            here = shifted(rows, offset)
            target[rows] = (
                dot(gate_act[here], gate[...], (1, 1)) + dot(up_act[here], up[...], (1, 1))
            ).astype(target.dtype)

        return part

    tiles(2 * count, 256, second_rows(far, 2 * count))
    scatter.start()
    tiles(2 * count, 256, second_rows(near, 0))
    scatter.relay()
    wait_all(last_loads)

    def weight_part(target, grads, k):
        here = pl.ds(k * quarter, quarter)
        target[here] = dot(rows_here[:, here], grads[...], (0, 0)).astype(target.dtype)

    weight_part(gate, gate_act, 0)
    weight_part(gate, gate_act, 1)
    down_sum.relay()
    weight_part(gate, gate_act, 2)
    weight_part(gate, gate_act, 3)

    def out_rows(target, offset):
        def part(rows):
            target[rows] = dot(hidden[shifted(rows, offset)], down[...], (1, 0)).astype(target.dtype)

        return part

    for k in range(4):
        weight_part(up, up_act, k)
    stores = [p.copy(up, up_parts).start()]
    scatter.sibling.left()
    tiles(2 * count, 256, out_rows(far, 2 * count))
    out_scatter.start()
    down_sum.settle()
    gate_sum.start()
    tiles(2 * count, 256, out_rows(near_out, 0))
    scatter.arrived()
    gain = vectors[2:3]
    gain_sum[...] = jnp.zeros_like(gain_sum)
    shift_sum[...] = jnp.zeros_like(shift_sum)

    def middle_back(rows):
        incoming = scatter.total(rows)
        back, product = norm_back_rows(value[rows], incoming, gain)
        gain_sum[...] += fold(product)
        shift_sum[...] += fold(incoming)
        grad = cot[rows].astype(jnp.float32) + back
        value[rows] = grad
        cot[rows] = grad.astype(cot.dtype)

    tiles(count, CHUNK, middle_back)
    gather = GatherRows(p, cot.at[pl.ds(0, count)], rows_branch).start()
    stores.append(p.copy(value, grad_middle).start())
    gain_sum[0:1] = jnp.sum(gain_sum[...], axis=0, keepdims=True)
    gain_sum[1:2] = jnp.sum(shift_sum[...], axis=0, keepdims=True)
    stores.append(p.copy(gain_sum, sums).start())
    scatter.beside.left()
    out_scatter.sibling.arrived()
    combine(near_out, [near_out, got_out], 32)
    stores.append(p.copy(near_out, out_half).start())
    gather.relay()
    gate_sum.relay()
    down_sum.finish(down_owned)
    gate_sum.gather()
    for k in (0, 1):
        stores.append(p.copy(gate_sum.half(gate_quarters[2 + k], 0), gate_sums.at[k]).start())
    gate_sum.left()
    down_sum.stored()
    gather.finish()
    out_scatter.sibling.left()
    wait_all(stores)


def last_kernel(
    rows_branch, out_full, heads_in, mixed_in, rows_one, proj_full, inputs, vectors,
    turns, grad_middle, sums, up_parts, gate_sums, out_half, middle,
    outputs, input_grads, proj_owned, out_owned, vector_grads, bias_grad, gu_owned,
    branch, out_here, heads, mixed, grad_mixed, grad_pre, rows_here, proj_here, out_send,
    own, got, got_beside, result, all_sums, shift_sum, vector_got, vector_total, z_got,
    bias_here, bias_got, turns_here, got_out, gate_home, gate_even, up_result, out_result, third_result, *rest,
):
    weight_refs = [rest[4 * k : 4 * k + 4] for k in range(5)]
    p = Place(*rest[20:])
    count, width = own.shape
    quarter = width // 4
    late = lax.rem(p.tensor, 2)
    tables = [turns_here.at[k] for k in range(3)]
    first, second = p.core == 0, p.core == 1
    first_loads = [p.copy(rows_branch, branch).start(), p.copy(out_full, out_here).start()]
    p.greet()

    def weight_sum(send, rows, refs, total):
        keep, got_quarters, last, home = refs
        return ScatterWeight(
            p, send, [keep.at[0], keep.at[1]], rows, got_quarters, last, home, total
        )

    up_quarters = [up_parts.at[pl.ds(k * quarter, quarter)] for k in range(4)]
    up = weight_sum(up_quarters[:2], True, weight_refs[0], up_result).start()
    gate = HomeSum(p, gate_sums.at[0], gate_sums.at[1], gate_even, gate_home, up_result).start()
    out = weight_sum([out_send.at[0], out_send.at[1]], False, weight_refs[1], out_result)
    proj_send = [[heads.at[j, pl.ds(k * quarter, quarter)] for k in (0, 1)] for j in range(3)]
    thirds = [
        weight_sum(proj_send[j], True, weight_refs[2 + j], third_result.at[j]) for j in range(3)
    ]
    out_beside = p.send(out_half.at[pl.ds(count, count)], got_out, p.at(near=1)).start()
    out_loads = [p.copy(out_half.at[pl.ds(0, count)], own).start(), p.copy(middle, result).start()]
    wait_all(first_loads)
    mixed_load = p.copy(mixed_in, mixed).start()
    head_load = p.copy(heads_in, heads).start()
    out_loads.append(p.copy(turns, turns_here).start())

    @pl.loop(0, 4)
    def _(index):
        rows = pl.ds(pl.multiple_of(index * HALF, HALF), HALF)
        _, target = swapped_half(index, late)
        grad_mixed[target] = dot(branch[rows], out_here[...], (1, 1)).astype(grad_mixed.dtype)

    mixed_load.wait()

    def out_part(k):
        target = out_send.at[k] if k < 2 else weight_refs[1][0].at[k - 2]
        target[...] = dot(
            mixed[...], branch[:, pl.ds(k * quarter, quarter)], (0, 0)
        ).astype(target.dtype)

    for k in range(4):
        out_part(k)
    head_load.wait()
    later_loads = [p.copy(proj_full, proj_here).start(), p.copy(rows_one, rows_here).start()]
    wait_all(out_loads)
    gate_load = p.copy(gate_sums.at[0], gate_even).start()
    up.load(up_quarters[2:])
    attend_pair_back(heads, grad_mixed, grad_pre, tables, late)
    wait_all(later_loads)
    up.relay()
    near, far = branch.at[pl.ds(0, 2 * count)], branch.at[pl.ds(2 * count, 2 * count)]
    scatter = ScatterRows(p, far, near, got, got_beside)

    def term_rows(target, offset):
        def part(rows):
            here = shifted(rows, offset)
            total = dot(grad_pre[0, here], proj_here[0], (1, 1))
            for j in (1, 2):
                total = total + dot(grad_pre[j, here], proj_here[j], (1, 1))
            target[rows] = total.astype(target.dtype)

        return part

    def proj_part(j, k):
        target = proj_send[j][k] if k < 2 else weight_refs[2 + j][0].at[k - 2]
        target[...] = dot(
            rows_here[:, pl.ds(k * quarter, quarter)], grad_pre[j], (0, 0)
        ).astype(target.dtype)

    tiles(2 * count, 256, term_rows(far, 2 * count))
    scatter.start()
    tiles(2 * count, 256, term_rows(near, 0))
    scatter.relay()
    out_beside.arrived()

    def out_total(rows):
        total = result[rows] + own[rows].astype(jnp.float32) + got_out[rows].astype(jnp.float32)
        own[rows] = total.astype(own.dtype)

    tiles(count, CHUNK, out_total)
    stores = store_natural(p, own, outputs)
    for j in range(3):
        proj_part(j, 0)
        proj_part(j, 1)
    up.settle()
    out.start()
    thirds[0].start()
    thirds[1].start()
    wait_all(stores)
    loads = load_local(p, inputs, own)
    loads.append(p.copy(grad_middle, result).start())
    for j in range(3):
        proj_part(j, 2)
        proj_part(j, 3)
    out.relay()

    bias_here[...] = jnp.zeros_like(bias_here)
    for j in range(3):
        def bias_rows(rows):
            bias_here[j : j + 1] += jnp.sum(
                grad_pre[j, rows].astype(jnp.float32), axis=0, keepdims=True
            )

        tiles(4 * count, 256, bias_rows)
    bias_x = p.send(bias_here, bias_got.at[0], p.at(x=1)).start()
    bias_x.arrived()
    bias_x.left()
    bias_here[...] += bias_got[0]
    bias_y = p.send(bias_here, bias_got.at[1], p.at(y=1)).start()
    gate_load.wait()
    gate.finish(gu_owned.at[0])
    bias_y.arrived()
    bias_y.left()
    bias_here[...] += bias_got[1]
    near_sem, far_sem = p.take("recv"), p.take("recv")
    bias_home = [
        p.send(bias_here, bias_got.at[2], p.at(core=1), near_sem, first).start(),
        p.send(bias_here, bias_got.at[2], p.at(core=1, far=1), near_sem, second).start(),
        p.send(bias_here, bias_got.at[3], p.at(far=1), far_sem, second).start(),
    ]
    thirds[0].relay()
    thirds[2].start()
    out.settle()
    wait_all(loads)
    scatter.arrived()
    gain = vectors[0:1]
    all_sums[...] = jnp.zeros_like(all_sums)
    shift_sum[...] = jnp.zeros_like(shift_sum)

    def first_back(rows):
        incoming = scatter.total(rows)
        back, product = norm_back_rows(own[rows].astype(jnp.float32), incoming, gain)
        all_sums[...] += fold(product)
        shift_sum[...] += fold(incoming)
        result[rows] = result[rows] + back

    tiles(count, CHUNK, first_back)
    stores = store_natural(p, result, input_grads)
    all_sums[0:1] = jnp.sum(all_sums[...], axis=0, keepdims=True)
    all_sums[1:2] = jnp.sum(shift_sum[...], axis=0, keepdims=True)
    all_sums[2:4] = sums[0:2]
    slots = {key: j for j, key in enumerate(ORDER)}
    vector_sends = []
    for dy in (0, 1):
        for dx in (0, 1):
            for core in (0, 1):
                if not (dy or dx or core):
                    continue
                straight, crossed = slots[(dy, dx, core)], slots[(dy, dx, 1 - core)]
                slot = straight + p.core * (crossed - straight)
                columns = pl.ds(pl.multiple_of(slot * EIGHTH, EIGHTH), EIGHTH)
                vector_sends.append(
                    p.send(
                        all_sums.at[:, columns], vector_got.at[len(vector_sends)],
                        p.at(x=dx, y=dy, core=core),
                    ).start()
                )
    thirds[1].relay()
    thirds[0].settle()
    own_slot = slots[(0, 0, 0)] + p.core * (slots[(0, 0, 1)] - slots[(0, 0, 0)])
    total = all_sums[:, pl.ds(pl.multiple_of(own_slot * EIGHTH, EIGHTH), EIGHTH)]
    for k, sent in enumerate(vector_sends):
        sent.arrived()
        total = total + vector_got[k]
    vector_total[0] = total
    z_near = p.send(vector_total.at[0], z_got.at[0], p.at(near=1)).start()
    thirds[2].relay()
    thirds[1].settle()
    z_near.arrived()
    vector_total[1] = vector_total[0] + z_got[0]
    z_far = p.send(vector_total.at[1], z_got.at[1], p.at(far=1)).start()
    thirds[2].settle()
    z_far.arrived()
    z_near.left()
    z_far.left()
    vector_total[0] = vector_total[1] + z_got[1]
    vector_store = p.copy(vector_total.at[0], vector_grads).start()
    bias_home[0].arrived()
    bias_home[2].arrived(second)
    for sent in bias_home:
        sent.left()
    pl.when(second)(lambda: combine(bias_got.at[2], [bias_got.at[2], bias_got.at[3]], 8))
    pl.when(first)(lambda: combine(bias_got.at[2], [bias_got.at[2], bias_here], 8))
    bias_store = p.copy(bias_got.at[2], bias_grad).start()
    gate.stored()
    up.finish(gu_owned.at[1])
    out.finish(out_owned)
    for j in range(3):
        thirds[j].finish(proj_owned.at[j])
    for weight in (up, out, *thirds):
        weight.stored()
    scatter.finish()
    for sent in vector_sends:
        sent.left()
    out_beside.left()
    wait_all(stores)
    vector_store.wait()
    bias_store.wait()


def call(body, name, collective, inputs, in_specs, outs, scratch, counts):
    bf16_bytes = sum(math.prod(o.shape) * o.dtype.itemsize for o in outs)
    return pl.pallas_call(
        body,
        out_shape=outs,
        in_specs=in_specs,
        out_specs=[ANY] * len(outs),
        scratch_shapes=[
            *scratch,
            pltpu.SemaphoreType.DMA((counts[0],)),
            pltpu.SemaphoreType.DMA((counts[1],)),
            pltpu.SemaphoreType.DMA((counts[2],)),
        ],
        compiler_params=pltpu.CompilerParams(
            collective_id=collective, has_side_effects=True, vmem_limit_bytes=VMEM_BYTES
        ),
        cost_estimate=pl.CostEstimate(
            flops=0, bytes_accessed=2 * bf16_bytes, transcendentals=0
        ),
        name=name,
    )(*inputs)


def bf16(*shape):
    return jax.ShapeDtypeStruct(shape, jnp.bfloat16)


def f32(*shape):
    return jax.ShapeDtypeStruct(shape, jnp.float32)


def held(shape_struct):
    return pltpu.VMEM(shape_struct.shape, shape_struct.dtype)


def weight_scratch(quarter, eighth):
    return [
        held(bf16(2, *quarter)), held(bf16(2, *quarter)), held(bf16(2, *eighth)),
        held(bf16(2, *eighth)),
    ]


WHOLE = pl.BlockSpec(memory_space=pltpu.VMEM)
EIGHTH = 256


def local_pairs(
    inputs,
    gain_first,
    shift_first,
    projections,
    biases,
    output_weight,
    gain_second,
    shift_second,
    gate_up,
    down_weight,
    cotangent,
):
    count, width = inputs.shape
    rows = 4 * count
    heads_width = output_weight.shape[0]
    hidden_width = down_weight.shape[0]
    cosine, sine = angle_tables()
    rest = ((0, 0), (0, HD - ROTARY))
    turns = jnp.stack([
        jnp.tile(jnp.pad(table, rest, constant_values=fill), (1, 128 // HD))
        for table, fill in (
            (jnp.concatenate([cosine, cosine], axis=1), 1.0),
            (jnp.concatenate([-sine, jnp.zeros_like(sine)], axis=1), 0.0),
            (jnp.concatenate([jnp.zeros_like(sine), sine], axis=1), 0.0),
        )
    ])
    wide = bf16(rows, width)
    inner = bf16(rows, hidden_width)
    own = bf16(count, width)
    half_rows = bf16(2 * count, width)
    (
        proj_full, out_full, gu_full, down_full, vectors, gathered_one, gathered_cot, heads, mixed_rows,
        middle, gathered_two, hidden, gate_act, up_act, down_parts,
    ) = call(
        forward_kernel, "forward", 1,
        (
            inputs, cotangent,
            jnp.concatenate([gain_first, shift_first, gain_second, shift_second]).reshape(4, -1),
            biases, turns,
            projections, output_weight, gate_up, down_weight,
        ),
        [ANY] * 2 + [WHOLE] * 2 + [ANY] * 5,
        [
            bf16(3, width, heads_width), bf16(heads_width, width), bf16(2, width, hidden_width),
            bf16(hidden_width, width), f32(8, width), wide, wide, bf16(3, rows, heads_width),
            bf16(rows, heads_width), f32(count, width), wide, inner, inner, inner,
            bf16(4, hidden_width, 2 * EIGHTH),
        ],
        [
            held(own), held(own), held(own), held(f32(8, width)), held(f32(8, heads_width)),
            held(bf16(3, width, heads_width)), held(bf16(heads_width, width)), held(wide),
            held(bf16(3, rows, heads_width)), held(bf16(rows, heads_width)),
            held(half_rows), held(half_rows), held(half_rows), held(own), held(f32(count, width)),
            held(wide), held(bf16(2, width, hidden_width)), held(f32(rows, hidden_width)),
            held(inner), held(inner), held(inner), held(f32(8, EIGHTH)), held(f32(8, heads_width)),
            held(f32(*turns.shape)),
        ],
        (128, 96, 64),
    )

    by_rows = ((2 * EIGHTH, hidden_width), (EIGHTH, hidden_width))
    by_columns = ((hidden_width, 2 * EIGHTH), (hidden_width, EIGHTH))
    (
        out_half, grad_middle, gathered_branch, sums, down_owned, gate_sums, up_parts,
    ) = call(
        back_kernel, "backward_first", 2,
        (
            hidden, gate_act, up_act, gathered_cot, gathered_two, gu_full, down_full, down_parts,
            middle, vectors,
        ),
        [ANY] * 9 + [WHOLE],
        [
            half_rows, f32(count, width), wide, f32(8, width), f32(hidden_width, EIGHTH),
            bf16(2, EIGHTH, hidden_width), bf16(width, hidden_width),
        ],
        [
            held(inner), held(inner), held(inner), held(wide), held(wide),
            held(bf16(width, hidden_width)), held(bf16(width, hidden_width)),
            held(bf16(hidden_width, width)), held(f32(count, width)),
            held(half_rows), held(half_rows), held(own), held(half_rows),
            held(f32(8, width)), held(f32(8, width)), held(bf16(2, hidden_width, 2 * EIGHTH)),
            *weight_scratch(*by_columns)[1:], held(f32(hidden_width, EIGHTH)),
            *weight_scratch(*by_rows)[1:3],
        ],
        (64, 64, 48),
    )
    third = ((2 * EIGHTH, heads_width), (EIGHTH, heads_width))
    outputs, input_grads, proj_owned, out_owned, vector_grads, bias_grad, gu_owned = call(
        last_kernel, "backward_last", 3,
        (
            gathered_branch, out_full, heads, mixed_rows, gathered_one, proj_full, inputs, vectors,
            turns, grad_middle, sums, up_parts, gate_sums,
            out_half, middle,
        ),
        [ANY] * 7 + [WHOLE] + [ANY] * 2 + [WHOLE] + [ANY] * 4,
        [
            own, f32(count, width), f32(3, EIGHTH, heads_width), f32(heads_width, EIGHTH),
            f32(8, EIGHTH), f32(8, heads_width), f32(2, EIGHTH, hidden_width),
        ],
        [
            held(wide), held(bf16(heads_width, width)), held(bf16(3, rows, heads_width)),
            held(bf16(rows, heads_width)), held(bf16(rows, heads_width)),
            held(bf16(3, rows, heads_width)), held(wide), held(bf16(3, width, heads_width)),
            held(bf16(2, heads_width, 2 * EIGHTH)),
            held(own), held(half_rows), held(own), held(f32(count, width)),
            held(f32(8, width)), held(f32(8, width)),
            held(f32(7, 8, EIGHTH)), held(f32(2, 8, EIGHTH)), held(f32(2, 8, EIGHTH)),
            held(f32(8, heads_width)), held(f32(4, 8, heads_width)), held(f32(*turns.shape)),
            held(own),
            held(bf16(2, EIGHTH, hidden_width)), held(bf16(EIGHTH, hidden_width)),
            held(f32(EIGHTH, hidden_width)), held(f32(heads_width, EIGHTH)),
            held(f32(3, EIGHTH, heads_width)),
            *weight_scratch(*by_rows),
            *weight_scratch((heads_width, 2 * EIGHTH), (heads_width, EIGHTH)),
            *weight_scratch(*third), *weight_scratch(*third), *weight_scratch(*third),
        ],
        (64, 64, 48),
    )
    return (
        outputs,
        input_grads,
        vector_grads[0],
        vector_grads[1],
        proj_owned,
        bias_grad[:3],
        out_owned,
        vector_grads[2],
        vector_grads[3],
        gu_owned,
        down_owned,
    )


def solution(mesh):
    whole_pairs = dict(mesh.shape) == {"dp": 8, "tensor": 4}
    return jax.shard_map(
        local_pairs if whole_pairs else local,
        mesh=mesh,
        in_specs=(
            P(("dp", "tensor"), None),
            P("dp"),
            P("dp"),
            P(None, "dp", "tensor"),
            P(None, "tensor"),
            P("tensor", "dp"),
            P("dp"),
            P("dp"),
            P(None, "dp", "tensor"),
            P("tensor", "dp"),
            P(("dp", "tensor"), None),
        ),
        out_specs=(
            P(("dp", "tensor"), None),
            P(("dp", "tensor"), None),
            P("dp"),
            P("dp"),
            P(None, "dp", "tensor"),
            P(None, "tensor"),
            P("tensor", "dp"),
            P("dp"),
            P("dp"),
            P(None, "dp", "tensor"),
            P("tensor", "dp"),
        ),
        check_vma=False,
    )
```
